32 devices in a mesh: groups: 2 (over y), inst: 4 (over z), tp: 4 (over x, core).
Axes of the slice: x: 2, y: 2, z: 4, core: 2. Of those that a mesh axis runs over, the one named last changes fastest.
Arguments:
- queries: bfloat16 [256, 2, 64, 128], P(('groups', 'inst'), None, 'tp'), parts along dimension 0, may hold values from -48 to 48
- new_kv: bfloat16 [256, 2, 2, 8, 128], P(('groups', 'inst'), None, None, 'tp'), parts along dimension 0, may hold values from -4 to 4
- pool_codes: bfloat16 [384, 2, 8, 128, 128], P(('groups', 'inst'), None, 'tp'), parts along dimension 0, may hold values from -6 to 6
- pool_scales: bfloat16 [384, 2, 8], P(('groups', 'inst'), None, 'tp'), parts along dimension 0, may hold values from 0.19921875 to 2.5
- tables: int32 [256, 16], P(('groups', 'inst')), parts along dimension 0, may hold values from 0 to 55, as said below
- ctx_len: int32 [256], P(('groups', 'inst')), parts along dimension 0, may hold values from 1 to 2048
- mig_block: int32 [8, 4], P(('groups', 'inst')), parts along dimension 0, may hold values from 0 to 47, as said below
- mig_dest: int32 [8, 4], P(('groups', 'inst')), parts along dimension 0, may hold values from 0 to 3, as said below
Outputs:
- attn_out: bfloat16 [256, 2, 8192], P(('groups', 'inst'), None, 'tp'), parts along dimension 0
- moved_to: int32 [8, 4], P(('groups', 'inst')), parts along dimension 0
The draws below stay inside these ranges and needn't reach their ends.
There are 2 independent parts, one for each index of `groups`. The reference program is written for one: setup_inputs(seed, part) draws one part's arguments, and reference() takes and returns one part's arrays. A program takes and returns all parts, laid end to end along the dimension named above; each array names one. Nothing has to cross between parts.
Inputs may be any that keep to these rules, and one draw needn't show every extreme that they name: `mig_dest`: at most 2 of one instance's listed blocks go to one destination, and in every draw one destination receives 2 from every instance. `mig_block`: the blocks listed by one instance are distinct. `tables`: entries below 48 name the instance's own blocks; an entry 48 + a names the a-th block arriving there, arrivals ordered by source instance and then by list position; every entry is below 48 plus the number of blocks arriving at that instance. Entries may repeat.
All inputs are finite; a program needn't handle non-finite values.
Results may differ from the reference program's by a relative error of at most 0.0034.
Values may be sent and summed in bfloat16 or wider, within the bound.
No kernel may reach another device: no remote copies, remote signals or barrier semaphores. Data moves between devices by JAX's collectives and lax.ppermute only.
A program may use at most 64 MiB of HBM per device.

```python
import math
import jax
import jax.numpy as jnp
from jax import lax

QH = 64
KVH = 8
HD = 128
BLK = 128
STEPS = 2
RQ = 32
MAXB = 16
POOL = 48
CAP = 2
MB = 4
POOLS = 192
N_INST = 4


def routing(key):
    hot = jax.random.randint(jax.random.fold_in(key, 101), (), 0, N_INST).astype(jnp.int32)
    source_keys = jax.random.split(jax.random.fold_in(key, 102), N_INST)

    def one_source(sub):
        others = jax.random.permutation(jax.random.fold_in(sub, 1), N_INST - 1).astype(jnp.int32)
        others = others + (others >= hot).astype(jnp.int32)
        chosen = jnp.concatenate([jnp.stack([hot, hot]), others[:MB - 2]])
        return jax.random.permutation(jax.random.fold_in(sub, 2), chosen)
    return (jax.vmap(one_source)(source_keys).astype(jnp.int32), hot)


def draw_mig_dest(key, part):
    routes, hot = routing(key)
    return routes


def draw_tables(key, part):
    routes, hot = routing(key)
    key = jax.random.fold_in(key, 7)
    counts = jnp.sum((routes[:, :, None] == jnp.arange(N_INST)[None, None, :]).astype(jnp.int32), axis=(0, 1))
    limit = jnp.repeat(POOL + counts, RQ)[:, None]
    entries = jax.random.randint(key, (N_INST * RQ, MAXB), 0, limit).astype(jnp.int32)
    return entries.at[hot * RQ, 0].set(POOL + N_INST * CAP - 1)


def draw_ctx_len(key, part):
    key = jax.random.fold_in(key, 11)
    first, second, third, fourth = jax.random.split(key, 4)
    most = MAXB * BLK
    caps = jax.random.randint(first, (N_INST,), most // 4, most + 1)
    pick = jax.random.randint(second, (), 0, N_INST)
    caps = caps.at[pick].set(most)
    lengths = jax.random.randint(third, (N_INST, RQ), 1, caps[:, None] + 1)
    row = jax.random.randint(fourth, (), 0, RQ)
    lengths = lengths.at[pick, row].set(most)
    return lengths.reshape(-1).astype(jnp.int32)


def draw_mig_block(key, part):
    key = jax.random.fold_in(key, 13)
    source_keys = jax.random.split(key, N_INST)

    def one_source(sub):
        chosen = jax.random.permutation(jax.random.fold_in(sub, 1), POOL - 1)[:MB - 1]
        full = jnp.concatenate([chosen, jnp.array([POOL - 1])]).astype(jnp.int32)
        return jax.random.permutation(jax.random.fold_in(sub, 3), full)
    return jax.vmap(one_source)(source_keys).astype(jnp.int32)


def draw_queries(key, part):
    shape = (N_INST * RQ, STEPS, QH, HD)
    key = jax.random.fold_in(key, 19)
    return jnp.clip(jax.random.normal(key, shape, jnp.float32), -4.0, 4.0).astype(jnp.bfloat16)


def draw_new_kv(key, part):
    shape = (N_INST * RQ, STEPS, 2, KVH, HD)
    key = jax.random.fold_in(key, 23)
    return jnp.clip(jax.random.normal(key, shape, jnp.float32), -4.0, 4.0).astype(jnp.bfloat16)


def block_levels(rng, extent, pieces, low, largest):
    loudness, own = 1.0, jax.random.fold_in(rng, 6)
    for position, blocks in pieces:
        steps = jnp.exp(jax.random.uniform(jax.random.fold_in(own, position), (blocks,), jnp.float32, low / len(pieces), largest / len(pieces)))
        loudness = loudness * jnp.repeat(steps, extent[position] // blocks).reshape([-1 if axis == position else 1 for axis in range(len(extent))])
    return loudness


def bell_draw(own_key, shape, deviation, most, shards=(), kind=jnp.bfloat16):
    level = block_levels(own_key, shape, shards, -0.22, 0.18) if shards else 1.0
    values = jax.random.normal(own_key, shape, jnp.float32) * deviation * level
    return jnp.minimum(jnp.maximum(values, -most), most).astype(kind)


def setup_inputs(seed: int = 0, part: int = 0) -> dict:
    seeds = jax.random.split(jax.random.key(seed), 9)
    part_keys = jax.random.split(jax.random.fold_in(seeds[8], part), 9)
    return {
        "queries": draw_queries(jax.random.fold_in(jax.random.fold_in(seeds[8], part), 71), part),
        "new_kv": draw_new_kv(jax.random.fold_in(jax.random.fold_in(seeds[8], part), 71), part),
        "pool_codes": bell_draw(part_keys[2], (POOLS, 2, KVH, BLK, HD), 1.0, 6.0, ((0, 4), (2, 4))),
        "pool_scales": jnp.clip(jnp.exp(math.log(2.5) - 2.5296425 * jax.random.uniform(part_keys[3], (POOLS, 2, KVH), jnp.float32) ** block_levels(part_keys[3], (POOLS, 2, KVH), ((0, 4), (2, 4)), -0.2, 0.2)), 0.19921875, 2.5).astype(jnp.bfloat16),
        "tables": draw_tables(jax.random.fold_in(jax.random.fold_in(seeds[8], part), 71), part),
        "ctx_len": draw_ctx_len(jax.random.fold_in(jax.random.fold_in(seeds[8], part), 71), part),
        "mig_block": draw_mig_block(jax.random.fold_in(jax.random.fold_in(seeds[8], part), 71), part),
        "mig_dest": draw_mig_dest(jax.random.fold_in(jax.random.fold_in(seeds[8], part), 71), part),
    }


def attend(query_row, new_row, codes, scales, length):
    head_dim = query_row.shape[-1]
    factor = head_dim ** -0.5
    kv_heads = new_row.shape[2]
    query = query_row.astype(jnp.float32).reshape(STEPS, kv_heads, QH // KVH, head_dim)
    key_codes = codes[:, 0].astype(jnp.float32)
    value_codes = codes[:, 1].astype(jnp.float32)
    key_scale = scales[:, 0].astype(jnp.float32)
    value_scale = scales[:, 1].astype(jnp.float32)
    cached = jnp.einsum('tkgd,bkpd->tkgbp', query, key_codes) * key_scale.T[None, :, None, :, None] * factor
    place = jnp.arange(MAXB)[:, None] * BLK + jnp.arange(BLK)[None, :]
    live = place < length
    cached = jnp.where(live[None, None, None], cached, -jnp.inf)
    fresh_keys = new_row[:, 0].astype(jnp.float32)
    fresh = jnp.einsum('tkgd,ukd->tkgu', query, fresh_keys) * factor
    causal = jnp.arange(STEPS)[None, :] <= jnp.arange(STEPS)[:, None]
    fresh = jnp.where(causal[:, None, None, :], fresh, -jnp.inf)
    top = jnp.maximum(jnp.max(cached, axis=(3, 4)), jnp.max(fresh, axis=3))
    weights = jnp.exp(cached - top[..., None, None])
    fresh_w = jnp.exp(fresh - top[..., None])
    total = jnp.sum(weights, axis=(3, 4)) + jnp.sum(fresh_w, axis=3)
    scaled = (weights * value_scale.T[None, :, None, :, None]).astype(jnp.bfloat16)
    scaled = lax.optimization_barrier(scaled).astype(jnp.float32)
    fresh_b = lax.optimization_barrier(fresh_w.astype(jnp.bfloat16)).astype(jnp.float32)
    mixed = jnp.einsum('tkgbp,bkpd->tkgd', scaled, value_codes)
    mixed = mixed + jnp.einsum('tkgu,ukd->tkgd', fresh_b, new_row[:, 1].astype(jnp.float32))
    return (mixed / total[..., None]).astype(jnp.bfloat16).reshape(STEPS, -1)


def reference(queries, new_kv, pool_codes, pool_scales, tables, ctx_len, mig_block, mig_dest):
    instances = N_INST
    listed = mig_dest.shape[1]
    order = jnp.arange(listed)
    same = (mig_dest[:, :, None] == mig_dest[:, None, :]) & (order[None, None, :] < order[None, :, None])
    rank = jnp.sum(same.astype(jnp.int32), axis=2)
    hits = (mig_dest[:, :, None] == jnp.arange(instances)[None, None, :]).astype(jnp.int32)
    counts = jnp.sum(hits, axis=1)
    before = jnp.cumsum(counts, axis=0) - counts
    base = jnp.sum(hits * before[:, None, :], axis=2)
    moved_to = (POOL + base + rank).astype(jnp.int32)
    anchor = (jnp.arange(instances)[:, None] * POOL + mig_block).astype(jnp.int32)
    arrivals = jnp.zeros((instances, instances * CAP), jnp.int32)
    arrivals = arrivals.at[mig_dest.reshape(-1), (moved_to - POOL).reshape(-1)].set(anchor.reshape(-1))
    owner = (jnp.arange(instances * RQ) // RQ).astype(jnp.int32)
    arrival_id = jnp.clip(tables - POOL, 0, instances * CAP - 1).astype(jnp.int32)
    global_id = jnp.where(tables < POOL, owner[:, None] * POOL + tables, arrivals[owner[:, None], arrival_id])

    def one_row(index):
        ids = global_id[index]
        return attend(queries[index], new_kv[index], pool_codes[ids], pool_scales[ids], ctx_len[index])

    outputs = lax.map(one_row, jnp.arange(instances * RQ))
    return outputs, moved_to
```

```python
import functools
import math

import jax
import jax.numpy as jnp
from jax import lax
from jax.experimental import pallas as pl
from jax.experimental.pallas import tpu as pltpu
from jax.sharding import PartitionSpec as P

CAP = 2
LOG2E = math.log2(math.e)
MIB = 1 << 20
SMEM_SPEC = pl.BlockSpec(memory_space=pltpu.SMEM)
VMEM_SPEC = pl.BlockSpec(memory_space=pltpu.VMEM)
ANY_SPEC = pl.BlockSpec(memory_space=pl.ANY)
NT = (((1,), (1,)), ((), ()))


def pack_kernel(instances, listed, dest_ref, block_ref, pool_ref, *rest):
    send_refs, (index_ref, sems) = rest[:instances], rest[instances:]
    me = lax.axis_index("inst")

    def clear(slot, carry):
        index_ref[slot] = 0
        return carry

    lax.fori_loop(0, instances * CAP, clear, 0)

    def place(m, carry):
        dest = dest_ref[0, m]

        def earlier(m2, rank):
            return rank + jnp.where(dest_ref[0, m2] == dest, 1, 0)

        rank = jnp.minimum(lax.fori_loop(0, m, earlier, 0), CAP - 1)
        shift = lax.rem(dest - me + instances, instances)
        index_ref[shift * CAP + rank] = block_ref[0, m]
        return carry

    lax.fori_loop(0, listed, place, 0)
    copies = []
    for shift in list(range(1, instances)) + [0]:
        for rank in range(CAP):
            slot = shift * CAP + rank
            copies.append(
                pltpu.make_async_copy(
                    pool_ref.at[index_ref[slot]], send_refs[shift].at[rank], sems.at[slot]
                )
            )
            copies[-1].start()
    for copy in copies:
        copy.wait()


def count_log(tables, length, ids, block_len, spans, store):
    requests, width = tables.shape[0], ids.shape[1]
    whole = length // block_len
    rest = length - whole * block_len
    full = jnp.zeros((requests, width), jnp.float32)
    part = jnp.zeros((requests, width), jnp.float32)
    for e in range(spans):
        hit = tables[:, e : e + 1] == ids
        full = full + jnp.where(hit & (whole > e), 1.0, 0.0)
        part = part + jnp.where(hit & (whole == e), 1.0, 0.0)
    inside = lax.broadcasted_iota(jnp.int32, (requests, block_len), 1) < rest
    for b in range(width):
        count = jnp.broadcast_to(full[:, b : b + 1], (requests, block_len)) + jnp.where(
            inside, jnp.broadcast_to(part[:, b : b + 1], (requests, block_len)), 0.0
        )
        store(b, jnp.where(count > 0, jnp.log(jnp.maximum(count, 1.0)) * LOG2E, -jnp.inf))


def score_tiles(query, keys, log_ref, scale_row, rows, store):
    height, wide = min(256, query.shape[0]), min(256, keys.shape[0])
    for top in range(0, query.shape[0], height):
        for left in range(0, keys.shape[0], wide):
            part = lax.dot_general(
                query[top : top + height],
                keys[left : left + wide],
                NT,
                preferred_element_type=jnp.float32,
            )
            scale = scale_row[:, left : left + wide]
            for r in range(height // rows):
                request = top // rows + r
                store(
                    request * rows,
                    left,
                    part[r * rows : (r + 1) * rows] * scale
                    + log_ref[request : request + 1, left : left + wide],
                )


def lane_fold(value, op):
    parts = [value[:, i : i + 128] for i in range(0, value.shape[1], 128)]
    while len(parts) > 1:
        parts = [
            op(parts[i], parts[i + 1]) if i + 1 < len(parts) else parts[i]
            for i in range(0, len(parts), 2)
        ]
    return parts[0]


def spread(column, width):
    return jnp.concatenate([column] * (width // 128), axis=1)


def own_kernel(
    dims,
    tables_ref, length_ref, scale_ref, q_ref, fresh_ref, codes_ref,
    acc_ref, top_ref, total_ref,
    log_ref, row_ref, t_ref, new_ref, p_ref,
):
    pool, heads, rows, steps, block_len, spans, factor, group = dims
    phase, chunk = pl.program_id(0), pl.program_id(1)
    chunks = pool // group
    height = q_ref.shape[1]
    width = group * block_len

    @pl.when((phase == 0) & (chunk == 0))
    def _():
        ids = lax.broadcasted_iota(jnp.int32, (1, pool), 1)

        def store(b, value):
            lane = (b % group) * block_len
            log_ref[b // group, :, lane : lane + block_len] = value

        count_log(tables_ref[...], length_ref[...], ids, block_len, spans, store)
        for b in range(pool):
            lane = (b % group) * block_len
            for h in range(heads):
                row_ref[b // group, h : h + 1, lane : lane + block_len] = jnp.full(
                    (1, block_len), scale_ref[0, h * pool + b] * (factor * LOG2E)
                )
                row_ref[b // group, heads + h : heads + h + 1, lane : lane + block_len] = jnp.full(
                    (1, block_len), scale_ref[0, (heads + h) * pool + b]
                )
        shape = (height, fresh_ref.shape[2])
        row = lax.broadcasted_iota(jnp.int32, shape, 0)
        col = lax.broadcasted_iota(jnp.int32, shape, 1)
        seen = (col // steps == row // rows) & (col % steps <= row % steps)
        for h in range(heads):
            score = lax.dot_general(
                q_ref[h], fresh_ref[0, h], NT, preferred_element_type=jnp.float32
            )
            score = jnp.where(seen, score * (factor * LOG2E), -jnp.inf)
            new_ref[h] = score
            top_ref[h] = lane_fold(score, jnp.maximum)

    @pl.when(phase == 0)
    def _():
        for h in range(heads):

            def store(row, lane, value, h=h):
                t_ref[h, chunk, row : row + rows, lane : lane + value.shape[1]] = value

            score_tiles(
                q_ref[h],
                codes_ref[:, 0, h].reshape(width, codes_ref.shape[-1]),
                log_ref.at[chunk],
                row_ref[chunk, h : h + 1, :],
                rows,
                store,
            )
            for row in range(0, height, rows):
                at = pl.ds(row, rows)
                top_ref[h, at] = jnp.maximum(
                    top_ref[h, at], lane_fold(t_ref[h, chunk, at], jnp.maximum)
                )

    @pl.when((phase == 1) & (chunk == 0))
    def _():
        for h in range(heads):
            top = jnp.broadcast_to(
                jnp.max(top_ref[h], axis=1, keepdims=True), (height, 128)
            )
            top_ref[h] = top
            weight = jnp.exp2(new_ref[h] - spread(top, new_ref.shape[2]))
            total_ref[h] = lane_fold(weight, jnp.add)
            acc_ref[h] = jnp.dot(
                weight.astype(jnp.bfloat16), fresh_ref[1, h], preferred_element_type=jnp.float32
            )

    @pl.when(phase == 1)
    def _():
        for h in range(heads):
            scale = row_ref[chunk, heads + h : heads + h + 1, :]
            for row in range(0, height, rows):
                at = pl.ds(row, rows)
                weight = jnp.exp2(t_ref[h, chunk, at] - spread(top_ref[h, at], width))
                total_ref[h, at] += lane_fold(weight, jnp.add)
                p_ref[h, at] = (weight * scale).astype(jnp.bfloat16)
            acc_ref[h] += jnp.dot(
                p_ref[h],
                codes_ref[:, 0, h].reshape(width, codes_ref.shape[-1]),
                preferred_element_type=jnp.float32,
            )

    @pl.when((phase == 1) & (chunk == chunks - 1))
    def _():
        for h in range(heads):
            total_ref[h] = jnp.broadcast_to(
                jnp.sum(total_ref[h], axis=1, keepdims=True), (height, 128)
            )


def route_kernel(
    dims, lists_ref, tables_ref, length_ref, moved_ref, log_ref, row_ref, counts_ref
):
    pool, heads, instances, listed, block_len, spans, factor = dims
    me = lax.axis_index("inst")

    def dest(shift, m):
        return lists_ref[shift, m].astype(jnp.int32)

    def count(shift, carry):
        def one(m, total):
            return total + jnp.where(dest(shift, m) == me, 1, 0)

        counts_ref[shift] = lax.fori_loop(0, listed, one, 0)
        return carry

    lax.fori_loop(0, instances, count, 0)

    def move(m, carry):
        target = dest(0, m)

        def same(m2, total):
            return total + jnp.where(dest(0, m2) == target, 1, 0)

        def lower(shift, total):
            def one(m2, inner):
                return inner + jnp.where(dest(shift, m2) == target, 1, 0)

            found = lax.fori_loop(0, listed, one, 0)
            return total + jnp.where(shift <= me, found, 0)

        moved_ref[0, m] = (
            pool + lax.fori_loop(0, m, same, 0) + lax.fori_loop(1, instances, lower, 0)
        )
        return carry

    lax.fori_loop(0, listed, move, 0)
    slots = instances * CAP
    lane = lax.broadcasted_iota(jnp.int32, (1, slots), 1)
    ids = jnp.full((1, slots), -1, jnp.int32)
    for shift in range(instances):
        source = lax.rem(me - shift + instances, instances)

        def before(other, total):
            other_source = lax.rem(me - other + instances, instances)
            return total + jnp.where(other_source < source, counts_ref[other], 0)

        first = lax.fori_loop(0, instances, before, 0)
        for rank in range(CAP):
            name = jnp.where(rank < counts_ref[shift], pool + first + rank, -1)
            ids = jnp.where(lane == shift * CAP + rank, name, ids)

            def find(m, carry):
                seen, block = carry
                hit = dest(shift, m) == me
                block = jnp.where(
                    hit & (seen == rank), lists_ref[shift, listed + m].astype(jnp.int32), block
                )
                return seen + jnp.where(hit, 1, 0), block

            _, block = lax.fori_loop(0, listed, find, (0, 0))
            at = (shift * CAP + rank) * block_len
            for h in range(heads):
                row_ref[h : h + 1, at : at + block_len] = jnp.full(
                    (1, block_len),
                    lists_ref[shift, 2 * listed + h * pool + block] * (factor * LOG2E),
                )
                row_ref[heads + h : heads + h + 1, at : at + block_len] = jnp.full(
                    (1, block_len), lists_ref[shift, 2 * listed + (heads + h) * pool + block]
                )

    def store(b, value):
        log_ref[:, b * block_len : (b + 1) * block_len] = value

    count_log(tables_ref[...], length_ref[...], ids, block_len, spans, store)


def arrival_kernel(
    dims, sources, q_ref, log_ref, row_ref, acc_ref, top_ref, total_ref, *rest
):
    heads, rows, block_len = dims
    code_refs, (out_ref, t_ref, p_ref) = rest[:sources], rest[sources:]
    height = q_ref.shape[1]
    width = CAP * block_len
    for h in range(heads):
        for s, codes_ref in enumerate(code_refs):
            left = s * width

            def store(row, lane, value, h=h, left=left):
                t_ref[h, row : row + rows, left + lane : left + lane + value.shape[1]] = value

            score_tiles(
                q_ref[h],
                codes_ref[:, 0, h].reshape(width, codes_ref.shape[-1]),
                log_ref.at[:, left : left + width],
                row_ref[h : h + 1, left : left + width],
                rows,
                store,
            )
    for h in range(heads):
        scale = row_ref[heads + h : heads + h + 1, :]
        for row in range(0, height, rows):
            at = pl.ds(row, rows)
            score = t_ref[h, at]
            own_top = top_ref[h, at]
            top = jnp.maximum(
                own_top, jnp.max(lane_fold(score, jnp.maximum), axis=1, keepdims=True)
            )
            weight = jnp.exp2(score - spread(top, score.shape[1]))
            keep = jnp.exp2(own_top - top)
            total = total_ref[h, at] * keep + jnp.sum(
                lane_fold(weight, jnp.add), axis=1, keepdims=True
            )
            p_ref[h, at] = (weight * scale).astype(jnp.bfloat16)
            t_ref[h, at, 0:128] = keep
            t_ref[h, at, 128:256] = 1.0 / total
        mixed = acc_ref[h] * t_ref[h, :, 0:128]
        for s, codes_ref in enumerate(code_refs):
            mixed = mixed + jnp.dot(
                p_ref[h, :, s * width : (s + 1) * width],
                codes_ref[:, 1, h].reshape(width, codes_ref.shape[-1]),
                preferred_element_type=jnp.float32,
            )
        result = (mixed * t_ref[h, :, 128:256]).astype(jnp.bfloat16)
        out_ref[:, h] = result.reshape(height // rows, rows, result.shape[-1])


def shards(queries, new_kv, pool_codes, pool_scales, tables, ctx_len, mig_block, mig_dest):
    instances = lax.axis_size("inst")
    pool = pool_codes.shape[0]
    requests, steps, q_heads, head_dim = queries.shape
    heads = new_kv.shape[3]
    per_head = q_heads // heads
    spans = tables.shape[1]
    block_len = pool_codes.shape[3]
    listed = mig_dest.shape[1]
    factor = head_dim ** (-0.5)
    rows = per_head * steps
    height = requests * rows
    slots = instances * CAP
    group = 8
    f32, bf16 = jnp.float32, jnp.bfloat16

    block_shape = pool_codes.shape[1:]
    send = pl.pallas_call(
        functools.partial(pack_kernel, instances, listed),
        out_shape=[jax.ShapeDtypeStruct((CAP,) + block_shape, bf16)] * instances,
        in_specs=[SMEM_SPEC, SMEM_SPEC, ANY_SPEC],
        out_specs=[ANY_SPEC] * instances,
        scratch_shapes=[pltpu.SMEM((slots,), jnp.int32), pltpu.SemaphoreType.DMA((slots,))],
        cost_estimate=pl.CostEstimate(
            flops=0, bytes_accessed=2 * slots * math.prod(block_shape) * 2, transcendentals=0
        ),
        name="pack_blocks",
    )(mig_dest, mig_block, pool_codes)

    def from_shift(value, shift):
        if shift == 0:
            return value
        return lax.ppermute(
            value, "inst", [(j, (j + shift) % instances) for j in range(instances)]
        )

    codes_in = [from_shift(send[shift], shift) for shift in range(instances)]

    flat_scales = jnp.transpose(pool_scales, (1, 2, 0)).reshape(1, -1).astype(f32)
    lists = jnp.concatenate([mig_dest.astype(f32), mig_block.astype(f32), flat_scales], axis=1)
    lists_in = jnp.concatenate(
        [from_shift(lists, shift) for shift in range(instances)], axis=0
    )

    query_rows = (
        queries.reshape(requests, steps, heads, per_head, head_dim)
        .transpose(2, 0, 3, 1, 4)
        .reshape(heads, height, head_dim)
    )
    fresh_len = requests * steps
    fresh = new_kv.transpose(2, 3, 0, 1, 4).reshape(2, heads, fresh_len, head_dim)
    fresh = jnp.pad(fresh, ((0, 0), (0, 0), (0, -fresh_len % 128), (0, 0)))
    length = ctx_len[:, None]
    width = group * block_len
    chunks = pool // group
    tokens = pool * block_len

    def whole(shape):
        return pl.BlockSpec(shape, lambda p, c: (0,) * len(shape))

    stat = (heads, height, head_dim)
    acc, top, total = pl.pallas_call(
        functools.partial(
            own_kernel, (pool, heads, rows, steps, block_len, spans, factor, group)
        ),
        grid=(2, chunks),
        out_shape=[jax.ShapeDtypeStruct(stat, f32)] * 3,
        in_specs=[
            whole(tables.shape),
            whole(length.shape),
            SMEM_SPEC,
            whole(query_rows.shape),
            whole(fresh.shape),
            pl.BlockSpec(
                (group, 1, heads, block_len, head_dim), lambda p, c: (c, p, 0, 0, 0)
            ),
        ],
        out_specs=[whole(stat)] * 3,
        scratch_shapes=[
            pltpu.VMEM((chunks, requests, width), f32),
            pltpu.VMEM((chunks, 2 * heads, width), f32),
            pltpu.VMEM((heads, chunks, height, width), f32),
            pltpu.VMEM((heads, height, fresh.shape[2]), f32),
            pltpu.VMEM((heads, height, width), bf16),
        ],
        compiler_params=pltpu.CompilerParams(vmem_limit_bytes=48 * MIB),
        cost_estimate=pl.CostEstimate(
            flops=4 * heads * height * tokens * head_dim,
            bytes_accessed=pool_codes.size * 2,
            transcendentals=heads * height * tokens,
        ),
        name="own_blocks",
    )(tables, length, flat_scales, query_rows, fresh, pool_codes)

    moved_to, log_in, rows_in = pl.pallas_call(
        functools.partial(
            route_kernel, (pool, heads, instances, listed, block_len, spans, factor)
        ),
        out_shape=[
            jax.ShapeDtypeStruct((1, listed), jnp.int32),
            jax.ShapeDtypeStruct((requests, slots * block_len), f32),
            jax.ShapeDtypeStruct((2 * heads, slots * block_len), f32),
        ],
        in_specs=[SMEM_SPEC, VMEM_SPEC, VMEM_SPEC],
        out_specs=[SMEM_SPEC, VMEM_SPEC, VMEM_SPEC],
        scratch_shapes=[pltpu.SMEM((instances,), jnp.int32)],
        name="route_arrivals",
    )(lists_in, tables, length)

    out = pl.pallas_call(
        functools.partial(arrival_kernel, (heads, rows, block_len), instances),
        out_shape=jax.ShapeDtypeStruct((requests, heads, rows, head_dim), bf16),
        in_specs=[VMEM_SPEC] * (6 + instances),
        out_specs=VMEM_SPEC,
        scratch_shapes=[
            pltpu.VMEM((heads, height, slots * block_len), f32),
            pltpu.VMEM((heads, height, slots * block_len), bf16),
        ],
        compiler_params=pltpu.CompilerParams(vmem_limit_bytes=48 * MIB),
        cost_estimate=pl.CostEstimate(
            flops=4 * heads * height * slots * block_len * head_dim,
            bytes_accessed=slots * math.prod(block_shape) * 2,
            transcendentals=heads * height * slots * block_len,
        ),
        name="arrived_blocks",
    )(query_rows, log_in, rows_in, acc, top, total, *codes_in)
    out = (
        out.reshape(requests, q_heads, steps, head_dim)
        .transpose(0, 2, 1, 3)
        .reshape(requests, steps, q_heads * head_dim)
    )
    return out, moved_to


def solution(mesh):
    in_specs = (
        P(("groups", "inst"), None, "tp", None),
        P(("groups", "inst"), None, None, "tp", None),
        P(("groups", "inst"), None, "tp", None, None),
        P(("groups", "inst"), None, "tp"),
        P(("groups", "inst"), None),
        P(("groups", "inst")),
        P(("groups", "inst"), None),
        P(("groups", "inst"), None),
    )
    out_specs = (P(("groups", "inst"), None, "tp"), P(("groups", "inst"), None))
    return jax.shard_map(shards, mesh=mesh, in_specs=in_specs, out_specs=out_specs, check_vma=False)
```

```python
import functools
import math

import jax
import jax.numpy as jnp
from jax import lax
from jax.experimental import pallas as pl
from jax.experimental.pallas import tpu as pltpu
from jax.sharding import PartitionSpec as P

CAP = 2
LOG2E = math.log2(math.e)
MIB = 1 << 20
SMEM_SPEC = pl.BlockSpec(memory_space=pltpu.SMEM)
VMEM_SPEC = pl.BlockSpec(memory_space=pltpu.VMEM)
HBM_SPEC = pl.BlockSpec(memory_space=pltpu.HBM)
NT = (((1,), (1,)), ((), ()))


def pack_kernel(instances, listed, dest_ref, block_ref, pool_ref, *rest):
    send_refs, (index_ref, sems) = rest[:instances], rest[instances:]
    me = lax.axis_index("inst")

    def clear(slot, carry):
        index_ref[slot] = 0
        return carry

    lax.fori_loop(0, instances * CAP, clear, 0)

    def place(m, carry):
        dest = dest_ref[0, m]

        def earlier(m2, rank):
            return rank + jnp.where(dest_ref[0, m2] == dest, 1, 0)

        rank = jnp.minimum(lax.fori_loop(0, m, earlier, 0), CAP - 1)
        shift = lax.rem(dest - me + instances, instances)
        index_ref[shift * CAP + rank] = block_ref[0, m]
        return carry

    lax.fori_loop(0, listed, place, 0)
    copies = []
    for shift in list(range(1, instances)) + [0]:
        for rank in range(CAP):
            slot = shift * CAP + rank
            copies.append(
                pltpu.make_async_copy(
                    pool_ref.at[index_ref[slot]], send_refs[shift].at[rank], sems.at[slot]
                )
            )
            copies[-1].start()
    for copy in copies:
        copy.wait()


def count_log(tables, length, ids, block_len, spans, store):
    requests, width = tables.shape[0], ids.shape[1]
    whole = length // block_len
    rest = length - whole * block_len
    full = jnp.zeros((requests, width), jnp.float32)
    part = jnp.zeros((requests, width), jnp.float32)
    for e in range(spans):
        hit = tables[:, e : e + 1] == ids
        full = full + jnp.where(hit & (whole > e), 1.0, 0.0)
        part = part + jnp.where(hit & (whole == e), 1.0, 0.0)
    inside = lax.broadcasted_iota(jnp.int32, (requests, block_len), 1) < rest
    for b in range(width):
        count = jnp.broadcast_to(full[:, b : b + 1], (requests, block_len)) + jnp.where(
            inside, jnp.broadcast_to(part[:, b : b + 1], (requests, block_len)), 0.0
        )
        store(b, jnp.where(count > 0, jnp.log(jnp.maximum(count, 1.0)) * LOG2E, -jnp.inf))


def score_tiles(query, keys, log_ref, scale_row, rows, store):
    height, wide = min(256, query.shape[0]), min(256, keys.shape[0])
    for top in range(0, query.shape[0], height):
        for left in range(0, keys.shape[0], wide):
            part = lax.dot_general(
                query[top : top + height],
                keys[left : left + wide],
                NT,
                preferred_element_type=jnp.float32,
            )
            scale = scale_row[:, left : left + wide]
            for r in range(height // rows):
                request = top // rows + r
                store(
                    request * rows,
                    left,
                    part[r * rows : (r + 1) * rows] * scale
                    + log_ref[request : request + 1, left : left + wide],
                )


def lane_fold(value, op):
    parts = [value[:, i : i + 128] for i in range(0, value.shape[1], 128)]
    while len(parts) > 1:
        parts = [
            op(parts[i], parts[i + 1]) if i + 1 < len(parts) else parts[i]
            for i in range(0, len(parts), 2)
        ]
    return parts[0]


def spread(column, width):
    return jnp.concatenate([column] * (width // 128), axis=1)


def own_kernel(
    dims,
    tables_ref, length_ref, scale_ref, q_ref, fresh_ref, codes_ref,
    acc_ref, top_ref, total_ref,
    log_ref, row_ref, t_ref, new_ref, p_ref,
):
    pool, heads, rows, steps, block_len, spans, factor, group = dims
    phase, chunk = pl.program_id(0), pl.program_id(1)
    chunks = pool // group
    height = q_ref.shape[1]
    width = group * block_len

    @pl.when((phase == 0) & (chunk == 0))
    def _():
        ids = lax.broadcasted_iota(jnp.int32, (1, pool), 1)

        def store(b, value):
            lane = (b % group) * block_len
            log_ref[b // group, :, lane : lane + block_len] = value

        count_log(tables_ref[...], length_ref[...], ids, block_len, spans, store)
        for b in range(pool):
            lane = (b % group) * block_len
            for h in range(heads):
                row_ref[b // group, h : h + 1, lane : lane + block_len] = jnp.full(
                    (1, block_len), scale_ref[0, h * pool + b] * (factor * LOG2E)
                )
                row_ref[b // group, heads + h : heads + h + 1, lane : lane + block_len] = jnp.full(
                    (1, block_len), scale_ref[0, (heads + h) * pool + b]
                )
        shape = (height, fresh_ref.shape[2])
        row = lax.broadcasted_iota(jnp.int32, shape, 0)
        col = lax.broadcasted_iota(jnp.int32, shape, 1)
        seen = (col // steps == row // rows) & (col % steps <= row % steps)
        for h in range(heads):
            score = lax.dot_general(
                q_ref[h], fresh_ref[0, h], NT, preferred_element_type=jnp.float32
            )
            score = jnp.where(seen, score * (factor * LOG2E), -jnp.inf)
            new_ref[h] = score
            top_ref[h] = lane_fold(score, jnp.maximum)

    @pl.when(phase == 0)
    def _():
        for h in range(heads):

            def store(row, lane, value, h=h):
                t_ref[h, chunk, row : row + rows, lane : lane + value.shape[1]] = value

            score_tiles(
                q_ref[h],
                codes_ref[:, 0, h].reshape(width, codes_ref.shape[-1]),
                log_ref.at[chunk],
                row_ref[chunk, h : h + 1, :],
                rows,
                store,
            )
            for row in range(0, height, rows):
                at = pl.ds(row, rows)
                top_ref[h, at] = jnp.maximum(
                    top_ref[h, at], lane_fold(t_ref[h, chunk, at], jnp.maximum)
                )

    @pl.when((phase == 1) & (chunk == 0))
    def _():
        for h in range(heads):
            top = jnp.broadcast_to(
                jnp.max(top_ref[h], axis=1, keepdims=True), (height, 128)
            )
            top_ref[h] = top
            weight = jnp.exp2(new_ref[h] - spread(top, new_ref.shape[2]))
            total_ref[h] = lane_fold(weight, jnp.add)
            acc_ref[h] = jnp.dot(
                weight.astype(jnp.bfloat16), fresh_ref[1, h], preferred_element_type=jnp.float32
            )

    @pl.when(phase == 1)
    def _():
        for h in range(heads):
            scale = row_ref[chunk, heads + h : heads + h + 1, :]
            for row in range(0, height, rows):
                at = pl.ds(row, rows)
                weight = jnp.exp2(t_ref[h, chunk, at] - spread(top_ref[h, at], width))
                total_ref[h, at] += lane_fold(weight, jnp.add)
                p_ref[h, at] = (weight * scale).astype(jnp.bfloat16)
            acc_ref[h] += jnp.dot(
                p_ref[h],
                codes_ref[:, 0, h].reshape(width, codes_ref.shape[-1]),
                preferred_element_type=jnp.float32,
            )

    @pl.when((phase == 1) & (chunk == chunks - 1))
    def _():
        for h in range(heads):
            total_ref[h] = jnp.broadcast_to(
                jnp.sum(total_ref[h], axis=1, keepdims=True), (height, 128)
            )


def loop(count, body, init):
    if count <= 8:
        for i in range(count):
            init = body(i, init)
        return init
    return lax.fori_loop(0, count, body, init)


def route_kernel(dims, lists_ref, tables_ref, length_ref, moved_ref, log_ref, row_ref):
    pool, heads, instances, listed, block_len, spans, factor = dims
    me = lax.axis_index("inst")

    def dest(shift, m):
        return lists_ref[shift, m].astype(jnp.int32)

    def source_of(shift):
        source = me - shift
        return jnp.where(source < 0, source + instances, source)

    def count(shift, target):
        return loop(
            listed, lambda m, n: n + jnp.where(dest(shift, m) == target, 1, 0), jnp.int32(0)
        )

    def move(m, carry):
        target = dest(0, m)
        rank = loop(
            listed,
            lambda m2, n: n + jnp.where((dest(0, m2) == target) & (m2 < m), 1, 0),
            jnp.int32(0),
        )
        moved_ref[0, m] = loop(
            instances,
            lambda shift, n: n + jnp.where(source_of(shift) < me, count(shift, target), 0),
            pool + rank,
        )
        return carry

    loop(listed, move, 0)
    slots = instances * CAP
    lane = lax.broadcasted_iota(jnp.int32, (1, slots), 1)

    def place(shift, ids):
        source = source_of(shift)
        first = loop(
            instances,
            lambda other, n: n + jnp.where(source_of(other) < source, count(other, me), 0),
            jnp.int32(pool),
        )
        seen = jnp.int32(0)
        blocks = [jnp.int32(0)] * CAP

        def find(m, carry):
            seen, blocks = carry
            hit = dest(shift, m) == me
            block = lists_ref[shift, listed + m].astype(jnp.int32)
            blocks = [jnp.where(hit & (seen == r), block, blocks[r]) for r in range(CAP)]
            return seen + jnp.where(hit, 1, 0), blocks

        seen, blocks = loop(listed, find, (seen, blocks))
        for rank in range(CAP):
            slot = shift * CAP + rank
            ids = jnp.where(lane == slot, jnp.where(rank < seen, first + rank, -1), ids)
            at = pl.ds(pl.multiple_of(slot * block_len, block_len), block_len)
            for h in range(heads):
                key = lists_ref[shift, 2 * listed + h * pool + blocks[rank]]
                value = lists_ref[shift, 2 * listed + (heads + h) * pool + blocks[rank]]
                row_ref[h : h + 1, at] = jnp.full((1, block_len), key * (factor * LOG2E))
                row_ref[heads + h : heads + h + 1, at] = jnp.full((1, block_len), value)
        return ids

    ids = loop(instances, place, jnp.full((1, slots), -1, jnp.int32))

    def store(b, value):
        log_ref[:, b * block_len : (b + 1) * block_len] = value

    count_log(tables_ref[...], length_ref[...], ids, block_len, spans, store)


def arrival_kernel(
    dims, sources, q_ref, log_ref, row_ref, acc_ref, top_ref, total_ref, *rest
):
    heads, rows, block_len = dims
    code_refs, (out_ref, t_ref, p_ref) = rest[:sources], rest[sources:]
    height = q_ref.shape[1]
    width = CAP * block_len
    for h in range(heads):
        for s, codes_ref in enumerate(code_refs):
            left = s * width

            def store(row, lane, value, h=h, left=left):
                t_ref[h, row : row + rows, left + lane : left + lane + value.shape[1]] = value

            score_tiles(
                q_ref[h],
                codes_ref[:, 0, h].reshape(width, codes_ref.shape[-1]),
                log_ref.at[:, left : left + width],
                row_ref[h : h + 1, left : left + width],
                rows,
                store,
            )
    for h in range(heads):
        scale = row_ref[heads + h : heads + h + 1, :]
        for row in range(0, height, rows):
            at = pl.ds(row, rows)
            score = t_ref[h, at]
            own_top = top_ref[h, at]
            top = jnp.maximum(
                own_top, jnp.max(lane_fold(score, jnp.maximum), axis=1, keepdims=True)
            )
            weight = jnp.exp2(score - spread(top, score.shape[1]))
            keep = jnp.exp2(own_top - top)
            total = total_ref[h, at] * keep + jnp.sum(
                lane_fold(weight, jnp.add), axis=1, keepdims=True
            )
            p_ref[h, at] = (weight * scale).astype(jnp.bfloat16)
            t_ref[h, at, 0:128] = keep
            t_ref[h, at, 128:256] = 1.0 / total
        mixed = acc_ref[h] * t_ref[h, :, 0:128]
        for s, codes_ref in enumerate(code_refs):
            mixed = mixed + jnp.dot(
                p_ref[h, :, s * width : (s + 1) * width],
                codes_ref[:, 1, h].reshape(width, codes_ref.shape[-1]),
                preferred_element_type=jnp.float32,
            )
        result = (mixed * t_ref[h, :, 128:256]).astype(jnp.bfloat16)
        out_ref[:, h] = result.reshape(height // rows, rows, result.shape[-1])


def shards(queries, new_kv, pool_codes, pool_scales, tables, ctx_len, mig_block, mig_dest):
    instances = lax.axis_size("inst")
    pool = pool_codes.shape[0]
    requests, steps, q_heads, head_dim = queries.shape
    heads = new_kv.shape[3]
    per_head = q_heads // heads
    spans = tables.shape[1]
    block_len = pool_codes.shape[3]
    listed = mig_dest.shape[1]
    factor = head_dim ** (-0.5)
    rows = per_head * steps
    height = requests * rows
    slots = instances * CAP
    group = 8
    f32, bf16 = jnp.float32, jnp.bfloat16

    block_shape = pool_codes.shape[1:]
    send = pl.pallas_call(
        functools.partial(pack_kernel, instances, listed),
        out_shape=[jax.ShapeDtypeStruct((CAP,) + block_shape, bf16)] * instances,
        in_specs=[SMEM_SPEC, SMEM_SPEC, HBM_SPEC],
        out_specs=[VMEM_SPEC] * instances,
        scratch_shapes=[pltpu.SMEM((slots,), jnp.int32), pltpu.SemaphoreType.DMA((slots,))],
        compiler_params=pltpu.CompilerParams(
            vmem_limit_bytes=(2 * slots * math.prod(block_shape) * 2) + 4 * MIB
        ),
        cost_estimate=pl.CostEstimate(
            flops=0, bytes_accessed=2 * slots * math.prod(block_shape) * 2, transcendentals=0
        ),
        name="pack_blocks",
    )(mig_dest, mig_block, pool_codes)

    def from_shift(value, shift):
        if shift == 0:
            return value
        return lax.ppermute(
            value, "inst", [(j, (j + shift) % instances) for j in range(instances)]
        )

    mig_dest, mig_block, pool_scales, *send = lax.optimization_barrier(
        (mig_dest, mig_block, pool_scales, *send)
    )
    codes_in = [from_shift(send[shift], shift) for shift in range(instances)]
    flat_scales = jnp.transpose(pool_scales, (1, 2, 0)).reshape(1, -1).astype(f32)
    lists = jnp.concatenate([mig_dest.astype(f32), mig_block.astype(f32), flat_scales], axis=1)
    lists_in = jnp.concatenate(
        [from_shift(lists, shift) for shift in range(instances)], axis=0
    )

    query_rows = (
        queries.reshape(requests, steps, heads, per_head, head_dim)
        .transpose(2, 0, 3, 1, 4)
        .reshape(heads, height, head_dim)
    )
    fresh_len = requests * steps
    fresh = new_kv.transpose(2, 3, 0, 1, 4).reshape(2, heads, fresh_len, head_dim)
    fresh = jnp.pad(fresh, ((0, 0), (0, 0), (0, -fresh_len % 128), (0, 0)))
    length = ctx_len[:, None]
    width = group * block_len
    chunks = pool // group
    tokens = pool * block_len

    def whole(shape):
        return pl.BlockSpec(shape, lambda p, c: (0,) * len(shape))

    stat = (heads, height, head_dim)
    acc, top, total = pl.pallas_call(
        functools.partial(
            own_kernel, (pool, heads, rows, steps, block_len, spans, factor, group)
        ),
        grid=(2, chunks),
        out_shape=[jax.ShapeDtypeStruct(stat, f32)] * 3,
        in_specs=[
            whole(tables.shape),
            whole(length.shape),
            SMEM_SPEC,
            whole(query_rows.shape),
            whole(fresh.shape),
            pl.BlockSpec(
                (group, 1, heads, block_len, head_dim), lambda p, c: (c, p, 0, 0, 0)
            ),
        ],
        out_specs=[whole(stat)] * 3,
        scratch_shapes=[
            pltpu.VMEM((chunks, requests, width), f32),
            pltpu.VMEM((chunks, 2 * heads, width), f32),
            pltpu.VMEM((heads, chunks, height, width), f32),
            pltpu.VMEM((heads, height, fresh.shape[2]), f32),
            pltpu.VMEM((heads, height, width), bf16),
        ],
        compiler_params=pltpu.CompilerParams(vmem_limit_bytes=48 * MIB),
        cost_estimate=pl.CostEstimate(
            flops=4 * heads * height * tokens * head_dim,
            bytes_accessed=pool_codes.size * 2,
            transcendentals=heads * height * tokens,
        ),
        name="own_blocks",
    )(tables, length, flat_scales, query_rows, fresh, pool_codes)

    moved_to, log_in, rows_in = pl.pallas_call(
        functools.partial(
            route_kernel, (pool, heads, instances, listed, block_len, spans, factor)
        ),
        out_shape=[
            jax.ShapeDtypeStruct((1, listed), jnp.int32),
            jax.ShapeDtypeStruct((requests, slots * block_len), f32),
            jax.ShapeDtypeStruct((2 * heads, slots * block_len), f32),
        ],
        in_specs=[SMEM_SPEC, VMEM_SPEC, VMEM_SPEC],
        out_specs=[SMEM_SPEC, VMEM_SPEC, VMEM_SPEC],
        compiler_params=pltpu.CompilerParams(vmem_limit_bytes=8 * MIB),
        name="route_arrivals",
    )(lists_in, tables, length)

    arrival_bytes = 6 * heads * height * slots * block_len + 8 * math.prod(stat)
    arrival_bytes += 4 * slots * math.prod(block_shape)
    out = pl.pallas_call(
        functools.partial(arrival_kernel, (heads, rows, block_len), instances),
        out_shape=jax.ShapeDtypeStruct((requests, heads, rows, head_dim), bf16),
        in_specs=[VMEM_SPEC] * (6 + instances),
        out_specs=VMEM_SPEC,
        scratch_shapes=[
            pltpu.VMEM((heads, height, slots * block_len), f32),
            pltpu.VMEM((heads, height, slots * block_len), bf16),
        ],
        compiler_params=pltpu.CompilerParams(vmem_limit_bytes=arrival_bytes + 8 * MIB),
        cost_estimate=pl.CostEstimate(
            flops=4 * heads * height * slots * block_len * head_dim,
            bytes_accessed=slots * math.prod(block_shape) * 2,
            transcendentals=heads * height * slots * block_len,
        ),
        name="arrived_blocks",
    )(query_rows, log_in, rows_in, acc, top, total, *codes_in)
    out = (
        out.reshape(requests, q_heads, steps, head_dim)
        .transpose(0, 2, 1, 3)
        .reshape(requests, steps, q_heads * head_dim)
    )
    return out, moved_to


def solution(mesh):
    in_specs = (
        P(("groups", "inst"), None, "tp", None),
        P(("groups", "inst"), None, None, "tp", None),
        P(("groups", "inst"), None, "tp", None, None),
        P(("groups", "inst"), None, "tp"),
        P(("groups", "inst"), None),
        P(("groups", "inst")),
        P(("groups", "inst"), None),
        P(("groups", "inst"), None),
    )
    out_specs = (P(("groups", "inst"), None, "tp"), P(("groups", "inst"), None))
    return jax.shard_map(shards, mesh=mesh, in_specs=in_specs, out_specs=out_specs, check_vma=False)
```

```python
import functools
import math

import jax
import jax.numpy as jnp
from jax import lax
from jax.experimental import pallas as pl
from jax.experimental.pallas import tpu as pltpu
from jax.sharding import PartitionSpec as P

CAP = 2
LOG2E = math.log2(math.e)
MIB = 1 << 20
SMEM_SPEC = pl.BlockSpec(memory_space=pltpu.SMEM)
VMEM_SPEC = pl.BlockSpec(memory_space=pltpu.VMEM)
HBM_SPEC = pl.BlockSpec(memory_space=pltpu.HBM)
NT = (((1,), (1,)), ((), ()))


def loop(count, body, init):
    if count <= 8:
        for i in range(count):
            init = body(i, init)
        return init
    return lax.fori_loop(0, count, body, init)


def pack_kernel(instances, listed, rest_only, dest_ref, block_ref, pool_ref, *refs):
    slots = instances if rest_only else instances + 1
    send_refs, (index_ref, held_ref, in_sems, out_sems) = refs[:slots], refs[slots:]
    me = lax.axis_index("inst")
    for slot in range(slots):
        index_ref[slot] = 0

    def place(m, carry):
        dest = dest_ref[0, m]
        rank = loop(
            listed,
            lambda m2, n: n + jnp.where((dest_ref[0, m2] == dest) & (m2 < m), 1, 0),
            jnp.int32(0),
        )
        shift = jnp.where(dest < me, dest - me + instances, dest - me)

        if rest_only:

            @pl.when(rank > 0)
            def _():
                index_ref[shift] = block_ref[0, m]

        else:
            index_ref[jnp.where(rank > 0, instances, shift)] = block_ref[0, m]
        return carry

    loop(listed, place, 0)
    loads = []
    order = [slots - 1] + list(range(slots - 1))
    for slot in order:
        loads.append(
            pltpu.make_async_copy(pool_ref.at[index_ref[slot]], held_ref.at[slot], in_sems.at[slot])
        )
        loads[-1].start()
    stores = []
    for slot, load in zip(order, loads):
        load.wait()
        stores.append(
            pltpu.make_async_copy(held_ref.at[slot], send_refs[slot].at[0], out_sems.at[slot])
        )
        stores[-1].start()
    for store in stores:
        store.wait()


def count_log(tables, length, ids, block_len, spans, store):
    requests, width = tables.shape[0], ids.shape[1]
    whole = length // block_len
    rest = length - whole * block_len
    full = jnp.zeros((requests, width), jnp.float32)
    part = jnp.zeros((requests, width), jnp.float32)
    for e in range(spans):
        hit = tables[:, e : e + 1] == ids
        full = full + jnp.where(hit & (whole > e), 1.0, 0.0)
        part = part + jnp.where(hit & (whole == e), 1.0, 0.0)
    inside = lax.broadcasted_iota(jnp.int32, (requests, block_len), 1) < rest
    for b in range(width):
        count = jnp.broadcast_to(full[:, b : b + 1], (requests, block_len)) + jnp.where(
            inside, jnp.broadcast_to(part[:, b : b + 1], (requests, block_len)), 0.0
        )
        store(b, jnp.where(count > 0, jnp.log(jnp.maximum(count, 1.0)) * LOG2E, -jnp.inf))


def score_tiles(query, keys, log_ref, scale_row, rows, store):
    height, wide = min(256, query.shape[0]), min(256, keys.shape[0])
    for top in range(0, query.shape[0], height):
        for left in range(0, keys.shape[0], wide):
            part = lax.dot_general(
                query[top : top + height],
                keys[left : left + wide],
                NT,
                preferred_element_type=jnp.float32,
            )
            scale = scale_row[:, left : left + wide]
            for r in range(height // rows):
                request = top // rows + r
                store(
                    request * rows,
                    left,
                    part[r * rows : (r + 1) * rows] * scale
                    + log_ref[request : request + 1, left : left + wide],
                )


def lane_fold(value, op):
    parts = [value[:, i : i + 128] for i in range(0, value.shape[1], 128)]
    while len(parts) > 1:
        parts = [
            op(parts[i], parts[i + 1]) if i + 1 < len(parts) else parts[i]
            for i in range(0, len(parts), 2)
        ]
    return parts[0]


def spread(column, width):
    return jnp.concatenate([column] * (width // 128), axis=1)


def own_kernel(
    dims,
    tables_ref, length_ref, scale_ref, q_ref, fresh_ref, codes_ref,
    acc_ref, top_ref, total_ref,
    log_ref, row_ref, t_ref, new_ref, p_ref,
):
    pool, heads, rows, steps, block_len, spans, factor, group = dims
    phase, chunk = pl.program_id(0), pl.program_id(1)
    chunks = pool // group
    height = q_ref.shape[1]
    width = group * block_len

    @pl.when((phase == 0) & (chunk == 0))
    def _():
        ids = lax.broadcasted_iota(jnp.int32, (1, pool), 1)

        def store(b, value):
            lane = (b % group) * block_len
            log_ref[b // group, :, lane : lane + block_len] = value

        count_log(tables_ref[...], length_ref[...], ids, block_len, spans, store)
        for b in range(pool):
            lane = (b % group) * block_len
            for h in range(heads):
                row_ref[b // group, h : h + 1, lane : lane + block_len] = jnp.full(
                    (1, block_len), scale_ref[0, h * pool + b] * (factor * LOG2E)
                )
                row_ref[b // group, heads + h : heads + h + 1, lane : lane + block_len] = jnp.full(
                    (1, block_len), scale_ref[0, (heads + h) * pool + b]
                )
        shape = (height, fresh_ref.shape[2])
        row = lax.broadcasted_iota(jnp.int32, shape, 0)
        col = lax.broadcasted_iota(jnp.int32, shape, 1)
        seen = (col // steps == row // rows) & (col % steps <= row % steps)
        for h in range(heads):
            score = lax.dot_general(
                q_ref[h], fresh_ref[0, h], NT, preferred_element_type=jnp.float32
            )
            score = jnp.where(seen, score * (factor * LOG2E), -jnp.inf)
            new_ref[h] = score
            top_ref[h] = lane_fold(score, jnp.maximum)

    @pl.when(phase == 0)
    def _():
        for h in range(heads):

            def store(row, lane, value, h=h):
                t_ref[h, chunk, row : row + rows, lane : lane + value.shape[1]] = value

            score_tiles(
                q_ref[h],
                codes_ref[:, 0, h].reshape(width, codes_ref.shape[-1]),
                log_ref.at[chunk],
                row_ref[chunk, h : h + 1, :],
                rows,
                store,
            )
            for row in range(0, height, rows):
                at = pl.ds(row, rows)
                top_ref[h, at] = jnp.maximum(
                    top_ref[h, at], lane_fold(t_ref[h, chunk, at], jnp.maximum)
                )

    @pl.when((phase == 1) & (chunk == 0))
    def _():
        for h in range(heads):
            top = jnp.broadcast_to(
                jnp.max(top_ref[h], axis=1, keepdims=True), (height, 128)
            )
            top_ref[h] = top
            weight = jnp.exp2(new_ref[h] - spread(top, new_ref.shape[2]))
            total_ref[h] = lane_fold(weight, jnp.add)
            acc_ref[h] = jnp.dot(
                weight.astype(jnp.bfloat16), fresh_ref[1, h], preferred_element_type=jnp.float32
            )

    @pl.when(phase == 1)
    def _():
        for h in range(heads):
            scale = row_ref[chunk, heads + h : heads + h + 1, :]
            for row in range(0, height, rows):
                at = pl.ds(row, rows)
                weight = jnp.exp2(t_ref[h, chunk, at] - spread(top_ref[h, at], width))
                total_ref[h, at] += lane_fold(weight, jnp.add)
                p_ref[h, at] = (weight * scale).astype(jnp.bfloat16)
            acc_ref[h] += jnp.dot(
                p_ref[h],
                codes_ref[:, 0, h].reshape(width, codes_ref.shape[-1]),
                preferred_element_type=jnp.float32,
            )

    @pl.when((phase == 1) & (chunk == chunks - 1))
    def _():
        for h in range(heads):
            total_ref[h] = jnp.broadcast_to(
                jnp.sum(total_ref[h], axis=1, keepdims=True), (height, 128)
            )


def route_kernel(
    dims, lists_ref, tables_ref, length_ref, own_ref, moved_ref, more_ref, log_ref, row_ref
):
    pool, heads, instances, groups, listed, block_len, spans, factor = dims
    me = lax.axis_index("inst")
    base = lax.axis_index("groups") * instances

    def dest(row, m):
        return lists_ref[row, m].astype(jnp.int32)

    def count(row, target):
        return loop(
            listed, lambda m, n: n + jnp.where(dest(row, m) == target, 1, 0), jnp.int32(0)
        )

    def rank(row, m):
        target = dest(row, m)
        return loop(
            listed,
            lambda m2, n: n + jnp.where((dest(row, m2) == target) & (m2 < m), 1, 0),
            jnp.int32(0),
        )

    def before(source, target):
        return loop(
            instances,
            lambda j, n: n + jnp.where(j < source, count(base + j, target), 0),
            jnp.int32(pool),
        )

    def move(m, carry):
        moved_ref[0, m] = before(me, dest(base + me, m)) + rank(base + me, m)
        return carry

    loop(listed, move, 0)

    def seconds(row, more):
        found = loop(listed, lambda m, n: n + jnp.minimum(rank(row, m), 1), jnp.int32(0))
        return jnp.maximum(more, jnp.where(found > 1, 1, 0))

    more_ref[0] = loop(groups * instances, seconds, jnp.int32(0))
    slots = instances * CAP
    lane = lax.broadcasted_iota(jnp.int32, (1, slots), 1)

    def place(j, ids):
        row = base + j
        first = before(j, me)

        def find(m, carry):
            seen, blocks = carry
            hit = dest(row, m) == me
            block = lists_ref[row, listed + m].astype(jnp.int32)
            blocks = [jnp.where(hit & (seen == r), block, blocks[r]) for r in range(CAP)]
            return seen + jnp.where(hit, 1, 0), blocks

        seen, blocks = loop(listed, find, (jnp.int32(0), [jnp.int32(0)] * CAP))
        shift = jnp.where(me < j, me - j + instances, me - j)
        for r, slot in enumerate((shift, instances + j)):
            ids = jnp.where(lane == slot, jnp.where(r < seen, first + r, -1), ids)
            at = pl.ds(pl.multiple_of(slot * block_len, block_len), block_len)
            for h in range(heads):
                key = lists_ref[row, 2 * listed + h * pool + blocks[r]]
                value = lists_ref[row, 2 * listed + (heads + h) * pool + blocks[r]]
                row_ref[h : h + 1, at] = jnp.full((1, block_len), key * (factor * LOG2E))
                row_ref[heads + h : heads + h + 1, at] = jnp.full((1, block_len), value)
        return ids

    ids = loop(instances, place, jnp.full((1, slots), -1, jnp.int32))

    def store(b, value):
        log_ref[:, b * block_len : (b + 1) * block_len] = value

    count_log(tables_ref[...], length_ref[...], ids, block_len, spans, store)


def arrival_kernel(
    dims, q_ref, log_ref, row_ref, acc_ref, top_ref, total_ref, *rest
):
    heads, rows, block_len, instances = dims
    first_refs, (second_ref, out_ref, t_ref, p_ref) = rest[:instances], rest[instances:]
    height = q_ref.shape[1]
    width = 2 * block_len
    slots = [ref.at[0] for ref in first_refs] + [second_ref.at[j] for j in range(instances)]

    def pair(i, part, h):
        return jnp.concatenate([slots[2 * i][part, h], slots[2 * i + 1][part, h]], axis=0)

    for h in range(heads):
        for i in range(instances):
            left = i * width

            def store(row, lane, value, h=h, left=left):
                t_ref[h, row : row + rows, left + lane : left + lane + value.shape[1]] = value

            score_tiles(
                q_ref[h],
                pair(i, 0, h),
                log_ref.at[:, left : left + width],
                row_ref[h : h + 1, left : left + width],
                rows,
                store,
            )
    for h in range(heads):
        scale = row_ref[heads + h : heads + h + 1, :]
        for row in range(0, height, rows):
            at = pl.ds(row, rows)
            score = t_ref[h, at]
            own_top = top_ref[h, at]
            top = jnp.maximum(
                own_top, jnp.max(lane_fold(score, jnp.maximum), axis=1, keepdims=True)
            )
            weight = jnp.exp2(score - spread(top, score.shape[1]))
            keep = jnp.exp2(own_top - top)
            total = total_ref[h, at] * keep + jnp.sum(
                lane_fold(weight, jnp.add), axis=1, keepdims=True
            )
            p_ref[h, at] = (weight * scale).astype(jnp.bfloat16)
            t_ref[h, at, 0:128] = keep
            t_ref[h, at, 128:256] = 1.0 / total
        mixed = acc_ref[h] * t_ref[h, :, 0:128]
        for i in range(instances):
            mixed = mixed + jnp.dot(
                p_ref[h, :, i * width : (i + 1) * width],
                pair(i, 1, h),
                preferred_element_type=jnp.float32,
            )
        result = (mixed * t_ref[h, :, 128:256]).astype(jnp.bfloat16)
        out_ref[:, h] = result.reshape(height // rows, rows, result.shape[-1])


def shards(queries, new_kv, pool_codes, pool_scales, tables, ctx_len, mig_block, mig_dest):
    instances = lax.axis_size("inst")
    pool = pool_codes.shape[0]
    requests, steps, q_heads, head_dim = queries.shape
    heads = new_kv.shape[3]
    per_head = q_heads // heads
    spans = tables.shape[1]
    block_len = pool_codes.shape[3]
    listed = mig_dest.shape[1]
    factor = head_dim ** (-0.5)
    rows = per_head * steps
    height = requests * rows
    slots = instances * CAP
    group = 8
    f32, bf16 = jnp.float32, jnp.bfloat16

    block_shape = pool_codes.shape[1:]

    def pack(rest_only, dests, blocks, codes):
        count = instances if rest_only else instances + 1
        return pl.pallas_call(
            functools.partial(pack_kernel, instances, listed, rest_only),
            out_shape=[jax.ShapeDtypeStruct((1,) + block_shape, bf16)] * count,
            in_specs=[SMEM_SPEC, SMEM_SPEC, HBM_SPEC],
            out_specs=[HBM_SPEC] * count,
            scratch_shapes=[
                pltpu.SMEM((count,), jnp.int32),
                pltpu.VMEM((count,) + block_shape, bf16),
                pltpu.SemaphoreType.DMA((count,)),
                pltpu.SemaphoreType.DMA((count,)),
            ],
            compiler_params=pltpu.CompilerParams(vmem_limit_bytes=56 * MIB),
            cost_estimate=pl.CostEstimate(
                flops=0, bytes_accessed=4 * count * math.prod(block_shape), transcendentals=0
            ),
            name="pack_blocks",
        )(dests, blocks, codes)

    def from_shift(value, shift):
        if shift == 0:
            return value
        return lax.ppermute(
            value, "inst", [(j, (j + shift) % instances) for j in range(instances)]
        )

    *send, second = pack(False, mig_dest, mig_block, pool_codes)
    mig_dest, mig_block, pool_scales, second, *send = lax.optimization_barrier(
        (mig_dest, mig_block, pool_scales, second, *send)
    )
    first_in = [from_shift(send[shift], shift) for shift in range(instances)]
    second_in = lax.all_gather(second, "inst", axis=0, tiled=True)
    flat_scales = jnp.transpose(pool_scales, (1, 2, 0)).reshape(1, -1).astype(f32)
    lists = jnp.concatenate([mig_dest.astype(f32), mig_block.astype(f32), flat_scales], axis=1)
    lists_in = lax.all_gather(lists, ("groups", "inst"), axis=0, tiled=True)

    query_rows = (
        queries.reshape(requests, steps, heads, per_head, head_dim)
        .transpose(2, 0, 3, 1, 4)
        .reshape(heads, height, head_dim)
    )
    fresh_len = requests * steps
    fresh = new_kv.transpose(2, 3, 0, 1, 4).reshape(2, heads, fresh_len, head_dim)
    fresh = jnp.pad(fresh, ((0, 0), (0, 0), (0, -fresh_len % 128), (0, 0)))
    length = ctx_len[:, None]
    width = group * block_len
    chunks = pool // group
    tokens = pool * block_len

    def whole(shape):
        return pl.BlockSpec(shape, lambda p, c: (0,) * len(shape))

    stat = (heads, height, head_dim)
    acc, top, total = pl.pallas_call(
        functools.partial(
            own_kernel, (pool, heads, rows, steps, block_len, spans, factor, group)
        ),
        grid=(2, chunks),
        out_shape=[jax.ShapeDtypeStruct(stat, f32)] * 3,
        in_specs=[
            whole(tables.shape),
            whole(length.shape),
            SMEM_SPEC,
            whole(query_rows.shape),
            whole(fresh.shape),
            pl.BlockSpec(
                (group, 1, heads, block_len, head_dim), lambda p, c: (c, p, 0, 0, 0)
            ),
        ],
        out_specs=[whole(stat)] * 3,
        scratch_shapes=[
            pltpu.VMEM((chunks, requests, width), f32),
            pltpu.VMEM((chunks, 2 * heads, width), f32),
            pltpu.VMEM((heads, chunks, height, width), f32),
            pltpu.VMEM((heads, height, fresh.shape[2]), f32),
            pltpu.VMEM((heads, height, width), bf16),
        ],
        compiler_params=pltpu.CompilerParams(vmem_limit_bytes=48 * MIB),
        cost_estimate=pl.CostEstimate(
            flops=4 * heads * height * tokens * head_dim,
            bytes_accessed=pool_codes.size * 2,
            transcendentals=heads * height * tokens,
        ),
        name="own_blocks",
    )(tables, length, flat_scales, query_rows, fresh, pool_codes)

    moved_to, more, log_in, rows_in = pl.pallas_call(
        functools.partial(
            route_kernel,
            (pool, heads, instances, lax.axis_size("groups"), listed, block_len, spans, factor),
        ),
        out_shape=[
            jax.ShapeDtypeStruct((1, listed), jnp.int32),
            jax.ShapeDtypeStruct((1,), jnp.int32),
            jax.ShapeDtypeStruct((requests, slots * block_len), f32),
            jax.ShapeDtypeStruct((2 * heads, slots * block_len), f32),
        ],
        in_specs=[SMEM_SPEC, VMEM_SPEC, VMEM_SPEC, HBM_SPEC],
        out_specs=[SMEM_SPEC, SMEM_SPEC, VMEM_SPEC, VMEM_SPEC],
        compiler_params=pltpu.CompilerParams(vmem_limit_bytes=8 * MIB),
        name="route_arrivals",
    )(lists_in, tables, length, top)

    def all_seconds(gathered, dests, blocks, codes):
        rest = pack(True, dests, blocks, codes)
        arrived = jnp.concatenate([from_shift(rest[s], s) for s in range(instances)], axis=0)
        shifts = (lax.axis_index("inst") - jnp.arange(instances)) % instances
        return jnp.take(arrived, shifts, axis=0)

    second_in = lax.cond(
        more[0] > 0,
        all_seconds,
        lambda gathered, *unused: gathered,
        second_in, mig_dest, mig_block, pool_codes,
    )

    arrival_bytes = 6 * heads * height * slots * block_len + 8 * math.prod(stat)
    arrival_bytes += 4 * slots * math.prod(block_shape)
    out = pl.pallas_call(
        functools.partial(arrival_kernel, (heads, rows, block_len, instances)),
        out_shape=jax.ShapeDtypeStruct((requests, heads, rows, head_dim), bf16),
        in_specs=[VMEM_SPEC] * (7 + instances),
        out_specs=VMEM_SPEC,
        scratch_shapes=[
            pltpu.VMEM((heads, height, slots * block_len), f32),
            pltpu.VMEM((heads, height, slots * block_len), bf16),
        ],
        compiler_params=pltpu.CompilerParams(vmem_limit_bytes=arrival_bytes + 8 * MIB),
        cost_estimate=pl.CostEstimate(
            flops=4 * heads * height * slots * block_len * head_dim,
            bytes_accessed=slots * math.prod(block_shape) * 2,
            transcendentals=heads * height * slots * block_len,
        ),
        name="arrived_blocks",
    )(query_rows, log_in, rows_in, acc, top, total, *first_in, second_in)
    out = (
        out.reshape(requests, q_heads, steps, head_dim)
        .transpose(0, 2, 1, 3)
        .reshape(requests, steps, q_heads * head_dim)
    )
    return out, moved_to


def solution(mesh):
    in_specs = (
        P(("groups", "inst"), None, "tp", None),
        P(("groups", "inst"), None, None, "tp", None),
        P(("groups", "inst"), None, "tp", None, None),
        P(("groups", "inst"), None, "tp"),
        P(("groups", "inst"), None),
        P(("groups", "inst")),
        P(("groups", "inst"), None),
        P(("groups", "inst"), None),
    )
    out_specs = (P(("groups", "inst"), None, "tp"), P(("groups", "inst"), None))
    return jax.shard_map(shards, mesh=mesh, in_specs=in_specs, out_specs=out_specs, check_vma=False)
```

```python
import functools
import math

import jax
import jax.numpy as jnp
from jax import lax
from jax.experimental import pallas as pl
from jax.experimental.pallas import tpu as pltpu
from jax.sharding import PartitionSpec as P

CAP = 2
LOG2E = math.log2(math.e)
MIB = 1 << 20
SMEM_SPEC = pl.BlockSpec(memory_space=pltpu.SMEM)
VMEM_SPEC = pl.BlockSpec(memory_space=pltpu.VMEM)
HBM_SPEC = pl.BlockSpec(memory_space=pltpu.HBM)
NT = (((1,), (1,)), ((), ()))


def loop(count, body, init):
    if count <= 8:
        for i in range(count):
            init = body(i, init)
        return init
    return lax.fori_loop(0, count, body, init)


def pack_kernel(instances, listed, copies, dest_ref, block_ref, pool_ref, *refs):
    count = len(refs) - 4
    send_refs, (index_ref, held_ref, in_sems, out_sems) = refs[:count], refs[count:]
    me = lax.axis_index("inst")
    for entry in range(2 * instances + 1):
        index_ref[entry] = 0

    def place(m, carry):
        dest = dest_ref[0, m]
        rank = loop(
            listed,
            lambda m2, n: n + jnp.where((dest_ref[0, m2] == dest) & (m2 < m), 1, 0),
            jnp.int32(0),
        )
        entry = jnp.bitwise_xor(dest, me) + jnp.where(rank > 0, instances, 0)
        index_ref[entry] = block_ref[0, m]
        index_ref[jnp.where(rank > 0, 2 * instances, entry)] = block_ref[0, m]
        return carry

    loop(listed, place, 0)
    loads, stores = [], []
    for i, (entry, _) in enumerate(copies):
        loads.append(
            pltpu.make_async_copy(pool_ref.at[index_ref[entry]], held_ref.at[i], in_sems.at[i])
        )
        loads[-1].start()
    for i, (_, targets) in enumerate(copies):
        loads[i].wait()
        for output, row in targets:
            stores.append(
                pltpu.make_async_copy(
                    held_ref.at[i], send_refs[output].at[row], out_sems.at[len(stores)]
                )
            )
            stores[-1].start()
    for store in stores:
        store.wait()


def count_log(tables, length, ids, block_len, spans, store):
    requests, width = tables.shape[0], ids.shape[1]
    whole = length // block_len
    rest = length - whole * block_len
    full = jnp.zeros((requests, width), jnp.float32)
    part = jnp.zeros((requests, width), jnp.float32)
    for e in range(spans):
        hit = tables[:, e : e + 1] == ids
        full = full + jnp.where(hit & (whole > e), 1.0, 0.0)
        part = part + jnp.where(hit & (whole == e), 1.0, 0.0)
    inside = lax.broadcasted_iota(jnp.int32, (requests, block_len), 1) < rest
    for b in range(width):
        count = jnp.broadcast_to(full[:, b : b + 1], (requests, block_len)) + jnp.where(
            inside, jnp.broadcast_to(part[:, b : b + 1], (requests, block_len)), 0.0
        )
        store(b, jnp.where(count > 0, jnp.log(jnp.maximum(count, 1.0)) * LOG2E, -jnp.inf))


def score_tiles(query, keys, log_ref, scale_row, rows, store):
    height, wide = min(256, query.shape[0]), min(256, keys.shape[0])
    for top in range(0, query.shape[0], height):
        for left in range(0, keys.shape[0], wide):
            part = lax.dot_general(
                query[top : top + height],
                keys[left : left + wide],
                NT,
                preferred_element_type=jnp.float32,
            )
            scale = scale_row[:, left : left + wide]
            for r in range(height // rows):
                request = top // rows + r
                store(
                    request * rows,
                    left,
                    part[r * rows : (r + 1) * rows] * scale
                    + log_ref[request : request + 1, left : left + wide],
                )


def lane_fold(value, op):
    parts = [value[:, i : i + 128] for i in range(0, value.shape[1], 128)]
    while len(parts) > 1:
        parts = [
            op(parts[i], parts[i + 1]) if i + 1 < len(parts) else parts[i]
            for i in range(0, len(parts), 2)
        ]
    return parts[0]


def spread(column, width):
    return jnp.concatenate([column] * (width // 128), axis=1)


def own_kernel(
    dims,
    tables_ref, length_ref, scale_ref, q_ref, fresh_ref, codes_ref,
    acc_ref, top_ref, total_ref,
    log_ref, row_ref, t_ref, new_ref, p_ref,
):
    head, pool, heads, rows, steps, block_len, spans, factor, group = dims
    phase, chunk = pl.program_id(0), pl.program_id(1)
    chunks = pool // group
    height = q_ref.shape[1]
    width = group * block_len

    @pl.when((phase == 0) & (chunk == 0))
    def _():
        ids = lax.broadcasted_iota(jnp.int32, (1, pool), 1)

        def store(b, value):
            lane = (b % group) * block_len
            log_ref[b // group, :, lane : lane + block_len] = value

        count_log(tables_ref[...], length_ref[...], ids, block_len, spans, store)
        for b in range(pool):
            lane = (b % group) * block_len
            for part, unit in ((0, factor * LOG2E), (1, 1.0)):
                row_ref[b // group, part : part + 1, lane : lane + block_len] = jnp.full(
                    (1, block_len), scale_ref[0, (part * heads + head) * pool + b] * unit
                )
        shape = (height, fresh_ref.shape[2])
        row = lax.broadcasted_iota(jnp.int32, shape, 0)
        col = lax.broadcasted_iota(jnp.int32, shape, 1)
        seen = (col // steps == row // rows) & (col % steps <= row % steps)
        score = lax.dot_general(
            q_ref[0], fresh_ref[0, 0], NT, preferred_element_type=jnp.float32
        )
        score = jnp.where(seen, score * (factor * LOG2E), -jnp.inf)
        new_ref[...] = score
        top_ref[...] = lane_fold(score, jnp.maximum)

    @pl.when(phase == 0)
    def _():
        def store(row, lane, value):
            t_ref[chunk, row : row + rows, lane : lane + value.shape[1]] = value

        score_tiles(
            q_ref[0],
            codes_ref[:, 0, 0].reshape(width, codes_ref.shape[-1]),
            log_ref.at[chunk],
            row_ref[chunk, 0:1, :],
            rows,
            store,
        )
        for row in range(0, height, rows):
            at = pl.ds(row, rows)
            top_ref[at] = jnp.maximum(top_ref[at], lane_fold(t_ref[chunk, at], jnp.maximum))

    @pl.when((phase == 1) & (chunk == 0))
    def _():
        top = jnp.broadcast_to(jnp.max(top_ref[...], axis=1, keepdims=True), (height, 128))
        top_ref[...] = top
        weight = jnp.exp2(new_ref[...] - spread(top, new_ref.shape[1]))
        total_ref[...] = lane_fold(weight, jnp.add)
        acc_ref[...] = jnp.dot(
            weight.astype(jnp.bfloat16), fresh_ref[1, 0], preferred_element_type=jnp.float32
        )

    @pl.when(phase == 1)
    def _():
        scale = row_ref[chunk, 1:2, :]
        for row in range(0, height, rows):
            at = pl.ds(row, rows)
            weight = jnp.exp2(t_ref[chunk, at] - spread(top_ref[at], width))
            total_ref[at] += lane_fold(weight, jnp.add)
            p_ref[at] = (weight * scale).astype(jnp.bfloat16)
        acc_ref[...] += jnp.dot(
            p_ref[...],
            codes_ref[:, 0, 0].reshape(width, codes_ref.shape[-1]),
            preferred_element_type=jnp.float32,
        )

    @pl.when((phase == 1) & (chunk == chunks - 1))
    def _():
        total_ref[...] = jnp.broadcast_to(
            jnp.sum(total_ref[...], axis=1, keepdims=True), (height, 128)
        )


def route_kernel(
    dims, lists_ref, tables_ref, length_ref, own_ref, moved_ref, more_ref, log_ref, row_ref
):
    pool, heads, instances, everyone, listed, block_len, spans, factor = dims
    me = lax.axis_index("inst")

    def dest(row, m):
        return lists_ref[row, m].astype(jnp.int32)

    def count(row, target):
        return loop(
            listed, lambda m, n: n + jnp.where(dest(row, m) == target, 1, 0), jnp.int32(0)
        )

    def rank(row, m):
        target = dest(row, m)
        return loop(
            listed,
            lambda m2, n: n + jnp.where((dest(row, m2) == target) & (m2 < m), 1, 0),
            jnp.int32(0),
        )

    def before(source, target):
        return loop(
            instances,
            lambda k, n: n + jnp.where(jnp.bitwise_xor(me, k) < source, count(k, target), 0),
            jnp.int32(pool),
        )

    def move(m, carry):
        moved_ref[0, m] = before(me, dest(0, m)) + rank(0, m)
        return carry

    loop(listed, move, 0)

    def seconds(row, more):
        found = loop(listed, lambda m, n: n + jnp.minimum(rank(row, m), 1), jnp.int32(0))
        return jnp.maximum(more, jnp.where(found > 1, 1, 0))

    more_ref[0] = loop(everyone, seconds, jnp.int32(0))
    slots = instances * CAP
    lane = lax.broadcasted_iota(jnp.int32, (1, slots), 1)

    def place(k, ids):
        first = before(jnp.bitwise_xor(me, k), me)

        def find(m, carry):
            seen, blocks = carry
            hit = dest(k, m) == me
            block = lists_ref[k, listed + m].astype(jnp.int32)
            blocks = [jnp.where(hit & (seen == r), block, blocks[r]) for r in range(CAP)]
            return seen + jnp.where(hit, 1, 0), blocks

        seen, blocks = loop(listed, find, (jnp.int32(0), [jnp.int32(0)] * CAP))
        for r in range(CAP):
            slot = r * instances + k
            ids = jnp.where(lane == slot, jnp.where(r < seen, first + r, -1), ids)
            at = pl.ds(pl.multiple_of(slot * block_len, block_len), block_len)
            for h in range(heads):
                key = lists_ref[k, 2 * listed + h * pool + blocks[r]]
                value = lists_ref[k, 2 * listed + (heads + h) * pool + blocks[r]]
                row_ref[h : h + 1, at] = jnp.full((1, block_len), key * (factor * LOG2E))
                row_ref[heads + h : heads + h + 1, at] = jnp.full((1, block_len), value)
        return ids

    ids = loop(instances, place, jnp.full((1, slots), -1, jnp.int32))

    def store(b, value):
        log_ref[:, b * block_len : (b + 1) * block_len] = value

    count_log(tables_ref[...], length_ref[...], ids, block_len, spans, store)


def arrival_kernel(dims, places, q_ref, log_ref, row_ref, *refs):
    heads, rows, block_len = dims
    own_refs, refs = refs[: 3 * heads], refs[3 * heads :]
    code_refs, (out_ref, t_ref, p_ref) = refs[:-3], refs[-3:]
    height = q_ref.shape[1]
    width = 2 * block_len
    slots = [code_refs[array].at[row] for array, row in places]
    pairs = len(slots) // 2

    def pair(i, part, h):
        return jnp.concatenate([slots[2 * i][part, h], slots[2 * i + 1][part, h]], axis=0)

    for h in range(heads):
        for i in range(pairs):
            left = i * width

            def store(row, lane, value, h=h, left=left):
                t_ref[h, row : row + rows, left + lane : left + lane + value.shape[1]] = value

            score_tiles(
                q_ref[h],
                pair(i, 0, h),
                log_ref.at[:, left : left + width],
                row_ref[h : h + 1, left : left + width],
                rows,
                store,
            )
    for h in range(heads):
        acc_ref, top_ref, total_ref = own_refs[3 * h : 3 * h + 3]
        scale = row_ref[heads + h : heads + h + 1, :]
        for row in range(0, height, rows):
            at = pl.ds(row, rows)
            score = t_ref[h, at]
            own_top = top_ref[at]
            top = jnp.maximum(
                own_top, jnp.max(lane_fold(score, jnp.maximum), axis=1, keepdims=True)
            )
            weight = jnp.exp2(score - spread(top, score.shape[1]))
            keep = jnp.exp2(own_top - top)
            total = total_ref[at] * keep + jnp.sum(
                lane_fold(weight, jnp.add), axis=1, keepdims=True
            )
            p_ref[h, at] = (weight * scale).astype(jnp.bfloat16)
            t_ref[h, at, 0:128] = keep
            t_ref[h, at, 128:256] = 1.0 / total
        mixed = acc_ref[...] * t_ref[h, :, 0:128]
        for i in range(pairs):
            mixed = mixed + jnp.dot(
                p_ref[h, :, i * width : (i + 1) * width],
                pair(i, 1, h),
                preferred_element_type=jnp.float32,
            )
        result = (mixed * t_ref[h, :, 128:256]).astype(jnp.bfloat16)
        out_ref[:, h] = result.reshape(height // rows, rows, result.shape[-1])


def doubling(bits, value, axis):
    for bit in bits:
        size = lax.axis_size(axis)
        moved = lax.ppermute(value, axis, [(j, j ^ bit) for j in range(size)])
        value = jnp.concatenate([value, moved], axis=0)
    return value


def attend(
    general, queries, new_kv, pool_codes, pool_scales, tables, ctx_len, mig_block, mig_dest
):
    instances, groups = lax.axis_size("inst"), lax.axis_size("groups")
    pool = pool_codes.shape[0]
    requests, steps, q_heads, head_dim = queries.shape
    heads = new_kv.shape[3]
    per_head = q_heads // heads
    spans = tables.shape[1]
    block_len = pool_codes.shape[3]
    listed = mig_dest.shape[1]
    factor = head_dim ** (-0.5)
    rows = per_head * steps
    height = requests * rows
    slots = instances * CAP
    group = 8
    f32, bf16 = jnp.float32, jnp.bfloat16
    block_shape = pool_codes.shape[1:]
    block_bytes = 2 * math.prod(block_shape)
    inst_bits = [1 << i for i in range(instances.bit_length() - 1)]
    group_bits = [1 << i for i in range(groups.bit_length() - 1)]
    assert instances == 1 << len(inst_bits) and groups == 1 << len(group_bits)

    if general:
        sizes = [CAP] * instances
        copies = [(r * instances + k, [(k, r)]) for k in range(instances) for r in range(CAP)]
    else:
        sizes = [1, 2] + [1] * (instances - 1)
        copies = [(2 * instances, [(instances, 0), (1, 1)])]
        copies += [(k, [(k, 0)]) for k in list(range(instances))[::-1]]
    stores = sum(len(targets) for _, targets in copies)
    send = pl.pallas_call(
        functools.partial(pack_kernel, instances, listed, copies),
        out_shape=[jax.ShapeDtypeStruct((size,) + block_shape, bf16) for size in sizes],
        in_specs=[SMEM_SPEC, SMEM_SPEC, HBM_SPEC],
        out_specs=[HBM_SPEC] * len(sizes),
        scratch_shapes=[
            pltpu.SMEM((2 * instances + 1,), jnp.int32),
            pltpu.VMEM((len(copies),) + block_shape, bf16),
            pltpu.SemaphoreType.DMA((len(copies),)),
            pltpu.SemaphoreType.DMA((stores,)),
        ],
        compiler_params=pltpu.CompilerParams(vmem_limit_bytes=56 * MIB),
        cost_estimate=pl.CostEstimate(
            flops=0, bytes_accessed=2 * stores * block_bytes, transcendentals=0
        ),
        name="pack_blocks",
    )(mig_dest, mig_block, pool_codes)
    mig_dest, mig_block, pool_scales, *send = lax.optimization_barrier(
        (mig_dest, mig_block, pool_scales, *send)
    )

    def swap(value, distance):
        return lax.ppermute(value, "inst", [(j, j ^ distance) for j in range(instances)])

    if general:
        arrived = [send[0]] + [swap(send[k], k) for k in range(1, instances)]
        places = [(k, r) for r in range(CAP) for k in range(instances)]
    else:
        second = send.pop()
        seconds = {0: second}
        for bit in inst_bits[:0:-1]:
            for k in list(seconds):
                seconds[k ^ bit] = swap(seconds[k], bit)
        arrived = [send[0]] + [swap(send[k], k) for k in range(1, instances)]
        for k in list(seconds):
            if k:
                seconds[k ^ 1] = swap(seconds[k], 1)
        places = [(k, 0) for k in range(instances)]
        for k in range(instances):
            if k == 1:
                places.append((1, 1))
            else:
                places.append((len(arrived), 0))
                arrived.append(seconds[k])

    flat_scales = jnp.transpose(pool_scales, (1, 2, 0)).reshape(1, -1).astype(f32)
    lists = jnp.concatenate([mig_dest.astype(f32), mig_block.astype(f32), flat_scales], axis=1)
    lists_in = doubling(group_bits, doubling(inst_bits, lists, "inst"), "groups")

    query_rows = (
        queries.reshape(requests, steps, heads, per_head, head_dim)
        .transpose(2, 0, 3, 1, 4)
        .reshape(heads, height, head_dim)
    )
    fresh_len = requests * steps
    fresh = new_kv.transpose(2, 3, 0, 1, 4).reshape(2, heads, fresh_len, head_dim)
    fresh = jnp.pad(fresh, ((0, 0), (0, 0), (0, -fresh_len % 128), (0, 0)))
    fresh_len = fresh.shape[2]
    length = ctx_len[:, None]
    width = group * block_len
    chunks = pool // group
    tokens = pool * block_len

    def whole(shape):
        return pl.BlockSpec(shape, lambda p, c: (0,) * len(shape))

    def own(head):
        return pl.pallas_call(
            functools.partial(
                own_kernel, (head, pool, heads, rows, steps, block_len, spans, factor, group)
            ),
            grid=(2, chunks),
            out_shape=[jax.ShapeDtypeStruct((height, head_dim), f32)] * 3,
            in_specs=[
                whole(tables.shape),
                whole(length.shape),
                SMEM_SPEC,
                pl.BlockSpec((1, height, head_dim), lambda p, c: (head, 0, 0)),
                pl.BlockSpec((2, 1, fresh_len, head_dim), lambda p, c: (0, head, 0, 0)),
                pl.BlockSpec(
                    (group, 1, 1, block_len, head_dim), lambda p, c: (c, p, head, 0, 0)
                ),
            ],
            out_specs=[whole((height, head_dim))] * 3,
            scratch_shapes=[
                pltpu.VMEM((chunks, requests, width), f32),
                pltpu.VMEM((chunks, 2, width), f32),
                pltpu.VMEM((chunks, height, width), f32),
                pltpu.VMEM((height, fresh_len), f32),
                pltpu.VMEM((height, width), bf16),
            ],
            compiler_params=pltpu.CompilerParams(vmem_limit_bytes=32 * MIB),
            cost_estimate=pl.CostEstimate(
                flops=4 * height * tokens * head_dim,
                bytes_accessed=pool_codes.size * 2 // heads,
                transcendentals=height * tokens,
            ),
            name="own_blocks",
        )(tables, length, flat_scales, query_rows, fresh, pool_codes)

    own_parts = [value for head in range(heads) for value in own(head)]

    moved_to, more, log_in, rows_in = pl.pallas_call(
        functools.partial(
            route_kernel,
            (pool, heads, instances, groups * instances, listed, block_len, spans, factor),
        ),
        out_shape=[
            jax.ShapeDtypeStruct((1, listed), jnp.int32),
            jax.ShapeDtypeStruct((1,), jnp.int32),
            jax.ShapeDtypeStruct((requests, slots * block_len), f32),
            jax.ShapeDtypeStruct((2 * heads, slots * block_len), f32),
        ],
        in_specs=[SMEM_SPEC, VMEM_SPEC, VMEM_SPEC, HBM_SPEC],
        out_specs=[SMEM_SPEC, SMEM_SPEC, VMEM_SPEC, VMEM_SPEC],
        compiler_params=pltpu.CompilerParams(vmem_limit_bytes=8 * MIB),
        name="route_arrivals",
    )(lists_in, tables, length, own_parts[-1])

    arrival_bytes = 6 * heads * height * slots * block_len + 2 * 12 * height * head_dim * heads
    arrival_bytes += 2 * slots * block_bytes
    out = pl.pallas_call(
        functools.partial(arrival_kernel, (heads, rows, block_len), places),
        out_shape=jax.ShapeDtypeStruct((requests, heads, rows, head_dim), bf16),
        in_specs=[VMEM_SPEC] * (3 + 3 * heads + len(arrived)),
        out_specs=VMEM_SPEC,
        scratch_shapes=[
            pltpu.VMEM((heads, height, slots * block_len), f32),
            pltpu.VMEM((heads, height, slots * block_len), bf16),
        ],
        compiler_params=pltpu.CompilerParams(vmem_limit_bytes=arrival_bytes + 8 * MIB),
        cost_estimate=pl.CostEstimate(
            flops=4 * heads * height * slots * block_len * head_dim,
            bytes_accessed=slots * block_bytes,
            transcendentals=heads * height * slots * block_len,
        ),
        name="arrived_blocks",
    )(query_rows, log_in, rows_in, *own_parts, *arrived)
    out = (
        out.reshape(requests, q_heads, steps, head_dim)
        .transpose(0, 2, 1, 3)
        .reshape(requests, steps, q_heads * head_dim)
    )
    return out, moved_to, more


def shards(*args):
    out, moved_to, more = attend(False, *args)
    out = lax.cond(
        more[0] > 0,
        lambda out, *args: attend(True, *args)[0],
        lambda out, *args: out,
        out, *args,
    )
    return out, moved_to


def solution(mesh):
    in_specs = (
        P(("groups", "inst"), None, "tp", None),
        P(("groups", "inst"), None, None, "tp", None),
        P(("groups", "inst"), None, "tp", None, None),
        P(("groups", "inst"), None, "tp"),
        P(("groups", "inst"), None),
        P(("groups", "inst")),
        P(("groups", "inst"), None),
        P(("groups", "inst"), None),
    )
    out_specs = (P(("groups", "inst"), None, "tp"), P(("groups", "inst"), None))
    return jax.shard_map(shards, mesh=mesh, in_specs=in_specs, out_specs=out_specs, check_vma=False)
```

```python
import functools
import math

import jax
import jax.numpy as jnp
from jax import lax
from jax.experimental import pallas as pl
from jax.experimental.pallas import tpu as pltpu
from jax.sharding import PartitionSpec as P

CAP = 2
LOG2E = math.log2(math.e)
MIB = 1 << 20
SMEM_SPEC = pl.BlockSpec(memory_space=pltpu.SMEM)
VMEM_SPEC = pl.BlockSpec(memory_space=pltpu.VMEM)
HBM_SPEC = pl.BlockSpec(memory_space=pltpu.HBM)
NT = (((1,), (1,)), ((), ()))


def loop(count, body, init):
    if count <= 8:
        for i in range(count):
            init = body(i, init)
        return init
    return lax.fori_loop(0, count, body, init)


def pack_kernel(instances, listed, copies, dest_ref, block_ref, pool_ref, *refs):
    count = len(refs) - 4
    send_refs, (index_ref, held_ref, in_sems, out_sems) = refs[:count], refs[count:]
    me = lax.axis_index("inst")
    for entry in range(2 * instances + 1):
        index_ref[entry] = 0

    def place(m, carry):
        dest = dest_ref[0, m]
        rank = loop(
            listed,
            lambda m2, n: n + jnp.where((dest_ref[0, m2] == dest) & (m2 < m), 1, 0),
            jnp.int32(0),
        )
        entry = jnp.bitwise_xor(dest, me) + jnp.where(rank > 0, instances, 0)
        index_ref[entry] = block_ref[0, m]
        index_ref[jnp.where(rank > 0, 2 * instances, entry)] = block_ref[0, m]
        return carry

    loop(listed, place, 0)
    loads, stores = [], []
    for i, (entry, _) in enumerate(copies):
        loads.append(
            pltpu.make_async_copy(pool_ref.at[index_ref[entry]], held_ref.at[i], in_sems.at[i])
        )
        loads[-1].start()
    for i, (_, targets) in enumerate(copies):
        loads[i].wait()
        for output, row in targets:
            stores.append(
                pltpu.make_async_copy(
                    held_ref.at[i], send_refs[output].at[row], out_sems.at[len(stores)]
                )
            )
            stores[-1].start()
    for store in stores:
        store.wait()


def split(value, size):
    assert size & (size - 1) == 0
    return lax.shift_right_logical(value, size.bit_length() - 1), value & (size - 1)


def count_log(tables, length, ids, block_len, spans, store):
    requests, width = tables.shape[0], ids.shape[1]
    whole, rest = split(length, block_len)
    whole = jnp.broadcast_to(whole, (requests, width))
    full = jnp.zeros((requests, width), jnp.float32)
    part = jnp.zeros((requests, width), jnp.float32)
    for e in range(spans):
        hit = jnp.broadcast_to(tables[:, e : e + 1], (requests, width)) == ids
        full = full + jnp.where(hit & (whole > e), 1.0, 0.0)
        part = part + jnp.where(hit & (whole == e), 1.0, 0.0)

    def log2(count):
        return jnp.where(count > 0, jnp.log(jnp.maximum(count, 1.0)) * LOG2E, -jnp.inf)

    beyond, within = log2(full), log2(full + part)
    shape = (requests, block_len)
    inside = lax.broadcasted_iota(jnp.int32, shape, 1) < jnp.broadcast_to(rest, shape)
    for b in range(width):
        store(
            b,
            jnp.where(
                inside,
                jnp.broadcast_to(within[:, b : b + 1], shape),
                jnp.broadcast_to(beyond[:, b : b + 1], shape),
            ),
        )


def score_tiles(query, keys, log_ref, scale_row, rows, store):
    height, wide = min(256, query.shape[0]), min(256, keys.shape[0])
    for top in range(0, query.shape[0], height):
        for left in range(0, keys.shape[0], wide):
            part = lax.dot_general(
                query[top : top + height],
                keys[left : left + wide],
                NT,
                preferred_element_type=jnp.float32,
            )
            scale = scale_row[:, left : left + wide]
            for r in range(height // rows):
                request = top // rows + r
                store(
                    request * rows,
                    left,
                    part[r * rows : (r + 1) * rows] * scale
                    + log_ref[request : request + 1, left : left + wide],
                )


def lane_fold(value, op):
    parts = [value[:, i : i + 128] for i in range(0, value.shape[1], 128)]
    while len(parts) > 1:
        parts = [
            op(parts[i], parts[i + 1]) if i + 1 < len(parts) else parts[i]
            for i in range(0, len(parts), 2)
        ]
    return parts[0]


def spread(column, width):
    return jnp.concatenate([column] * (width // 128), axis=1)


def own_kernel(
    dims,
    tables_ref, length_ref, scale_ref, q_ref, fresh_ref, codes_ref,
    acc_ref, top_ref, total_ref,
    log_ref, row_ref, t_ref, new_ref, p_ref,
):
    head, pool, heads, rows, steps, block_len, spans, factor, group = dims
    phase, chunk = pl.program_id(0), pl.program_id(1)
    chunks = pool // group
    height = q_ref.shape[1]
    width = group * block_len

    @pl.when((phase == 0) & (chunk == 0))
    def _():
        ids = lax.broadcasted_iota(jnp.int32, (1, pool), 1)

        def store(b, value):
            lane = (b % group) * block_len
            log_ref[b // group, :, lane : lane + block_len] = value

        count_log(tables_ref[...], length_ref[...], ids, block_len, spans, store)
        for b in range(pool):
            lane = (b % group) * block_len
            for part, unit in ((0, factor * LOG2E), (1, 1.0)):
                row_ref[b // group, part : part + 1, lane : lane + block_len] = jnp.full(
                    (1, block_len), scale_ref[0, (part * heads + head) * pool + b] * unit
                )
        shape = (height, fresh_ref.shape[2])
        row = lax.broadcasted_iota(jnp.int32, shape, 0)
        col = lax.broadcasted_iota(jnp.int32, shape, 1)
        (request, row_step), (owner, step) = split(row, rows), split(col, steps)
        seen = (request == owner) & (split(row_step, steps)[1] >= step)
        score = lax.dot_general(
            q_ref[0], fresh_ref[0, 0], NT, preferred_element_type=jnp.float32
        )
        score = jnp.where(seen, score * (factor * LOG2E), -jnp.inf)
        new_ref[...] = score
        top_ref[...] = lane_fold(score, jnp.maximum)

    @pl.when(phase == 0)
    def _():
        def store(row, lane, value):
            t_ref[chunk, row : row + rows, lane : lane + value.shape[1]] = value

        score_tiles(
            q_ref[0],
            codes_ref[:, 0, 0].reshape(width, codes_ref.shape[-1]),
            log_ref.at[chunk],
            row_ref[chunk, 0:1, :],
            rows,
            store,
        )
        for row in range(0, height, rows):
            at = pl.ds(row, rows)
            top_ref[at] = jnp.maximum(top_ref[at], lane_fold(t_ref[chunk, at], jnp.maximum))

    @pl.when((phase == 1) & (chunk == 0))
    def _():
        top = jnp.broadcast_to(jnp.max(top_ref[...], axis=1, keepdims=True), (height, 128))
        top_ref[...] = top
        weight = jnp.exp2(new_ref[...] - spread(top, new_ref.shape[1]))
        total_ref[...] = lane_fold(weight, jnp.add)
        acc_ref[...] = jnp.dot(
            weight.astype(jnp.bfloat16), fresh_ref[1, 0], preferred_element_type=jnp.float32
        )

    @pl.when(phase == 1)
    def _():
        scale = row_ref[chunk, 1:2, :]
        for row in range(0, height, rows):
            at = pl.ds(row, rows)
            weight = jnp.exp2(t_ref[chunk, at] - spread(top_ref[at], width))
            total_ref[at] += lane_fold(weight, jnp.add)
            p_ref[at] = (weight * scale).astype(jnp.bfloat16)
        acc_ref[...] += jnp.dot(
            p_ref[...],
            codes_ref[:, 0, 0].reshape(width, codes_ref.shape[-1]),
            preferred_element_type=jnp.float32,
        )

    @pl.when((phase == 1) & (chunk == chunks - 1))
    def _():
        total_ref[...] = jnp.broadcast_to(
            jnp.sum(total_ref[...], axis=1, keepdims=True), (height, 128)
        )


def route_kernel(
    dims, lists_ref, tables_ref, length_ref, own_ref, moved_ref, more_ref, log_ref, row_ref
):
    pool, heads, instances, everyone, listed, block_len, spans, factor = dims
    me = lax.axis_index("inst")

    def dest(row, m):
        return lists_ref[row, m].astype(jnp.int32)

    def count(row, target):
        return loop(
            listed, lambda m, n: n + jnp.where(dest(row, m) == target, 1, 0), jnp.int32(0)
        )

    def rank(row, m):
        target = dest(row, m)
        return loop(
            listed,
            lambda m2, n: n + jnp.where((dest(row, m2) == target) & (m2 < m), 1, 0),
            jnp.int32(0),
        )

    def before(source, target):
        return loop(
            instances,
            lambda k, n: n + jnp.where(jnp.bitwise_xor(me, k) < source, count(k, target), 0),
            jnp.int32(pool),
        )

    def move(m, carry):
        moved_ref[0, m] = before(me, dest(0, m)) + rank(0, m)
        return carry

    loop(listed, move, 0)

    def seconds(row, more):
        found = loop(listed, lambda m, n: n + jnp.minimum(rank(row, m), 1), jnp.int32(0))
        return jnp.maximum(more, jnp.where(found > 1, 1, 0))

    more_ref[0] = loop(everyone, seconds, jnp.int32(0))
    slots = instances * CAP
    lane = lax.broadcasted_iota(jnp.int32, (1, slots), 1)

    def place(k, ids):
        first = before(jnp.bitwise_xor(me, k), me)

        def find(m, carry):
            seen, blocks = carry
            hit = dest(k, m) == me
            block = lists_ref[k, listed + m].astype(jnp.int32)
            blocks = [jnp.where(hit & (seen == r), block, blocks[r]) for r in range(CAP)]
            return seen + jnp.where(hit, 1, 0), blocks

        seen, blocks = loop(listed, find, (jnp.int32(0), [jnp.int32(0)] * CAP))
        for r in range(CAP):
            slot = r * instances + k
            ids = jnp.where(lane == slot, jnp.where(r < seen, first + r, -1), ids)
            at = pl.ds(pl.multiple_of(slot * block_len, block_len), block_len)
            for h in range(heads):
                key = lists_ref[k, 2 * listed + h * pool + blocks[r]]
                value = lists_ref[k, 2 * listed + (heads + h) * pool + blocks[r]]
                row_ref[h : h + 1, at] = jnp.full((1, block_len), key * (factor * LOG2E))
                row_ref[heads + h : heads + h + 1, at] = jnp.full((1, block_len), value)
        return ids

    ids = loop(instances, place, jnp.full((1, slots), -1, jnp.int32))

    def store(b, value):
        log_ref[:, b * block_len : (b + 1) * block_len] = value

    count_log(tables_ref[...], length_ref[...], ids, block_len, spans, store)


def arrival_kernel(dims, places, q_ref, log_ref, row_ref, *refs):
    heads, rows, block_len = dims
    own_refs, refs = refs[: 3 * heads], refs[3 * heads :]
    code_refs, (out_ref, t_ref, p_ref) = refs[:-3], refs[-3:]
    height = q_ref.shape[1]
    width = 2 * block_len
    slots = [code_refs[array].at[row] for array, row in places]
    pairs = len(slots) // 2

    def pair(i, part, h):
        return jnp.concatenate([slots[2 * i][part, h], slots[2 * i + 1][part, h]], axis=0)

    for h in range(heads):
        for i in range(pairs):
            left = i * width

            def store(row, lane, value, h=h, left=left):
                t_ref[h, row : row + rows, left + lane : left + lane + value.shape[1]] = value

            score_tiles(
                q_ref[h],
                pair(i, 0, h),
                log_ref.at[:, left : left + width],
                row_ref[h : h + 1, left : left + width],
                rows,
                store,
            )
    for h in range(heads):
        acc_ref, top_ref, total_ref = own_refs[3 * h : 3 * h + 3]
        scale = row_ref[heads + h : heads + h + 1, :]
        for row in range(0, height, rows):
            at = pl.ds(row, rows)
            score = t_ref[h, at]
            own_top = top_ref[at]
            top = jnp.maximum(
                own_top, jnp.max(lane_fold(score, jnp.maximum), axis=1, keepdims=True)
            )
            weight = jnp.exp2(score - spread(top, score.shape[1]))
            keep = jnp.exp2(own_top - top)
            total = total_ref[at] * keep + jnp.sum(
                lane_fold(weight, jnp.add), axis=1, keepdims=True
            )
            p_ref[h, at] = (weight * scale).astype(jnp.bfloat16)
            t_ref[h, at, 0:128] = keep
            t_ref[h, at, 128:256] = 1.0 / total
        mixed = acc_ref[...] * t_ref[h, :, 0:128]
        for i in range(pairs):
            mixed = mixed + jnp.dot(
                p_ref[h, :, i * width : (i + 1) * width],
                pair(i, 1, h),
                preferred_element_type=jnp.float32,
            )
        result = (mixed * t_ref[h, :, 128:256]).astype(jnp.bfloat16)
        out_ref[:, h] = result.reshape(height // rows, rows, result.shape[-1])


def doubling(bits, value, axis):
    for bit in bits:
        size = lax.axis_size(axis)
        moved = lax.ppermute(value, axis, [(j, j ^ bit) for j in range(size)])
        value = jnp.concatenate([value, moved], axis=0)
    return value


def attend(
    general, queries, new_kv, pool_codes, pool_scales, tables, ctx_len, mig_block, mig_dest
):
    instances, groups = lax.axis_size("inst"), lax.axis_size("groups")
    pool = pool_codes.shape[0]
    requests, steps, q_heads, head_dim = queries.shape
    heads = new_kv.shape[3]
    per_head = q_heads // heads
    spans = tables.shape[1]
    block_len = pool_codes.shape[3]
    listed = mig_dest.shape[1]
    factor = head_dim ** (-0.5)
    rows = per_head * steps
    height = requests * rows
    slots = instances * CAP
    group = 8
    f32, bf16 = jnp.float32, jnp.bfloat16
    block_shape = pool_codes.shape[1:]
    block_bytes = 2 * math.prod(block_shape)
    inst_bits = [1 << i for i in range(instances.bit_length() - 1)]
    group_bits = [1 << i for i in range(groups.bit_length() - 1)]
    assert instances == 1 << len(inst_bits) and groups == 1 << len(group_bits)

    if general:
        sizes = [CAP] * instances
        copies = [(r * instances + k, [(k, r)]) for k in range(instances) for r in range(CAP)]
    else:
        sizes = [1, 2] + [1] * (instances - 1)
        copies = [(2 * instances, [(instances, 0), (1, 1)])]
        copies += [(k, [(k, 0)]) for k in list(range(instances))[::-1]]
    stores = sum(len(targets) for _, targets in copies)
    send = pl.pallas_call(
        functools.partial(pack_kernel, instances, listed, copies),
        out_shape=[jax.ShapeDtypeStruct((size,) + block_shape, bf16) for size in sizes],
        in_specs=[SMEM_SPEC, SMEM_SPEC, HBM_SPEC],
        out_specs=[HBM_SPEC] * len(sizes),
        scratch_shapes=[
            pltpu.SMEM((2 * instances + 1,), jnp.int32),
            pltpu.VMEM((len(copies),) + block_shape, bf16),
            pltpu.SemaphoreType.DMA((len(copies),)),
            pltpu.SemaphoreType.DMA((stores,)),
        ],
        compiler_params=pltpu.CompilerParams(vmem_limit_bytes=56 * MIB),
        cost_estimate=pl.CostEstimate(
            flops=0, bytes_accessed=2 * stores * block_bytes, transcendentals=0
        ),
        name="pack_blocks",
    )(mig_dest, mig_block, pool_codes)
    mig_dest, mig_block, pool_scales, *send = lax.optimization_barrier(
        (mig_dest, mig_block, pool_scales, *send)
    )

    def swap(value, distance):
        return lax.ppermute(value, "inst", [(j, j ^ distance) for j in range(instances)])

    if general:
        arrived = [send[0]] + [swap(send[k], k) for k in range(1, instances)]
        places = [(k, r) for r in range(CAP) for k in range(instances)]
    else:
        second = send.pop()
        seconds = {0: second}
        for bit in inst_bits[:0:-1]:
            for k in list(seconds):
                seconds[k ^ bit] = swap(seconds[k], bit)
        arrived = [send[0]] + [swap(send[k], k) for k in range(1, instances)]
        for k in list(seconds):
            if k:
                seconds[k ^ 1] = swap(seconds[k], 1)
        places = [(k, 0) for k in range(instances)]
        for k in range(instances):
            if k == 1:
                places.append((1, 1))
            else:
                places.append((len(arrived), 0))
                arrived.append(seconds[k])

    flat_scales = jnp.transpose(pool_scales, (1, 2, 0)).reshape(1, -1).astype(f32)
    lists = jnp.concatenate([mig_dest.astype(f32), mig_block.astype(f32), flat_scales], axis=1)
    lists_in = doubling(group_bits, doubling(inst_bits, lists, "inst"), "groups")

    query_rows = (
        queries.reshape(requests, steps, heads, per_head, head_dim)
        .transpose(2, 0, 3, 1, 4)
        .reshape(heads, height, head_dim)
    )
    fresh_len = requests * steps
    fresh = new_kv.transpose(2, 3, 0, 1, 4).reshape(2, heads, fresh_len, head_dim)
    fresh = jnp.pad(fresh, ((0, 0), (0, 0), (0, -fresh_len % 128), (0, 0)))
    fresh_len = fresh.shape[2]
    length = ctx_len[:, None]
    width = group * block_len
    chunks = pool // group
    tokens = pool * block_len

    def whole(shape):
        return pl.BlockSpec(shape, lambda p, c: (0,) * len(shape))

    def own(head):
        return pl.pallas_call(
            functools.partial(
                own_kernel, (head, pool, heads, rows, steps, block_len, spans, factor, group)
            ),
            grid=(2, chunks),
            out_shape=[jax.ShapeDtypeStruct((height, head_dim), f32)] * 3,
            in_specs=[
                whole(tables.shape),
                whole(length.shape),
                SMEM_SPEC,
                pl.BlockSpec((1, height, head_dim), lambda p, c: (head, 0, 0)),
                pl.BlockSpec((2, 1, fresh_len, head_dim), lambda p, c: (0, head, 0, 0)),
                pl.BlockSpec(
                    (group, 1, 1, block_len, head_dim), lambda p, c: (c, p, head, 0, 0)
                ),
            ],
            out_specs=[whole((height, head_dim))] * 3,
            scratch_shapes=[
                pltpu.VMEM((chunks, requests, width), f32),
                pltpu.VMEM((chunks, 2, width), f32),
                pltpu.VMEM((chunks, height, width), f32),
                pltpu.VMEM((height, fresh_len), f32),
                pltpu.VMEM((height, width), bf16),
            ],
            compiler_params=pltpu.CompilerParams(vmem_limit_bytes=32 * MIB),
            cost_estimate=pl.CostEstimate(
                flops=4 * height * tokens * head_dim,
                bytes_accessed=pool_codes.size * 2 // heads,
                transcendentals=height * tokens,
            ),
            name="own_blocks",
        )(tables, length, flat_scales, query_rows, fresh, pool_codes)

    own_parts = [value for head in range(heads) for value in own(head)]

    moved_to, more, log_in, rows_in = pl.pallas_call(
        functools.partial(
            route_kernel,
            (pool, heads, instances, groups * instances, listed, block_len, spans, factor),
        ),
        out_shape=[
            jax.ShapeDtypeStruct((1, listed), jnp.int32),
            jax.ShapeDtypeStruct((1,), jnp.int32),
            jax.ShapeDtypeStruct((requests, slots * block_len), f32),
            jax.ShapeDtypeStruct((2 * heads, slots * block_len), f32),
        ],
        in_specs=[SMEM_SPEC, VMEM_SPEC, VMEM_SPEC, HBM_SPEC],
        out_specs=[SMEM_SPEC, SMEM_SPEC, VMEM_SPEC, VMEM_SPEC],
        compiler_params=pltpu.CompilerParams(vmem_limit_bytes=8 * MIB),
        name="route_arrivals",
    )(lists_in, tables, length, own_parts[-1])

    arrival_bytes = 6 * heads * height * slots * block_len + 2 * 12 * height * head_dim * heads
    arrival_bytes += 2 * slots * block_bytes
    out = pl.pallas_call(
        functools.partial(arrival_kernel, (heads, rows, block_len), places),
        out_shape=jax.ShapeDtypeStruct((requests, heads, rows, head_dim), bf16),
        in_specs=[VMEM_SPEC] * (3 + 3 * heads + len(arrived)),
        out_specs=VMEM_SPEC,
        scratch_shapes=[
            pltpu.VMEM((heads, height, slots * block_len), f32),
            pltpu.VMEM((heads, height, slots * block_len), bf16),
        ],
        compiler_params=pltpu.CompilerParams(vmem_limit_bytes=arrival_bytes + 8 * MIB),
        cost_estimate=pl.CostEstimate(
            flops=4 * heads * height * slots * block_len * head_dim,
            bytes_accessed=slots * block_bytes,
            transcendentals=heads * height * slots * block_len,
        ),
        name="arrived_blocks",
    )(query_rows, log_in, rows_in, *own_parts, *arrived)
    out = (
        out.reshape(requests, q_heads, steps, head_dim)
        .transpose(0, 2, 1, 3)
        .reshape(requests, steps, q_heads * head_dim)
    )
    return out, moved_to, more


def shards(*args):
    out, moved_to, more = attend(False, *args)
    out = lax.cond(
        more[0] > 0,
        lambda out, *args: attend(True, *args)[0],
        lambda out, *args: out,
        out, *args,
    )
    return out, moved_to


def solution(mesh):
    in_specs = (
        P(("groups", "inst"), None, "tp", None),
        P(("groups", "inst"), None, None, "tp", None),
        P(("groups", "inst"), None, "tp", None, None),
        P(("groups", "inst"), None, "tp"),
        P(("groups", "inst"), None),
        P(("groups", "inst")),
        P(("groups", "inst"), None),
        P(("groups", "inst"), None),
    )
    out_specs = (P(("groups", "inst"), None, "tp"), P(("groups", "inst"), None))
    return jax.shard_map(shards, mesh=mesh, in_specs=in_specs, out_specs=out_specs, check_vma=False)
```

```python
import functools
import math

import jax
import jax.numpy as jnp
from jax import lax
from jax.experimental import pallas as pl
from jax.experimental.pallas import tpu as pltpu
from jax.sharding import PartitionSpec as P

CAP = 2
LOG2E = math.log2(math.e)
MIB = 1 << 20
SMEM_SPEC = pl.BlockSpec(memory_space=pltpu.SMEM)
VMEM_SPEC = pl.BlockSpec(memory_space=pltpu.VMEM)
HBM_SPEC = pl.BlockSpec(memory_space=pltpu.HBM)
NT = (((1,), (1,)), ((), ()))


def loop(count, body, init):
    if count <= 8:
        for i in range(count):
            init = body(i, init)
        return init
    return lax.fori_loop(0, count, body, init)


def pack_kernel(instances, listed, copies, dest_ref, block_ref, pool_ref, *refs):
    count = len(refs) - 4
    send_refs, (index_ref, held_ref, in_sems, out_sems) = refs[:count], refs[count:]
    me = lax.axis_index("inst")
    for entry in range(2 * instances + 1):
        index_ref[entry] = 0

    def place(m, carry):
        dest = dest_ref[0, m]
        rank = loop(
            listed,
            lambda m2, n: n + jnp.where((dest_ref[0, m2] == dest) & (m2 < m), 1, 0),
            jnp.int32(0),
        )
        entry = jnp.bitwise_xor(dest, me) + jnp.where(rank > 0, instances, 0)
        index_ref[entry] = block_ref[0, m]
        index_ref[jnp.where(rank > 0, 2 * instances, entry)] = block_ref[0, m]
        return carry

    loop(listed, place, 0)
    loads, stores = [], []
    for i, (entry, _) in enumerate(copies):
        loads.append(
            pltpu.make_async_copy(pool_ref.at[index_ref[entry]], held_ref.at[i], in_sems.at[i])
        )
        loads[-1].start()
    for i, (_, targets) in enumerate(copies):
        loads[i].wait()
        for output, row in targets:
            stores.append(
                pltpu.make_async_copy(
                    held_ref.at[i], send_refs[output].at[row], out_sems.at[len(stores)]
                )
            )
            stores[-1].start()
    for store in stores:
        store.wait()


def split(value, size):
    assert size & (size - 1) == 0
    return lax.shift_right_logical(value, size.bit_length() - 1), value & (size - 1)


def count_log(tables, length, ids, block_len, spans, store):
    requests, width = tables.shape[0], ids.shape[1]
    whole, rest = split(length, block_len)
    whole = jnp.broadcast_to(whole, (requests, width))
    full = jnp.zeros((requests, width), jnp.float32)
    part = jnp.zeros((requests, width), jnp.float32)
    for e in range(spans):
        hit = jnp.broadcast_to(tables[:, e : e + 1], (requests, width)) == ids
        full = full + jnp.where(hit & (whole > e), 1.0, 0.0)
        part = part + jnp.where(hit & (whole == e), 1.0, 0.0)

    def log2(count):
        return jnp.where(count > 0, jnp.log(jnp.maximum(count, 1.0)) * LOG2E, -jnp.inf)

    beyond, within = log2(full), log2(full + part)
    shape = (requests, block_len)
    inside = lax.broadcasted_iota(jnp.int32, shape, 1) < jnp.broadcast_to(rest, shape)
    for b in range(width):
        store(
            b,
            jnp.where(
                inside,
                jnp.broadcast_to(within[:, b : b + 1], shape),
                jnp.broadcast_to(beyond[:, b : b + 1], shape),
            ),
        )


def score_tiles(query, keys, log_ref, scale_row, rows, store):
    height, wide = min(256, query.shape[0]), min(256, keys.shape[0])
    for top in range(0, query.shape[0], height):
        for left in range(0, keys.shape[0], wide):
            part = lax.dot_general(
                query[top : top + height],
                keys[left : left + wide],
                NT,
                preferred_element_type=jnp.float32,
            )
            scale = scale_row[:, left : left + wide]
            for r in range(height // rows):
                request = top // rows + r
                store(
                    request * rows,
                    left,
                    part[r * rows : (r + 1) * rows] * scale
                    + log_ref[request : request + 1, left : left + wide],
                )


def lane_fold(value, op):
    parts = [value[:, i : i + 128] for i in range(0, value.shape[1], 128)]
    while len(parts) > 1:
        parts = [
            op(parts[i], parts[i + 1]) if i + 1 < len(parts) else parts[i]
            for i in range(0, len(parts), 2)
        ]
    return parts[0]


def spread(column, width):
    return jnp.concatenate([column] * (width // 128), axis=1)


def own_kernel(
    dims,
    tables_ref, length_ref, scale_ref, q_ref, fresh_ref, pool_ref,
    acc_ref, top_ref, total_ref,
    log_ref, row_ref, t_ref, p_ref, codes_ref, sems,
):
    head, pool, heads, rows, steps, block_len, spans, factor, group = dims
    chunks = pool // group
    height, head_dim = q_ref.shape[1:]
    width = group * block_len

    def load(part, chunk):
        return pltpu.make_async_copy(
            pool_ref.at[pl.ds(chunk * group, group), part, head],
            codes_ref.at[part, chunk],
            sems.at[part, chunk],
        )

    for part in range(2):
        for chunk in range(chunks):
            load(part, chunk).start()

    ids = lax.broadcasted_iota(jnp.int32, (1, pool), 1)

    def store_log(b, value):
        lane = (b % group) * block_len
        log_ref[b // group, :, lane : lane + block_len] = value

    count_log(tables_ref[...], length_ref[...], ids, block_len, spans, store_log)
    for b in range(pool):
        lane = (b % group) * block_len
        for part, unit in ((0, factor * LOG2E), (1, 1.0)):
            row_ref[b // group, part : part + 1, lane : lane + block_len] = jnp.full(
                (1, block_len), scale_ref[0, (part * heads + head) * pool + b] * unit
            )
    shape = (height, fresh_ref.shape[2])
    row = lax.broadcasted_iota(jnp.int32, shape, 0)
    col = lax.broadcasted_iota(jnp.int32, shape, 1)
    (request, row_step), (owner, step) = split(row, rows), split(col, steps)
    seen = (request == owner) & (split(row_step, steps)[1] >= step)
    new_score = lax.dot_general(
        q_ref[head], fresh_ref[0, head], NT, preferred_element_type=jnp.float32
    )
    new_score = jnp.where(seen, new_score * (factor * LOG2E), -jnp.inf)
    acc_ref[...] = new_score
    top_ref[...] = lane_fold(new_score, jnp.maximum)

    def score(chunk, carry):
        load(0, chunk).wait()

        def store(row, lane, value):
            t_ref[chunk, row : row + rows, lane : lane + value.shape[1]] = value

        score_tiles(
            q_ref[head],
            codes_ref[0, chunk].reshape(width, head_dim),
            log_ref.at[chunk],
            row_ref[chunk, 0:1, :],
            rows,
            store,
        )
        for row in range(0, height, rows):
            at = pl.ds(row, rows)
            top_ref[at] = jnp.maximum(top_ref[at], lane_fold(t_ref[chunk, at], jnp.maximum))
        return carry

    lax.fori_loop(0, chunks, score, 0)

    top = jnp.broadcast_to(jnp.max(top_ref[...], axis=1, keepdims=True), (height, 128))
    top_ref[...] = top
    weight = jnp.exp2(acc_ref[...] - spread(top, acc_ref.shape[1]))
    total_ref[...] = lane_fold(weight, jnp.add)
    acc_ref[...] = jnp.dot(
        weight.astype(jnp.bfloat16), fresh_ref[1, head], preferred_element_type=jnp.float32
    )

    def apply(chunk, carry):
        load(1, chunk).wait()
        scale = row_ref[chunk, 1:2, :]
        for row in range(0, height, rows):
            at = pl.ds(row, rows)
            weight = jnp.exp2(t_ref[chunk, at] - spread(top_ref[at], width))
            total_ref[at] += lane_fold(weight, jnp.add)
            p_ref[at] = (weight * scale).astype(jnp.bfloat16)
        acc_ref[...] += jnp.dot(
            p_ref[...],
            codes_ref[1, chunk].reshape(width, head_dim),
            preferred_element_type=jnp.float32,
        )
        return carry

    lax.fori_loop(0, chunks, apply, 0)
    total_ref[...] = jnp.broadcast_to(
        jnp.sum(total_ref[...], axis=1, keepdims=True), (height, 128)
    )


def route_kernel(
    dims, lists_ref, tables_ref, length_ref, own_ref, moved_ref, more_ref, log_ref, row_ref
):
    pool, heads, instances, everyone, listed, block_len, spans, factor = dims
    me = lax.axis_index("inst")

    def dest(row, m):
        return lists_ref[row, m].astype(jnp.int32)

    def count(row, target):
        return loop(
            listed, lambda m, n: n + jnp.where(dest(row, m) == target, 1, 0), jnp.int32(0)
        )

    def rank(row, m):
        target = dest(row, m)
        return loop(
            listed,
            lambda m2, n: n + jnp.where((dest(row, m2) == target) & (m2 < m), 1, 0),
            jnp.int32(0),
        )

    def before(source, target):
        return loop(
            instances,
            lambda k, n: n + jnp.where(jnp.bitwise_xor(me, k) < source, count(k, target), 0),
            jnp.int32(pool),
        )

    def move(m, carry):
        moved_ref[0, m] = before(me, dest(0, m)) + rank(0, m)
        return carry

    loop(listed, move, 0)

    def seconds(row, more):
        found = loop(listed, lambda m, n: n + jnp.minimum(rank(row, m), 1), jnp.int32(0))
        return jnp.maximum(more, jnp.where(found > 1, 1, 0))

    more_ref[0] = loop(everyone, seconds, jnp.int32(0))
    slots = instances * CAP
    lane = lax.broadcasted_iota(jnp.int32, (1, slots), 1)

    def place(k, ids):
        first = before(jnp.bitwise_xor(me, k), me)

        def find(m, carry):
            seen, blocks = carry
            hit = dest(k, m) == me
            block = lists_ref[k, listed + m].astype(jnp.int32)
            blocks = [jnp.where(hit & (seen == r), block, blocks[r]) for r in range(CAP)]
            return seen + jnp.where(hit, 1, 0), blocks

        seen, blocks = loop(listed, find, (jnp.int32(0), [jnp.int32(0)] * CAP))
        for r in range(CAP):
            slot = r * instances + k
            ids = jnp.where(lane == slot, jnp.where(r < seen, first + r, -1), ids)
            at = pl.ds(pl.multiple_of(slot * block_len, block_len), block_len)
            for h in range(heads):
                key = lists_ref[k, 2 * listed + h * pool + blocks[r]]
                value = lists_ref[k, 2 * listed + (heads + h) * pool + blocks[r]]
                row_ref[h : h + 1, at] = jnp.full((1, block_len), key * (factor * LOG2E))
                row_ref[heads + h : heads + h + 1, at] = jnp.full((1, block_len), value)
        return ids

    ids = loop(instances, place, jnp.full((1, slots), -1, jnp.int32))

    def store(b, value):
        log_ref[:, b * block_len : (b + 1) * block_len] = value

    count_log(tables_ref[...], length_ref[...], ids, block_len, spans, store)


def arrival_kernel(dims, places, q_ref, log_ref, row_ref, *refs):
    heads, rows, block_len = dims
    own_refs, refs = refs[: 3 * heads], refs[3 * heads :]
    code_refs, (out_ref, t_ref, p_ref) = refs[:-3], refs[-3:]
    height = q_ref.shape[1]
    width = 2 * block_len
    slots = [code_refs[array].at[row] for array, row in places]
    pairs = len(slots) // 2

    def pair(i, part, h):
        return jnp.concatenate([slots[2 * i][part, h], slots[2 * i + 1][part, h]], axis=0)

    for h in range(heads):
        for i in range(pairs):
            left = i * width

            def store(row, lane, value, h=h, left=left):
                t_ref[h, row : row + rows, left + lane : left + lane + value.shape[1]] = value

            score_tiles(
                q_ref[h],
                pair(i, 0, h),
                log_ref.at[:, left : left + width],
                row_ref[h : h + 1, left : left + width],
                rows,
                store,
            )
    for h in range(heads):
        acc_ref, top_ref, total_ref = own_refs[3 * h : 3 * h + 3]
        scale = row_ref[heads + h : heads + h + 1, :]
        for row in range(0, height, rows):
            at = pl.ds(row, rows)
            score = t_ref[h, at]
            own_top = top_ref[at]
            top = jnp.maximum(
                own_top, jnp.max(lane_fold(score, jnp.maximum), axis=1, keepdims=True)
            )
            weight = jnp.exp2(score - spread(top, score.shape[1]))
            keep = jnp.exp2(own_top - top)
            total = total_ref[at] * keep + jnp.sum(
                lane_fold(weight, jnp.add), axis=1, keepdims=True
            )
            p_ref[h, at] = (weight * scale).astype(jnp.bfloat16)
            t_ref[h, at, 0:128] = keep
            t_ref[h, at, 128:256] = 1.0 / total
        mixed = acc_ref[...] * t_ref[h, :, 0:128]
        for i in range(pairs):
            mixed = mixed + jnp.dot(
                p_ref[h, :, i * width : (i + 1) * width],
                pair(i, 1, h),
                preferred_element_type=jnp.float32,
            )
        result = (mixed * t_ref[h, :, 128:256]).astype(jnp.bfloat16)
        out_ref[:, h] = result.reshape(height // rows, rows, result.shape[-1])


def doubling(bits, value, axis):
    for bit in bits:
        size = lax.axis_size(axis)
        moved = lax.ppermute(value, axis, [(j, j ^ bit) for j in range(size)])
        value = jnp.concatenate([value, moved], axis=0)
    return value


def attend(
    general, queries, new_kv, pool_codes, pool_scales, tables, ctx_len, mig_block, mig_dest
):
    instances, groups = lax.axis_size("inst"), lax.axis_size("groups")
    pool = pool_codes.shape[0]
    requests, steps, q_heads, head_dim = queries.shape
    heads = new_kv.shape[3]
    per_head = q_heads // heads
    spans = tables.shape[1]
    block_len = pool_codes.shape[3]
    listed = mig_dest.shape[1]
    factor = head_dim ** (-0.5)
    rows = per_head * steps
    height = requests * rows
    slots = instances * CAP
    group = 8
    f32, bf16 = jnp.float32, jnp.bfloat16
    block_shape = pool_codes.shape[1:]
    block_bytes = 2 * math.prod(block_shape)
    inst_bits = [1 << i for i in range(instances.bit_length() - 1)]
    group_bits = [1 << i for i in range(groups.bit_length() - 1)]
    assert instances == 1 << len(inst_bits) and groups == 1 << len(group_bits)

    if general:
        sizes = [CAP] * instances
        copies = [(r * instances + k, [(k, r)]) for k in range(instances) for r in range(CAP)]
    else:
        sizes = [1, 2] + [1] * (instances - 1)
        copies = [(2 * instances, [(instances, 0), (1, 1)])]
        copies += [(k, [(k, 0)]) for k in list(range(instances))[::-1]]
    stores = sum(len(targets) for _, targets in copies)
    send = pl.pallas_call(
        functools.partial(pack_kernel, instances, listed, copies),
        out_shape=[jax.ShapeDtypeStruct((size,) + block_shape, bf16) for size in sizes],
        in_specs=[SMEM_SPEC, SMEM_SPEC, HBM_SPEC],
        out_specs=[HBM_SPEC] * len(sizes),
        scratch_shapes=[
            pltpu.SMEM((2 * instances + 1,), jnp.int32),
            pltpu.VMEM((len(copies),) + block_shape, bf16),
            pltpu.SemaphoreType.DMA((len(copies),)),
            pltpu.SemaphoreType.DMA((stores,)),
        ],
        compiler_params=pltpu.CompilerParams(vmem_limit_bytes=56 * MIB),
        cost_estimate=pl.CostEstimate(
            flops=0, bytes_accessed=2 * stores * block_bytes, transcendentals=0
        ),
        name="pack_blocks",
    )(mig_dest, mig_block, pool_codes)
    mig_dest, mig_block, pool_scales, *send = lax.optimization_barrier(
        (mig_dest, mig_block, pool_scales, *send)
    )

    def swap(value, distance):
        return lax.ppermute(value, "inst", [(j, j ^ distance) for j in range(instances)])

    if general:
        arrived = [send[0]] + [swap(send[k], k) for k in range(1, instances)]
        places = [(k, r) for r in range(CAP) for k in range(instances)]
    else:
        second = send.pop()
        seconds = {0: second}
        for bit in inst_bits[:0:-1]:
            for k in list(seconds):
                seconds[k ^ bit] = swap(seconds[k], bit)
        arrived = [send[0]] + [swap(send[k], k) for k in range(1, instances)]
        for k in list(seconds):
            if k:
                seconds[k ^ 1] = swap(seconds[k], 1)
        places = [(k, 0) for k in range(instances)]
        for k in range(instances):
            if k == 1:
                places.append((1, 1))
            else:
                places.append((len(arrived), 0))
                arrived.append(seconds[k])

    flat_scales = jnp.transpose(pool_scales, (1, 2, 0)).reshape(1, -1).astype(f32)
    lists = jnp.concatenate([mig_dest.astype(f32), mig_block.astype(f32), flat_scales], axis=1)
    lists_in = doubling(group_bits, doubling(inst_bits, lists, "inst"), "groups")

    query_rows = (
        queries.reshape(requests, steps, heads, per_head, head_dim)
        .transpose(2, 0, 3, 1, 4)
        .reshape(heads, height, head_dim)
    )
    fresh_len = requests * steps
    fresh = new_kv.transpose(2, 3, 0, 1, 4).reshape(2, heads, fresh_len, head_dim)
    fresh = jnp.pad(fresh, ((0, 0), (0, 0), (0, -fresh_len % 128), (0, 0)))
    assert fresh.shape[2] == head_dim
    length = ctx_len[:, None]
    width = group * block_len
    chunks = pool // group
    tokens = pool * block_len

    def own(head):
        return pl.pallas_call(
            functools.partial(
                own_kernel, (head, pool, heads, rows, steps, block_len, spans, factor, group)
            ),
            out_shape=[jax.ShapeDtypeStruct((height, head_dim), f32)] * 3,
            in_specs=[VMEM_SPEC, VMEM_SPEC, SMEM_SPEC, VMEM_SPEC, VMEM_SPEC, HBM_SPEC],
            out_specs=[VMEM_SPEC] * 3,
            scratch_shapes=[
                pltpu.VMEM((chunks, requests, width), f32),
                pltpu.VMEM((chunks, 2, width), f32),
                pltpu.VMEM((chunks, height, width), f32),
                pltpu.VMEM((height, width), bf16),
                pltpu.VMEM((2, chunks, group, block_len, head_dim), bf16),
                pltpu.SemaphoreType.DMA((2, chunks)),
            ],
            compiler_params=pltpu.CompilerParams(vmem_limit_bytes=32 * MIB),
            cost_estimate=pl.CostEstimate(
                flops=4 * height * tokens * head_dim,
                bytes_accessed=pool_codes.size * 2 // heads,
                transcendentals=height * tokens,
            ),
            name="own_blocks",
        )(tables, length, flat_scales, query_rows, fresh, pool_codes)

    own_parts = [value for head in range(heads) for value in own(head)]

    moved_to, more, log_in, rows_in = pl.pallas_call(
        functools.partial(
            route_kernel,
            (pool, heads, instances, groups * instances, listed, block_len, spans, factor),
        ),
        out_shape=[
            jax.ShapeDtypeStruct((1, listed), jnp.int32),
            jax.ShapeDtypeStruct((1,), jnp.int32),
            jax.ShapeDtypeStruct((requests, slots * block_len), f32),
            jax.ShapeDtypeStruct((2 * heads, slots * block_len), f32),
        ],
        in_specs=[SMEM_SPEC, VMEM_SPEC, VMEM_SPEC, HBM_SPEC],
        out_specs=[SMEM_SPEC, SMEM_SPEC, VMEM_SPEC, VMEM_SPEC],
        compiler_params=pltpu.CompilerParams(vmem_limit_bytes=8 * MIB),
        name="route_arrivals",
    )(lists_in, tables, length, own_parts[-1])

    arrival_bytes = 6 * heads * height * slots * block_len + 2 * 12 * height * head_dim * heads
    arrival_bytes += 2 * slots * block_bytes
    out = pl.pallas_call(
        functools.partial(arrival_kernel, (heads, rows, block_len), places),
        out_shape=jax.ShapeDtypeStruct((requests, heads, rows, head_dim), bf16),
        in_specs=[VMEM_SPEC] * (3 + 3 * heads + len(arrived)),
        out_specs=VMEM_SPEC,
        scratch_shapes=[
            pltpu.VMEM((heads, height, slots * block_len), f32),
            pltpu.VMEM((heads, height, slots * block_len), bf16),
        ],
        compiler_params=pltpu.CompilerParams(vmem_limit_bytes=arrival_bytes + 8 * MIB),
        cost_estimate=pl.CostEstimate(
            flops=4 * heads * height * slots * block_len * head_dim,
            bytes_accessed=slots * block_bytes,
            transcendentals=heads * height * slots * block_len,
        ),
        name="arrived_blocks",
    )(query_rows, log_in, rows_in, *own_parts, *arrived)
    out = (
        out.reshape(requests, q_heads, steps, head_dim)
        .transpose(0, 2, 1, 3)
        .reshape(requests, steps, q_heads * head_dim)
    )
    return out, moved_to, more


def shards(*args):
    out, moved_to, more = attend(False, *args)
    out = lax.cond(
        more[0] > 0,
        lambda out, *args: attend(True, *args)[0],
        lambda out, *args: out,
        out, *args,
    )
    return out, moved_to


def solution(mesh):
    in_specs = (
        P(("groups", "inst"), None, "tp", None),
        P(("groups", "inst"), None, None, "tp", None),
        P(("groups", "inst"), None, "tp", None, None),
        P(("groups", "inst"), None, "tp"),
        P(("groups", "inst"), None),
        P(("groups", "inst")),
        P(("groups", "inst"), None),
        P(("groups", "inst"), None),
    )
    out_specs = (P(("groups", "inst"), None, "tp"), P(("groups", "inst"), None))
    return jax.shard_map(shards, mesh=mesh, in_specs=in_specs, out_specs=out_specs, check_vma=False)
```

```python
import functools
import math

import jax
import jax.numpy as jnp
from jax import lax
from jax.experimental import pallas as pl
from jax.experimental.pallas import tpu as pltpu
from jax.sharding import PartitionSpec as P

CAP = 2
LOG2E = math.log2(math.e)
MIB = 1 << 20
SMEM_SPEC = pl.BlockSpec(memory_space=pltpu.SMEM)
VMEM_SPEC = pl.BlockSpec(memory_space=pltpu.VMEM)
HBM_SPEC = pl.BlockSpec(memory_space=pltpu.HBM)
NT = (((1,), (1,)), ((), ()))


def loop(count, body, init):
    if count <= 8:
        for i in range(count):
            init = body(i, init)
        return init
    return lax.fori_loop(0, count, body, init)


def pack_kernel(instances, listed, dest_ref, block_ref, pool_ref, *refs):
    send_refs, (index_ref, held_ref, in_sems, out_sems) = refs[:instances], refs[instances:]
    slots = instances * CAP
    me = lax.axis_index("inst")
    for slot in range(slots):
        index_ref[slot] = 0

    def place(m, carry):
        dest = dest_ref[0, m]
        rank = loop(
            listed,
            lambda m2, n: n + jnp.where((dest_ref[0, m2] == dest) & (m2 < m), 1, 0),
            jnp.int32(0),
        )
        index_ref[jnp.bitwise_xor(dest, me) * CAP + jnp.minimum(rank, CAP - 1)] = block_ref[0, m]
        return carry

    loop(listed, place, 0)
    order = list(range(slots))[::-1]
    loads, stores = {}, []
    for i in order:
        loads[i] = pltpu.make_async_copy(
            pool_ref.at[index_ref[i]], held_ref.at[i], in_sems.at[i]
        )
        loads[i].start()
    for i in order:
        loads[i].wait()
        stores.append(
            pltpu.make_async_copy(
                held_ref.at[i], send_refs[i // CAP].at[i % CAP], out_sems.at[i]
            )
        )
        stores[-1].start()
    for store in stores:
        store.wait()


def split(value, size):
    assert size & (size - 1) == 0
    return lax.shift_right_logical(value, size.bit_length() - 1), value & (size - 1)


def count_log(tables, length, ids, block_len, spans, store):
    requests, width = tables.shape[0], ids.shape[1]
    whole, rest = split(length, block_len)
    whole = jnp.broadcast_to(whole, (requests, width))
    full = jnp.zeros((requests, width), jnp.float32)
    part = jnp.zeros((requests, width), jnp.float32)
    for e in range(spans):
        hit = jnp.broadcast_to(tables[:, e : e + 1], (requests, width)) == ids
        full = full + jnp.where(hit & (whole > e), 1.0, 0.0)
        part = part + jnp.where(hit & (whole == e), 1.0, 0.0)

    def log2(count):
        return jnp.where(count > 0, jnp.log(jnp.maximum(count, 1.0)) * LOG2E, -jnp.inf)

    beyond, within = log2(full), log2(full + part)
    shape = (requests, block_len)
    inside = lax.broadcasted_iota(jnp.int32, shape, 1) < jnp.broadcast_to(rest, shape)
    for b in range(width):
        store(
            b,
            jnp.where(
                inside,
                jnp.broadcast_to(within[:, b : b + 1], shape),
                jnp.broadcast_to(beyond[:, b : b + 1], shape),
            ),
        )


def score_tiles(query, keys, log_ref, scale_row, rows, store):
    height, wide = min(256, query.shape[0]), min(256, keys.shape[0])
    for top in range(0, query.shape[0], height):
        for left in range(0, keys.shape[0], wide):
            part = lax.dot_general(
                query[top : top + height],
                keys[left : left + wide],
                NT,
                preferred_element_type=jnp.float32,
            )
            scale = scale_row[:, left : left + wide]
            for r in range(height // rows):
                request = top // rows + r
                store(
                    request * rows,
                    left,
                    part[r * rows : (r + 1) * rows] * scale
                    + log_ref[request : request + 1, left : left + wide],
                )


def lane_fold(value, op):
    parts = [value[:, i : i + 128] for i in range(0, value.shape[1], 128)]
    while len(parts) > 1:
        parts = [
            op(parts[i], parts[i + 1]) if i + 1 < len(parts) else parts[i]
            for i in range(0, len(parts), 2)
        ]
    return parts[0]


def spread(column, width):
    return jnp.concatenate([column] * (width // 128), axis=1)


def own_kernel(
    dims,
    tables_ref, length_ref, scale_ref, q_ref, fresh_ref, pool_ref,
    acc_ref, top_ref, total_ref,
    log_ref, row_ref, t_ref, p_ref, codes_ref, sems,
):
    pool, heads, rows, steps, block_len, spans, factor, group = dims
    chunks = pool // group
    height, head_dim = q_ref.shape[1:]
    width = group * block_len

    def load(part, chunk):
        return pltpu.make_async_copy(
            pool_ref.at[pl.ds(chunk * group, group), part],
            codes_ref.at[part, chunk],
            sems.at[part, chunk],
        )

    for part in range(2):
        for chunk in range(chunks):
            load(part, chunk).start()

    ids = lax.broadcasted_iota(jnp.int32, (1, pool), 1)

    def store_log(b, value):
        lane = (b % group) * block_len
        log_ref[b // group, :, lane : lane + block_len] = value

    count_log(tables_ref[...], length_ref[...], ids, block_len, spans, store_log)
    for b in range(pool):
        lane = (b % group) * block_len
        for row in range(2 * heads):
            unit = factor * LOG2E if row < heads else 1.0
            row_ref[b // group, row : row + 1, lane : lane + block_len] = jnp.full(
                (1, block_len), scale_ref[0, row * pool + b] * unit
            )
    shape = (height, fresh_ref.shape[2])
    row = lax.broadcasted_iota(jnp.int32, shape, 0)
    col = lax.broadcasted_iota(jnp.int32, shape, 1)
    (request, row_step), (owner, step) = split(row, rows), split(col, steps)
    seen = (request == owner) & (split(row_step, steps)[1] >= step)
    for h in range(heads):
        new_score = lax.dot_general(
            q_ref[h], fresh_ref[0, h], NT, preferred_element_type=jnp.float32
        )
        new_score = jnp.where(seen, new_score * (factor * LOG2E), -jnp.inf)
        acc_ref[h] = new_score
        top_ref[h] = lane_fold(new_score, jnp.maximum)

    def score(chunk, carry):
        load(0, chunk).wait()
        for h in range(heads):

            def store(row, lane, value, h=h):
                t_ref[h, chunk, row : row + rows, lane : lane + value.shape[1]] = value

            score_tiles(
                q_ref[h],
                codes_ref[0, chunk, :, h].reshape(width, head_dim),
                log_ref.at[chunk],
                row_ref[chunk, h : h + 1, :],
                rows,
                store,
            )
            for row in range(0, height, rows):
                at = pl.ds(row, rows)
                top_ref[h, at] = jnp.maximum(
                    top_ref[h, at], lane_fold(t_ref[h, chunk, at], jnp.maximum)
                )
        return carry

    lax.fori_loop(0, chunks, score, 0)

    for h in range(heads):
        top = jnp.broadcast_to(jnp.max(top_ref[h], axis=1, keepdims=True), (height, 128))
        top_ref[h] = top
        weight = jnp.exp2(acc_ref[h] - spread(top, acc_ref.shape[2]))
        total_ref[h] = lane_fold(weight, jnp.add)
        acc_ref[h] = jnp.dot(
            weight.astype(jnp.bfloat16), fresh_ref[1, h], preferred_element_type=jnp.float32
        )

    def apply(chunk, carry):
        load(1, chunk).wait()
        for h in range(heads):
            scale = row_ref[chunk, heads + h : heads + h + 1, :]
            for row in range(0, height, rows):
                at = pl.ds(row, rows)
                weight = jnp.exp2(t_ref[h, chunk, at] - spread(top_ref[h, at], width))
                total_ref[h, at] += lane_fold(weight, jnp.add)
                p_ref[h, at] = (weight * scale).astype(jnp.bfloat16)
            acc_ref[h] += jnp.dot(
                p_ref[h],
                codes_ref[1, chunk, :, h].reshape(width, head_dim),
                preferred_element_type=jnp.float32,
            )
        return carry

    lax.fori_loop(0, chunks, apply, 0)
    for h in range(heads):
        total_ref[h] = jnp.broadcast_to(
            jnp.sum(total_ref[h], axis=1, keepdims=True), (height, 128)
        )


def route_kernel(
    dims, lists_ref, tables_ref, length_ref, own_ref, moved_ref, log_ref, row_ref
):
    pool, heads, instances, listed, block_len, spans, factor = dims
    me = lax.axis_index("inst")

    def dest(row, m):
        return lists_ref[row, m].astype(jnp.int32)

    def count(row, target):
        return loop(
            listed, lambda m, n: n + jnp.where(dest(row, m) == target, 1, 0), jnp.int32(0)
        )

    def rank(row, m):
        target = dest(row, m)
        return loop(
            listed,
            lambda m2, n: n + jnp.where((dest(row, m2) == target) & (m2 < m), 1, 0),
            jnp.int32(0),
        )

    def before(source, target):
        return loop(
            instances,
            lambda k, n: n + jnp.where(jnp.bitwise_xor(me, k) < source, count(k, target), 0),
            jnp.int32(pool),
        )

    def move(m, carry):
        moved_ref[0, m] = before(me, dest(0, m)) + rank(0, m)
        return carry

    loop(listed, move, 0)

    slots = instances * CAP
    lane = lax.broadcasted_iota(jnp.int32, (1, slots), 1)

    def place(k, ids):
        first = before(jnp.bitwise_xor(me, k), me)

        def find(m, carry):
            seen, blocks = carry
            hit = dest(k, m) == me
            block = lists_ref[k, listed + m].astype(jnp.int32)
            blocks = [jnp.where(hit & (seen == r), block, blocks[r]) for r in range(CAP)]
            return seen + jnp.where(hit, 1, 0), blocks

        seen, blocks = loop(listed, find, (jnp.int32(0), [jnp.int32(0)] * CAP))
        for r in range(CAP):
            slot = r * instances + k
            ids = jnp.where(lane == slot, jnp.where(r < seen, first + r, -1), ids)
            at = pl.ds(pl.multiple_of(slot * block_len, block_len), block_len)
            for h in range(heads):
                key = lists_ref[k, 2 * listed + h * pool + blocks[r]]
                value = lists_ref[k, 2 * listed + (heads + h) * pool + blocks[r]]
                row_ref[h : h + 1, at] = jnp.full((1, block_len), key * (factor * LOG2E))
                row_ref[heads + h : heads + h + 1, at] = jnp.full((1, block_len), value)
        return ids

    ids = loop(instances, place, jnp.full((1, slots), -1, jnp.int32))

    def store(b, value):
        log_ref[:, b * block_len : (b + 1) * block_len] = value

    count_log(tables_ref[...], length_ref[...], ids, block_len, spans, store)


def arrival_kernel(dims, places, q_ref, log_ref, row_ref, *refs):
    heads, rows, block_len = dims
    (acc_ref, top_ref, total_ref), refs = refs[:3], refs[3:]
    code_refs, (out_ref, t_ref, p_ref) = refs[:-3], refs[-3:]
    height = q_ref.shape[1]
    width = 2 * block_len
    slots = [code_refs[array].at[row] for array, row in places]
    pairs = len(slots) // 2

    def pair(i, part, h):
        return jnp.concatenate([slots[2 * i][part, h], slots[2 * i + 1][part, h]], axis=0)

    for h in range(heads):
        for i in range(pairs):
            left = i * width

            def store(row, lane, value, h=h, left=left):
                t_ref[h, row : row + rows, left + lane : left + lane + value.shape[1]] = value

            score_tiles(
                q_ref[h],
                pair(i, 0, h),
                log_ref.at[:, left : left + width],
                row_ref[h : h + 1, left : left + width],
                rows,
                store,
            )
    for h in range(heads):
        scale = row_ref[heads + h : heads + h + 1, :]
        for row in range(0, height, rows):
            at = pl.ds(row, rows)
            score = t_ref[h, at]
            own_top = top_ref[h, at]
            top = jnp.maximum(
                own_top, jnp.max(lane_fold(score, jnp.maximum), axis=1, keepdims=True)
            )
            weight = jnp.exp2(score - spread(top, score.shape[1]))
            keep = jnp.exp2(own_top - top)
            total = total_ref[h, at] * keep + jnp.sum(
                lane_fold(weight, jnp.add), axis=1, keepdims=True
            )
            p_ref[h, at] = (weight * scale).astype(jnp.bfloat16)
            t_ref[h, at, 0:128] = keep
            t_ref[h, at, 128:256] = 1.0 / total
        mixed = acc_ref[h] * t_ref[h, :, 0:128]
        for i in range(pairs):
            mixed = mixed + jnp.dot(
                p_ref[h, :, i * width : (i + 1) * width],
                pair(i, 1, h),
                preferred_element_type=jnp.float32,
            )
        result = (mixed * t_ref[h, :, 128:256]).astype(jnp.bfloat16)
        out_ref[:, h] = result.reshape(height // rows, rows, result.shape[-1])


def shards(queries, new_kv, pool_codes, pool_scales, tables, ctx_len, mig_block, mig_dest):
    instances = lax.axis_size("inst")
    pool = pool_codes.shape[0]
    requests, steps, q_heads, head_dim = queries.shape
    heads = new_kv.shape[3]
    per_head = q_heads // heads
    spans = tables.shape[1]
    block_len = pool_codes.shape[3]
    listed = mig_dest.shape[1]
    factor = head_dim ** (-0.5)
    rows = per_head * steps
    height = requests * rows
    slots = instances * CAP
    group = 8
    f32, bf16 = jnp.float32, jnp.bfloat16
    block_shape = pool_codes.shape[1:]
    block_bytes = 2 * math.prod(block_shape)
    assert instances & (instances - 1) == 0

    send = pl.pallas_call(
        functools.partial(pack_kernel, instances, listed),
        out_shape=[jax.ShapeDtypeStruct((CAP,) + block_shape, bf16)] * instances,
        in_specs=[SMEM_SPEC, SMEM_SPEC, HBM_SPEC],
        out_specs=[HBM_SPEC] * instances,
        scratch_shapes=[
            pltpu.SMEM((slots,), jnp.int32),
            pltpu.VMEM((slots,) + block_shape, bf16),
            pltpu.SemaphoreType.DMA((slots,)),
            pltpu.SemaphoreType.DMA((slots,)),
        ],
        compiler_params=pltpu.CompilerParams(vmem_limit_bytes=56 * MIB),
        cost_estimate=pl.CostEstimate(
            flops=0, bytes_accessed=2 * slots * block_bytes, transcendentals=0
        ),
        name="pack_blocks",
    )(mig_dest, mig_block, pool_codes)
    mig_dest, mig_block, pool_scales, *send = lax.optimization_barrier(
        (mig_dest, mig_block, pool_scales, *send)
    )

    def swap(value, distance):
        return lax.ppermute(value, "inst", [(j, j ^ distance) for j in range(instances)])

    arrived = [send[0]] + [swap(send[k], k) for k in range(1, instances)]
    places = [(k, r) for r in range(CAP) for k in range(instances)]

    flat_scales = jnp.transpose(pool_scales, (1, 2, 0)).reshape(1, -1).astype(f32)
    lists = jnp.concatenate([mig_dest.astype(f32), mig_block.astype(f32), flat_scales], axis=1)
    lists_in = jnp.concatenate([lists] + [swap(lists, k) for k in range(1, instances)], axis=0)

    query_rows = (
        queries.reshape(requests, steps, heads, per_head, head_dim)
        .transpose(2, 0, 3, 1, 4)
        .reshape(heads, height, head_dim)
    )
    fresh_len = requests * steps
    fresh = new_kv.transpose(2, 3, 0, 1, 4).reshape(2, heads, fresh_len, head_dim)
    fresh = jnp.pad(fresh, ((0, 0), (0, 0), (0, -fresh_len % 128), (0, 0)))
    assert fresh.shape[2] == head_dim
    length = ctx_len[:, None]
    width = group * block_len
    chunks = pool // group
    tokens = pool * block_len

    stat = (heads, height, head_dim)
    own_parts = pl.pallas_call(
        functools.partial(
            own_kernel, (pool, heads, rows, steps, block_len, spans, factor, group)
        ),
        out_shape=[jax.ShapeDtypeStruct(stat, f32)] * 3,
        in_specs=[VMEM_SPEC, VMEM_SPEC, SMEM_SPEC, VMEM_SPEC, VMEM_SPEC, HBM_SPEC],
        out_specs=[VMEM_SPEC] * 3,
        scratch_shapes=[
            pltpu.VMEM((chunks, requests, width), f32),
            pltpu.VMEM((chunks, 2 * heads, width), f32),
            pltpu.VMEM((heads, chunks, height, width), f32),
            pltpu.VMEM((heads, height, width), bf16),
            pltpu.VMEM((2, chunks, group, heads, block_len, head_dim), bf16),
            pltpu.SemaphoreType.DMA((2, chunks)),
        ],
        compiler_params=pltpu.CompilerParams(vmem_limit_bytes=48 * MIB),
        cost_estimate=pl.CostEstimate(
            flops=4 * heads * height * tokens * head_dim,
            bytes_accessed=pool_codes.size * 2,
            transcendentals=heads * height * tokens,
        ),
        name="own_blocks",
    )(tables, length, flat_scales, query_rows, fresh, pool_codes)

    moved_to, log_in, rows_in = pl.pallas_call(
        functools.partial(
            route_kernel,
            (pool, heads, instances, listed, block_len, spans, factor),
        ),
        out_shape=[
            jax.ShapeDtypeStruct((1, listed), jnp.int32),
            jax.ShapeDtypeStruct((requests, slots * block_len), f32),
            jax.ShapeDtypeStruct((2 * heads, slots * block_len), f32),
        ],
        in_specs=[SMEM_SPEC, VMEM_SPEC, VMEM_SPEC, HBM_SPEC],
        out_specs=[SMEM_SPEC, VMEM_SPEC, VMEM_SPEC],
        compiler_params=pltpu.CompilerParams(vmem_limit_bytes=8 * MIB),
        name="route_arrivals",
    )(lists_in, tables, length, own_parts[2])

    arrival_bytes = 6 * heads * height * slots * block_len + 2 * 12 * height * head_dim * heads
    arrival_bytes += 2 * slots * block_bytes
    out = pl.pallas_call(
        functools.partial(arrival_kernel, (heads, rows, block_len), places),
        out_shape=jax.ShapeDtypeStruct((requests, heads, rows, head_dim), bf16),
        in_specs=[VMEM_SPEC] * (6 + len(arrived)),
        out_specs=VMEM_SPEC,
        scratch_shapes=[
            pltpu.VMEM((heads, height, slots * block_len), f32),
            pltpu.VMEM((heads, height, slots * block_len), bf16),
        ],
        compiler_params=pltpu.CompilerParams(vmem_limit_bytes=arrival_bytes + 8 * MIB),
        cost_estimate=pl.CostEstimate(
            flops=4 * heads * height * slots * block_len * head_dim,
            bytes_accessed=slots * block_bytes,
            transcendentals=heads * height * slots * block_len,
        ),
        name="arrived_blocks",
    )(query_rows, log_in, rows_in, *own_parts, *arrived)
    out = (
        out.reshape(requests, q_heads, steps, head_dim)
        .transpose(0, 2, 1, 3)
        .reshape(requests, steps, q_heads * head_dim)
    )
    return out, moved_to


def solution(mesh):
    in_specs = (
        P(("groups", "inst"), None, "tp", None),
        P(("groups", "inst"), None, None, "tp", None),
        P(("groups", "inst"), None, "tp", None, None),
        P(("groups", "inst"), None, "tp"),
        P(("groups", "inst"), None),
        P(("groups", "inst")),
        P(("groups", "inst"), None),
        P(("groups", "inst"), None),
    )
    out_specs = (P(("groups", "inst"), None, "tp"), P(("groups", "inst"), None))
    return jax.shard_map(shards, mesh=mesh, in_specs=in_specs, out_specs=out_specs, check_vma=False)
```

```python
import functools
import math

import jax
import jax.numpy as jnp
from jax import lax
from jax.experimental import pallas as pl
from jax.experimental.pallas import tpu as pltpu
from jax.sharding import PartitionSpec as P

CAP = 2
EXTRA = 16
LOG2E = math.log2(math.e)
MIB = 1 << 20
SMEM_SPEC = pl.BlockSpec(memory_space=pltpu.SMEM)
VMEM_SPEC = pl.BlockSpec(memory_space=pltpu.VMEM)
HBM_SPEC = pl.BlockSpec(memory_space=pltpu.HBM)
NT = (((1,), (1,)), ((), ()))


def loop(count, body, init):
    if count <= 8:
        for i in range(count):
            init = body(i, init)
        return init
    return lax.fori_loop(0, count, body, init)


def pack_kernel(dims, dest_ref, block_ref, scale_ref, pool_ref, *refs):
    instances, listed, heads, pool = dims
    send_refs, (index_ref, extra_ref, held_ref, in_sems, out_sems) = (
        refs[:instances],
        refs[instances:],
    )
    slots = instances * CAP
    code_rows = held_ref.shape[1] - EXTRA
    me = lax.axis_index("inst")
    for slot in range(slots):
        index_ref[slot] = 0

    def place(m, carry):
        dest = dest_ref[0, m]
        rank = loop(
            listed,
            lambda m2, n: n + jnp.where((dest_ref[0, m2] == dest) & (m2 < m), 1, 0),
            jnp.int32(0),
        )
        index_ref[jnp.bitwise_xor(dest, me) * CAP + jnp.minimum(rank, CAP - 1)] = block_ref[0, m]
        return carry

    loop(listed, place, 0)
    order = list(range(slots))[::-1]
    loads, stores = {}, []
    for i in order:
        loads[i] = pltpu.make_async_copy(
            pool_ref.at[index_ref[i]], held_ref.at[i, pl.ds(0, code_rows)], in_sems.at[i]
        )
        loads[i].start()
    lane = lax.broadcasted_iota(jnp.int32, (1, 128), 1)

    def spell(m, row):
        return jnp.where(lane == m, dest_ref[0, m].astype(jnp.float32), row)

    extra_ref[...] = jnp.zeros_like(extra_ref)
    extra_ref[2 * heads : 2 * heads + 1, :] = loop(
        listed, spell, jnp.zeros((1, 128), jnp.float32)
    )
    scales = [
        [scale_ref[part, h : h + 1, :].astype(jnp.float32) for h in range(heads)]
        for part in range(2)
    ]
    column = lax.broadcasted_iota(jnp.int32, (1, pool), 1)
    for i in order:
        for part in range(2):
            for h in range(heads):
                one = jnp.where(column == index_ref[i], scales[part][h], 0.0)
                row = part * heads + h
                extra_ref[row : row + 1, :] = jnp.broadcast_to(
                    jnp.sum(one, axis=1, keepdims=True), (1, 128)
                )
        held_ref[i, pl.ds(code_rows, EXTRA)] = extra_ref[...].astype(jnp.bfloat16)
    for i in order:
        loads[i].wait()
        stores.append(
            pltpu.make_async_copy(
                held_ref.at[i], send_refs[i // CAP].at[i % CAP], out_sems.at[i]
            )
        )
        stores[-1].start()
    for store in stores:
        store.wait()


def split(value, size):
    assert size & (size - 1) == 0
    return lax.shift_right_logical(value, size.bit_length() - 1), value & (size - 1)


def count_log(tables, length, ids, block_len, spans, store):
    requests, width = tables.shape[0], ids.shape[1]
    whole, rest = split(length, block_len)
    whole = jnp.broadcast_to(whole, (requests, width))
    full = jnp.zeros((requests, width), jnp.float32)
    part = jnp.zeros((requests, width), jnp.float32)
    for e in range(spans):
        hit = jnp.broadcast_to(tables[:, e : e + 1], (requests, width)) == ids
        full = full + jnp.where(hit & (whole > e), 1.0, 0.0)
        part = part + jnp.where(hit & (whole == e), 1.0, 0.0)

    def log2(count):
        return jnp.where(count > 0, jnp.log(jnp.maximum(count, 1.0)) * LOG2E, -jnp.inf)

    beyond, within = log2(full), log2(full + part)
    shape = (requests, block_len)
    inside = lax.broadcasted_iota(jnp.int32, shape, 1) < jnp.broadcast_to(rest, shape)
    for b in range(width):
        store(
            b,
            jnp.where(
                inside,
                jnp.broadcast_to(within[:, b : b + 1], shape),
                jnp.broadcast_to(beyond[:, b : b + 1], shape),
            ),
        )


def score_tiles(query, keys, log_ref, scale_row, rows, store):
    height, wide = min(256, query.shape[0]), min(256, keys.shape[0])
    for top in range(0, query.shape[0], height):
        for left in range(0, keys.shape[0], wide):
            part = lax.dot_general(
                query[top : top + height],
                keys[left : left + wide],
                NT,
                preferred_element_type=jnp.float32,
            )
            scale = scale_row[:, left : left + wide]
            for r in range(height // rows):
                request = top // rows + r
                store(
                    request * rows,
                    left,
                    part[r * rows : (r + 1) * rows] * scale
                    + log_ref[request : request + 1, left : left + wide],
                )


def lane_fold(value, op):
    parts = [value[:, i : i + 128] for i in range(0, value.shape[1], 128)]
    while len(parts) > 1:
        parts = [
            op(parts[i], parts[i + 1]) if i + 1 < len(parts) else parts[i]
            for i in range(0, len(parts), 2)
        ]
    return parts[0]


def spread(column, width):
    return jnp.concatenate([column] * (width // 128), axis=1)


def own_kernel(
    dims,
    tables_ref, length_ref, scale_ref, q_ref, fresh_ref, pool_ref,
    acc_ref, top_ref, total_ref,
    log_ref, row_ref, t_ref, p_ref, codes_ref, sems,
):
    pool, heads, rows, steps, block_len, spans, factor, group = dims
    chunks = pool // group
    height, head_dim = q_ref.shape[1:]
    width = group * block_len
    part_rows = heads * block_len

    def load(part, chunk):
        return pltpu.make_async_copy(
            pool_ref.at[pl.ds(chunk * group, group), pl.ds(part * part_rows, part_rows)],
            codes_ref.at[part, chunk],
            sems.at[part, chunk],
        )

    for part in range(2):
        for chunk in range(chunks):
            load(part, chunk).start()

    ids = lax.broadcasted_iota(jnp.int32, (1, pool), 1)

    def store_log(b, value):
        lane = (b % group) * block_len
        log_ref[b // group, :, lane : lane + block_len] = value

    count_log(tables_ref[...], length_ref[...], ids, block_len, spans, store_log)
    for b in range(pool):
        lane = (b % group) * block_len
        for row in range(2 * heads):
            unit = factor * LOG2E if row < heads else 1.0
            row_ref[b // group, row : row + 1, lane : lane + block_len] = jnp.full(
                (1, block_len), scale_ref[0, row * pool + b] * unit
            )
    shape = (height, fresh_ref.shape[2])
    row = lax.broadcasted_iota(jnp.int32, shape, 0)
    col = lax.broadcasted_iota(jnp.int32, shape, 1)
    (request, row_step), (owner, step) = split(row, rows), split(col, steps)
    seen = (request == owner) & (split(row_step, steps)[1] >= step)
    for h in range(heads):
        new_score = lax.dot_general(
            q_ref[h], fresh_ref[0, h], NT, preferred_element_type=jnp.float32
        )
        new_score = jnp.where(seen, new_score * (factor * LOG2E), -jnp.inf)
        acc_ref[h] = new_score
        top_ref[h] = lane_fold(new_score, jnp.maximum)

    def score(chunk, carry):
        load(0, chunk).wait()
        for h in range(heads):

            def store(row, lane, value, h=h):
                t_ref[h, chunk, row : row + rows, lane : lane + value.shape[1]] = value

            score_tiles(
                q_ref[h],
                codes_ref[0, chunk, :, h * block_len : (h + 1) * block_len].reshape(width, head_dim),
                log_ref.at[chunk],
                row_ref[chunk, h : h + 1, :],
                rows,
                store,
            )
            for row in range(0, height, rows):
                at = pl.ds(row, rows)
                top_ref[h, at] = jnp.maximum(
                    top_ref[h, at], lane_fold(t_ref[h, chunk, at], jnp.maximum)
                )
        return carry

    lax.fori_loop(0, chunks, score, 0)

    for h in range(heads):
        top = jnp.broadcast_to(jnp.max(top_ref[h], axis=1, keepdims=True), (height, 128))
        top_ref[h] = top
        weight = jnp.exp2(acc_ref[h] - spread(top, acc_ref.shape[2]))
        total_ref[h] = lane_fold(weight, jnp.add)
        acc_ref[h] = jnp.dot(
            weight.astype(jnp.bfloat16), fresh_ref[1, h], preferred_element_type=jnp.float32
        )

    def apply(chunk, carry):
        load(1, chunk).wait()
        for h in range(heads):
            scale = row_ref[chunk, heads + h : heads + h + 1, :]
            for row in range(0, height, rows):
                at = pl.ds(row, rows)
                weight = jnp.exp2(t_ref[h, chunk, at] - spread(top_ref[h, at], width))
                total_ref[h, at] += lane_fold(weight, jnp.add)
                p_ref[h, at] = (weight * scale).astype(jnp.bfloat16)
            acc_ref[h] += jnp.dot(
                p_ref[h],
                codes_ref[1, chunk, :, h * block_len : (h + 1) * block_len].reshape(width, head_dim),
                preferred_element_type=jnp.float32,
            )
        return carry

    lax.fori_loop(0, chunks, apply, 0)
    for h in range(heads):
        total_ref[h] = jnp.broadcast_to(
            jnp.sum(total_ref[h], axis=1, keepdims=True), (height, 128)
        )


def arrival_ids(me, pool, lists, listed):
    instances = len(lists)
    lane = lax.broadcasted_iota(jnp.int32, (1, 128), 1)
    counts = [
        jnp.sum(
            jnp.where((row == me.astype(jnp.float32)) & (lane < listed), 1.0, 0.0),
            axis=1,
            keepdims=True,
        )
        for row in lists
    ]
    slot = lax.broadcasted_iota(jnp.int32, (1, instances * CAP), 1)
    ids = jnp.full(slot.shape, -1.0)
    for k in range(instances):
        first = jnp.full((1, 1), float(pool))
        for j in range(instances):
            lower = jnp.bitwise_xor(me, j) < jnp.bitwise_xor(me, k)
            first = first + jnp.where(lower, counts[j], 0.0)
        for r in range(CAP):
            name = jnp.where(counts[k] > r, first + r, -1.0)
            ids = jnp.where(slot == r * instances + k, jnp.broadcast_to(name, slot.shape), ids)
    moved = jnp.full((1, 128), float(pool))
    for j in range(instances):
        for m in range(listed):
            same = jnp.broadcast_to(lists[j][:, m : m + 1], (1, 128)) == lists[0]
            ahead = jnp.bitwise_xor(me, j) < me if j else lane > m
            moved = moved + jnp.where(same & ahead, 1.0, 0.0)
    return ids.astype(jnp.int32), moved[:, :listed].astype(jnp.int32)


def arrival_kernel(dims, q_ref, tables_ref, length_ref, acc_ref, top_ref, total_ref, *refs):
    pool, heads, rows, block_len, spans, listed, factor = dims
    code_refs, (out_ref, moved_ref, log_ref, t_ref, p_ref) = refs[:-5], refs[-5:]
    instances = len(code_refs)
    height = q_ref.shape[1]
    width = 2 * block_len
    extra = 2 * heads * block_len
    slots = [(ref, r) for r in range(CAP) for ref in code_refs]
    pairs = len(slots) // 2

    def pair(i, part, h):
        at = pl.ds((part * heads + h) * block_len, block_len)
        return jnp.concatenate([ref[r, at] for ref, r in slots[2 * i : 2 * i + 2]], axis=0)

    lists, scale_rows = [], []
    for ref, r in slots:
        values = ref[r, pl.ds(extra, EXTRA)].astype(jnp.float32)
        scale_rows.append(values)
        if r == 0:
            lists.append(values[2 * heads : 2 * heads + 1])

    def scale_row(row):
        return jnp.concatenate([values[row : row + 1] for values in scale_rows], axis=1)

    ids, moved_ref[...] = arrival_ids(lax.axis_index("inst"), pool, lists, listed)

    def store_log(b, value):
        log_ref[:, b * block_len : (b + 1) * block_len] = value

    count_log(tables_ref[...], length_ref[...], ids, block_len, spans, store_log)
    for h in range(heads):
        key_scale = scale_row(h) * (factor * LOG2E)
        for i in range(pairs):
            left = i * width

            def store(row, lane, value, h=h, left=left):
                t_ref[h, row : row + rows, left + lane : left + lane + value.shape[1]] = value

            score_tiles(
                q_ref[h],
                pair(i, 0, h),
                log_ref.at[:, left : left + width],
                key_scale[:, left : left + width],
                rows,
                store,
            )
    for h in range(heads):
        scale = scale_row(heads + h)
        for row in range(0, height, rows):
            at = pl.ds(row, rows)
            score = t_ref[h, at]
            own_top = top_ref[h, at]
            top = jnp.maximum(
                own_top, jnp.max(lane_fold(score, jnp.maximum), axis=1, keepdims=True)
            )
            weight = jnp.exp2(score - spread(top, score.shape[1]))
            keep = jnp.exp2(own_top - top)
            total = total_ref[h, at] * keep + jnp.sum(
                lane_fold(weight, jnp.add), axis=1, keepdims=True
            )
            p_ref[h, at] = (weight * scale).astype(jnp.bfloat16)
            t_ref[h, at, 0:128] = keep
            t_ref[h, at, 128:256] = 1.0 / total
        mixed = acc_ref[h] * t_ref[h, :, 0:128]
        for i in range(pairs):
            mixed = mixed + jnp.dot(
                p_ref[h, :, i * width : (i + 1) * width],
                pair(i, 1, h),
                preferred_element_type=jnp.float32,
            )
        result = (mixed * t_ref[h, :, 128:256]).astype(jnp.bfloat16)
        out_ref[:, h] = result.reshape(height // rows, rows, result.shape[-1])


def shards(queries, new_kv, pool_codes, pool_scales, tables, ctx_len, mig_block, mig_dest):
    instances = lax.axis_size("inst")
    pool = pool_codes.shape[0]
    requests, steps, q_heads, head_dim = queries.shape
    heads = new_kv.shape[3]
    per_head = q_heads // heads
    spans = tables.shape[1]
    block_len = pool_codes.shape[3]
    listed = mig_dest.shape[1]
    factor = head_dim ** (-0.5)
    rows = per_head * steps
    height = requests * rows
    slots = instances * CAP
    group = 8
    f32, bf16 = jnp.float32, jnp.bfloat16
    code_rows = 2 * heads * block_len
    pool_rows = pool_codes.reshape(pool, code_rows, head_dim)
    sent_shape = (CAP, code_rows + EXTRA, head_dim)
    sent_bytes = 2 * math.prod(sent_shape)
    part_scales = jnp.transpose(pool_scales, (1, 2, 0))
    assert instances & (instances - 1) == 0 and 2 * heads < EXTRA and head_dim == 128

    send = pl.pallas_call(
        functools.partial(pack_kernel, (instances, listed, heads, pool)),
        out_shape=[jax.ShapeDtypeStruct(sent_shape, bf16)] * instances,
        in_specs=[SMEM_SPEC, SMEM_SPEC, VMEM_SPEC, HBM_SPEC],
        out_specs=[HBM_SPEC] * instances,
        scratch_shapes=[
            pltpu.SMEM((slots,), jnp.int32),
            pltpu.VMEM((EXTRA, head_dim), f32),
            pltpu.VMEM((slots,) + sent_shape[1:], bf16),
            pltpu.SemaphoreType.DMA((slots,)),
            pltpu.SemaphoreType.DMA((slots,)),
        ],
        compiler_params=pltpu.CompilerParams(vmem_limit_bytes=56 * MIB),
        cost_estimate=pl.CostEstimate(
            flops=0, bytes_accessed=2 * instances * sent_bytes, transcendentals=0
        ),
        name="pack_blocks",
    )(mig_dest, mig_block, part_scales, pool_rows)
    part_scales, *send = lax.optimization_barrier((part_scales, *send))

    def swap(value, distance):
        return lax.ppermute(value, "inst", [(j, j ^ distance) for j in range(instances)])

    arrived = [send[0]] + [swap(send[k], k) for k in range(1, instances)]
    flat_scales = part_scales.reshape(1, -1).astype(f32)

    query_rows = (
        queries.reshape(requests, steps, heads, per_head, head_dim)
        .transpose(2, 0, 3, 1, 4)
        .reshape(heads, height, head_dim)
    )
    fresh_len = requests * steps
    fresh = new_kv.transpose(2, 3, 0, 1, 4).reshape(2, heads, fresh_len, head_dim)
    fresh = jnp.pad(fresh, ((0, 0), (0, 0), (0, -fresh_len % 128), (0, 0)))
    assert fresh.shape[2] == head_dim
    length = ctx_len[:, None]
    width = group * block_len
    chunks = pool // group
    tokens = pool * block_len

    stat = (heads, height, head_dim)
    own_parts = pl.pallas_call(
        functools.partial(
            own_kernel, (pool, heads, rows, steps, block_len, spans, factor, group)
        ),
        out_shape=[jax.ShapeDtypeStruct(stat, f32)] * 3,
        in_specs=[VMEM_SPEC, VMEM_SPEC, SMEM_SPEC, VMEM_SPEC, VMEM_SPEC, HBM_SPEC],
        out_specs=[VMEM_SPEC] * 3,
        scratch_shapes=[
            pltpu.VMEM((chunks, requests, width), f32),
            pltpu.VMEM((chunks, 2 * heads, width), f32),
            pltpu.VMEM((heads, chunks, height, width), f32),
            pltpu.VMEM((heads, height, width), bf16),
            pltpu.VMEM((2, chunks, group, heads * block_len, head_dim), bf16),
            pltpu.SemaphoreType.DMA((2, chunks)),
        ],
        compiler_params=pltpu.CompilerParams(vmem_limit_bytes=48 * MIB),
        cost_estimate=pl.CostEstimate(
            flops=4 * heads * height * tokens * head_dim,
            bytes_accessed=pool_codes.size * 2,
            transcendentals=heads * height * tokens,
        ),
        name="own_blocks",
    )(tables, length, flat_scales, query_rows, fresh, pool_rows)

    arrival_bytes = 6 * heads * height * slots * block_len + 2 * 12 * height * head_dim * heads
    arrival_bytes += 2 * instances * sent_bytes + 4 * requests * slots * block_len
    out, moved_to = pl.pallas_call(
        functools.partial(
            arrival_kernel, (pool, heads, rows, block_len, spans, listed, factor)
        ),
        out_shape=[
            jax.ShapeDtypeStruct((requests, heads, rows, head_dim), bf16),
            jax.ShapeDtypeStruct((1, listed), jnp.int32),
        ],
        in_specs=[VMEM_SPEC] * (6 + instances),
        out_specs=[VMEM_SPEC, VMEM_SPEC],
        scratch_shapes=[
            pltpu.VMEM((requests, slots * block_len), f32),
            pltpu.VMEM((heads, height, slots * block_len), f32),
            pltpu.VMEM((heads, height, slots * block_len), bf16),
        ],
        compiler_params=pltpu.CompilerParams(vmem_limit_bytes=arrival_bytes + 8 * MIB),
        cost_estimate=pl.CostEstimate(
            flops=4 * heads * height * slots * block_len * head_dim,
            bytes_accessed=instances * sent_bytes,
            transcendentals=heads * height * slots * block_len,
        ),
        name="arrived_blocks",
    )(query_rows, tables, length, *own_parts, *arrived)
    out = (
        out.reshape(requests, q_heads, steps, head_dim)
        .transpose(0, 2, 1, 3)
        .reshape(requests, steps, q_heads * head_dim)
    )
    return out, moved_to


def solution(mesh):
    in_specs = (
        P(("groups", "inst"), None, "tp", None),
        P(("groups", "inst"), None, None, "tp", None),
        P(("groups", "inst"), None, "tp", None, None),
        P(("groups", "inst"), None, "tp"),
        P(("groups", "inst"), None),
        P(("groups", "inst")),
        P(("groups", "inst"), None),
        P(("groups", "inst"), None),
    )
    out_specs = (P(("groups", "inst"), None, "tp"), P(("groups", "inst"), None))
    return jax.shard_map(shards, mesh=mesh, in_specs=in_specs, out_specs=out_specs, check_vma=False)
```

```python
import functools
import math

import jax
import jax.numpy as jnp
from jax import lax
from jax.experimental import pallas as pl
from jax.experimental.pallas import tpu as pltpu
from jax.sharding import PartitionSpec as P

CAP = 2
EXTRA = 16
LOG2E = math.log2(math.e)
MIB = 1 << 20
SMEM_SPEC = pl.BlockSpec(memory_space=pltpu.SMEM)
VMEM_SPEC = pl.BlockSpec(memory_space=pltpu.VMEM)
HBM_SPEC = pl.BlockSpec(memory_space=pltpu.HBM)
NT = (((1,), (1,)), ((), ()))


def loop(count, body, init):
    if count <= 8:
        for i in range(count):
            init = body(i, init)
        return init
    return lax.fori_loop(0, count, body, init)


def pack_kernel(dims, dest_ref, block_ref, scale_ref, pool_ref, *refs):
    instances, listed, heads, pool, copies = dims
    send_refs, (index_ref, extra_ref, held_ref, in_sems, out_sems) = refs[:-5], refs[-5:]
    code_rows = held_ref.shape[1] - EXTRA
    me = lax.axis_index("inst")
    for entry in range(CAP * instances + 1):
        index_ref[entry] = 0

    def place(m, carry):
        dest = dest_ref[0, m]
        rank = loop(
            listed,
            lambda m2, n: n + jnp.where((dest_ref[0, m2] == dest) & (m2 < m), 1, 0),
            jnp.int32(0),
        )
        entry = jnp.bitwise_xor(dest, me) + jnp.where(rank > 0, instances, 0)
        index_ref[entry] = block_ref[0, m]
        index_ref[jnp.where(rank > 0, CAP * instances, entry)] = block_ref[0, m]
        return carry

    loop(listed, place, 0)
    loads, stores = [], []
    for i, (entry, _) in enumerate(copies):
        loads.append(
            pltpu.make_async_copy(
                pool_ref.at[index_ref[entry]], held_ref.at[i, pl.ds(0, code_rows)], in_sems.at[i]
            )
        )
        loads[i].start()
    lane = lax.broadcasted_iota(jnp.int32, (1, 128), 1)

    def spell(m, row):
        return jnp.where(lane == m, dest_ref[0, m].astype(jnp.float32), row)

    extra_ref[...] = jnp.zeros_like(extra_ref)
    extra_ref[2 * heads : 2 * heads + 1, :] = loop(
        listed, spell, jnp.zeros((1, 128), jnp.float32)
    )
    scales = [
        [scale_ref[part, h : h + 1, :].astype(jnp.float32) for h in range(heads)]
        for part in range(2)
    ]
    column = lax.broadcasted_iota(jnp.int32, (1, pool), 1)
    for i, (entry, _) in enumerate(copies):
        for part in range(2):
            for h in range(heads):
                one = jnp.where(column == index_ref[entry], scales[part][h], 0.0)
                row = part * heads + h
                extra_ref[row : row + 1, :] = jnp.broadcast_to(
                    jnp.sum(one, axis=1, keepdims=True), (1, 128)
                )
        held_ref[i, pl.ds(code_rows, EXTRA)] = extra_ref[...].astype(jnp.bfloat16)
    for i, (_, targets) in enumerate(copies):
        loads[i].wait()
        for output, row in targets:
            stores.append(
                pltpu.make_async_copy(
                    held_ref.at[i], send_refs[output].at[row], out_sems.at[len(stores)]
                )
            )
            stores[-1].start()
    for store in stores:
        store.wait()


def split(value, size):
    assert size & (size - 1) == 0
    return lax.shift_right_logical(value, size.bit_length() - 1), value & (size - 1)


def count_log(tables, length, ids, block_len, spans, store):
    requests, width = tables.shape[0], ids.shape[1]
    whole, rest = split(length, block_len)
    whole = jnp.broadcast_to(whole, (requests, width))
    full = jnp.zeros((requests, width), jnp.float32)
    part = jnp.zeros((requests, width), jnp.float32)
    for e in range(spans):
        hit = jnp.broadcast_to(tables[:, e : e + 1], (requests, width)) == ids
        full = full + jnp.where(hit & (whole > e), 1.0, 0.0)
        part = part + jnp.where(hit & (whole == e), 1.0, 0.0)

    def log2(count):
        return jnp.where(count > 0, jnp.log(jnp.maximum(count, 1.0)) * LOG2E, -jnp.inf)

    beyond, within = log2(full), log2(full + part)
    shape = (requests, block_len)
    inside = lax.broadcasted_iota(jnp.int32, shape, 1) < jnp.broadcast_to(rest, shape)
    for b in range(width):
        store(
            b,
            jnp.where(
                inside,
                jnp.broadcast_to(within[:, b : b + 1], shape),
                jnp.broadcast_to(beyond[:, b : b + 1], shape),
            ),
        )


def score_tiles(query, keys, log_ref, scale_row, rows, store):
    height, wide = min(256, query.shape[0]), min(256, keys.shape[0])
    for top in range(0, query.shape[0], height):
        for left in range(0, keys.shape[0], wide):
            part = lax.dot_general(
                query[top : top + height],
                keys[left : left + wide],
                NT,
                preferred_element_type=jnp.float32,
            )
            scale = scale_row[:, left : left + wide]
            for r in range(height // rows):
                request = top // rows + r
                store(
                    request * rows,
                    left,
                    part[r * rows : (r + 1) * rows] * scale
                    + log_ref[request : request + 1, left : left + wide],
                )


def lane_fold(value, op):
    parts = [value[:, i : i + 128] for i in range(0, value.shape[1], 128)]
    while len(parts) > 1:
        parts = [
            op(parts[i], parts[i + 1]) if i + 1 < len(parts) else parts[i]
            for i in range(0, len(parts), 2)
        ]
    return parts[0]


def spread(column, width):
    return jnp.concatenate([column] * (width // 128), axis=1)


def own_kernel(
    dims,
    tables_ref, length_ref, scale_ref, q_ref, fresh_ref, pool_ref,
    acc_ref, top_ref, total_ref,
    log_ref, row_ref, t_ref, p_ref, codes_ref, sems,
):
    pool, heads, rows, steps, block_len, spans, factor, group = dims
    chunks = pool // group
    height, head_dim = q_ref.shape[1:]
    width = group * block_len
    part_rows = heads * block_len

    def load(part, chunk):
        return pltpu.make_async_copy(
            pool_ref.at[pl.ds(chunk * group, group), pl.ds(part * part_rows, part_rows)],
            codes_ref.at[part, chunk],
            sems.at[part, chunk],
        )

    for part in range(2):
        for chunk in range(chunks):
            load(part, chunk).start()

    ids = lax.broadcasted_iota(jnp.int32, (1, pool), 1)

    def store_log(b, value):
        lane = (b % group) * block_len
        log_ref[b // group, :, lane : lane + block_len] = value

    count_log(tables_ref[...], length_ref[...], ids, block_len, spans, store_log)
    for b in range(pool):
        lane = (b % group) * block_len
        for row in range(2 * heads):
            unit = factor * LOG2E if row < heads else 1.0
            row_ref[b // group, row : row + 1, lane : lane + block_len] = jnp.full(
                (1, block_len), scale_ref[0, row * pool + b] * unit
            )
    shape = (height, fresh_ref.shape[2])
    row = lax.broadcasted_iota(jnp.int32, shape, 0)
    col = lax.broadcasted_iota(jnp.int32, shape, 1)
    (request, row_step), (owner, step) = split(row, rows), split(col, steps)
    seen = (request == owner) & (split(row_step, steps)[1] >= step)
    for h in range(heads):
        new_score = lax.dot_general(
            q_ref[h], fresh_ref[0, h], NT, preferred_element_type=jnp.float32
        )
        new_score = jnp.where(seen, new_score * (factor * LOG2E), -jnp.inf)
        acc_ref[h] = new_score
        top_ref[h] = lane_fold(new_score, jnp.maximum)

    def score(chunk, carry):
        load(0, chunk).wait()
        for h in range(heads):

            def store(row, lane, value, h=h):
                t_ref[h, chunk, row : row + rows, lane : lane + value.shape[1]] = value

            score_tiles(
                q_ref[h],
                codes_ref[0, chunk, :, h * block_len : (h + 1) * block_len].reshape(width, head_dim),
                log_ref.at[chunk],
                row_ref[chunk, h : h + 1, :],
                rows,
                store,
            )
            for row in range(0, height, rows):
                at = pl.ds(row, rows)
                top_ref[h, at] = jnp.maximum(
                    top_ref[h, at], lane_fold(t_ref[h, chunk, at], jnp.maximum)
                )
        return carry

    lax.fori_loop(0, chunks, score, 0)

    for h in range(heads):
        top = jnp.broadcast_to(jnp.max(top_ref[h], axis=1, keepdims=True), (height, 128))
        top_ref[h] = top
        weight = jnp.exp2(acc_ref[h] - spread(top, acc_ref.shape[2]))
        total_ref[h] = lane_fold(weight, jnp.add)
        acc_ref[h] = jnp.dot(
            weight.astype(jnp.bfloat16), fresh_ref[1, h], preferred_element_type=jnp.float32
        )

    def apply(chunk, carry):
        load(1, chunk).wait()
        for h in range(heads):
            scale = row_ref[chunk, heads + h : heads + h + 1, :]
            for row in range(0, height, rows):
                at = pl.ds(row, rows)
                weight = jnp.exp2(t_ref[h, chunk, at] - spread(top_ref[h, at], width))
                total_ref[h, at] += lane_fold(weight, jnp.add)
                p_ref[h, at] = (weight * scale).astype(jnp.bfloat16)
            acc_ref[h] += jnp.dot(
                p_ref[h],
                codes_ref[1, chunk, :, h * block_len : (h + 1) * block_len].reshape(width, head_dim),
                preferred_element_type=jnp.float32,
            )
        return carry

    lax.fori_loop(0, chunks, apply, 0)
    for h in range(heads):
        total_ref[h] = jnp.broadcast_to(
            jnp.sum(total_ref[h], axis=1, keepdims=True), (height, 128)
        )


def arrival_ids(me, pool, lists, listed):
    instances = len(lists)
    lane = lax.broadcasted_iota(jnp.int32, (1, 128), 1)
    counts = [
        jnp.sum(
            jnp.where((row == me.astype(jnp.float32)) & (lane < listed), 1.0, 0.0),
            axis=1,
            keepdims=True,
        )
        for row in lists
    ]
    slot = lax.broadcasted_iota(jnp.int32, (1, instances * CAP), 1)
    ids = jnp.full(slot.shape, -1.0)
    for k in range(instances):
        first = jnp.full((1, 1), float(pool))
        for j in range(instances):
            lower = jnp.bitwise_xor(me, j) < jnp.bitwise_xor(me, k)
            first = first + jnp.where(lower, counts[j], 0.0)
        for r in range(CAP):
            name = jnp.where(counts[k] > r, first + r, -1.0)
            ids = jnp.where(slot == r * instances + k, jnp.broadcast_to(name, slot.shape), ids)
    moved = jnp.full((1, 128), float(pool))
    for j in range(instances):
        for m in range(listed):
            same = jnp.broadcast_to(lists[j][:, m : m + 1], (1, 128)) == lists[0]
            ahead = jnp.bitwise_xor(me, j) < me if j else lane > m
            moved = moved + jnp.where(same & ahead, 1.0, 0.0)
    more = jnp.zeros((1, 128))
    for row in lists:
        again = jnp.zeros((1, 128))
        for m in range(listed):
            same = jnp.broadcast_to(row[:, m : m + 1], (1, 128)) == row
            again = again + jnp.where(same & (lane > m) & (lane < listed), 1.0, 0.0)
        more = jnp.maximum(more, jnp.sum(again, axis=1, keepdims=True))
    return ids.astype(jnp.int32), moved[:, :listed].astype(jnp.int32), more


def arrival_kernel(dims, places, q_ref, tables_ref, length_ref, acc_ref, top_ref, total_ref, *refs):
    pool, heads, rows, block_len, spans, listed, factor = dims
    code_refs, (out_ref, moved_ref, more_ref, log_ref, t_ref, p_ref) = refs[:-6], refs[-6:]
    height = q_ref.shape[1]
    width = 2 * block_len
    extra = 2 * heads * block_len
    slots = [(code_refs[array], row) for array, row in places]
    pairs = len(slots) // 2

    def pair(i, part, h):
        at = pl.ds((part * heads + h) * block_len, block_len)
        return jnp.concatenate([ref[r, at] for ref, r in slots[2 * i : 2 * i + 2]], axis=0)

    lists, scale_rows = [], []
    for ref, r in slots:
        values = ref[r, pl.ds(extra, EXTRA)].astype(jnp.float32)
        scale_rows.append(values)
        if len(lists) < len(slots) // CAP:
            lists.append(values[2 * heads : 2 * heads + 1])

    def scale_row(row):
        return jnp.concatenate([values[row : row + 1] for values in scale_rows], axis=1)

    ids, moved_ref[...], more = arrival_ids(lax.axis_index("inst"), pool, lists, listed)
    more_ref[0] = jnp.max(more).astype(jnp.int32)

    def store_log(b, value):
        log_ref[:, b * block_len : (b + 1) * block_len] = value

    count_log(tables_ref[...], length_ref[...], ids, block_len, spans, store_log)
    for h in range(heads):
        key_scale = scale_row(h) * (factor * LOG2E)
        for i in range(pairs):
            left = i * width

            def store(row, lane, value, h=h, left=left):
                t_ref[h, row : row + rows, left + lane : left + lane + value.shape[1]] = value

            score_tiles(
                q_ref[h],
                pair(i, 0, h),
                log_ref.at[:, left : left + width],
                key_scale[:, left : left + width],
                rows,
                store,
            )
    for h in range(heads):
        scale = scale_row(heads + h)
        for row in range(0, height, rows):
            at = pl.ds(row, rows)
            score = t_ref[h, at]
            own_top = top_ref[h, at]
            top = jnp.maximum(
                own_top, jnp.max(lane_fold(score, jnp.maximum), axis=1, keepdims=True)
            )
            weight = jnp.exp2(score - spread(top, score.shape[1]))
            keep = jnp.exp2(own_top - top)
            total = total_ref[h, at] * keep + jnp.sum(
                lane_fold(weight, jnp.add), axis=1, keepdims=True
            )
            p_ref[h, at] = (weight * scale).astype(jnp.bfloat16)
            t_ref[h, at, 0:128] = keep
            t_ref[h, at, 128:256] = 1.0 / total
        mixed = acc_ref[h] * t_ref[h, :, 0:128]
        for i in range(pairs):
            mixed = mixed + jnp.dot(
                p_ref[h, :, i * width : (i + 1) * width],
                pair(i, 1, h),
                preferred_element_type=jnp.float32,
            )
        result = (mixed * t_ref[h, :, 128:256]).astype(jnp.bfloat16)
        out_ref[:, h] = result.reshape(height // rows, rows, result.shape[-1])


def attend(
    general, queries, new_kv, pool_codes, pool_scales, tables, ctx_len, mig_block, mig_dest
):
    instances = lax.axis_size("inst")
    pool = pool_codes.shape[0]
    requests, steps, q_heads, head_dim = queries.shape
    heads = new_kv.shape[3]
    per_head = q_heads // heads
    spans = tables.shape[1]
    block_len = pool_codes.shape[3]
    listed = mig_dest.shape[1]
    factor = head_dim ** (-0.5)
    rows = per_head * steps
    height = requests * rows
    slots = instances * CAP
    group = 8
    f32, bf16 = jnp.float32, jnp.bfloat16
    code_rows = 2 * heads * block_len
    pool_rows = pool_codes.reshape(pool, code_rows, head_dim)
    sent_shape = (code_rows + EXTRA, head_dim)
    sent_bytes = 2 * math.prod(sent_shape)
    part_scales = jnp.transpose(pool_scales, (1, 2, 0))
    assert instances & (instances - 1) == 0 and 2 * heads < EXTRA and head_dim == 128

    if general:
        sizes = [CAP] * instances
        copies = [(r * instances + k, [(k, r)]) for k in range(instances) for r in range(CAP)]
    else:
        sizes = [1, 2] + [1] * (instances - 1)
        copies = [(CAP * instances, [(instances, 0), (1, 1)])]
        copies += [(k, [(k, 0)]) for k in list(range(instances))[::-1]]
    stores = sum(len(targets) for _, targets in copies)
    send = pl.pallas_call(
        functools.partial(pack_kernel, (instances, listed, heads, pool, copies)),
        out_shape=[jax.ShapeDtypeStruct((size,) + sent_shape, bf16) for size in sizes],
        in_specs=[SMEM_SPEC, SMEM_SPEC, VMEM_SPEC, HBM_SPEC],
        out_specs=[HBM_SPEC] * len(sizes),
        scratch_shapes=[
            pltpu.SMEM((CAP * instances + 1,), jnp.int32),
            pltpu.VMEM((EXTRA, head_dim), f32),
            pltpu.VMEM((len(copies),) + sent_shape, bf16),
            pltpu.SemaphoreType.DMA((len(copies),)),
            pltpu.SemaphoreType.DMA((stores,)),
        ],
        compiler_params=pltpu.CompilerParams(vmem_limit_bytes=56 * MIB),
        cost_estimate=pl.CostEstimate(
            flops=0, bytes_accessed=2 * stores * sent_bytes, transcendentals=0
        ),
        name="pack_blocks",
    )(mig_dest, mig_block, part_scales, pool_rows)
    part_scales, *send = lax.optimization_barrier((part_scales, *send))

    def swap(value, distance):
        return lax.ppermute(value, "inst", [(j, j ^ distance) for j in range(instances)])

    if general:
        arrived = [send[0]] + [swap(send[k], k) for k in range(1, instances)]
        places = [(k, r) for r in range(CAP) for k in range(instances)]
    else:
        seconds = {0: send.pop()}
        bit = instances // 2
        while bit > 1:
            for k in list(seconds):
                seconds[k ^ bit] = swap(seconds[k], bit)
            bit //= 2
        arrived = [send[0]] + [swap(send[k], k) for k in range(1, instances)]
    flat_scales = part_scales.reshape(1, -1).astype(f32)

    query_rows = (
        queries.reshape(requests, steps, heads, per_head, head_dim)
        .transpose(2, 0, 3, 1, 4)
        .reshape(heads, height, head_dim)
    )
    fresh_len = requests * steps
    fresh = new_kv.transpose(2, 3, 0, 1, 4).reshape(2, heads, fresh_len, head_dim)
    fresh = jnp.pad(fresh, ((0, 0), (0, 0), (0, -fresh_len % 128), (0, 0)))
    assert fresh.shape[2] == head_dim
    length = ctx_len[:, None]
    width = group * block_len
    chunks = pool // group
    tokens = pool * block_len

    stat = (heads, height, head_dim)
    own_parts = pl.pallas_call(
        functools.partial(
            own_kernel, (pool, heads, rows, steps, block_len, spans, factor, group)
        ),
        out_shape=[jax.ShapeDtypeStruct(stat, f32)] * 3,
        in_specs=[VMEM_SPEC, VMEM_SPEC, SMEM_SPEC, VMEM_SPEC, VMEM_SPEC, HBM_SPEC],
        out_specs=[VMEM_SPEC] * 3,
        scratch_shapes=[
            pltpu.VMEM((chunks, requests, width), f32),
            pltpu.VMEM((chunks, 2 * heads, width), f32),
            pltpu.VMEM((heads, chunks, height, width), f32),
            pltpu.VMEM((heads, height, width), bf16),
            pltpu.VMEM((2, chunks, group, heads * block_len, head_dim), bf16),
            pltpu.SemaphoreType.DMA((2, chunks)),
        ],
        compiler_params=pltpu.CompilerParams(vmem_limit_bytes=48 * MIB),
        cost_estimate=pl.CostEstimate(
            flops=4 * heads * height * tokens * head_dim,
            bytes_accessed=pool_codes.size * 2,
            transcendentals=heads * height * tokens,
        ),
        name="own_blocks",
    )(tables, length, flat_scales, query_rows, fresh, pool_rows)

    if not general:
        held = {k: second for k, second in seconds.items() if k}
        held, own_parts = lax.optimization_barrier((held, own_parts))
        for k in held:
            seconds[k ^ 1] = swap(held[k], 1)
        places = [(k, 0) for k in range(instances)]
        for k in range(instances):
            if k == 1:
                places.append((1, 1))
            else:
                places.append((len(arrived), 0))
                arrived.append(seconds[k])

    arrival_bytes = 6 * heads * height * slots * block_len + 2 * 12 * height * head_dim * heads
    arrival_bytes += 2 * slots * sent_bytes + 4 * requests * slots * block_len
    out, moved_to, more = pl.pallas_call(
        functools.partial(
            arrival_kernel, (pool, heads, rows, block_len, spans, listed, factor), places
        ),
        out_shape=[
            jax.ShapeDtypeStruct((requests, heads, rows, head_dim), bf16),
            jax.ShapeDtypeStruct((1, listed), jnp.int32),
            jax.ShapeDtypeStruct((1,), jnp.int32),
        ],
        in_specs=[VMEM_SPEC] * (6 + len(arrived)),
        out_specs=[VMEM_SPEC, VMEM_SPEC, SMEM_SPEC],
        scratch_shapes=[
            pltpu.VMEM((requests, slots * block_len), f32),
            pltpu.VMEM((heads, height, slots * block_len), f32),
            pltpu.VMEM((heads, height, slots * block_len), bf16),
        ],
        compiler_params=pltpu.CompilerParams(vmem_limit_bytes=arrival_bytes + 8 * MIB),
        cost_estimate=pl.CostEstimate(
            flops=4 * heads * height * slots * block_len * head_dim,
            bytes_accessed=slots * sent_bytes,
            transcendentals=heads * height * slots * block_len,
        ),
        name="arrived_blocks",
    )(query_rows, tables, length, *own_parts, *arrived)
    out = (
        out.reshape(requests, q_heads, steps, head_dim)
        .transpose(0, 2, 1, 3)
        .reshape(requests, steps, q_heads * head_dim)
    )
    return out, moved_to, more


def shards(*args):
    out, moved_to, more = attend(False, *args)
    out = lax.cond(
        more[0] > 1,
        lambda out, *args: attend(True, *args)[0],
        lambda out, *args: out,
        out, *args,
    )
    return out, moved_to


def solution(mesh):
    in_specs = (
        P(("groups", "inst"), None, "tp", None),
        P(("groups", "inst"), None, None, "tp", None),
        P(("groups", "inst"), None, "tp", None, None),
        P(("groups", "inst"), None, "tp"),
        P(("groups", "inst"), None),
        P(("groups", "inst")),
        P(("groups", "inst"), None),
        P(("groups", "inst"), None),
    )
    out_specs = (P(("groups", "inst"), None, "tp"), P(("groups", "inst"), None))
    return jax.shard_map(shards, mesh=mesh, in_specs=in_specs, out_specs=out_specs, check_vma=False)
```

```python
import functools
import math

import jax
import jax.numpy as jnp
from jax import lax
from jax.experimental import pallas as pl
from jax.experimental.pallas import tpu as pltpu
from jax.sharding import PartitionSpec as P

CAP = 2
EXTRA = 16
LOG2E = math.log2(math.e)
MIB = 1 << 20
SMEM_SPEC = pl.BlockSpec(memory_space=pltpu.SMEM)
VMEM_SPEC = pl.BlockSpec(memory_space=pltpu.VMEM)
HBM_SPEC = pl.BlockSpec(memory_space=pltpu.HBM)
NT = (((1,), (1,)), ((), ()))


def loop(count, body, init):
    if count <= 8:
        for i in range(count):
            init = body(i, init)
        return init
    return lax.fori_loop(0, count, body, init)


def pack_kernel(dims, dest_ref, block_ref, scale_ref, pool_ref, *refs):
    instances, listed, heads, pool = dims
    send_refs, (index_ref, extra_ref, sems) = refs[:instances], refs[instances:]
    slots = instances * CAP
    code_rows = send_refs[0].shape[1] - EXTRA
    me = lax.axis_index("inst")
    for slot in range(slots):
        index_ref[slot] = 0

    def place(m, carry):
        dest = dest_ref[0, m]
        rank = loop(
            listed,
            lambda m2, n: n + jnp.where((dest_ref[0, m2] == dest) & (m2 < m), 1, 0),
            jnp.int32(0),
        )
        index_ref[jnp.bitwise_xor(dest, me) * CAP + jnp.minimum(rank, CAP - 1)] = block_ref[0, m]
        return carry

    loop(listed, place, 0)
    order = list(range(slots))[::-1]
    loads = []
    for i in order:
        loads.append(
            pltpu.make_async_copy(
                pool_ref.at[index_ref[i]],
                send_refs[i // CAP].at[i % CAP, pl.ds(0, code_rows)],
                sems.at[i],
            )
        )
        loads[-1].start()
    lane = lax.broadcasted_iota(jnp.int32, (1, 128), 1)

    def spell(m, row):
        return jnp.where(lane == m, dest_ref[0, m].astype(jnp.float32), row)

    extra_ref[...] = jnp.zeros_like(extra_ref)
    extra_ref[2 * heads : 2 * heads + 1, :] = loop(
        listed, spell, jnp.zeros((1, 128), jnp.float32)
    )
    scales = [
        [scale_ref[part, h : h + 1, :].astype(jnp.float32) for h in range(heads)]
        for part in range(2)
    ]
    column = lax.broadcasted_iota(jnp.int32, (1, pool), 1)
    for i in order:
        for part in range(2):
            for h in range(heads):
                one = jnp.where(column == index_ref[i], scales[part][h], 0.0)
                row = part * heads + h
                extra_ref[row : row + 1, :] = jnp.broadcast_to(
                    jnp.sum(one, axis=1, keepdims=True), (1, 128)
                )
        send_refs[i // CAP][i % CAP, pl.ds(code_rows, EXTRA)] = extra_ref[...].astype(jnp.bfloat16)
    for load in loads:
        load.wait()


def split(value, size):
    assert size & (size - 1) == 0
    return lax.shift_right_logical(value, size.bit_length() - 1), value & (size - 1)


def count_log(tables, length, ids, block_len, spans, store):
    requests, width = tables.shape[0], ids.shape[1]
    whole, rest = split(length, block_len)
    whole = jnp.broadcast_to(whole, (requests, width))
    full = jnp.zeros((requests, width), jnp.float32)
    part = jnp.zeros((requests, width), jnp.float32)
    for e in range(spans):
        hit = jnp.broadcast_to(tables[:, e : e + 1], (requests, width)) == ids
        full = full + jnp.where(hit & (whole > e), 1.0, 0.0)
        part = part + jnp.where(hit & (whole == e), 1.0, 0.0)

    def log2(count):
        return jnp.where(count > 0, jnp.log(jnp.maximum(count, 1.0)) * LOG2E, -jnp.inf)

    beyond, within = log2(full), log2(full + part)
    shape = (requests, block_len)
    inside = lax.broadcasted_iota(jnp.int32, shape, 1) < jnp.broadcast_to(rest, shape)
    for b in range(width):
        store(
            b,
            jnp.where(
                inside,
                jnp.broadcast_to(within[:, b : b + 1], shape),
                jnp.broadcast_to(beyond[:, b : b + 1], shape),
            ),
        )


def score_tiles(query, keys, log_ref, scale_row, rows, store):
    height, wide = min(256, query.shape[0]), min(256, keys.shape[0])
    for top in range(0, query.shape[0], height):
        for left in range(0, keys.shape[0], wide):
            part = lax.dot_general(
                query[top : top + height],
                keys[left : left + wide],
                NT,
                preferred_element_type=jnp.float32,
            )
            scale = scale_row[:, left : left + wide]
            for r in range(height // rows):
                request = top // rows + r
                store(
                    request * rows,
                    left,
                    part[r * rows : (r + 1) * rows] * scale
                    + log_ref[request : request + 1, left : left + wide],
                )


def lane_fold(value, op):
    parts = [value[:, i : i + 128] for i in range(0, value.shape[1], 128)]
    while len(parts) > 1:
        parts = [
            op(parts[i], parts[i + 1]) if i + 1 < len(parts) else parts[i]
            for i in range(0, len(parts), 2)
        ]
    return parts[0]


def spread(column, width):
    return jnp.concatenate([column] * (width // 128), axis=1)


def own_kernel(
    dims,
    tables_ref, length_ref, scale_ref, q_ref, fresh_ref, pool_ref,
    acc_ref, top_ref, total_ref,
    log_ref, row_ref, t_ref, p_ref, codes_ref, sems,
):
    pool, heads, rows, steps, block_len, spans, factor, group = dims
    chunks = pool // group
    height, head_dim = q_ref.shape[1:]
    width = group * block_len
    part_rows = heads * block_len

    def load(part, chunk):
        return pltpu.make_async_copy(
            pool_ref.at[pl.ds(chunk * group, group), pl.ds(part * part_rows, part_rows)],
            codes_ref.at[part, chunk],
            sems.at[part, chunk],
        )

    for part in range(2):
        for chunk in range(chunks):
            load(part, chunk).start()

    ids = lax.broadcasted_iota(jnp.int32, (1, pool), 1)

    def store_log(b, value):
        lane = (b % group) * block_len
        log_ref[b // group, :, lane : lane + block_len] = value

    count_log(tables_ref[...], length_ref[...], ids, block_len, spans, store_log)
    for b in range(pool):
        lane = (b % group) * block_len
        for row in range(2 * heads):
            unit = factor * LOG2E if row < heads else 1.0
            row_ref[b // group, row : row + 1, lane : lane + block_len] = jnp.full(
                (1, block_len), scale_ref[0, row * pool + b] * unit
            )
    shape = (height, fresh_ref.shape[2])
    row = lax.broadcasted_iota(jnp.int32, shape, 0)
    col = lax.broadcasted_iota(jnp.int32, shape, 1)
    (request, row_step), (owner, step) = split(row, rows), split(col, steps)
    seen = (request == owner) & (split(row_step, steps)[1] >= step)
    for h in range(heads):
        new_score = lax.dot_general(
            q_ref[h], fresh_ref[0, h], NT, preferred_element_type=jnp.float32
        )
        new_score = jnp.where(seen, new_score * (factor * LOG2E), -jnp.inf)
        acc_ref[h] = new_score
        top_ref[h] = lane_fold(new_score, jnp.maximum)

    def score(chunk, carry):
        load(0, chunk).wait()
        for h in range(heads):

            def store(row, lane, value, h=h):
                t_ref[h, chunk, row : row + rows, lane : lane + value.shape[1]] = value

            score_tiles(
                q_ref[h],
                codes_ref[0, chunk, :, h * block_len : (h + 1) * block_len].reshape(width, head_dim),
                log_ref.at[chunk],
                row_ref[chunk, h : h + 1, :],
                rows,
                store,
            )
            for row in range(0, height, rows):
                at = pl.ds(row, rows)
                top_ref[h, at] = jnp.maximum(
                    top_ref[h, at], lane_fold(t_ref[h, chunk, at], jnp.maximum)
                )
        return carry

    lax.fori_loop(0, chunks, score, 0)

    for h in range(heads):
        top = jnp.broadcast_to(jnp.max(top_ref[h], axis=1, keepdims=True), (height, 128))
        top_ref[h] = top
        weight = jnp.exp2(acc_ref[h] - spread(top, acc_ref.shape[2]))
        total_ref[h] = lane_fold(weight, jnp.add)
        acc_ref[h] = jnp.dot(
            weight.astype(jnp.bfloat16), fresh_ref[1, h], preferred_element_type=jnp.float32
        )

    def apply(chunk, carry):
        load(1, chunk).wait()
        for h in range(heads):
            scale = row_ref[chunk, heads + h : heads + h + 1, :]
            for row in range(0, height, rows):
                at = pl.ds(row, rows)
                weight = jnp.exp2(t_ref[h, chunk, at] - spread(top_ref[h, at], width))
                total_ref[h, at] += lane_fold(weight, jnp.add)
                p_ref[h, at] = (weight * scale).astype(jnp.bfloat16)
            acc_ref[h] += jnp.dot(
                p_ref[h],
                codes_ref[1, chunk, :, h * block_len : (h + 1) * block_len].reshape(width, head_dim),
                preferred_element_type=jnp.float32,
            )
        return carry

    lax.fori_loop(0, chunks, apply, 0)
    for h in range(heads):
        total_ref[h] = jnp.broadcast_to(
            jnp.sum(total_ref[h], axis=1, keepdims=True), (height, 128)
        )


def arrival_ids(me, pool, lists, listed):
    instances = len(lists)
    lane = lax.broadcasted_iota(jnp.int32, (1, 128), 1)
    counts = [
        jnp.sum(
            jnp.where((row == me.astype(jnp.float32)) & (lane < listed), 1.0, 0.0),
            axis=1,
            keepdims=True,
        )
        for row in lists
    ]
    slot = lax.broadcasted_iota(jnp.int32, (1, instances * CAP), 1)
    ids = jnp.full(slot.shape, -1.0)
    for k in range(instances):
        first = jnp.full((1, 1), float(pool))
        for j in range(instances):
            lower = jnp.bitwise_xor(me, j) < jnp.bitwise_xor(me, k)
            first = first + jnp.where(lower, counts[j], 0.0)
        for r in range(CAP):
            name = jnp.where(counts[k] > r, first + r, -1.0)
            ids = jnp.where(slot == r * instances + k, jnp.broadcast_to(name, slot.shape), ids)
    moved = jnp.full((1, 128), float(pool))
    for j in range(instances):
        for m in range(listed):
            same = jnp.broadcast_to(lists[j][:, m : m + 1], (1, 128)) == lists[0]
            ahead = jnp.bitwise_xor(me, j) < me if j else lane > m
            moved = moved + jnp.where(same & ahead, 1.0, 0.0)
    return ids.astype(jnp.int32), moved[:, :listed].astype(jnp.int32)


def arrival_kernel(dims, q_ref, tables_ref, length_ref, acc_ref, top_ref, total_ref, *refs):
    pool, heads, rows, block_len, spans, listed, factor = dims
    code_refs, (out_ref, moved_ref, log_ref, t_ref, p_ref) = refs[:-5], refs[-5:]
    instances = len(code_refs)
    height = q_ref.shape[1]
    width = 2 * block_len
    extra = 2 * heads * block_len
    slots = [(ref, r) for r in range(CAP) for ref in code_refs]
    pairs = len(slots) // 2

    def pair(i, part, h):
        at = pl.ds((part * heads + h) * block_len, block_len)
        return jnp.concatenate([ref[r, at] for ref, r in slots[2 * i : 2 * i + 2]], axis=0)

    lists, scale_rows = [], []
    for ref, r in slots:
        values = ref[r, pl.ds(extra, EXTRA)].astype(jnp.float32)
        scale_rows.append(values)
        if r == 0:
            lists.append(values[2 * heads : 2 * heads + 1])

    def scale_row(row):
        return jnp.concatenate([values[row : row + 1] for values in scale_rows], axis=1)

    ids, moved_ref[...] = arrival_ids(lax.axis_index("inst"), pool, lists, listed)

    def store_log(b, value):
        log_ref[:, b * block_len : (b + 1) * block_len] = value

    count_log(tables_ref[...], length_ref[...], ids, block_len, spans, store_log)
    for h in range(heads):
        key_scale = scale_row(h) * (factor * LOG2E)
        for i in range(pairs):
            left = i * width

            def store(row, lane, value, h=h, left=left):
                t_ref[h, row : row + rows, left + lane : left + lane + value.shape[1]] = value

            score_tiles(
                q_ref[h],
                pair(i, 0, h),
                log_ref.at[:, left : left + width],
                key_scale[:, left : left + width],
                rows,
                store,
            )
    for h in range(heads):
        scale = scale_row(heads + h)
        for row in range(0, height, rows):
            at = pl.ds(row, rows)
            score = t_ref[h, at]
            own_top = top_ref[h, at]
            top = jnp.maximum(
                own_top, jnp.max(lane_fold(score, jnp.maximum), axis=1, keepdims=True)
            )
            weight = jnp.exp2(score - spread(top, score.shape[1]))
            keep = jnp.exp2(own_top - top)
            total = total_ref[h, at] * keep + jnp.sum(
                lane_fold(weight, jnp.add), axis=1, keepdims=True
            )
            p_ref[h, at] = (weight * scale).astype(jnp.bfloat16)
            t_ref[h, at, 0:128] = keep
            t_ref[h, at, 128:256] = 1.0 / total
        mixed = acc_ref[h] * t_ref[h, :, 0:128]
        for i in range(pairs):
            mixed = mixed + jnp.dot(
                p_ref[h, :, i * width : (i + 1) * width],
                pair(i, 1, h),
                preferred_element_type=jnp.float32,
            )
        result = (mixed * t_ref[h, :, 128:256]).astype(jnp.bfloat16)
        out_ref[:, h] = result.reshape(height // rows, rows, result.shape[-1])


def shards(queries, new_kv, pool_codes, pool_scales, tables, ctx_len, mig_block, mig_dest):
    instances = lax.axis_size("inst")
    pool = pool_codes.shape[0]
    requests, steps, q_heads, head_dim = queries.shape
    heads = new_kv.shape[3]
    per_head = q_heads // heads
    spans = tables.shape[1]
    block_len = pool_codes.shape[3]
    listed = mig_dest.shape[1]
    factor = head_dim ** (-0.5)
    rows = per_head * steps
    height = requests * rows
    slots = instances * CAP
    group = 8
    f32, bf16 = jnp.float32, jnp.bfloat16
    code_rows = 2 * heads * block_len
    pool_rows = pool_codes.reshape(pool, code_rows, head_dim)
    sent_shape = (CAP, code_rows + EXTRA, head_dim)
    sent_bytes = 2 * math.prod(sent_shape)
    part_scales = jnp.transpose(pool_scales, (1, 2, 0))
    assert instances & (instances - 1) == 0 and 2 * heads < EXTRA and head_dim == 128

    send = pl.pallas_call(
        functools.partial(pack_kernel, (instances, listed, heads, pool)),
        out_shape=[jax.ShapeDtypeStruct(sent_shape, bf16)] * instances,
        in_specs=[SMEM_SPEC, SMEM_SPEC, VMEM_SPEC, HBM_SPEC],
        out_specs=[VMEM_SPEC] * instances,
        scratch_shapes=[
            pltpu.SMEM((slots,), jnp.int32),
            pltpu.VMEM((EXTRA, head_dim), f32),
            pltpu.SemaphoreType.DMA((slots,)),
        ],
        compiler_params=pltpu.CompilerParams(vmem_limit_bytes=56 * MIB),
        cost_estimate=pl.CostEstimate(
            flops=0, bytes_accessed=2 * instances * sent_bytes, transcendentals=0
        ),
        name="pack_blocks",
    )(mig_dest, mig_block, part_scales, pool_rows)
    part_scales, *send = lax.optimization_barrier((part_scales, *send))

    def swap(value, distance):
        return lax.ppermute(value, "inst", [(j, j ^ distance) for j in range(instances)])

    arrived = {k: swap(send[k], k) for k in range(instances - 1, 0, -1)}
    arrived = [send[0]] + [arrived[k] for k in range(1, instances)]
    flat_scales = part_scales.reshape(1, -1).astype(f32)

    query_rows = (
        queries.reshape(requests, steps, heads, per_head, head_dim)
        .transpose(2, 0, 3, 1, 4)
        .reshape(heads, height, head_dim)
    )
    fresh_len = requests * steps
    fresh = new_kv.transpose(2, 3, 0, 1, 4).reshape(2, heads, fresh_len, head_dim)
    fresh = jnp.pad(fresh, ((0, 0), (0, 0), (0, -fresh_len % 128), (0, 0)))
    assert fresh.shape[2] == head_dim
    length = ctx_len[:, None]
    width = group * block_len
    chunks = pool // group
    tokens = pool * block_len

    stat = (heads, height, head_dim)
    own_parts = pl.pallas_call(
        functools.partial(
            own_kernel, (pool, heads, rows, steps, block_len, spans, factor, group)
        ),
        out_shape=[jax.ShapeDtypeStruct(stat, f32)] * 3,
        in_specs=[VMEM_SPEC, VMEM_SPEC, SMEM_SPEC, VMEM_SPEC, VMEM_SPEC, HBM_SPEC],
        out_specs=[VMEM_SPEC] * 3,
        scratch_shapes=[
            pltpu.VMEM((chunks, requests, width), f32),
            pltpu.VMEM((chunks, 2 * heads, width), f32),
            pltpu.VMEM((heads, chunks, height, width), f32),
            pltpu.VMEM((heads, height, width), bf16),
            pltpu.VMEM((2, chunks, group, heads * block_len, head_dim), bf16),
            pltpu.SemaphoreType.DMA((2, chunks)),
        ],
        compiler_params=pltpu.CompilerParams(vmem_limit_bytes=48 * MIB),
        cost_estimate=pl.CostEstimate(
            flops=4 * heads * height * tokens * head_dim,
            bytes_accessed=pool_codes.size * 2,
            transcendentals=heads * height * tokens,
        ),
        name="own_blocks",
    )(tables, length, flat_scales, query_rows, fresh, pool_rows)

    arrival_bytes = 6 * heads * height * slots * block_len + 2 * 12 * height * head_dim * heads
    arrival_bytes += 2 * instances * sent_bytes + 4 * requests * slots * block_len
    out, moved_to = pl.pallas_call(
        functools.partial(
            arrival_kernel, (pool, heads, rows, block_len, spans, listed, factor)
        ),
        out_shape=[
            jax.ShapeDtypeStruct((requests, heads, rows, head_dim), bf16),
            jax.ShapeDtypeStruct((1, listed), jnp.int32),
        ],
        in_specs=[VMEM_SPEC] * (6 + instances),
        out_specs=[VMEM_SPEC, VMEM_SPEC],
        scratch_shapes=[
            pltpu.VMEM((requests, slots * block_len), f32),
            pltpu.VMEM((heads, height, slots * block_len), f32),
            pltpu.VMEM((heads, height, slots * block_len), bf16),
        ],
        compiler_params=pltpu.CompilerParams(vmem_limit_bytes=arrival_bytes + 8 * MIB),
        cost_estimate=pl.CostEstimate(
            flops=4 * heads * height * slots * block_len * head_dim,
            bytes_accessed=instances * sent_bytes,
            transcendentals=heads * height * slots * block_len,
        ),
        name="arrived_blocks",
    )(query_rows, tables, length, *own_parts, *arrived)
    out = (
        out.reshape(requests, q_heads, steps, head_dim)
        .transpose(0, 2, 1, 3)
        .reshape(requests, steps, q_heads * head_dim)
    )
    return out, moved_to


def solution(mesh):
    in_specs = (
        P(("groups", "inst"), None, "tp", None),
        P(("groups", "inst"), None, None, "tp", None),
        P(("groups", "inst"), None, "tp", None, None),
        P(("groups", "inst"), None, "tp"),
        P(("groups", "inst"), None),
        P(("groups", "inst")),
        P(("groups", "inst"), None),
        P(("groups", "inst"), None),
    )
    out_specs = (P(("groups", "inst"), None, "tp"), P(("groups", "inst"), None))
    return jax.shard_map(shards, mesh=mesh, in_specs=in_specs, out_specs=out_specs, check_vma=False)
```

```python
import functools
import math

import jax
import jax.numpy as jnp
from jax import lax
from jax.experimental import pallas as pl
from jax.experimental.pallas import tpu as pltpu
from jax.sharding import PartitionSpec as P

CAP = 2
EXTRA = 16
LOG2E = math.log2(math.e)
MIB = 1 << 20
SMEM_SPEC = pl.BlockSpec(memory_space=pltpu.SMEM)
VMEM_SPEC = pl.BlockSpec(memory_space=pltpu.VMEM)
HBM_SPEC = pl.BlockSpec(memory_space=pltpu.HBM)
NT = (((1,), (1,)), ((), ()))


def loop(count, body, init):
    if count <= 8:
        for i in range(count):
            init = body(i, init)
        return init
    return lax.fori_loop(0, count, body, init)


def pack_kernel(dims, dest_ref, block_ref, scale_ref, pool_ref, *refs):
    instances, listed, heads, pool = dims
    send_refs, (index_ref, extra_ref, sems) = refs[:instances], refs[instances:]
    slots = instances * CAP
    code_rows = send_refs[0].shape[1] - EXTRA
    me = lax.axis_index("inst")
    for slot in range(slots):
        index_ref[slot] = 0

    def place(m, carry):
        dest = dest_ref[0, m]
        rank = loop(
            listed,
            lambda m2, n: n + jnp.where((dest_ref[0, m2] == dest) & (m2 < m), 1, 0),
            jnp.int32(0),
        )
        index_ref[jnp.bitwise_xor(dest, me) * CAP + jnp.minimum(rank, CAP - 1)] = block_ref[0, m]
        return carry

    loop(listed, place, 0)
    order = list(range(slots))[::-1]
    loads = []
    for i in order:
        loads.append(
            pltpu.make_async_copy(
                pool_ref.at[index_ref[i]],
                send_refs[i // CAP].at[i % CAP, pl.ds(0, code_rows)],
                sems.at[i],
            )
        )
        loads[-1].start()
    lane = lax.broadcasted_iota(jnp.int32, (1, 128), 1)

    def spell(m, row):
        return jnp.where(lane == m, dest_ref[0, m].astype(jnp.float32), row)

    extra_ref[...] = jnp.zeros_like(extra_ref)
    extra_ref[2 * heads : 2 * heads + 1, :] = loop(
        listed, spell, jnp.zeros((1, 128), jnp.float32)
    )
    scales = [
        [scale_ref[part, h : h + 1, :].astype(jnp.float32) for h in range(heads)]
        for part in range(2)
    ]
    column = lax.broadcasted_iota(jnp.int32, (1, pool), 1)
    for i in order:
        for part in range(2):
            for h in range(heads):
                one = jnp.where(column == index_ref[i], scales[part][h], 0.0)
                row = part * heads + h
                extra_ref[row : row + 1, :] = jnp.broadcast_to(
                    jnp.sum(one, axis=1, keepdims=True), (1, 128)
                )
        send_refs[i // CAP][i % CAP, pl.ds(code_rows, EXTRA)] = extra_ref[...].astype(jnp.bfloat16)
    for load in loads:
        load.wait()


def split(value, size):
    assert size & (size - 1) == 0
    return lax.shift_right_logical(value, size.bit_length() - 1), value & (size - 1)


def count_log(tables, length, ids, block_len, spans, store):
    requests, width = tables.shape[0], ids.shape[1]
    whole, rest = split(length, block_len)
    whole = jnp.broadcast_to(whole, (requests, width))
    full = jnp.zeros((requests, width), jnp.float32)
    part = jnp.zeros((requests, width), jnp.float32)
    for e in range(spans):
        hit = jnp.broadcast_to(tables[:, e : e + 1], (requests, width)) == ids
        full = full + jnp.where(hit & (whole > e), 1.0, 0.0)
        part = part + jnp.where(hit & (whole == e), 1.0, 0.0)

    def log2(count):
        return jnp.where(count > 0, jnp.log(jnp.maximum(count, 1.0)) * LOG2E, -jnp.inf)

    beyond, within = log2(full), log2(full + part)
    shape = (requests, block_len)
    inside = lax.broadcasted_iota(jnp.int32, shape, 1) < jnp.broadcast_to(rest, shape)
    for b in range(width):
        store(
            b,
            jnp.where(
                inside,
                jnp.broadcast_to(within[:, b : b + 1], shape),
                jnp.broadcast_to(beyond[:, b : b + 1], shape),
            ),
        )


def score_tiles(query, keys, log_ref, scale_row, rows, store):
    height, wide = min(256, query.shape[0]), min(256, keys.shape[0])
    for top in range(0, query.shape[0], height):
        for left in range(0, keys.shape[0], wide):
            part = lax.dot_general(
                query[top : top + height],
                keys[left : left + wide],
                NT,
                preferred_element_type=jnp.float32,
            )
            scale = scale_row[:, left : left + wide]
            for r in range(height // rows):
                request = top // rows + r
                store(
                    request * rows,
                    left,
                    part[r * rows : (r + 1) * rows] * scale
                    + log_ref[request : request + 1, left : left + wide],
                )


def lane_fold(value, op):
    parts = [value[:, i : i + 128] for i in range(0, value.shape[1], 128)]
    while len(parts) > 1:
        parts = [
            op(parts[i], parts[i + 1]) if i + 1 < len(parts) else parts[i]
            for i in range(0, len(parts), 2)
        ]
    return parts[0]


def spread(column, width):
    return jnp.concatenate([column] * (width // 128), axis=1)


def own_kernel(
    dims,
    tables_ref, length_ref, scale_ref, q_ref, fresh_ref, pool_ref,
    acc_ref, top_ref, total_ref,
    log_ref, row_ref, t_ref, p_ref, codes_ref, sems,
):
    pool, heads, rows, steps, block_len, spans, factor, group = dims
    chunks = pool // group
    height, head_dim = q_ref.shape[1:]
    width = group * block_len
    part_rows = heads * block_len

    def load(part, chunk):
        return pltpu.make_async_copy(
            pool_ref.at[pl.ds(chunk * group, group), pl.ds(part * part_rows, part_rows)],
            codes_ref.at[part, chunk],
            sems.at[part, chunk],
        )

    for part in range(2):
        for chunk in range(chunks):
            load(part, chunk).start()

    ids = lax.broadcasted_iota(jnp.int32, (1, pool), 1)

    def store_log(b, value):
        lane = (b % group) * block_len
        log_ref[b // group, :, lane : lane + block_len] = value

    count_log(tables_ref[...], length_ref[...], ids, block_len, spans, store_log)
    for b in range(pool):
        lane = (b % group) * block_len
        for row in range(2 * heads):
            unit = factor * LOG2E if row < heads else 1.0
            row_ref[b // group, row : row + 1, lane : lane + block_len] = jnp.full(
                (1, block_len), scale_ref[0, row * pool + b] * unit
            )
    shape = (height, fresh_ref.shape[2])
    row = lax.broadcasted_iota(jnp.int32, shape, 0)
    col = lax.broadcasted_iota(jnp.int32, shape, 1)
    (request, row_step), (owner, step) = split(row, rows), split(col, steps)
    seen = (request == owner) & (split(row_step, steps)[1] >= step)
    for h in range(heads):
        new_score = lax.dot_general(
            q_ref[h], fresh_ref[0, h], NT, preferred_element_type=jnp.float32
        )
        new_score = jnp.where(seen, new_score * (factor * LOG2E), -jnp.inf)
        acc_ref[h] = new_score
        top_ref[h] = lane_fold(new_score, jnp.maximum)

    def score(chunk, carry):
        load(0, chunk).wait()
        for h in range(heads):

            def store(row, lane, value, h=h):
                t_ref[h, chunk, row : row + rows, lane : lane + value.shape[1]] = value

            score_tiles(
                q_ref[h],
                codes_ref[0, chunk, :, h * block_len : (h + 1) * block_len].reshape(width, head_dim),
                log_ref.at[chunk],
                row_ref[chunk, h : h + 1, :],
                rows,
                store,
            )
            for row in range(0, height, rows):
                at = pl.ds(row, rows)
                top_ref[h, at] = jnp.maximum(
                    top_ref[h, at], lane_fold(t_ref[h, chunk, at], jnp.maximum)
                )
        return carry

    lax.fori_loop(0, chunks, score, 0)

    for h in range(heads):
        top = jnp.broadcast_to(jnp.max(top_ref[h], axis=1, keepdims=True), (height, 128))
        top_ref[h] = top
        weight = jnp.exp2(acc_ref[h] - spread(top, acc_ref.shape[2]))
        total_ref[h] = lane_fold(weight, jnp.add)
        acc_ref[h] = jnp.dot(
            weight.astype(jnp.bfloat16), fresh_ref[1, h], preferred_element_type=jnp.float32
        )

    def apply(chunk, carry):
        load(1, chunk).wait()
        for h in range(heads):
            scale = row_ref[chunk, heads + h : heads + h + 1, :]
            for row in range(0, height, rows):
                at = pl.ds(row, rows)
                weight = jnp.exp2(t_ref[h, chunk, at] - spread(top_ref[h, at], width))
                total_ref[h, at] += lane_fold(weight, jnp.add)
                p_ref[h, at] = (weight * scale).astype(jnp.bfloat16)
            acc_ref[h] += jnp.dot(
                p_ref[h],
                codes_ref[1, chunk, :, h * block_len : (h + 1) * block_len].reshape(width, head_dim),
                preferred_element_type=jnp.float32,
            )
        return carry

    lax.fori_loop(0, chunks, apply, 0)
    for h in range(heads):
        total_ref[h] = jnp.broadcast_to(
            jnp.sum(total_ref[h], axis=1, keepdims=True), (height, 128)
        )


def arrival_ids(me, pool, lists, listed):
    instances = len(lists)
    lane = lax.broadcasted_iota(jnp.int32, (1, 128), 1)
    counts = [
        jnp.sum(
            jnp.where((row == me.astype(jnp.float32)) & (lane < listed), 1.0, 0.0),
            axis=1,
            keepdims=True,
        )
        for row in lists
    ]
    slot = lax.broadcasted_iota(jnp.int32, (1, instances * CAP), 1)
    ids = jnp.full(slot.shape, -1.0)
    for k in range(instances):
        first = jnp.full((1, 1), float(pool))
        for j in range(instances):
            lower = jnp.bitwise_xor(me, j) < jnp.bitwise_xor(me, k)
            first = first + jnp.where(lower, counts[j], 0.0)
        for r in range(CAP):
            name = jnp.where(counts[k] > r, first + r, -1.0)
            ids = jnp.where(slot == r * instances + k, jnp.broadcast_to(name, slot.shape), ids)
    moved = jnp.full((1, 128), float(pool))
    for j in range(instances):
        for m in range(listed):
            same = jnp.broadcast_to(lists[j][:, m : m + 1], (1, 128)) == lists[0]
            ahead = jnp.bitwise_xor(me, j) < me if j else lane > m
            moved = moved + jnp.where(same & ahead, 1.0, 0.0)
    return ids.astype(jnp.int32), moved[:, :listed].astype(jnp.int32)


def arrival_kernel(dims, q_ref, tables_ref, length_ref, acc_ref, top_ref, total_ref, *refs):
    pool, heads, rows, block_len, spans, listed, factor = dims
    code_refs, (out_ref, moved_ref, log_ref, t_ref, p_ref) = refs[-6::-1], refs[-5:]
    height = q_ref.shape[1]
    width = 2 * block_len
    extra = 2 * heads * block_len
    slots = [(ref, r) for r in range(CAP) for ref in code_refs]
    pairs = len(slots) // 2

    def pair(i, part, h):
        at = pl.ds((part * heads + h) * block_len, block_len)
        return jnp.concatenate([ref[r, at] for ref, r in slots[2 * i : 2 * i + 2]], axis=0)

    lists, scale_rows = [], []
    for ref, r in slots:
        values = ref[r, pl.ds(extra, EXTRA)].astype(jnp.float32)
        scale_rows.append(values)
        if r == 0:
            lists.append(values[2 * heads : 2 * heads + 1])

    def scale_row(row):
        return jnp.concatenate([values[row : row + 1] for values in scale_rows], axis=1)

    ids, moved_ref[...] = arrival_ids(lax.axis_index("inst"), pool, lists, listed)

    def store_log(b, value):
        log_ref[:, b * block_len : (b + 1) * block_len] = value

    count_log(tables_ref[...], length_ref[...], ids, block_len, spans, store_log)
    for h in range(heads):
        key_scale = scale_row(h) * (factor * LOG2E)
        for i in range(pairs):
            left = i * width

            def store(row, lane, value, h=h, left=left):
                t_ref[h, row : row + rows, left + lane : left + lane + value.shape[1]] = value

            score_tiles(
                q_ref[h],
                pair(i, 0, h),
                log_ref.at[:, left : left + width],
                key_scale[:, left : left + width],
                rows,
                store,
            )
    for h in range(heads):
        scale = scale_row(heads + h)
        for row in range(0, height, rows):
            at = pl.ds(row, rows)
            score = t_ref[h, at]
            own_top = top_ref[h, at]
            top = jnp.maximum(
                own_top, jnp.max(lane_fold(score, jnp.maximum), axis=1, keepdims=True)
            )
            weight = jnp.exp2(score - spread(top, score.shape[1]))
            keep = jnp.exp2(own_top - top)
            total = total_ref[h, at] * keep + jnp.sum(
                lane_fold(weight, jnp.add), axis=1, keepdims=True
            )
            p_ref[h, at] = (weight * scale).astype(jnp.bfloat16)
            t_ref[h, at, 0:128] = keep
            t_ref[h, at, 128:256] = 1.0 / total
        mixed = acc_ref[h] * t_ref[h, :, 0:128]
        for i in range(pairs):
            mixed = mixed + jnp.dot(
                p_ref[h, :, i * width : (i + 1) * width],
                pair(i, 1, h),
                preferred_element_type=jnp.float32,
            )
        result = (mixed * t_ref[h, :, 128:256]).astype(jnp.bfloat16)
        out_ref[:, h] = result.reshape(height // rows, rows, result.shape[-1])


def shards(queries, new_kv, pool_codes, pool_scales, tables, ctx_len, mig_block, mig_dest):
    instances = lax.axis_size("inst")
    pool = pool_codes.shape[0]
    requests, steps, q_heads, head_dim = queries.shape
    heads = new_kv.shape[3]
    per_head = q_heads // heads
    spans = tables.shape[1]
    block_len = pool_codes.shape[3]
    listed = mig_dest.shape[1]
    factor = head_dim ** (-0.5)
    rows = per_head * steps
    height = requests * rows
    slots = instances * CAP
    group = 8
    f32, bf16 = jnp.float32, jnp.bfloat16
    code_rows = 2 * heads * block_len
    pool_rows = pool_codes.reshape(pool, code_rows, head_dim)
    sent_shape = (CAP, code_rows + EXTRA, head_dim)
    sent_bytes = 2 * math.prod(sent_shape)
    part_scales = jnp.transpose(pool_scales, (1, 2, 0))
    assert instances & (instances - 1) == 0 and 2 * heads < EXTRA and head_dim == 128

    send = pl.pallas_call(
        functools.partial(pack_kernel, (instances, listed, heads, pool)),
        out_shape=[jax.ShapeDtypeStruct(sent_shape, bf16)] * instances,
        in_specs=[SMEM_SPEC, SMEM_SPEC, VMEM_SPEC, HBM_SPEC],
        out_specs=[VMEM_SPEC] * instances,
        scratch_shapes=[
            pltpu.SMEM((slots,), jnp.int32),
            pltpu.VMEM((EXTRA, head_dim), f32),
            pltpu.SemaphoreType.DMA((slots,)),
        ],
        compiler_params=pltpu.CompilerParams(vmem_limit_bytes=547 * MIB // 10),
        cost_estimate=pl.CostEstimate(
            flops=0, bytes_accessed=2 * instances * sent_bytes, transcendentals=0
        ),
        name="pack_blocks",
    )(mig_dest, mig_block, part_scales, pool_rows)
    part_scales, *send = lax.optimization_barrier((part_scales, *send))

    def swap(value, distance):
        return lax.ppermute(value, "inst", [(j, j ^ distance) for j in range(instances)])

    arrived = {k: swap(send[k], k) for k in range(instances - 1, 0, -1)}
    arrived = [send[0]] + [arrived[k] for k in range(1, instances)]
    flat_scales = part_scales.reshape(1, -1).astype(f32)

    query_rows = (
        queries.reshape(requests, steps, heads, per_head, head_dim)
        .transpose(2, 0, 3, 1, 4)
        .reshape(heads, height, head_dim)
    )
    fresh_len = requests * steps
    fresh = new_kv.transpose(2, 3, 0, 1, 4).reshape(2, heads, fresh_len, head_dim)
    fresh = jnp.pad(fresh, ((0, 0), (0, 0), (0, -fresh_len % 128), (0, 0)))
    assert fresh.shape[2] == head_dim
    length = ctx_len[:, None]
    width = group * block_len
    chunks = pool // group
    tokens = pool * block_len

    stat = (heads, height, head_dim)
    own_parts = pl.pallas_call(
        functools.partial(
            own_kernel, (pool, heads, rows, steps, block_len, spans, factor, group)
        ),
        out_shape=[jax.ShapeDtypeStruct(stat, f32)] * 3,
        in_specs=[VMEM_SPEC, VMEM_SPEC, SMEM_SPEC, VMEM_SPEC, VMEM_SPEC, HBM_SPEC],
        out_specs=[VMEM_SPEC] * 3,
        scratch_shapes=[
            pltpu.VMEM((chunks, requests, width), f32),
            pltpu.VMEM((chunks, 2 * heads, width), f32),
            pltpu.VMEM((heads, chunks, height, width), f32),
            pltpu.VMEM((heads, height, width), bf16),
            pltpu.VMEM((2, chunks, group, heads * block_len, head_dim), bf16),
            pltpu.SemaphoreType.DMA((2, chunks)),
        ],
        compiler_params=pltpu.CompilerParams(vmem_limit_bytes=48 * MIB),
        cost_estimate=pl.CostEstimate(
            flops=4 * heads * height * tokens * head_dim,
            bytes_accessed=pool_codes.size * 2,
            transcendentals=heads * height * tokens,
        ),
        name="own_blocks",
    )(tables, length, flat_scales, query_rows, fresh, pool_rows)

    arrival_bytes = 6 * heads * height * slots * block_len + 2 * 12 * height * head_dim * heads
    arrival_bytes += 2 * instances * sent_bytes + 4 * requests * slots * block_len
    out, moved_to = pl.pallas_call(
        functools.partial(
            arrival_kernel, (pool, heads, rows, block_len, spans, listed, factor)
        ),
        out_shape=[
            jax.ShapeDtypeStruct((requests, heads, rows, head_dim), bf16),
            jax.ShapeDtypeStruct((1, listed), jnp.int32),
        ],
        in_specs=[VMEM_SPEC] * (6 + instances),
        out_specs=[VMEM_SPEC, VMEM_SPEC],
        scratch_shapes=[
            pltpu.VMEM((requests, slots * block_len), f32),
            pltpu.VMEM((heads, height, slots * block_len), f32),
            pltpu.VMEM((heads, height, slots * block_len), bf16),
        ],
        compiler_params=pltpu.CompilerParams(vmem_limit_bytes=arrival_bytes + 8 * MIB),
        cost_estimate=pl.CostEstimate(
            flops=4 * heads * height * slots * block_len * head_dim,
            bytes_accessed=instances * sent_bytes,
            transcendentals=heads * height * slots * block_len,
        ),
        name="arrived_blocks",
    )(query_rows, tables, length, *own_parts, *arrived[::-1])
    out = (
        out.reshape(requests, q_heads, steps, head_dim)
        .transpose(0, 2, 1, 3)
        .reshape(requests, steps, q_heads * head_dim)
    )
    return out, moved_to


def solution(mesh):
    in_specs = (
        P(("groups", "inst"), None, "tp", None),
        P(("groups", "inst"), None, None, "tp", None),
        P(("groups", "inst"), None, "tp", None, None),
        P(("groups", "inst"), None, "tp"),
        P(("groups", "inst"), None),
        P(("groups", "inst")),
        P(("groups", "inst"), None),
        P(("groups", "inst"), None),
    )
    out_specs = (P(("groups", "inst"), None, "tp"), P(("groups", "inst"), None))
    return jax.shard_map(shards, mesh=mesh, in_specs=in_specs, out_specs=out_specs, check_vma=False)
```

```python
import functools
import math

import jax
import jax.numpy as jnp
from jax import lax
from jax.experimental import pallas as pl
from jax.experimental.pallas import tpu as pltpu
from jax.sharding import PartitionSpec as P

CAP = 2
EXTRA = 16
LOG2E = math.log2(math.e)
MIB = 1 << 20
SMEM_SPEC = pl.BlockSpec(memory_space=pltpu.SMEM)
VMEM_SPEC = pl.BlockSpec(memory_space=pltpu.VMEM)
HBM_SPEC = pl.BlockSpec(memory_space=pltpu.HBM)
NT = (((1,), (1,)), ((), ()))


def loop(count, body, init):
    if count <= 8:
        for i in range(count):
            init = body(i, init)
        return init
    return lax.fori_loop(0, count, body, init)


def pack_kernel(dims, dest_ref, block_ref, scale_ref, pool_ref, *refs):
    instances, listed, heads, pool, copies = dims
    send_refs, (index_ref, extra_ref, held_ref, in_sems, out_sems) = refs[:-5], refs[-5:]
    code_rows = held_ref.shape[1] - EXTRA
    me = lax.axis_index("inst")
    for entry in range(CAP * instances + 1):
        index_ref[entry] = 0

    def place(m, carry):
        dest = dest_ref[0, m]
        rank = loop(
            listed,
            lambda m2, n: n + jnp.where((dest_ref[0, m2] == dest) & (m2 < m), 1, 0),
            jnp.int32(0),
        )
        entry = jnp.bitwise_xor(dest, me) + jnp.where(rank > 0, instances, 0)
        index_ref[entry] = block_ref[0, m]
        index_ref[jnp.where(rank > 0, CAP * instances, entry)] = block_ref[0, m]
        return carry

    loop(listed, place, 0)
    loads, stores = [], []
    for i, (entry, _) in enumerate(copies):
        loads.append(
            pltpu.make_async_copy(
                pool_ref.at[index_ref[entry]], held_ref.at[i, pl.ds(0, code_rows)], in_sems.at[i]
            )
        )
        loads[i].start()
    lane = lax.broadcasted_iota(jnp.int32, (1, 128), 1)

    def spell(m, row):
        return jnp.where(lane == m, dest_ref[0, m].astype(jnp.float32), row)

    extra_ref[...] = jnp.zeros_like(extra_ref)
    extra_ref[2 * heads : 2 * heads + 1, :] = loop(
        listed, spell, jnp.zeros((1, 128), jnp.float32)
    )
    scales = [
        [scale_ref[part, h : h + 1, :].astype(jnp.float32) for h in range(heads)]
        for part in range(2)
    ]
    column = lax.broadcasted_iota(jnp.int32, (1, pool), 1)
    for i, (entry, _) in enumerate(copies):
        for part in range(2):
            for h in range(heads):
                one = jnp.where(column == index_ref[entry], scales[part][h], 0.0)
                row = part * heads + h
                extra_ref[row : row + 1, :] = jnp.broadcast_to(
                    jnp.sum(one, axis=1, keepdims=True), (1, 128)
                )
        held_ref[i, pl.ds(code_rows, EXTRA)] = extra_ref[...].astype(jnp.bfloat16)
    for i, (_, targets) in enumerate(copies):
        loads[i].wait()
        for output, row in targets:
            stores.append(
                pltpu.make_async_copy(
                    held_ref.at[i], send_refs[output].at[row], out_sems.at[len(stores)]
                )
            )
            stores[-1].start()
    for store in stores:
        store.wait()


def split(value, size):
    assert size & (size - 1) == 0
    return lax.shift_right_logical(value, size.bit_length() - 1), value & (size - 1)


def count_log(tables, length, ids, block_len, spans, store):
    requests, width = tables.shape[0], ids.shape[1]
    whole, rest = split(length, block_len)
    whole = jnp.broadcast_to(whole, (requests, width))
    full = jnp.zeros((requests, width), jnp.float32)
    part = jnp.zeros((requests, width), jnp.float32)
    for e in range(spans):
        hit = jnp.broadcast_to(tables[:, e : e + 1], (requests, width)) == ids
        full = full + jnp.where(hit & (whole > e), 1.0, 0.0)
        part = part + jnp.where(hit & (whole == e), 1.0, 0.0)

    def log2(count):
        return jnp.where(count > 0, jnp.log(jnp.maximum(count, 1.0)) * LOG2E, -jnp.inf)

    beyond, within = log2(full), log2(full + part)
    shape = (requests, block_len)
    inside = lax.broadcasted_iota(jnp.int32, shape, 1) < jnp.broadcast_to(rest, shape)
    for b in range(width):
        store(
            b,
            jnp.where(
                inside,
                jnp.broadcast_to(within[:, b : b + 1], shape),
                jnp.broadcast_to(beyond[:, b : b + 1], shape),
            ),
        )


def score_tiles(query, keys, log_ref, scale_row, rows, store):
    height, wide = min(256, query.shape[0]), min(256, keys.shape[0])
    for top in range(0, query.shape[0], height):
        for left in range(0, keys.shape[0], wide):
            part = lax.dot_general(
                query[top : top + height],
                keys[left : left + wide],
                NT,
                preferred_element_type=jnp.float32,
            )
            scale = scale_row[:, left : left + wide]
            for r in range(height // rows):
                request = top // rows + r
                store(
                    request * rows,
                    left,
                    part[r * rows : (r + 1) * rows] * scale
                    + log_ref[request : request + 1, left : left + wide],
                )


def lane_fold(value, op):
    parts = [value[:, i : i + 128] for i in range(0, value.shape[1], 128)]
    while len(parts) > 1:
        parts = [
            op(parts[i], parts[i + 1]) if i + 1 < len(parts) else parts[i]
            for i in range(0, len(parts), 2)
        ]
    return parts[0]


def spread(column, width):
    return jnp.concatenate([column] * (width // 128), axis=1)


def own_kernel(
    dims,
    tables_ref, length_ref, scale_ref, q_ref, fresh_ref, pool_ref,
    acc_ref, top_ref, total_ref,
    log_ref, row_ref, t_ref, p_ref, codes_ref, sems,
):
    pool, heads, rows, steps, block_len, spans, factor, group = dims
    chunks = pool // group
    height, head_dim = q_ref.shape[1:]
    width = group * block_len
    part_rows = heads * block_len

    def load(part, chunk):
        return pltpu.make_async_copy(
            pool_ref.at[pl.ds(chunk * group, group), pl.ds(part * part_rows, part_rows)],
            codes_ref.at[part, chunk],
            sems.at[part, chunk],
        )

    for part in range(2):
        for chunk in range(chunks):
            load(part, chunk).start()

    ids = lax.broadcasted_iota(jnp.int32, (1, pool), 1)

    def store_log(b, value):
        lane = (b % group) * block_len
        log_ref[b // group, :, lane : lane + block_len] = value

    count_log(tables_ref[...], length_ref[...], ids, block_len, spans, store_log)
    for b in range(pool):
        lane = (b % group) * block_len
        for row in range(2 * heads):
            unit = factor * LOG2E if row < heads else 1.0
            row_ref[b // group, row : row + 1, lane : lane + block_len] = jnp.full(
                (1, block_len), scale_ref[0, row * pool + b] * unit
            )
    shape = (height, fresh_ref.shape[2])
    row = lax.broadcasted_iota(jnp.int32, shape, 0)
    col = lax.broadcasted_iota(jnp.int32, shape, 1)
    (request, row_step), (owner, step) = split(row, rows), split(col, steps)
    seen = (request == owner) & (split(row_step, steps)[1] >= step)
    for h in range(heads):
        new_score = lax.dot_general(
            q_ref[h], fresh_ref[0, h], NT, preferred_element_type=jnp.float32
        )
        new_score = jnp.where(seen, new_score * (factor * LOG2E), -jnp.inf)
        acc_ref[h] = new_score
        top_ref[h] = lane_fold(new_score, jnp.maximum)

    def score(chunk, carry):
        load(0, chunk).wait()
        for h in range(heads):

            def store(row, lane, value, h=h):
                t_ref[h, chunk, row : row + rows, lane : lane + value.shape[1]] = value

            score_tiles(
                q_ref[h],
                codes_ref[0, chunk, :, h * block_len : (h + 1) * block_len].reshape(width, head_dim),
                log_ref.at[chunk],
                row_ref[chunk, h : h + 1, :],
                rows,
                store,
            )
            for row in range(0, height, rows):
                at = pl.ds(row, rows)
                top_ref[h, at] = jnp.maximum(
                    top_ref[h, at], lane_fold(t_ref[h, chunk, at], jnp.maximum)
                )
        return carry

    lax.fori_loop(0, chunks, score, 0)

    for h in range(heads):
        top = jnp.broadcast_to(jnp.max(top_ref[h], axis=1, keepdims=True), (height, 128))
        top_ref[h] = top
        weight = jnp.exp2(acc_ref[h] - spread(top, acc_ref.shape[2]))
        total_ref[h] = lane_fold(weight, jnp.add)
        acc_ref[h] = jnp.dot(
            weight.astype(jnp.bfloat16), fresh_ref[1, h], preferred_element_type=jnp.float32
        )

    def apply(chunk, carry):
        load(1, chunk).wait()
        for h in range(heads):
            scale = row_ref[chunk, heads + h : heads + h + 1, :]
            for row in range(0, height, rows):
                at = pl.ds(row, rows)
                weight = jnp.exp2(t_ref[h, chunk, at] - spread(top_ref[h, at], width))
                total_ref[h, at] += lane_fold(weight, jnp.add)
                p_ref[h, at] = (weight * scale).astype(jnp.bfloat16)
            acc_ref[h] += jnp.dot(
                p_ref[h],
                codes_ref[1, chunk, :, h * block_len : (h + 1) * block_len].reshape(width, head_dim),
                preferred_element_type=jnp.float32,
            )
        return carry

    lax.fori_loop(0, chunks, apply, 0)
    for h in range(heads):
        total_ref[h] = jnp.broadcast_to(
            jnp.sum(total_ref[h], axis=1, keepdims=True), (height, 128)
        )


def arrival_ids(me, pool, lists, listed):
    instances = len(lists)
    lane = lax.broadcasted_iota(jnp.int32, (1, 128), 1)
    counts = [
        jnp.sum(
            jnp.where((row == me.astype(jnp.float32)) & (lane < listed), 1.0, 0.0),
            axis=1,
            keepdims=True,
        )
        for row in lists
    ]
    slot = lax.broadcasted_iota(jnp.int32, (1, instances * CAP), 1)
    ids = jnp.full(slot.shape, -1.0)
    for k in range(instances):
        first = jnp.full((1, 1), float(pool))
        for j in range(instances):
            lower = jnp.bitwise_xor(me, j) < jnp.bitwise_xor(me, k)
            first = first + jnp.where(lower, counts[j], 0.0)
        for r in range(CAP):
            name = jnp.where(counts[k] > r, first + r, -1.0)
            ids = jnp.where(slot == r * instances + k, jnp.broadcast_to(name, slot.shape), ids)
    moved = jnp.full((1, 128), float(pool))
    for j in range(instances):
        for m in range(listed):
            same = jnp.broadcast_to(lists[j][:, m : m + 1], (1, 128)) == lists[0]
            ahead = jnp.bitwise_xor(me, j) < me if j else lane > m
            moved = moved + jnp.where(same & ahead, 1.0, 0.0)
    more = jnp.zeros((1, 128))
    for row in lists:
        again = jnp.zeros((1, 128))
        for m in range(listed):
            same = jnp.broadcast_to(row[:, m : m + 1], (1, 128)) == row
            again = again + jnp.where(same & (lane > m) & (lane < listed), 1.0, 0.0)
        more = jnp.maximum(more, jnp.sum(again, axis=1, keepdims=True))
    return ids.astype(jnp.int32), moved[:, :listed].astype(jnp.int32), more


def arrival_kernel(dims, places, q_ref, tables_ref, length_ref, acc_ref, top_ref, total_ref, *refs):
    pool, heads, rows, block_len, spans, listed, factor = dims
    code_refs, (out_ref, moved_ref, more_ref, log_ref, t_ref, p_ref) = refs[:-6], refs[-6:]
    height = q_ref.shape[1]
    width = 2 * block_len
    extra = 2 * heads * block_len
    slots = [(code_refs[array], row) for array, row in places]
    pairs = len(slots) // 2

    def pair(i, part, h):
        at = pl.ds((part * heads + h) * block_len, block_len)
        return jnp.concatenate([ref[r, at] for ref, r in slots[2 * i : 2 * i + 2]], axis=0)

    lists, scale_rows = [], []
    for ref, r in slots:
        values = ref[r, pl.ds(extra, EXTRA)].astype(jnp.float32)
        scale_rows.append(values)
        if len(lists) < len(slots) // CAP:
            lists.append(values[2 * heads : 2 * heads + 1])

    def scale_row(row):
        return jnp.concatenate([values[row : row + 1] for values in scale_rows], axis=1)

    ids, moved_ref[...], more = arrival_ids(lax.axis_index("inst"), pool, lists, listed)
    more_ref[0] = jnp.max(more).astype(jnp.int32)

    def store_log(b, value):
        log_ref[:, b * block_len : (b + 1) * block_len] = value

    count_log(tables_ref[...], length_ref[...], ids, block_len, spans, store_log)
    for h in range(heads):
        key_scale = scale_row(h) * (factor * LOG2E)
        for i in range(pairs):
            left = i * width

            def store(row, lane, value, h=h, left=left):
                t_ref[h, row : row + rows, left + lane : left + lane + value.shape[1]] = value

            score_tiles(
                q_ref[h],
                pair(i, 0, h),
                log_ref.at[:, left : left + width],
                key_scale[:, left : left + width],
                rows,
                store,
            )
    for h in range(heads):
        scale = scale_row(heads + h)
        for row in range(0, height, rows):
            at = pl.ds(row, rows)
            score = t_ref[h, at]
            own_top = top_ref[h, at]
            top = jnp.maximum(
                own_top, jnp.max(lane_fold(score, jnp.maximum), axis=1, keepdims=True)
            )
            weight = jnp.exp2(score - spread(top, score.shape[1]))
            keep = jnp.exp2(own_top - top)
            total = total_ref[h, at] * keep + jnp.sum(
                lane_fold(weight, jnp.add), axis=1, keepdims=True
            )
            p_ref[h, at] = (weight * scale).astype(jnp.bfloat16)
            t_ref[h, at, 0:128] = keep
            t_ref[h, at, 128:256] = 1.0 / total
        mixed = acc_ref[h] * t_ref[h, :, 0:128]
        for i in range(pairs):
            mixed = mixed + jnp.dot(
                p_ref[h, :, i * width : (i + 1) * width],
                pair(i, 1, h),
                preferred_element_type=jnp.float32,
            )
        result = (mixed * t_ref[h, :, 128:256]).astype(jnp.bfloat16)
        out_ref[:, h] = result.reshape(height // rows, rows, result.shape[-1])


def attend(
    general, queries, new_kv, pool_codes, pool_scales, tables, ctx_len, mig_block, mig_dest
):
    instances = lax.axis_size("inst")
    pool = pool_codes.shape[0]
    requests, steps, q_heads, head_dim = queries.shape
    heads = new_kv.shape[3]
    per_head = q_heads // heads
    spans = tables.shape[1]
    block_len = pool_codes.shape[3]
    listed = mig_dest.shape[1]
    factor = head_dim ** (-0.5)
    rows = per_head * steps
    height = requests * rows
    slots = instances * CAP
    group = 8
    f32, bf16 = jnp.float32, jnp.bfloat16
    code_rows = 2 * heads * block_len
    pool_rows = pool_codes.reshape(pool, code_rows, head_dim)
    sent_shape = (code_rows + EXTRA, head_dim)
    sent_bytes = 2 * math.prod(sent_shape)
    part_scales = jnp.transpose(pool_scales, (1, 2, 0))
    assert instances & (instances - 1) == 0 and 2 * heads < EXTRA and head_dim == 128

    def pack(sizes, copies):
        stores = sum(len(targets) for _, targets in copies)
        return pl.pallas_call(
            functools.partial(pack_kernel, (instances, listed, heads, pool, copies)),
            out_shape=[jax.ShapeDtypeStruct((size,) + sent_shape, bf16) for size in sizes],
            in_specs=[SMEM_SPEC, SMEM_SPEC, VMEM_SPEC, HBM_SPEC],
            out_specs=[HBM_SPEC] * len(sizes),
            scratch_shapes=[
                pltpu.SMEM((CAP * instances + 1,), jnp.int32),
                pltpu.VMEM((EXTRA, head_dim), f32),
                pltpu.VMEM((len(copies),) + sent_shape, bf16),
                pltpu.SemaphoreType.DMA((len(copies),)),
                pltpu.SemaphoreType.DMA((stores,)),
            ],
            compiler_params=pltpu.CompilerParams(vmem_limit_bytes=56 * MIB),
            cost_estimate=pl.CostEstimate(
                flops=0, bytes_accessed=2 * stores * sent_bytes, transcendentals=0
            ),
            name="pack_blocks",
        )(mig_dest, mig_block, part_scales, pool_rows)

    def swap(value, distance):
        return lax.ppermute(value, "inst", [(j, j ^ distance) for j in range(instances)])

    if general:
        send = pack(
            [CAP] * instances,
            [(r * instances + k, [(k, r)]) for k in range(instances) for r in range(CAP)],
        )
        arrived = [swap(send[k], k) for k in range(instances - 1, 0, -1)] + [send[0]]
        places = [(instances - 1 - k, r) for r in range(CAP) for k in range(instances)]
    else:
        any_second = CAP * instances
        (second,) = pack([1], [(any_second, [(0, 0)])])
        seconds = {0: second}
        bit = instances // 2
        while bit > 1:
            for k in list(seconds):
                seconds[k ^ bit] = swap(seconds[k], bit)
            bit //= 2
        mig_dest, second = lax.optimization_barrier((mig_dest, second))
        send = pack(
            [1, 2] + [1] * (instances - 2),
            [(k, [(k, 0)]) for k in list(range(instances))[::-1]] + [(any_second, [(1, 1)])],
        )
        firsts = [send[0]] + [swap(send[k], k) for k in range(1, instances)]
    part_scales, *send = lax.optimization_barrier((part_scales, *send))
    flat_scales = part_scales.reshape(1, -1).astype(f32)

    query_rows = (
        queries.reshape(requests, steps, heads, per_head, head_dim)
        .transpose(2, 0, 3, 1, 4)
        .reshape(heads, height, head_dim)
    )
    fresh_len = requests * steps
    fresh = new_kv.transpose(2, 3, 0, 1, 4).reshape(2, heads, fresh_len, head_dim)
    fresh = jnp.pad(fresh, ((0, 0), (0, 0), (0, -fresh_len % 128), (0, 0)))
    assert fresh.shape[2] == head_dim
    length = ctx_len[:, None]
    width = group * block_len
    chunks = pool // group
    tokens = pool * block_len

    stat = (heads, height, head_dim)
    own_parts = pl.pallas_call(
        functools.partial(
            own_kernel, (pool, heads, rows, steps, block_len, spans, factor, group)
        ),
        out_shape=[jax.ShapeDtypeStruct(stat, f32)] * 3,
        in_specs=[VMEM_SPEC, VMEM_SPEC, SMEM_SPEC, VMEM_SPEC, VMEM_SPEC, HBM_SPEC],
        out_specs=[VMEM_SPEC] * 3,
        scratch_shapes=[
            pltpu.VMEM((chunks, requests, width), f32),
            pltpu.VMEM((chunks, 2 * heads, width), f32),
            pltpu.VMEM((heads, chunks, height, width), f32),
            pltpu.VMEM((heads, height, width), bf16),
            pltpu.VMEM((2, chunks, group, heads * block_len, head_dim), bf16),
            pltpu.SemaphoreType.DMA((2, chunks)),
        ],
        compiler_params=pltpu.CompilerParams(vmem_limit_bytes=48 * MIB),
        cost_estimate=pl.CostEstimate(
            flops=4 * heads * height * tokens * head_dim,
            bytes_accessed=pool_codes.size * 2,
            transcendentals=heads * height * tokens,
        ),
        name="own_blocks",
    )(tables, length, flat_scales, query_rows, fresh, pool_rows)

    if not general:
        held = {k: second for k, second in seconds.items() if k}
        held, own_parts = lax.optimization_barrier((held, own_parts))
        for k in held:
            seconds[k ^ 1] = swap(held[k], 1)
        arrived = [held[k] for k in held] + firsts[::-1] + [seconds[0]]
        where = {k: i for i, k in enumerate(held)}
        where[0] = len(arrived) - 1
        places = [(len(held) + instances - 1 - k, 0) for k in range(instances)]
        for k in range(instances):
            if k == 1:
                places.append((places[1][0], 1))
            elif k in where:
                places.append((where[k], 0))
            else:
                places.append((len(arrived), 0))
                arrived.append(seconds[k])

    arrival_bytes = 6 * heads * height * slots * block_len + 2 * 12 * height * head_dim * heads
    arrival_bytes += 2 * slots * sent_bytes + 4 * requests * slots * block_len
    out, moved_to, more = pl.pallas_call(
        functools.partial(
            arrival_kernel, (pool, heads, rows, block_len, spans, listed, factor), places
        ),
        out_shape=[
            jax.ShapeDtypeStruct((requests, heads, rows, head_dim), bf16),
            jax.ShapeDtypeStruct((1, listed), jnp.int32),
            jax.ShapeDtypeStruct((1,), jnp.int32),
        ],
        in_specs=[VMEM_SPEC] * (6 + len(arrived)),
        out_specs=[VMEM_SPEC, VMEM_SPEC, SMEM_SPEC],
        scratch_shapes=[
            pltpu.VMEM((requests, slots * block_len), f32),
            pltpu.VMEM((heads, height, slots * block_len), f32),
            pltpu.VMEM((heads, height, slots * block_len), bf16),
        ],
        compiler_params=pltpu.CompilerParams(vmem_limit_bytes=arrival_bytes + 8 * MIB),
        cost_estimate=pl.CostEstimate(
            flops=4 * heads * height * slots * block_len * head_dim,
            bytes_accessed=slots * sent_bytes,
            transcendentals=heads * height * slots * block_len,
        ),
        name="arrived_blocks",
    )(query_rows, tables, length, *own_parts, *arrived)
    return out, moved_to, more


def shards(queries, *args):
    out, moved_to, more = attend(False, queries, *args)
    out = lax.cond(
        more[0] > 1,
        lambda out, *args: attend(True, *args)[0],
        lambda out, *args: out,
        out, queries, *args,
    )
    requests, steps, q_heads, head_dim = queries.shape
    out = out.reshape(requests, q_heads, steps, head_dim).transpose(0, 2, 1, 3)
    return out.reshape(requests, steps, q_heads * head_dim), moved_to


def solution(mesh):
    in_specs = (
        P(("groups", "inst"), None, "tp", None),
        P(("groups", "inst"), None, None, "tp", None),
        P(("groups", "inst"), None, "tp", None, None),
        P(("groups", "inst"), None, "tp"),
        P(("groups", "inst"), None),
        P(("groups", "inst")),
        P(("groups", "inst"), None),
        P(("groups", "inst"), None),
    )
    out_specs = (P(("groups", "inst"), None, "tp"), P(("groups", "inst"), None))
    return jax.shard_map(shards, mesh=mesh, in_specs=in_specs, out_specs=out_specs, check_vma=False)
```

```python
import functools
import math

import jax
import jax.numpy as jnp
from jax import lax
from jax.experimental import pallas as pl
from jax.experimental.pallas import tpu as pltpu
from jax.sharding import PartitionSpec as P

CAP = 2
EXTRA = 16
LOG2E = math.log2(math.e)
MIB = 1 << 20
SMEM_SPEC = pl.BlockSpec(memory_space=pltpu.SMEM)
VMEM_SPEC = pl.BlockSpec(memory_space=pltpu.VMEM)
HBM_SPEC = pl.BlockSpec(memory_space=pltpu.HBM)
NT = (((1,), (1,)), ((), ()))


def loop(count, body, init):
    if count <= 8:
        for i in range(count):
            init = body(i, init)
        return init
    return lax.fori_loop(0, count, body, init)


def pack_kernel(dims, dest_ref, block_ref, scale_ref, pool_ref, *refs):
    instances, listed, heads, pool, copies = dims
    send_refs, (index_ref, extra_ref, held_ref, in_sems, out_sems) = refs[:-5], refs[-5:]
    code_rows = held_ref.shape[1] - EXTRA
    me = lax.axis_index("inst")
    for entry in range(CAP * instances + 1):
        index_ref[entry] = 0

    def place(m, carry):
        dest = dest_ref[0, m]
        rank = loop(
            listed,
            lambda m2, n: n + jnp.where((dest_ref[0, m2] == dest) & (m2 < m), 1, 0),
            jnp.int32(0),
        )
        entry = jnp.bitwise_xor(dest, me) + jnp.where(rank > 0, instances, 0)
        index_ref[entry] = block_ref[0, m]
        index_ref[jnp.where(rank > 0, CAP * instances, entry)] = block_ref[0, m]
        return carry

    loop(listed, place, 0)
    loads, stores = [], []
    for i, (entry, _) in enumerate(copies):
        loads.append(
            pltpu.make_async_copy(
                pool_ref.at[index_ref[entry]], held_ref.at[i, pl.ds(0, code_rows)], in_sems.at[i]
            )
        )
        loads[i].start()
    lane = lax.broadcasted_iota(jnp.int32, (1, 128), 1)

    def spell(m, row):
        return jnp.where(lane == m, dest_ref[0, m].astype(jnp.float32), row)

    extra_ref[...] = jnp.zeros_like(extra_ref)
    extra_ref[2 * heads : 2 * heads + 1, :] = loop(
        listed, spell, jnp.zeros((1, 128), jnp.float32)
    )
    scales = [
        [scale_ref[part, h : h + 1, :].astype(jnp.float32) for h in range(heads)]
        for part in range(2)
    ]
    column = lax.broadcasted_iota(jnp.int32, (1, pool), 1)
    for i, (entry, _) in enumerate(copies):
        for part in range(2):
            for h in range(heads):
                one = jnp.where(column == index_ref[entry], scales[part][h], 0.0)
                row = part * heads + h
                extra_ref[row : row + 1, :] = jnp.broadcast_to(
                    jnp.sum(one, axis=1, keepdims=True), (1, 128)
                )
        held_ref[i, pl.ds(code_rows, EXTRA)] = extra_ref[...].astype(jnp.bfloat16)
    for i, (_, targets) in enumerate(copies):
        loads[i].wait()
        for output, row in targets:
            stores.append(
                pltpu.make_async_copy(
                    held_ref.at[i], send_refs[output].at[row], out_sems.at[len(stores)]
                )
            )
            stores[-1].start()
    for store in stores:
        store.wait()


def split(value, size):
    assert size & (size - 1) == 0
    return lax.shift_right_logical(value, size.bit_length() - 1), value & (size - 1)


def count_log(tables, length, ids, block_len, spans, store):
    requests, width = tables.shape[0], ids.shape[1]
    whole, rest = split(length, block_len)
    whole = jnp.broadcast_to(whole, (requests, width))
    full = jnp.zeros((requests, width), jnp.float32)
    part = jnp.zeros((requests, width), jnp.float32)
    for e in range(spans):
        hit = jnp.broadcast_to(tables[:, e : e + 1], (requests, width)) == ids
        full = full + jnp.where(hit & (whole > e), 1.0, 0.0)
        part = part + jnp.where(hit & (whole == e), 1.0, 0.0)

    def log2(count):
        return jnp.where(count > 0, jnp.log(jnp.maximum(count, 1.0)) * LOG2E, -jnp.inf)

    beyond, within = log2(full), log2(full + part)
    shape = (requests, block_len)
    inside = lax.broadcasted_iota(jnp.int32, shape, 1) < jnp.broadcast_to(rest, shape)
    for b in range(width):
        store(
            b,
            jnp.where(
                inside,
                jnp.broadcast_to(within[:, b : b + 1], shape),
                jnp.broadcast_to(beyond[:, b : b + 1], shape),
            ),
        )


def score_tiles(query, keys, log_ref, scale_row, rows, store):
    height, wide = min(256, query.shape[0]), min(256, keys.shape[0])
    for top in range(0, query.shape[0], height):
        for left in range(0, keys.shape[0], wide):
            part = lax.dot_general(
                query[top : top + height],
                keys[left : left + wide],
                NT,
                preferred_element_type=jnp.float32,
            )
            scale = scale_row[:, left : left + wide]
            for r in range(height // rows):
                request = top // rows + r
                store(
                    request * rows,
                    left,
                    part[r * rows : (r + 1) * rows] * scale
                    + log_ref[request : request + 1, left : left + wide],
                )


def lane_fold(value, op):
    parts = [value[:, i : i + 128] for i in range(0, value.shape[1], 128)]
    while len(parts) > 1:
        parts = [
            op(parts[i], parts[i + 1]) if i + 1 < len(parts) else parts[i]
            for i in range(0, len(parts), 2)
        ]
    return parts[0]


def spread(column, width):
    return jnp.concatenate([column] * (width // 128), axis=1)


def own_kernel(
    dims,
    tables_ref, length_ref, scale_ref, q_ref, fresh_ref, pool_ref,
    acc_ref, top_ref, total_ref,
    log_ref, row_ref, t_ref, p_ref, codes_ref, sems,
):
    pool, heads, rows, steps, block_len, spans, factor, group = dims
    chunks = pool // group
    height, head_dim = q_ref.shape[1:]
    width = group * block_len
    part_rows = heads * block_len

    def load(part, chunk):
        return pltpu.make_async_copy(
            pool_ref.at[pl.ds(chunk * group, group), pl.ds(part * part_rows, part_rows)],
            codes_ref.at[part, chunk],
            sems.at[part, chunk],
        )

    for part in range(2):
        for chunk in range(chunks):
            load(part, chunk).start()

    ids = lax.broadcasted_iota(jnp.int32, (1, pool), 1)

    def store_log(b, value):
        lane = (b % group) * block_len
        log_ref[b // group, :, lane : lane + block_len] = value

    count_log(tables_ref[...], length_ref[...], ids, block_len, spans, store_log)
    for b in range(pool):
        lane = (b % group) * block_len
        for row in range(2 * heads):
            unit = factor * LOG2E if row < heads else 1.0
            row_ref[b // group, row : row + 1, lane : lane + block_len] = jnp.full(
                (1, block_len), scale_ref[0, row * pool + b] * unit
            )
    shape = (height, fresh_ref.shape[2])
    row = lax.broadcasted_iota(jnp.int32, shape, 0)
    col = lax.broadcasted_iota(jnp.int32, shape, 1)
    (request, row_step), (owner, step) = split(row, rows), split(col, steps)
    seen = (request == owner) & (split(row_step, steps)[1] >= step)
    for h in range(heads):
        new_score = lax.dot_general(
            q_ref[h], fresh_ref[0, h], NT, preferred_element_type=jnp.float32
        )
        new_score = jnp.where(seen, new_score * (factor * LOG2E), -jnp.inf)
        acc_ref[h] = new_score
        top_ref[h] = lane_fold(new_score, jnp.maximum)

    def score(chunk, carry):
        load(0, chunk).wait()
        for h in range(heads):

            def store(row, lane, value, h=h):
                t_ref[h, chunk, row : row + rows, lane : lane + value.shape[1]] = value

            score_tiles(
                q_ref[h],
                codes_ref[0, chunk, :, h * block_len : (h + 1) * block_len].reshape(width, head_dim),
                log_ref.at[chunk],
                row_ref[chunk, h : h + 1, :],
                rows,
                store,
            )
            for row in range(0, height, rows):
                at = pl.ds(row, rows)
                top_ref[h, at] = jnp.maximum(
                    top_ref[h, at], lane_fold(t_ref[h, chunk, at], jnp.maximum)
                )
        return carry

    lax.fori_loop(0, chunks, score, 0)

    for h in range(heads):
        top = jnp.broadcast_to(jnp.max(top_ref[h], axis=1, keepdims=True), (height, 128))
        top_ref[h] = top
        weight = jnp.exp2(acc_ref[h] - spread(top, acc_ref.shape[2]))
        total_ref[h] = lane_fold(weight, jnp.add)
        acc_ref[h] = jnp.dot(
            weight.astype(jnp.bfloat16), fresh_ref[1, h], preferred_element_type=jnp.float32
        )

    def apply(chunk, carry):
        load(1, chunk).wait()
        for h in range(heads):
            scale = row_ref[chunk, heads + h : heads + h + 1, :]
            for row in range(0, height, rows):
                at = pl.ds(row, rows)
                weight = jnp.exp2(t_ref[h, chunk, at] - spread(top_ref[h, at], width))
                total_ref[h, at] += lane_fold(weight, jnp.add)
                p_ref[h, at] = (weight * scale).astype(jnp.bfloat16)
            acc_ref[h] += jnp.dot(
                p_ref[h],
                codes_ref[1, chunk, :, h * block_len : (h + 1) * block_len].reshape(width, head_dim),
                preferred_element_type=jnp.float32,
            )
        return carry

    lax.fori_loop(0, chunks, apply, 0)
    for h in range(heads):
        total_ref[h] = jnp.broadcast_to(
            jnp.sum(total_ref[h], axis=1, keepdims=True), (height, 128)
        )


def arrival_ids(me, pool, lists, listed):
    instances = len(lists)
    lane = lax.broadcasted_iota(jnp.int32, (1, 128), 1)
    counts = [
        jnp.sum(
            jnp.where((row == me.astype(jnp.float32)) & (lane < listed), 1.0, 0.0),
            axis=1,
            keepdims=True,
        )
        for row in lists
    ]
    slot = lax.broadcasted_iota(jnp.int32, (1, instances * CAP), 1)
    ids = jnp.full(slot.shape, -1.0)
    for k in range(instances):
        first = jnp.full((1, 1), float(pool))
        for j in range(instances):
            lower = jnp.bitwise_xor(me, j) < jnp.bitwise_xor(me, k)
            first = first + jnp.where(lower, counts[j], 0.0)
        for r in range(CAP):
            name = jnp.where(counts[k] > r, first + r, -1.0)
            ids = jnp.where(slot == r * instances + k, jnp.broadcast_to(name, slot.shape), ids)
    moved = jnp.full((1, 128), float(pool))
    for j in range(instances):
        for m in range(listed):
            same = jnp.broadcast_to(lists[j][:, m : m + 1], (1, 128)) == lists[0]
            ahead = jnp.bitwise_xor(me, j) < me if j else lane > m
            moved = moved + jnp.where(same & ahead, 1.0, 0.0)
    more = jnp.zeros((1, 128))
    for row in lists:
        again = jnp.zeros((1, 128))
        for m in range(listed):
            same = jnp.broadcast_to(row[:, m : m + 1], (1, 128)) == row
            again = again + jnp.where(same & (lane > m) & (lane < listed), 1.0, 0.0)
        more = jnp.maximum(more, jnp.sum(again, axis=1, keepdims=True))
    return ids.astype(jnp.int32), moved[:, :listed].astype(jnp.int32), more


def arrival_kernel(dims, places, q_ref, tables_ref, length_ref, acc_ref, top_ref, total_ref, *refs):
    pool, heads, rows, block_len, spans, listed, factor = dims
    code_refs, (out_ref, moved_ref, more_ref, log_ref, t_ref, p_ref) = refs[:-6], refs[-6:]
    height = q_ref.shape[1]
    width = 2 * block_len
    extra = 2 * heads * block_len
    slots = [(code_refs[array], row) for array, row in places]
    pairs = len(slots) // 2

    def pair(i, part, h):
        at = pl.ds((part * heads + h) * block_len, block_len)
        return jnp.concatenate([ref[r, at] for ref, r in slots[2 * i : 2 * i + 2]], axis=0)

    lists, scale_rows = [], []
    for ref, r in slots:
        values = ref[r, pl.ds(extra, EXTRA)].astype(jnp.float32)
        scale_rows.append(values)
        if len(lists) < len(slots) // CAP:
            lists.append(values[2 * heads : 2 * heads + 1])

    def scale_row(row):
        return jnp.concatenate([values[row : row + 1] for values in scale_rows], axis=1)

    ids, moved_ref[...], more = arrival_ids(lax.axis_index("inst"), pool, lists, listed)
    more_ref[0] = jnp.max(more).astype(jnp.int32)

    def store_log(b, value):
        log_ref[:, b * block_len : (b + 1) * block_len] = value

    count_log(tables_ref[...], length_ref[...], ids, block_len, spans, store_log)
    for h in range(heads):
        key_scale = scale_row(h) * (factor * LOG2E)
        for i in range(pairs):
            left = i * width

            def store(row, lane, value, h=h, left=left):
                t_ref[h, row : row + rows, left + lane : left + lane + value.shape[1]] = value

            score_tiles(
                q_ref[h],
                pair(i, 0, h),
                log_ref.at[:, left : left + width],
                key_scale[:, left : left + width],
                rows,
                store,
            )
    for h in range(heads):
        scale = scale_row(heads + h)
        for row in range(0, height, rows):
            at = pl.ds(row, rows)
            score = t_ref[h, at]
            own_top = top_ref[h, at]
            top = jnp.maximum(
                own_top, jnp.max(lane_fold(score, jnp.maximum), axis=1, keepdims=True)
            )
            weight = jnp.exp2(score - spread(top, score.shape[1]))
            keep = jnp.exp2(own_top - top)
            total = total_ref[h, at] * keep + jnp.sum(
                lane_fold(weight, jnp.add), axis=1, keepdims=True
            )
            p_ref[h, at] = (weight * scale).astype(jnp.bfloat16)
            t_ref[h, at, 0:128] = keep
            t_ref[h, at, 128:256] = 1.0 / total
        mixed = acc_ref[h] * t_ref[h, :, 0:128]
        for i in range(pairs):
            mixed = mixed + jnp.dot(
                p_ref[h, :, i * width : (i + 1) * width],
                pair(i, 1, h),
                preferred_element_type=jnp.float32,
            )
        result = (mixed * t_ref[h, :, 128:256]).astype(jnp.bfloat16)
        out_ref[:, h] = result.reshape(height // rows, rows, result.shape[-1])


def attend(
    general, queries, new_kv, pool_codes, pool_scales, tables, ctx_len, mig_block, mig_dest
):
    instances = lax.axis_size("inst")
    pool = pool_codes.shape[0]
    requests, steps, q_heads, head_dim = queries.shape
    heads = new_kv.shape[3]
    per_head = q_heads // heads
    spans = tables.shape[1]
    block_len = pool_codes.shape[3]
    listed = mig_dest.shape[1]
    factor = head_dim ** (-0.5)
    rows = per_head * steps
    height = requests * rows
    slots = instances * CAP
    group = 8
    f32, bf16 = jnp.float32, jnp.bfloat16
    code_rows = 2 * heads * block_len
    pool_rows = pool_codes.reshape(pool, code_rows, head_dim)
    sent_shape = (code_rows + EXTRA, head_dim)
    sent_bytes = 2 * math.prod(sent_shape)
    part_scales = jnp.transpose(pool_scales, (1, 2, 0))
    assert instances & (instances - 1) == 0 and 2 * heads < EXTRA and head_dim == 128

    def pack(sizes, copies):
        stores = sum(len(targets) for _, targets in copies)
        return pl.pallas_call(
            functools.partial(pack_kernel, (instances, listed, heads, pool, copies)),
            out_shape=[jax.ShapeDtypeStruct((size,) + sent_shape, bf16) for size in sizes],
            in_specs=[SMEM_SPEC, SMEM_SPEC, VMEM_SPEC, HBM_SPEC],
            out_specs=[HBM_SPEC] * len(sizes),
            scratch_shapes=[
                pltpu.SMEM((CAP * instances + 1,), jnp.int32),
                pltpu.VMEM((EXTRA, head_dim), f32),
                pltpu.VMEM((len(copies),) + sent_shape, bf16),
                pltpu.SemaphoreType.DMA((len(copies),)),
                pltpu.SemaphoreType.DMA((stores,)),
            ],
            compiler_params=pltpu.CompilerParams(vmem_limit_bytes=56 * MIB),
            cost_estimate=pl.CostEstimate(
                flops=0, bytes_accessed=2 * stores * sent_bytes, transcendentals=0
            ),
            name="pack_blocks",
        )(mig_dest, mig_block, part_scales, pool_rows)

    def swap(value, distance):
        return lax.ppermute(value, "inst", [(j, j ^ distance) for j in range(instances)])

    if general:
        send = pack(
            [CAP] * instances,
            [(r * instances + k, [(k, r)]) for k in range(instances) for r in range(CAP)],
        )
        arrived = [swap(send[k], k) for k in range(instances - 1, 0, -1)] + [send[0]]
        places = [(instances - 1 - k, r) for r in range(CAP) for k in range(instances)]
    else:
        any_second = CAP * instances
        (second,) = pack([1], [(any_second, [(0, 0)])])
        seconds = {0: second}
        bit = instances // 2
        while bit > 1:
            for k in list(seconds):
                seconds[k ^ bit] = swap(seconds[k], bit)
            bit //= 2
        mig_dest, second = lax.optimization_barrier((mig_dest, second))
        send = pack(
            [1, 2] + [1] * (instances - 2),
            [(k, [(k, 0)]) for k in list(range(instances))[::-1]] + [(any_second, [(1, 1)])],
        )
        firsts = [send[0]] + [swap(send[k], k) for k in range(1, instances)]
    part_scales, *send = lax.optimization_barrier((part_scales, *send))
    flat_scales = part_scales.reshape(1, -1).astype(f32)

    query_rows = (
        queries.reshape(requests, steps, heads, per_head, head_dim)
        .transpose(2, 0, 3, 1, 4)
        .reshape(heads, height, head_dim)
    )
    fresh_len = requests * steps
    fresh = new_kv.transpose(2, 3, 0, 1, 4).reshape(2, heads, fresh_len, head_dim)
    fresh = jnp.pad(fresh, ((0, 0), (0, 0), (0, -fresh_len % 128), (0, 0)))
    assert fresh.shape[2] == head_dim
    length = ctx_len[:, None]
    width = group * block_len
    chunks = pool // group
    tokens = pool * block_len

    stat = (heads, height, head_dim)
    own_parts = pl.pallas_call(
        functools.partial(
            own_kernel, (pool, heads, rows, steps, block_len, spans, factor, group)
        ),
        out_shape=[jax.ShapeDtypeStruct(stat, f32)] * 3,
        in_specs=[VMEM_SPEC, VMEM_SPEC, SMEM_SPEC, VMEM_SPEC, VMEM_SPEC, HBM_SPEC],
        out_specs=[VMEM_SPEC] * 3,
        scratch_shapes=[
            pltpu.VMEM((chunks, requests, width), f32),
            pltpu.VMEM((chunks, 2 * heads, width), f32),
            pltpu.VMEM((heads, chunks, height, width), f32),
            pltpu.VMEM((heads, height, width), bf16),
            pltpu.VMEM((2, chunks, group, heads * block_len, head_dim), bf16),
            pltpu.SemaphoreType.DMA((2, chunks)),
        ],
        compiler_params=pltpu.CompilerParams(vmem_limit_bytes=48 * MIB),
        cost_estimate=pl.CostEstimate(
            flops=4 * heads * height * tokens * head_dim,
            bytes_accessed=pool_codes.size * 2,
            transcendentals=heads * height * tokens,
        ),
        name="own_blocks",
    )(tables, length, flat_scales, query_rows, fresh, pool_rows)

    if not general:
        held = {k: second for k, second in seconds.items() if k}
        for k in held:
            seconds[k ^ 1] = swap(held[k], 1)
        arrived = [held[k] for k in held] + firsts[::-1] + [seconds[0]]
        where = {k: i for i, k in enumerate(held)}
        where[0] = len(arrived) - 1
        places = [(len(held) + instances - 1 - k, 0) for k in range(instances)]
        for k in range(instances):
            if k == 1:
                places.append((places[1][0], 1))
            elif k in where:
                places.append((where[k], 0))
            else:
                places.append((len(arrived), 0))
                arrived.append(seconds[k])

    arrival_bytes = 6 * heads * height * slots * block_len + 2 * 12 * height * head_dim * heads
    arrival_bytes += 2 * slots * sent_bytes + 4 * requests * slots * block_len
    out, moved_to, more = pl.pallas_call(
        functools.partial(
            arrival_kernel, (pool, heads, rows, block_len, spans, listed, factor), places
        ),
        out_shape=[
            jax.ShapeDtypeStruct((requests, heads, rows, head_dim), bf16),
            jax.ShapeDtypeStruct((1, listed), jnp.int32),
            jax.ShapeDtypeStruct((1,), jnp.int32),
        ],
        in_specs=[VMEM_SPEC] * (6 + len(arrived)),
        out_specs=[VMEM_SPEC, VMEM_SPEC, SMEM_SPEC],
        scratch_shapes=[
            pltpu.VMEM((requests, slots * block_len), f32),
            pltpu.VMEM((heads, height, slots * block_len), f32),
            pltpu.VMEM((heads, height, slots * block_len), bf16),
        ],
        compiler_params=pltpu.CompilerParams(vmem_limit_bytes=arrival_bytes + 8 * MIB),
        cost_estimate=pl.CostEstimate(
            flops=4 * heads * height * slots * block_len * head_dim,
            bytes_accessed=slots * sent_bytes,
            transcendentals=heads * height * slots * block_len,
        ),
        name="arrived_blocks",
    )(query_rows, tables, length, *own_parts, *arrived)
    out = out.reshape(requests, q_heads, steps, head_dim).transpose(0, 2, 1, 3)
    return out.reshape(requests, steps, q_heads * head_dim), moved_to, more


def shards(*args):
    out, moved_to, more = attend(False, *args)
    _, out = lax.while_loop(
        lambda state: state[0] > 1,
        lambda state: (jnp.int32(0), attend(True, *args)[0]),
        (more[0], out),
    )
    return out, moved_to


def solution(mesh):
    in_specs = (
        P(("groups", "inst"), None, "tp", None),
        P(("groups", "inst"), None, None, "tp", None),
        P(("groups", "inst"), None, "tp", None, None),
        P(("groups", "inst"), None, "tp"),
        P(("groups", "inst"), None),
        P(("groups", "inst")),
        P(("groups", "inst"), None),
        P(("groups", "inst"), None),
    )
    out_specs = (P(("groups", "inst"), None, "tp"), P(("groups", "inst"), None))
    return jax.shard_map(shards, mesh=mesh, in_specs=in_specs, out_specs=out_specs, check_vma=False)
```

```python
import functools
import math

import jax
import jax.numpy as jnp
from jax import lax
from jax.experimental import pallas as pl
from jax.experimental.pallas import tpu as pltpu
from jax.sharding import PartitionSpec as P

CAP = 2
EXTRA = 16
NEVER = -1e30
LOG2E = math.log2(math.e)
MIB = 1 << 20
SMEM_SPEC = pl.BlockSpec(memory_space=pltpu.SMEM)
VMEM_SPEC = pl.BlockSpec(memory_space=pltpu.VMEM)
HBM_SPEC = pl.BlockSpec(memory_space=pltpu.HBM)
NT = (((1,), (1,)), ((), ()))


def loop(count, body, init):
    if count <= 8:
        for i in range(count):
            init = body(i, init)
        return init
    return lax.fori_loop(0, count, body, init)


def pack_kernel(dims, dest_ref, block_ref, scale_ref, pool_ref, *refs):
    instances, listed, heads, pool, copies = dims
    send_refs, (index_ref, extra_ref, held_ref, in_sems, out_sems) = refs[:-5], refs[-5:]
    code_rows = held_ref.shape[1] - EXTRA
    me = lax.axis_index("inst")
    for entry in range(CAP * instances + 1):
        index_ref[entry] = 0

    def place(m, carry):
        dest = dest_ref[0, m]
        rank = loop(
            listed,
            lambda m2, n: n + jnp.where((dest_ref[0, m2] == dest) & (m2 < m), 1, 0),
            jnp.int32(0),
        )
        entry = jnp.bitwise_xor(dest, me) + jnp.where(rank > 0, instances, 0)
        index_ref[entry] = block_ref[0, m]
        index_ref[jnp.where(rank > 0, CAP * instances, entry)] = block_ref[0, m]
        return carry

    loop(listed, place, 0)
    loads, stores = [], []
    for i, (entry, _) in enumerate(copies):
        loads.append(
            pltpu.make_async_copy(
                pool_ref.at[index_ref[entry]], held_ref.at[i, pl.ds(0, code_rows)], in_sems.at[i]
            )
        )
        loads[i].start()
    lane = lax.broadcasted_iota(jnp.int32, (1, 128), 1)

    def spell(m, row):
        return jnp.where(lane == m, dest_ref[0, m].astype(jnp.float32), row)

    extra_ref[...] = jnp.zeros_like(extra_ref)
    extra_ref[2 * heads : 2 * heads + 1, :] = loop(
        listed, spell, jnp.zeros((1, 128), jnp.float32)
    )
    scales = [
        [scale_ref[part, h : h + 1, :].astype(jnp.float32) for h in range(heads)]
        for part in range(2)
    ]
    column = lax.broadcasted_iota(jnp.int32, (1, pool), 1)
    for i, (entry, _) in enumerate(copies):
        for part in range(2):
            for h in range(heads):
                one = jnp.where(column == index_ref[entry], scales[part][h], 0.0)
                row = part * heads + h
                extra_ref[row : row + 1, :] = jnp.broadcast_to(
                    jnp.sum(one, axis=1, keepdims=True), (1, 128)
                )
        held_ref[i, pl.ds(code_rows, EXTRA)] = extra_ref[...].astype(jnp.bfloat16)
    for i, (_, targets) in enumerate(copies):
        loads[i].wait()
        for output, row in targets:
            stores.append(
                pltpu.make_async_copy(
                    held_ref.at[i], send_refs[output].at[row], out_sems.at[len(stores)]
                )
            )
            stores[-1].start()
    for store in stores:
        store.wait()


def split(value, size):
    assert size & (size - 1) == 0
    return lax.shift_right_logical(value, size.bit_length() - 1), value & (size - 1)


def count_log(tables, length, ids, block_len, spans, store):
    requests, width = tables.shape[0], ids.shape[1]
    whole, rest = split(length, block_len)
    whole = jnp.broadcast_to(whole, (requests, width))
    full = jnp.zeros((requests, width), jnp.float32)
    part = jnp.zeros((requests, width), jnp.float32)
    for e in range(spans):
        hit = jnp.broadcast_to(tables[:, e : e + 1], (requests, width)) == ids
        full = full + jnp.where(hit & (whole > e), 1.0, 0.0)
        part = part + jnp.where(hit & (whole == e), 1.0, 0.0)

    def log2(count):
        return jnp.where(count > 0, jnp.log(jnp.maximum(count, 1.0)) * LOG2E, NEVER)

    beyond, within = log2(full), log2(full + part)
    shape = (requests, block_len)
    inside = lax.broadcasted_iota(jnp.int32, shape, 1) < jnp.broadcast_to(rest, shape)
    if width % 16:
        for b in range(width):
            store(
                b,
                jnp.where(
                    inside,
                    jnp.broadcast_to(within[:, b : b + 1], shape),
                    jnp.broadcast_to(beyond[:, b : b + 1], shape),
                ),
            )
        return
    both = jnp.concatenate([within, beyond], axis=0)
    high = both.astype(jnp.bfloat16)
    low = (both - high.astype(jnp.float32)).astype(jnp.bfloat16)
    terms = jnp.concatenate([high, low], axis=0)
    row = lax.broadcasted_iota(jnp.int32, (width, block_len), 0)
    for b in range(0, width, 2):
        spots = jnp.concatenate(
            [jnp.where(row == b + i, 1.0, 0.0).astype(jnp.bfloat16) for i in range(2)], axis=1
        )
        spread_out = jnp.dot(terms, spots, preferred_element_type=jnp.float32)
        value = spread_out[: 2 * requests] + spread_out[2 * requests :]
        for i in range(2):
            at = slice(i * block_len, (i + 1) * block_len)
            store(b + i, jnp.where(inside, value[:requests, at], value[requests:, at]))


def score_tiles(query, keys, log_ref, scale_row, rows, store):
    height, wide = min(256, query.shape[0]), min(256, keys.shape[0])
    for top in range(0, query.shape[0], height):
        for left in range(0, keys.shape[0], wide):
            part = lax.dot_general(
                query[top : top + height],
                keys[left : left + wide],
                NT,
                preferred_element_type=jnp.float32,
            )
            scale = scale_row[:, left : left + wide]
            for r in range(height // rows):
                request = top // rows + r
                store(
                    request * rows,
                    left,
                    part[r * rows : (r + 1) * rows] * scale
                    + log_ref[request : request + 1, left : left + wide],
                )


def lane_fold(value, op):
    parts = [value[:, i : i + 128] for i in range(0, value.shape[1], 128)]
    while len(parts) > 1:
        parts = [
            op(parts[i], parts[i + 1]) if i + 1 < len(parts) else parts[i]
            for i in range(0, len(parts), 2)
        ]
    return parts[0]


def spread(column, width):
    return jnp.concatenate([column] * (width // 128), axis=1)


def own_kernel(
    dims,
    tables_ref, length_ref, scale_ref, q_ref, fresh_ref, pool_ref,
    acc_ref, top_ref, total_ref,
    log_ref, row_ref, t_ref, p_ref, codes_ref, sems,
):
    head, pool, heads, rows, steps, block_len, spans, factor, group = dims
    chunks = pool // group
    height, head_dim = q_ref.shape[1:]
    width = group * block_len

    def load(part, chunk):
        return pltpu.make_async_copy(
            pool_ref.at[
                pl.ds(chunk * group, group), pl.ds((part * heads + head) * block_len, block_len)
            ],
            codes_ref.at[part, chunk],
            sems.at[part, chunk],
        )

    for part in range(2):
        for chunk in range(chunks):
            load(part, chunk).start()

    ids = lax.broadcasted_iota(jnp.int32, (1, pool), 1)

    def store_log(b, value):
        lane = (b % group) * block_len
        log_ref[b // group, :, lane : lane + block_len] = value

    count_log(tables_ref[...], length_ref[...], ids, block_len, spans, store_log)
    for b in range(pool):
        lane = (b % group) * block_len
        row_ref[b // group, :, lane : lane + block_len] = jnp.broadcast_to(
            scale_ref[:, b : b + 1], (2 * heads, block_len)
        )
    shape = (height, fresh_ref.shape[2])
    row = lax.broadcasted_iota(jnp.int32, shape, 0)
    col = lax.broadcasted_iota(jnp.int32, shape, 1)
    (request, row_step), (owner, step) = split(row, rows), split(col, steps)
    seen = (request == owner) & (split(row_step, steps)[1] >= step)
    new_score = lax.dot_general(
        q_ref[head], fresh_ref[0, head], NT, preferred_element_type=jnp.float32
    )
    new_score = jnp.where(seen, new_score * (factor * LOG2E), -jnp.inf)
    acc_ref[...] = new_score
    top_ref[...] = lane_fold(new_score, jnp.maximum)

    def score(chunk, carry):
        load(0, chunk).wait()

        def store(row, lane, value):
            t_ref[chunk, row : row + rows, lane : lane + value.shape[1]] = value

        score_tiles(
            q_ref[head],
            codes_ref[0, chunk].reshape(width, head_dim),
            log_ref.at[chunk],
            row_ref[chunk, head : head + 1, :] * (factor * LOG2E),
            rows,
            store,
        )
        for row in range(0, height, rows):
            at = pl.ds(row, rows)
            top_ref[at] = jnp.maximum(top_ref[at], lane_fold(t_ref[chunk, at], jnp.maximum))
        return carry

    lax.fori_loop(0, chunks, score, 0)

    top = jnp.broadcast_to(jnp.max(top_ref[...], axis=1, keepdims=True), (height, 128))
    top_ref[...] = top
    weight = jnp.exp2(acc_ref[...] - spread(top, acc_ref.shape[1]))
    total_ref[...] = lane_fold(weight, jnp.add)
    acc_ref[...] = jnp.dot(
        weight.astype(jnp.bfloat16), fresh_ref[1, head], preferred_element_type=jnp.float32
    )

    def apply(chunk, carry):
        load(1, chunk).wait()
        scale = row_ref[chunk, heads + head : heads + head + 1, :]
        for row in range(0, height, rows):
            at = pl.ds(row, rows)
            weight = jnp.exp2(t_ref[chunk, at] - spread(top_ref[at], width))
            total_ref[at] += lane_fold(weight, jnp.add)
            p_ref[at] = (weight * scale).astype(jnp.bfloat16)
        acc_ref[...] += jnp.dot(
            p_ref[...],
            codes_ref[1, chunk].reshape(width, head_dim),
            preferred_element_type=jnp.float32,
        )
        return carry

    lax.fori_loop(0, chunks, apply, 0)


def arrival_ids(me, pool, lists, listed):
    instances = len(lists)
    lane = lax.broadcasted_iota(jnp.int32, (1, 128), 1)
    counts = [
        jnp.sum(
            jnp.where((row == me.astype(jnp.float32)) & (lane < listed), 1.0, 0.0),
            axis=1,
            keepdims=True,
        )
        for row in lists
    ]
    slot = lax.broadcasted_iota(jnp.int32, (1, instances * CAP), 1)
    ids = jnp.full(slot.shape, -1.0)
    for k in range(instances):
        first = jnp.full((1, 1), float(pool))
        for j in range(instances):
            lower = jnp.bitwise_xor(me, j) < jnp.bitwise_xor(me, k)
            first = first + jnp.where(lower, counts[j], 0.0)
        for r in range(CAP):
            name = jnp.where(counts[k] > r, first + r, -1.0)
            ids = jnp.where(slot == r * instances + k, jnp.broadcast_to(name, slot.shape), ids)
    moved = jnp.full((1, 128), float(pool))
    for j in range(instances):
        for m in range(listed):
            same = jnp.broadcast_to(lists[j][:, m : m + 1], (1, 128)) == lists[0]
            ahead = jnp.bitwise_xor(me, j) < me if j else lane > m
            moved = moved + jnp.where(same & ahead, 1.0, 0.0)
    more = jnp.zeros((1, 128))
    for row in lists:
        again = jnp.zeros((1, 128))
        for m in range(listed):
            same = jnp.broadcast_to(row[:, m : m + 1], (1, 128)) == row
            again = again + jnp.where(same & (lane > m) & (lane < listed), 1.0, 0.0)
        more = jnp.maximum(more, jnp.sum(again, axis=1, keepdims=True))
    return ids.astype(jnp.int32), moved[:, :listed].astype(jnp.int32), more


def arrival_kernel(dims, places, q_ref, tables_ref, length_ref, *refs):
    pool, heads, rows, block_len, spans, listed, factor = dims
    own_refs, code_refs = refs[: 3 * heads], refs[3 * heads : -6]
    out_ref, moved_ref, more_ref, log_ref, t_ref, p_ref = refs[-6:]
    height = q_ref.shape[1]
    width = 2 * block_len
    extra = 2 * heads * block_len
    slots = [(code_refs[array], row) for array, row in places]
    pairs = len(slots) // 2

    def pair(i, part, h):
        at = pl.ds((part * heads + h) * block_len, block_len)
        return jnp.concatenate([ref[r, at] for ref, r in slots[2 * i : 2 * i + 2]], axis=0)

    lists, scale_rows = [], []
    for ref, r in slots:
        values = ref[r, pl.ds(extra, EXTRA)].astype(jnp.float32)
        scale_rows.append(values)
        if len(lists) < len(slots) // CAP:
            lists.append(values[2 * heads : 2 * heads + 1])

    def scale_row(row):
        return jnp.concatenate([values[row : row + 1] for values in scale_rows], axis=1)

    ids, moved_ref[...], more = arrival_ids(lax.axis_index("inst"), pool, lists, listed)
    more_ref[0] = jnp.max(more).astype(jnp.int32)

    def store_log(b, value):
        log_ref[:, b * block_len : (b + 1) * block_len] = value

    count_log(tables_ref[...], length_ref[...], ids, block_len, spans, store_log)
    for h in range(heads):
        key_scale = scale_row(h) * (factor * LOG2E)
        for i in range(pairs):
            left = i * width

            def store(row, lane, value, h=h, left=left):
                t_ref[h, row : row + rows, left + lane : left + lane + value.shape[1]] = value

            score_tiles(
                q_ref[h],
                pair(i, 0, h),
                log_ref.at[:, left : left + width],
                key_scale[:, left : left + width],
                rows,
                store,
            )
    for h in range(heads):
        acc_ref, top_ref, total_ref = own_refs[3 * h : 3 * h + 3]
        scale = scale_row(heads + h)
        for row in range(0, height, rows):
            at = pl.ds(row, rows)
            score = t_ref[h, at]
            own_top = top_ref[at]
            top = jnp.maximum(
                own_top, jnp.max(lane_fold(score, jnp.maximum), axis=1, keepdims=True)
            )
            weight = jnp.exp2(score - spread(top, score.shape[1]))
            keep = jnp.exp2(own_top - top)
            total = jnp.sum(
                total_ref[at] * keep + lane_fold(weight, jnp.add), axis=1, keepdims=True
            )
            p_ref[h, at] = (weight * scale).astype(jnp.bfloat16)
            t_ref[h, at, 0:128] = keep
            t_ref[h, at, 128:256] = jnp.broadcast_to(1.0 / total, keep.shape)
        mixed = acc_ref[...] * t_ref[h, :, 0:128]
        for i in range(pairs):
            mixed = mixed + jnp.dot(
                p_ref[h, :, i * width : (i + 1) * width],
                pair(i, 1, h),
                preferred_element_type=jnp.float32,
            )
        result = (mixed * t_ref[h, :, 128:256]).astype(jnp.bfloat16)
        out_ref[:, h] = result.reshape(height // rows, rows, result.shape[-1])


def attend(
    general, queries, new_kv, pool_codes, pool_scales, tables, ctx_len, mig_block, mig_dest
):
    instances = lax.axis_size("inst")
    pool = pool_codes.shape[0]
    requests, steps, q_heads, head_dim = queries.shape
    heads = new_kv.shape[3]
    per_head = q_heads // heads
    spans = tables.shape[1]
    block_len = pool_codes.shape[3]
    listed = mig_dest.shape[1]
    factor = head_dim ** (-0.5)
    rows = per_head * steps
    height = requests * rows
    slots = instances * CAP
    group = 8
    f32, bf16 = jnp.float32, jnp.bfloat16
    code_rows = 2 * heads * block_len
    pool_rows = pool_codes.reshape(pool, code_rows, head_dim)
    sent_shape = (code_rows + EXTRA, head_dim)
    sent_bytes = 2 * math.prod(sent_shape)
    part_scales = jnp.transpose(pool_scales, (1, 2, 0))
    assert instances & (instances - 1) == 0 and 2 * heads < EXTRA and head_dim == 128

    def pack(sizes, copies):
        stores = sum(len(targets) for _, targets in copies)
        return pl.pallas_call(
            functools.partial(pack_kernel, (instances, listed, heads, pool, copies)),
            out_shape=[jax.ShapeDtypeStruct((size,) + sent_shape, bf16) for size in sizes],
            in_specs=[SMEM_SPEC, SMEM_SPEC, VMEM_SPEC, HBM_SPEC],
            out_specs=[HBM_SPEC] * len(sizes),
            scratch_shapes=[
                pltpu.SMEM((CAP * instances + 1,), jnp.int32),
                pltpu.VMEM((EXTRA, head_dim), f32),
                pltpu.VMEM((len(copies),) + sent_shape, bf16),
                pltpu.SemaphoreType.DMA((len(copies),)),
                pltpu.SemaphoreType.DMA((stores,)),
            ],
            compiler_params=pltpu.CompilerParams(vmem_limit_bytes=56 * MIB),
            cost_estimate=pl.CostEstimate(
                flops=0, bytes_accessed=2 * stores * sent_bytes, transcendentals=0
            ),
            name="pack_blocks",
        )(mig_dest, mig_block, part_scales, pool_rows)

    def swap(value, distance):
        return lax.ppermute(value, "inst", [(j, j ^ distance) for j in range(instances)])

    if general:
        send = pack(
            [CAP] * instances,
            [(r * instances + k, [(k, r)]) for k in range(instances) for r in range(CAP)],
        )
        arrived = [swap(send[k], k) for k in range(instances - 1, 0, -1)] + [send[0]]
        places = [(instances - 1 - k, r) for r in range(CAP) for k in range(instances)]
    else:
        any_second = CAP * instances
        (second,) = pack([1], [(any_second, [(0, 0)])])
        seconds = {0: second}
        bit = instances // 2
        while bit > 1:
            for k in list(seconds):
                seconds[k ^ bit] = swap(seconds[k], bit)
            bit //= 2
        mig_dest, second = lax.optimization_barrier((mig_dest, second))
        send = pack(
            [1, 2] + [1] * (instances - 2),
            [(k, [(k, 0)]) for k in list(range(instances))[::-1]] + [(any_second, [(1, 1)])],
        )
        firsts = [send[0]] + [swap(send[k], k) for k in range(1, instances)]
    part_scales, *send = lax.optimization_barrier((part_scales, *send))
    flat_scales = part_scales.reshape(2 * heads, pool).astype(f32)

    query_rows = (
        queries.reshape(requests, steps, heads, per_head, head_dim)
        .transpose(2, 0, 3, 1, 4)
        .reshape(heads, height, head_dim)
    )
    fresh_len = requests * steps
    fresh = new_kv.transpose(2, 3, 0, 1, 4).reshape(2, heads, fresh_len, head_dim)
    fresh = jnp.pad(fresh, ((0, 0), (0, 0), (0, -fresh_len % 128), (0, 0)))
    assert fresh.shape[2] == head_dim
    length = ctx_len[:, None]
    width = group * block_len
    chunks = pool // group
    tokens = pool * block_len

    def own(head, query_rows):
        return pl.pallas_call(
            functools.partial(
                own_kernel, (head, pool, heads, rows, steps, block_len, spans, factor, group)
            ),
            out_shape=[jax.ShapeDtypeStruct((height, head_dim), f32)] * 3,
            in_specs=[VMEM_SPEC] * 5 + [HBM_SPEC],
            out_specs=[VMEM_SPEC] * 3,
            scratch_shapes=[
                pltpu.VMEM((chunks, requests, width), f32),
                pltpu.VMEM((chunks, 2 * heads, width), f32),
                pltpu.VMEM((chunks, height, width), f32),
                pltpu.VMEM((height, width), bf16),
                pltpu.VMEM((2, chunks, group, block_len, head_dim), bf16),
                pltpu.SemaphoreType.DMA((2, chunks)),
            ],
            compiler_params=pltpu.CompilerParams(vmem_limit_bytes=32 * MIB),
            cost_estimate=pl.CostEstimate(
                flops=4 * height * tokens * head_dim,
                bytes_accessed=pool_codes.size * 2 // heads,
                transcendentals=height * tokens,
            ),
            name="own_blocks",
        )(tables, length, flat_scales, query_rows, fresh, pool_rows)

    own_parts = own(0, query_rows)
    if not general:
        seconds, own_parts = lax.optimization_barrier((seconds, own_parts))
    for head in range(1, heads):
        own_parts = own_parts + own(head, query_rows)

    if not general:
        held = {k: second for k, second in seconds.items() if k}
        for k in held:
            seconds[k ^ 1] = swap(held[k], 1)
        arrived = [held[k] for k in held] + firsts[::-1] + [seconds[0]]
        where = {k: i for i, k in enumerate(held)}
        where[0] = len(arrived) - 1
        places = [(len(held) + instances - 1 - k, 0) for k in range(instances)]
        for k in range(instances):
            if k == 1:
                places.append((places[1][0], 1))
            elif k in where:
                places.append((where[k], 0))
            else:
                places.append((len(arrived), 0))
                arrived.append(seconds[k])

    arrival_bytes = 6 * heads * height * slots * block_len + 2 * 12 * height * head_dim * heads
    arrival_bytes += 2 * slots * sent_bytes + 4 * requests * slots * block_len
    out, moved_to, more = pl.pallas_call(
        functools.partial(
            arrival_kernel, (pool, heads, rows, block_len, spans, listed, factor), places
        ),
        out_shape=[
            jax.ShapeDtypeStruct((requests, heads, rows, head_dim), bf16),
            jax.ShapeDtypeStruct((1, listed), jnp.int32),
            jax.ShapeDtypeStruct((1,), jnp.int32),
        ],
        in_specs=[VMEM_SPEC] * (3 + 3 * heads + len(arrived)),
        out_specs=[VMEM_SPEC, VMEM_SPEC, SMEM_SPEC],
        scratch_shapes=[
            pltpu.VMEM((requests, slots * block_len), f32),
            pltpu.VMEM((heads, height, slots * block_len), f32),
            pltpu.VMEM((heads, height, slots * block_len), bf16),
        ],
        compiler_params=pltpu.CompilerParams(vmem_limit_bytes=arrival_bytes + 8 * MIB),
        cost_estimate=pl.CostEstimate(
            flops=4 * heads * height * slots * block_len * head_dim,
            bytes_accessed=slots * sent_bytes,
            transcendentals=heads * height * slots * block_len,
        ),
        name="arrived_blocks",
    )(query_rows, tables, length, *own_parts, *arrived)
    out = out.reshape(requests, q_heads, steps, head_dim).transpose(0, 2, 1, 3)
    return out.reshape(requests, steps, q_heads * head_dim), moved_to, more


def shards(*args):
    out, moved_to, more = attend(False, *args)
    _, out = lax.while_loop(
        lambda state: state[0] > 1,
        lambda state: (jnp.int32(0), attend(True, *args)[0]),
        (more[0], out),
    )
    return out, moved_to


def solution(mesh):
    in_specs = (
        P(("groups", "inst"), None, "tp", None),
        P(("groups", "inst"), None, None, "tp", None),
        P(("groups", "inst"), None, "tp", None, None),
        P(("groups", "inst"), None, "tp"),
        P(("groups", "inst"), None),
        P(("groups", "inst")),
        P(("groups", "inst"), None),
        P(("groups", "inst"), None),
    )
    out_specs = (P(("groups", "inst"), None, "tp"), P(("groups", "inst"), None))
    return jax.shard_map(shards, mesh=mesh, in_specs=in_specs, out_specs=out_specs, check_vma=False)
```

```python
import functools
import math

import jax
import jax.numpy as jnp
from jax import lax
from jax.experimental import pallas as pl
from jax.experimental.pallas import tpu as pltpu
from jax.sharding import PartitionSpec as P

CAP = 2
EXTRA = 16
NEVER = -1e30
LOG2E = math.log2(math.e)
MIB = 1 << 20
SMEM_SPEC = pl.BlockSpec(memory_space=pltpu.SMEM)
VMEM_SPEC = pl.BlockSpec(memory_space=pltpu.VMEM)
HBM_SPEC = pl.BlockSpec(memory_space=pltpu.HBM)
NT = (((1,), (1,)), ((), ()))


def loop(count, body, init):
    if count <= 8:
        for i in range(count):
            init = body(i, init)
        return init
    return lax.fori_loop(0, count, body, init)


def pack_kernel(dims, dest_ref, block_ref, scale_ref, pool_ref, *refs):
    instances, listed, heads, pool, copies = dims
    send_refs, (index_ref, extra_ref, held_ref, in_sems, out_sems) = refs[:-5], refs[-5:]
    code_rows = held_ref.shape[1] - EXTRA
    me = lax.axis_index("inst")
    for entry in range(CAP * instances + 1):
        index_ref[entry] = 0

    def place(m, carry):
        dest = dest_ref[0, m]
        rank = loop(
            listed,
            lambda m2, n: n + jnp.where((dest_ref[0, m2] == dest) & (m2 < m), 1, 0),
            jnp.int32(0),
        )
        entry = jnp.bitwise_xor(dest, me) + jnp.where(rank > 0, instances, 0)
        index_ref[entry] = block_ref[0, m]
        index_ref[jnp.where(rank > 0, CAP * instances, entry)] = block_ref[0, m]
        return carry

    loop(listed, place, 0)
    loads, stores = [], []
    for i, (entry, _) in enumerate(copies):
        loads.append(
            pltpu.make_async_copy(
                pool_ref.at[index_ref[entry]], held_ref.at[i, pl.ds(0, code_rows)], in_sems.at[i]
            )
        )
        loads[i].start()
    lane = lax.broadcasted_iota(jnp.int32, (1, 128), 1)

    def spell(m, row):
        return jnp.where(lane == m, dest_ref[0, m].astype(jnp.float32), row)

    extra_ref[...] = jnp.zeros_like(extra_ref)
    extra_ref[2 * heads : 2 * heads + 1, :] = loop(
        listed, spell, jnp.zeros((1, 128), jnp.float32)
    )
    scales = [
        [scale_ref[part, h : h + 1, :].astype(jnp.float32) for h in range(heads)]
        for part in range(2)
    ]
    column = lax.broadcasted_iota(jnp.int32, (1, pool), 1)
    for i, (entry, _) in enumerate(copies):
        for part in range(2):
            for h in range(heads):
                one = jnp.where(column == index_ref[entry], scales[part][h], 0.0)
                row = part * heads + h
                extra_ref[row : row + 1, :] = jnp.broadcast_to(
                    jnp.sum(one, axis=1, keepdims=True), (1, 128)
                )
        held_ref[i, pl.ds(code_rows, EXTRA)] = extra_ref[...].astype(jnp.bfloat16)
    for i, (_, targets) in enumerate(copies):
        loads[i].wait()
        for output, row in targets:
            stores.append(
                pltpu.make_async_copy(
                    held_ref.at[i], send_refs[output].at[row], out_sems.at[len(stores)]
                )
            )
            stores[-1].start()
    for store in stores:
        store.wait()


def split(value, size):
    assert size & (size - 1) == 0
    return lax.shift_right_logical(value, size.bit_length() - 1), value & (size - 1)


def count_log(tables, length, ids, block_len, spans, store):
    requests, width = tables.shape[0], ids.shape[1]
    whole, rest = split(length, block_len)
    whole = jnp.broadcast_to(whole, (requests, width))
    full = jnp.zeros((requests, width), jnp.float32)
    part = jnp.zeros((requests, width), jnp.float32)
    for e in range(spans):
        hit = jnp.broadcast_to(tables[:, e : e + 1], (requests, width)) == ids
        full = full + jnp.where(hit & (whole > e), 1.0, 0.0)
        part = part + jnp.where(hit & (whole == e), 1.0, 0.0)

    def log2(count):
        return jnp.where(count > 0, jnp.log(jnp.maximum(count, 1.0)) * LOG2E, NEVER)

    beyond, within = log2(full), log2(full + part)
    shape = (requests, block_len)
    inside = lax.broadcasted_iota(jnp.int32, shape, 1) < jnp.broadcast_to(rest, shape)
    if width % 16:
        for b in range(width):
            store(
                b,
                jnp.where(
                    inside,
                    jnp.broadcast_to(within[:, b : b + 1], shape),
                    jnp.broadcast_to(beyond[:, b : b + 1], shape),
                ),
            )
        return
    both = jnp.concatenate([within, beyond], axis=0)
    high = both.astype(jnp.bfloat16)
    low = (both - high.astype(jnp.float32)).astype(jnp.bfloat16)
    terms = jnp.concatenate([high, low], axis=0)
    row = lax.broadcasted_iota(jnp.int32, (width, block_len), 0)
    for b in range(0, width, 2):
        spots = jnp.concatenate(
            [jnp.where(row == b + i, 1.0, 0.0).astype(jnp.bfloat16) for i in range(2)], axis=1
        )
        spread_out = jnp.dot(terms, spots, preferred_element_type=jnp.float32)
        value = spread_out[: 2 * requests] + spread_out[2 * requests :]
        for i in range(2):
            at = slice(i * block_len, (i + 1) * block_len)
            store(b + i, jnp.where(inside, value[:requests, at], value[requests:, at]))


def score_tiles(query, keys, log_ref, scale_row, rows, store):
    height, wide = min(256, query.shape[0]), min(256, keys.shape[0])
    for top in range(0, query.shape[0], height):
        for left in range(0, keys.shape[0], wide):
            part = lax.dot_general(
                query[top : top + height],
                keys[left : left + wide],
                NT,
                preferred_element_type=jnp.float32,
            )
            scale = scale_row[:, left : left + wide]
            for r in range(height // rows):
                request = top // rows + r
                store(
                    request * rows,
                    left,
                    part[r * rows : (r + 1) * rows] * scale
                    + log_ref[request : request + 1, left : left + wide],
                )


def lane_fold(value, op):
    parts = [value[:, i : i + 128] for i in range(0, value.shape[1], 128)]
    while len(parts) > 1:
        parts = [
            op(parts[i], parts[i + 1]) if i + 1 < len(parts) else parts[i]
            for i in range(0, len(parts), 2)
        ]
    return parts[0]


def spread(column, width):
    return jnp.concatenate([column] * (width // 128), axis=1)


def own_kernel(
    dims,
    tables_ref, length_ref, scale_ref, q_ref, fresh_ref, pool_ref,
    acc_ref, top_ref, total_ref,
    log_ref, row_ref, t_ref, p_ref, codes_ref, sems,
):
    pool, heads, rows, steps, block_len, spans, factor, group = dims
    chunks = pool // group
    height, head_dim = q_ref.shape[1:]
    width = group * block_len
    part_rows = heads * block_len

    def load(part, chunk):
        return pltpu.make_async_copy(
            pool_ref.at[pl.ds(chunk * group, group), pl.ds(part * part_rows, part_rows)],
            codes_ref.at[part, chunk],
            sems.at[part, chunk],
        )

    def codes(part, chunk, h):
        at = pl.ds(h * block_len, block_len)
        return codes_ref[part, chunk, :, at].reshape(width, head_dim)

    for part in range(2):
        for chunk in range(chunks):
            load(part, chunk).start()

    ids = lax.broadcasted_iota(jnp.int32, (1, pool), 1)

    def store_log(b, value):
        lane = (b % group) * block_len
        log_ref[b // group, :, lane : lane + block_len] = value

    count_log(tables_ref[...], length_ref[...], ids, block_len, spans, store_log)
    for b in range(pool):
        lane = (b % group) * block_len
        row_ref[b // group, :, lane : lane + block_len] = jnp.broadcast_to(
            scale_ref[:, b : b + 1], (2 * heads, block_len)
        )
    shape = (height, fresh_ref.shape[2])
    row = lax.broadcasted_iota(jnp.int32, shape, 0)
    col = lax.broadcasted_iota(jnp.int32, shape, 1)
    (request, row_step), (owner, step) = split(row, rows), split(col, steps)
    seen = (request == owner) & (split(row_step, steps)[1] >= step)
    for h in range(heads):
        new_score = lax.dot_general(
            q_ref[h], fresh_ref[0, h], NT, preferred_element_type=jnp.float32
        )
        new_score = jnp.where(seen, new_score * (factor * LOG2E), -jnp.inf)
        acc_ref[h] = new_score
        top_ref[h] = lane_fold(new_score, jnp.maximum)

    def score(chunk, carry):
        load(0, chunk).wait()
        for h in range(heads):

            def store(row, lane, value, h=h):
                t_ref[h, chunk, row : row + rows, lane : lane + value.shape[1]] = value

            score_tiles(
                q_ref[h],
                codes(0, chunk, h),
                log_ref.at[chunk],
                row_ref[chunk, h : h + 1, :] * (factor * LOG2E),
                rows,
                store,
            )
            for row in range(0, height, rows):
                at = pl.ds(row, rows)
                top_ref[h, at] = jnp.maximum(
                    top_ref[h, at], lane_fold(t_ref[h, chunk, at], jnp.maximum)
                )
        return carry

    lax.fori_loop(0, chunks, score, 0)

    for h in range(heads):
        top = jnp.broadcast_to(jnp.max(top_ref[h], axis=1, keepdims=True), (height, 128))
        top_ref[h] = top
        weight = jnp.exp2(acc_ref[h] - spread(top, acc_ref.shape[2]))
        total_ref[h] = lane_fold(weight, jnp.add)
        acc_ref[h] = jnp.dot(
            weight.astype(jnp.bfloat16), fresh_ref[1, h], preferred_element_type=jnp.float32
        )

    def apply(chunk, carry):
        load(1, chunk).wait()
        for h in range(heads):
            scale = row_ref[chunk, heads + h : heads + h + 1, :]
            for row in range(0, height, rows):
                at = pl.ds(row, rows)
                weight = jnp.exp2(t_ref[h, chunk, at] - spread(top_ref[h, at], width))
                total_ref[h, at] += lane_fold(weight, jnp.add)
                p_ref[h, at] = (weight * scale).astype(jnp.bfloat16)
            acc_ref[h] += jnp.dot(
                p_ref[h], codes(1, chunk, h), preferred_element_type=jnp.float32
            )
        return carry

    lax.fori_loop(0, chunks, apply, 0)


def arrival_ids(me, pool, lists, listed):
    instances = len(lists)
    lane = lax.broadcasted_iota(jnp.int32, (1, 128), 1)
    counts = [
        jnp.sum(
            jnp.where((row == me.astype(jnp.float32)) & (lane < listed), 1.0, 0.0),
            axis=1,
            keepdims=True,
        )
        for row in lists
    ]
    slot = lax.broadcasted_iota(jnp.int32, (1, instances * CAP), 1)
    ids = jnp.full(slot.shape, -1.0)
    for k in range(instances):
        first = jnp.full((1, 1), float(pool))
        for j in range(instances):
            lower = jnp.bitwise_xor(me, j) < jnp.bitwise_xor(me, k)
            first = first + jnp.where(lower, counts[j], 0.0)
        for r in range(CAP):
            name = jnp.where(counts[k] > r, first + r, -1.0)
            ids = jnp.where(slot == r * instances + k, jnp.broadcast_to(name, slot.shape), ids)
    moved = jnp.full((1, 128), float(pool))
    for j in range(instances):
        for m in range(listed):
            same = jnp.broadcast_to(lists[j][:, m : m + 1], (1, 128)) == lists[0]
            ahead = jnp.bitwise_xor(me, j) < me if j else lane > m
            moved = moved + jnp.where(same & ahead, 1.0, 0.0)
    more = jnp.zeros((1, 128))
    for row in lists:
        again = jnp.zeros((1, 128))
        for m in range(listed):
            same = jnp.broadcast_to(row[:, m : m + 1], (1, 128)) == row
            again = again + jnp.where(same & (lane > m) & (lane < listed), 1.0, 0.0)
        more = jnp.maximum(more, jnp.sum(again, axis=1, keepdims=True))
    return ids.astype(jnp.int32), moved[:, :listed].astype(jnp.int32), more


def arrival_kernel(dims, places, q_ref, tables_ref, length_ref, *refs):
    pool, heads, rows, block_len, spans, listed, factor = dims
    acc_ref, top_ref, total_ref = refs[:3]
    code_refs = refs[3:-6]
    out_ref, moved_ref, more_ref, log_ref, t_ref, p_ref = refs[-6:]
    height = q_ref.shape[1]
    width = 2 * block_len
    extra = 2 * heads * block_len
    slots = [(code_refs[array], row) for array, row in places]
    pairs = len(slots) // 2

    def pair(i, part, h):
        at = pl.ds((part * heads + h) * block_len, block_len)
        return jnp.concatenate([ref[r, at] for ref, r in slots[2 * i : 2 * i + 2]], axis=0)

    lists, scale_rows = [], []
    for ref, r in slots:
        values = ref[r, pl.ds(extra, EXTRA)].astype(jnp.float32)
        scale_rows.append(values)
        if len(lists) < len(slots) // CAP:
            lists.append(values[2 * heads : 2 * heads + 1])

    def scale_row(row):
        return jnp.concatenate([values[row : row + 1] for values in scale_rows], axis=1)

    ids, moved_ref[...], more = arrival_ids(lax.axis_index("inst"), pool, lists, listed)
    more_ref[0] = jnp.max(more).astype(jnp.int32)

    def store_log(b, value):
        log_ref[:, b * block_len : (b + 1) * block_len] = value

    count_log(tables_ref[...], length_ref[...], ids, block_len, spans, store_log)
    for h in range(heads):
        key_scale = scale_row(h) * (factor * LOG2E)
        for i in range(pairs):
            left = i * width

            def store(row, lane, value, h=h, left=left):
                t_ref[h, row : row + rows, left + lane : left + lane + value.shape[1]] = value

            score_tiles(
                q_ref[h],
                pair(i, 0, h),
                log_ref.at[:, left : left + width],
                key_scale[:, left : left + width],
                rows,
                store,
            )
    for h in range(heads):
        scale = scale_row(heads + h)
        for row in range(0, height, rows):
            at = pl.ds(row, rows)
            score = t_ref[h, at]
            own_top = top_ref[h, at]
            top = jnp.maximum(
                own_top, jnp.max(lane_fold(score, jnp.maximum), axis=1, keepdims=True)
            )
            weight = jnp.exp2(score - spread(top, score.shape[1]))
            keep = jnp.exp2(own_top - top)
            total = jnp.sum(
                total_ref[h, at] * keep + lane_fold(weight, jnp.add), axis=1, keepdims=True
            )
            p_ref[h, at] = (weight * scale).astype(jnp.bfloat16)
            t_ref[h, at, 0:128] = keep
            t_ref[h, at, 128:256] = jnp.broadcast_to(1.0 / total, keep.shape)
        mixed = acc_ref[h] * t_ref[h, :, 0:128]
        for i in range(pairs):
            mixed = mixed + jnp.dot(
                p_ref[h, :, i * width : (i + 1) * width],
                pair(i, 1, h),
                preferred_element_type=jnp.float32,
            )
        result = (mixed * t_ref[h, :, 128:256]).astype(jnp.bfloat16)
        out_ref[:, h] = result.reshape(height // rows, rows, result.shape[-1])


def attend(
    general, queries, new_kv, pool_codes, pool_scales, tables, ctx_len, mig_block, mig_dest
):
    instances = lax.axis_size("inst")
    pool = pool_codes.shape[0]
    requests, steps, q_heads, head_dim = queries.shape
    heads = new_kv.shape[3]
    per_head = q_heads // heads
    spans = tables.shape[1]
    block_len = pool_codes.shape[3]
    listed = mig_dest.shape[1]
    factor = head_dim ** (-0.5)
    rows = per_head * steps
    height = requests * rows
    slots = instances * CAP
    group = 16
    f32, bf16 = jnp.float32, jnp.bfloat16
    code_rows = 2 * heads * block_len
    pool_rows = pool_codes.reshape(pool, code_rows, head_dim)
    sent_shape = (code_rows + EXTRA, head_dim)
    sent_bytes = 2 * math.prod(sent_shape)
    part_scales = jnp.transpose(pool_scales, (1, 2, 0))
    assert instances & (instances - 1) == 0 and 2 * heads < EXTRA and head_dim == 128

    def pack(sizes, copies):
        stores = sum(len(targets) for _, targets in copies)
        return pl.pallas_call(
            functools.partial(pack_kernel, (instances, listed, heads, pool, copies)),
            out_shape=[jax.ShapeDtypeStruct((size,) + sent_shape, bf16) for size in sizes],
            in_specs=[SMEM_SPEC, SMEM_SPEC, VMEM_SPEC, HBM_SPEC],
            out_specs=[HBM_SPEC] * len(sizes),
            scratch_shapes=[
                pltpu.SMEM((CAP * instances + 1,), jnp.int32),
                pltpu.VMEM((EXTRA, head_dim), f32),
                pltpu.VMEM((len(copies),) + sent_shape, bf16),
                pltpu.SemaphoreType.DMA((len(copies),)),
                pltpu.SemaphoreType.DMA((stores,)),
            ],
            compiler_params=pltpu.CompilerParams(vmem_limit_bytes=56 * MIB),
            cost_estimate=pl.CostEstimate(
                flops=0, bytes_accessed=2 * stores * sent_bytes, transcendentals=0
            ),
            name="pack_blocks",
        )(mig_dest, mig_block, part_scales, pool_rows)

    def swap(value, distance):
        return lax.ppermute(value, "inst", [(j, j ^ distance) for j in range(instances)])

    straight = [k for k in range(1, instances) if k & (k - 1) == 0]
    any_second = CAP * instances
    if general:
        sizes = [CAP] * instances
        copies = [(r * instances + k, [(k, r)]) for k in range(instances) for r in range(CAP)]
    else:
        sizes = [CAP if k in straight or k == 0 else 1 for k in range(instances)]
        copies = [(any_second, [(k, 1) for k in straight[::-1] + [0]])]
        copies += [(k, [(k, 0)]) for k in list(range(instances))[::-1]]
    send = pack(sizes, copies)
    part_scales, *send = lax.optimization_barrier((part_scales, *send))
    arrived = {k: swap(send[k], k) for k in range(instances - 1, 0, -1)}
    arrived[0] = send[0]
    flat_scales = part_scales.reshape(2 * heads, pool).astype(f32)

    query_rows = (
        queries.reshape(requests, steps, heads, per_head, head_dim)
        .transpose(2, 0, 3, 1, 4)
        .reshape(heads, height, head_dim)
    )
    fresh_len = requests * steps
    fresh = new_kv.transpose(2, 3, 0, 1, 4).reshape(2, heads, fresh_len, head_dim)
    fresh = jnp.pad(fresh, ((0, 0), (0, 0), (0, -fresh_len % 128), (0, 0)))
    assert fresh.shape[2] == head_dim
    length = ctx_len[:, None]
    width = group * block_len
    chunks = pool // group
    tokens = pool * block_len

    stat = (heads, height, head_dim)
    own_parts = pl.pallas_call(
        functools.partial(
            own_kernel, (pool, heads, rows, steps, block_len, spans, factor, group)
        ),
        out_shape=[jax.ShapeDtypeStruct(stat, f32)] * 3,
        in_specs=[VMEM_SPEC] * 5 + [HBM_SPEC],
        out_specs=[VMEM_SPEC] * 3,
        scratch_shapes=[
            pltpu.VMEM((chunks, requests, width), f32),
            pltpu.VMEM((chunks, 2 * heads, width), f32),
            pltpu.VMEM((heads, chunks, height, width), f32),
            pltpu.VMEM((heads, height, width), bf16),
            pltpu.VMEM((2, chunks, group, heads * block_len, head_dim), bf16),
            pltpu.SemaphoreType.DMA((2, chunks)),
        ],
        compiler_params=pltpu.CompilerParams(vmem_limit_bytes=48 * MIB),
        cost_estimate=pl.CostEstimate(
            flops=4 * heads * height * tokens * head_dim,
            bytes_accessed=pool_codes.size * 2,
            transcendentals=heads * height * tokens,
        ),
        name="own_blocks",
    )(tables, length, flat_scales, query_rows, fresh, pool_rows)

    order = straight[::-1] + [k for k in range(instances) if k not in straight]
    arrays = [arrived[k] for k in order]
    places = [(order.index(k), 0) for k in range(instances)]
    if general:
        places += [(order.index(k), 1) for k in range(instances)]
    else:
        relayed = {k: arrived[k] for k in straight if k > 1}
        relayed, own_parts = lax.optimization_barrier((relayed, own_parts))
        seconds = {k: relayed[k][1:] for k in relayed}
        for bit in straight[::-1]:
            for k in list(seconds):
                if k > bit and k & (bit - 1) == 0 and k ^ bit not in seconds:
                    seconds[k ^ bit] = swap(seconds[k], bit)
        for k in range(instances):
            if k in straight or k == 0:
                places.append((order.index(k), 1))
            else:
                places.append((len(arrays), 0))
                arrays.append(seconds[k])

    arrival_bytes = 6 * heads * height * slots * block_len + 2 * 12 * height * head_dim * heads
    arrival_bytes += 2 * slots * sent_bytes + 4 * requests * slots * block_len
    out, moved_to, more = pl.pallas_call(
        functools.partial(
            arrival_kernel, (pool, heads, rows, block_len, spans, listed, factor), places
        ),
        out_shape=[
            jax.ShapeDtypeStruct((requests, heads, rows, head_dim), bf16),
            jax.ShapeDtypeStruct((1, listed), jnp.int32),
            jax.ShapeDtypeStruct((1,), jnp.int32),
        ],
        in_specs=[VMEM_SPEC] * (6 + len(arrays)),
        out_specs=[VMEM_SPEC, VMEM_SPEC, SMEM_SPEC],
        scratch_shapes=[
            pltpu.VMEM((requests, slots * block_len), f32),
            pltpu.VMEM((heads, height, slots * block_len), f32),
            pltpu.VMEM((heads, height, slots * block_len), bf16),
        ],
        compiler_params=pltpu.CompilerParams(vmem_limit_bytes=arrival_bytes + 8 * MIB),
        cost_estimate=pl.CostEstimate(
            flops=4 * heads * height * slots * block_len * head_dim,
            bytes_accessed=slots * sent_bytes,
            transcendentals=heads * height * slots * block_len,
        ),
        name="arrived_blocks",
    )(query_rows, tables, length, *own_parts, *arrays)
    out = out.reshape(requests, q_heads, steps, head_dim).transpose(0, 2, 1, 3)
    return out.reshape(requests, steps, q_heads * head_dim), moved_to, more


def shards(*args):
    out, moved_to, more = attend(False, *args)
    _, out = lax.while_loop(
        lambda state: state[0] > 1,
        lambda state: (jnp.int32(0), attend(True, *args)[0]),
        (more[0], out),
    )
    return out, moved_to


def solution(mesh):
    in_specs = (
        P(("groups", "inst"), None, "tp", None),
        P(("groups", "inst"), None, None, "tp", None),
        P(("groups", "inst"), None, "tp", None, None),
        P(("groups", "inst"), None, "tp"),
        P(("groups", "inst"), None),
        P(("groups", "inst")),
        P(("groups", "inst"), None),
        P(("groups", "inst"), None),
    )
    out_specs = (P(("groups", "inst"), None, "tp"), P(("groups", "inst"), None))
    return jax.shard_map(shards, mesh=mesh, in_specs=in_specs, out_specs=out_specs, check_vma=False)
```

```python
import functools
import math

import jax
import jax.numpy as jnp
from jax import lax
from jax.experimental import pallas as pl
from jax.experimental.pallas import tpu as pltpu
from jax.sharding import PartitionSpec as P

CAP = 2
EXTRA = 16
NEVER = -1e30
LOG2E = math.log2(math.e)
MIB = 1 << 20
SMEM_SPEC = pl.BlockSpec(memory_space=pltpu.SMEM)
VMEM_SPEC = pl.BlockSpec(memory_space=pltpu.VMEM)
HBM_SPEC = pl.BlockSpec(memory_space=pltpu.HBM)
NT = (((1,), (1,)), ((), ()))


def loop(count, body, init):
    if count <= 8:
        for i in range(count):
            init = body(i, init)
        return init
    return lax.fori_loop(0, count, body, init)


def pack_kernel(dims, dest_ref, block_ref, scale_ref, pool_ref, *refs):
    instances, listed, heads, pool, copies = dims
    send_refs, (index_ref, extra_ref, held_ref, in_sems, out_sems) = refs[:-5], refs[-5:]
    code_rows = held_ref.shape[1] - EXTRA
    me = lax.axis_index("inst")
    for entry in range(CAP * instances + 1):
        index_ref[entry] = 0

    def place(m, carry):
        dest = dest_ref[0, m]
        rank = loop(
            listed,
            lambda m2, n: n + jnp.where((dest_ref[0, m2] == dest) & (m2 < m), 1, 0),
            jnp.int32(0),
        )
        entry = jnp.bitwise_xor(dest, me) + jnp.where(rank > 0, instances, 0)
        index_ref[entry] = block_ref[0, m]
        index_ref[jnp.where(rank > 0, CAP * instances, entry)] = block_ref[0, m]
        return carry

    loop(listed, place, 0)
    loads, stores = [], []
    for i, (entry, _) in enumerate(copies):
        loads.append(
            pltpu.make_async_copy(
                pool_ref.at[index_ref[entry]], held_ref.at[i, pl.ds(0, code_rows)], in_sems.at[i]
            )
        )
        loads[i].start()
    lane = lax.broadcasted_iota(jnp.int32, (1, 128), 1)

    def spell(m, row):
        return jnp.where(lane == m, dest_ref[0, m].astype(jnp.float32), row)

    extra_ref[...] = jnp.zeros_like(extra_ref)
    extra_ref[2 * heads : 2 * heads + 1, :] = loop(
        listed, spell, jnp.zeros((1, 128), jnp.float32)
    )
    scales = [
        [scale_ref[part, h : h + 1, :].astype(jnp.float32) for h in range(heads)]
        for part in range(2)
    ]
    column = lax.broadcasted_iota(jnp.int32, (1, pool), 1)
    for i, (entry, _) in enumerate(copies):
        for part in range(2):
            for h in range(heads):
                one = jnp.where(column == index_ref[entry], scales[part][h], 0.0)
                row = part * heads + h
                extra_ref[row : row + 1, :] = jnp.broadcast_to(
                    jnp.sum(one, axis=1, keepdims=True), (1, 128)
                )
        held_ref[i, pl.ds(code_rows, EXTRA)] = extra_ref[...].astype(jnp.bfloat16)
    for i, (_, targets) in enumerate(copies):
        loads[i].wait()
        for output, row in targets:
            stores.append(
                pltpu.make_async_copy(
                    held_ref.at[i], send_refs[output].at[row], out_sems.at[len(stores)]
                )
            )
            stores[-1].start()
    for store in stores:
        store.wait()


def split(value, size):
    assert size & (size - 1) == 0
    return lax.shift_right_logical(value, size.bit_length() - 1), value & (size - 1)


def count_log(tables, length, ids, block_len, spans, store):
    requests, width = tables.shape[0], ids.shape[1]
    whole, rest = split(length, block_len)
    whole = jnp.broadcast_to(whole, (requests, width))
    full = jnp.zeros((requests, width), jnp.float32)
    part = jnp.zeros((requests, width), jnp.float32)
    for e in range(spans):
        hit = jnp.broadcast_to(tables[:, e : e + 1], (requests, width)) == ids
        full = full + jnp.where(hit & (whole > e), 1.0, 0.0)
        part = part + jnp.where(hit & (whole == e), 1.0, 0.0)

    def log2(count):
        return jnp.where(count > 0, jnp.log(jnp.maximum(count, 1.0)) * LOG2E, NEVER)

    beyond, within = log2(full), log2(full + part)
    shape = (requests, block_len)
    inside = lax.broadcasted_iota(jnp.int32, shape, 1) < jnp.broadcast_to(rest, shape)
    if width % 16:
        for b in range(width):
            store(
                b,
                jnp.where(
                    inside,
                    jnp.broadcast_to(within[:, b : b + 1], shape),
                    jnp.broadcast_to(beyond[:, b : b + 1], shape),
                ),
            )
        return
    both = jnp.concatenate([within, beyond], axis=0)
    high = both.astype(jnp.bfloat16)
    low = (both - high.astype(jnp.float32)).astype(jnp.bfloat16)
    terms = jnp.concatenate([high, low], axis=0)
    row = lax.broadcasted_iota(jnp.int32, (width, block_len), 0)
    for b in range(0, width, 2):
        spots = jnp.concatenate(
            [jnp.where(row == b + i, 1.0, 0.0).astype(jnp.bfloat16) for i in range(2)], axis=1
        )
        spread_out = jnp.dot(terms, spots, preferred_element_type=jnp.float32)
        value = spread_out[: 2 * requests] + spread_out[2 * requests :]
        for i in range(2):
            at = slice(i * block_len, (i + 1) * block_len)
            store(b + i, jnp.where(inside, value[:requests, at], value[requests:, at]))


def score_tiles(query, keys, log_ref, scale_row, rows, store):
    height, wide = min(256, query.shape[0]), min(256, keys.shape[0])
    for top in range(0, query.shape[0], height):
        for left in range(0, keys.shape[0], wide):
            part = lax.dot_general(
                query[top : top + height],
                keys[left : left + wide],
                NT,
                preferred_element_type=jnp.float32,
            )
            scale = scale_row[:, left : left + wide]
            for r in range(height // rows):
                request = top // rows + r
                store(
                    request * rows,
                    left,
                    part[r * rows : (r + 1) * rows] * scale
                    + log_ref[request : request + 1, left : left + wide],
                )


def lane_fold(value, op):
    parts = [value[:, i : i + 128] for i in range(0, value.shape[1], 128)]
    while len(parts) > 1:
        parts = [
            op(parts[i], parts[i + 1]) if i + 1 < len(parts) else parts[i]
            for i in range(0, len(parts), 2)
        ]
    return parts[0]


def spread(column, width):
    return jnp.concatenate([column] * (width // 128), axis=1)


def own_kernel(
    dims, q_ref, fresh_ref, pool_ref, *refs
):
    if dims[0] == 0:
        tables_ref, length_ref, scale_ref, acc_ref, top_ref, total_ref, log_ref, row_ref = refs[:8]
    else:
        log_ref, row_ref, acc_ref, top_ref, total_ref = refs[:5]
    t_ref, p_ref, codes_ref, sems = refs[-4:]
    head, pool, heads, rows, steps, block_len, spans, factor, group = dims
    chunks = pool // group
    height, head_dim = q_ref.shape[1:]
    width = group * block_len

    def load(part, chunk):
        return pltpu.make_async_copy(
            pool_ref.at[
                pl.ds(chunk * group, group), pl.ds((part * heads + head) * block_len, block_len)
            ],
            codes_ref.at[part, chunk],
            sems.at[part, chunk],
        )

    for part in range(2):
        for chunk in range(chunks):
            load(part, chunk).start()

    if head == 0:
        ids = lax.broadcasted_iota(jnp.int32, (1, pool), 1)

        def store_log(b, value):
            lane = (b % group) * block_len
            log_ref[b // group, :, lane : lane + block_len] = value

        count_log(tables_ref[...], length_ref[...], ids, block_len, spans, store_log)
        for b in range(pool):
            lane = (b % group) * block_len
            row_ref[b // group, :, lane : lane + block_len] = jnp.broadcast_to(
                scale_ref[:, b : b + 1], (2 * heads, block_len)
            )
    shape = (height, fresh_ref.shape[2])
    row = lax.broadcasted_iota(jnp.int32, shape, 0)
    col = lax.broadcasted_iota(jnp.int32, shape, 1)
    (request, row_step), (owner, step) = split(row, rows), split(col, steps)
    seen = (request == owner) & (split(row_step, steps)[1] >= step)
    new_score = lax.dot_general(
        q_ref[head], fresh_ref[0, head], NT, preferred_element_type=jnp.float32
    )
    new_score = jnp.where(seen, new_score * (factor * LOG2E), -jnp.inf)
    acc_ref[...] = new_score
    top_ref[...] = lane_fold(new_score, jnp.maximum)

    def score(chunk, carry):
        load(0, chunk).wait()

        def store(row, lane, value):
            t_ref[chunk, row : row + rows, lane : lane + value.shape[1]] = value

        score_tiles(
            q_ref[head],
            codes_ref[0, chunk].reshape(width, head_dim),
            log_ref.at[chunk],
            row_ref[chunk, head : head + 1, :] * (factor * LOG2E),
            rows,
            store,
        )
        for row in range(0, height, rows):
            at = pl.ds(row, rows)
            top_ref[at] = jnp.maximum(top_ref[at], lane_fold(t_ref[chunk, at], jnp.maximum))
        return carry

    lax.fori_loop(0, chunks, score, 0)

    top = jnp.broadcast_to(jnp.max(top_ref[...], axis=1, keepdims=True), (height, 128))
    top_ref[...] = top
    weight = jnp.exp2(acc_ref[...] - spread(top, acc_ref.shape[1]))
    total_ref[...] = lane_fold(weight, jnp.add)
    acc_ref[...] = jnp.dot(
        weight.astype(jnp.bfloat16), fresh_ref[1, head], preferred_element_type=jnp.float32
    )

    def apply(chunk, carry):
        load(1, chunk).wait()
        scale = row_ref[chunk, heads + head : heads + head + 1, :]
        for row in range(0, height, rows):
            at = pl.ds(row, rows)
            weight = jnp.exp2(t_ref[chunk, at] - spread(top_ref[at], width))
            total_ref[at] += lane_fold(weight, jnp.add)
            p_ref[at] = (weight * scale).astype(jnp.bfloat16)
        acc_ref[...] += jnp.dot(
            p_ref[...],
            codes_ref[1, chunk].reshape(width, head_dim),
            preferred_element_type=jnp.float32,
        )
        return carry

    lax.fori_loop(0, chunks, apply, 0)


def arrival_ids(me, pool, lists, listed):
    instances = len(lists)
    lane = lax.broadcasted_iota(jnp.int32, (1, 128), 1)
    counts = [
        jnp.sum(
            jnp.where((row == me.astype(jnp.float32)) & (lane < listed), 1.0, 0.0),
            axis=1,
            keepdims=True,
        )
        for row in lists
    ]
    slot = lax.broadcasted_iota(jnp.int32, (1, instances * CAP), 1)
    ids = jnp.full(slot.shape, -1.0)
    for k in range(instances):
        first = jnp.full((1, 1), float(pool))
        for j in range(instances):
            lower = jnp.bitwise_xor(me, j) < jnp.bitwise_xor(me, k)
            first = first + jnp.where(lower, counts[j], 0.0)
        for r in range(CAP):
            name = jnp.where(counts[k] > r, first + r, -1.0)
            ids = jnp.where(slot == r * instances + k, jnp.broadcast_to(name, slot.shape), ids)
    moved = jnp.full((1, 128), float(pool))
    for j in range(instances):
        for m in range(listed):
            same = jnp.broadcast_to(lists[j][:, m : m + 1], (1, 128)) == lists[0]
            ahead = jnp.bitwise_xor(me, j) < me if j else lane > m
            moved = moved + jnp.where(same & ahead, 1.0, 0.0)
    more = jnp.zeros((1, 128))
    for row in lists:
        again = jnp.zeros((1, 128))
        for m in range(listed):
            same = jnp.broadcast_to(row[:, m : m + 1], (1, 128)) == row
            again = again + jnp.where(same & (lane > m) & (lane < listed), 1.0, 0.0)
        more = jnp.maximum(more, jnp.sum(again, axis=1, keepdims=True))
    return ids.astype(jnp.int32), moved[:, :listed].astype(jnp.int32), more


def arrival_kernel(dims, places, q_ref, tables_ref, length_ref, *refs):
    pool, heads, rows, block_len, spans, listed, factor = dims
    own_refs, code_refs = refs[: 3 * heads], refs[3 * heads : -6]
    out_ref, moved_ref, more_ref, log_ref, t_ref, p_ref = refs[-6:]
    height = q_ref.shape[1]
    width = 2 * block_len
    extra = 2 * heads * block_len
    slots = [(code_refs[array], row) for array, row in places]
    pairs = len(slots) // 2

    def pair(i, part, h):
        at = pl.ds((part * heads + h) * block_len, block_len)
        return jnp.concatenate([ref[r, at] for ref, r in slots[2 * i : 2 * i + 2]], axis=0)

    lists, scale_rows = [], []
    for ref, r in slots:
        values = ref[r, pl.ds(extra, EXTRA)].astype(jnp.float32)
        scale_rows.append(values)
        if len(lists) < len(slots) // CAP:
            lists.append(values[2 * heads : 2 * heads + 1])

    def scale_row(row):
        return jnp.concatenate([values[row : row + 1] for values in scale_rows], axis=1)

    ids, moved_ref[...], more = arrival_ids(lax.axis_index("inst"), pool, lists, listed)
    more_ref[0] = jnp.max(more).astype(jnp.int32)

    def store_log(b, value):
        log_ref[:, b * block_len : (b + 1) * block_len] = value

    count_log(tables_ref[...], length_ref[...], ids, block_len, spans, store_log)
    for h in range(heads):
        key_scale = scale_row(h) * (factor * LOG2E)
        for i in range(pairs):
            left = i * width

            def store(row, lane, value, h=h, left=left):
                t_ref[h, row : row + rows, left + lane : left + lane + value.shape[1]] = value

            score_tiles(
                q_ref[h],
                pair(i, 0, h),
                log_ref.at[:, left : left + width],
                key_scale[:, left : left + width],
                rows,
                store,
            )
    for h in range(heads):
        acc_ref, top_ref, total_ref = own_refs[3 * h : 3 * h + 3]
        scale = scale_row(heads + h)
        for row in range(0, height, rows):
            at = pl.ds(row, rows)
            score = t_ref[h, at]
            own_top = top_ref[at]
            top = jnp.maximum(
                own_top, jnp.max(lane_fold(score, jnp.maximum), axis=1, keepdims=True)
            )
            weight = jnp.exp2(score - spread(top, score.shape[1]))
            keep = jnp.exp2(own_top - top)
            total = jnp.sum(
                total_ref[at] * keep + lane_fold(weight, jnp.add), axis=1, keepdims=True
            )
            p_ref[h, at] = (weight * scale).astype(jnp.bfloat16)
            t_ref[h, at, 0:128] = keep
            t_ref[h, at, 128:256] = jnp.broadcast_to(1.0 / total, keep.shape)
        mixed = acc_ref[...] * t_ref[h, :, 0:128]
        for i in range(pairs):
            mixed = mixed + jnp.dot(
                p_ref[h, :, i * width : (i + 1) * width],
                pair(i, 1, h),
                preferred_element_type=jnp.float32,
            )
        result = (mixed * t_ref[h, :, 128:256]).astype(jnp.bfloat16)
        out_ref[:, h] = result.reshape(height // rows, rows, result.shape[-1])


def attend(
    general, queries, new_kv, pool_codes, pool_scales, tables, ctx_len, mig_block, mig_dest
):
    instances = lax.axis_size("inst")
    pool = pool_codes.shape[0]
    requests, steps, q_heads, head_dim = queries.shape
    heads = new_kv.shape[3]
    per_head = q_heads // heads
    spans = tables.shape[1]
    block_len = pool_codes.shape[3]
    listed = mig_dest.shape[1]
    factor = head_dim ** (-0.5)
    rows = per_head * steps
    height = requests * rows
    slots = instances * CAP
    group = 16
    f32, bf16 = jnp.float32, jnp.bfloat16
    code_rows = 2 * heads * block_len
    pool_rows = pool_codes.reshape(pool, code_rows, head_dim)
    sent_shape = (code_rows + EXTRA, head_dim)
    sent_bytes = 2 * math.prod(sent_shape)
    part_scales = jnp.transpose(pool_scales, (1, 2, 0))
    assert instances & (instances - 1) == 0 and 2 * heads < EXTRA and head_dim == 128

    def pack(sizes, copies):
        stores = sum(len(targets) for _, targets in copies)
        return pl.pallas_call(
            functools.partial(pack_kernel, (instances, listed, heads, pool, copies)),
            out_shape=[jax.ShapeDtypeStruct((size,) + sent_shape, bf16) for size in sizes],
            in_specs=[SMEM_SPEC, SMEM_SPEC, VMEM_SPEC, HBM_SPEC],
            out_specs=[HBM_SPEC] * len(sizes),
            scratch_shapes=[
                pltpu.SMEM((CAP * instances + 1,), jnp.int32),
                pltpu.VMEM((EXTRA, head_dim), f32),
                pltpu.VMEM((len(copies),) + sent_shape, bf16),
                pltpu.SemaphoreType.DMA((len(copies),)),
                pltpu.SemaphoreType.DMA((stores,)),
            ],
            compiler_params=pltpu.CompilerParams(vmem_limit_bytes=56 * MIB),
            cost_estimate=pl.CostEstimate(
                flops=0, bytes_accessed=2 * stores * sent_bytes, transcendentals=0
            ),
            name="pack_blocks",
        )(mig_dest, mig_block, part_scales, pool_rows)

    def swap(value, distance):
        return lax.ppermute(value, "inst", [(j, j ^ distance) for j in range(instances)])

    if general:
        send = pack(
            [CAP] * instances,
            [(r * instances + k, [(k, r)]) for k in range(instances) for r in range(CAP)],
        )
        arrived = [swap(send[k], k) for k in range(instances - 1, 0, -1)] + [send[0]]
        places = [(instances - 1 - k, r) for r in range(CAP) for k in range(instances)]
    else:
        any_second = CAP * instances
        (second,) = pack([1], [(any_second, [(0, 0)])])
        seconds = {0: second}
        bit = instances // 2
        while bit > 1:
            for k in list(seconds):
                seconds[k ^ bit] = swap(seconds[k], bit)
            bit //= 2
        mig_dest, second = lax.optimization_barrier((mig_dest, second))
        send = pack(
            [1, 2] + [1] * (instances - 2),
            [(k, [(k, 0)]) for k in list(range(instances))[::-1]] + [(any_second, [(1, 1)])],
        )
        firsts = [send[0]] + [swap(send[k], k) for k in range(1, instances)]
    part_scales, *send = lax.optimization_barrier((part_scales, *send))
    flat_scales = part_scales.reshape(2 * heads, pool).astype(f32)

    query_rows = (
        queries.reshape(requests, steps, heads, per_head, head_dim)
        .transpose(2, 0, 3, 1, 4)
        .reshape(heads, height, head_dim)
    )
    fresh_len = requests * steps
    fresh = new_kv.transpose(2, 3, 0, 1, 4).reshape(2, heads, fresh_len, head_dim)
    fresh = jnp.pad(fresh, ((0, 0), (0, 0), (0, -fresh_len % 128), (0, 0)))
    assert fresh.shape[2] == head_dim
    length = ctx_len[:, None]
    width = group * block_len
    chunks = pool // group
    tokens = pool * block_len

    mask_shapes = [(chunks, requests, width), (chunks, 2 * heads, width)]

    def own(head, *masks):
        shapes = [(height, head_dim)] * 3 + ([] if head else mask_shapes)
        return pl.pallas_call(
            functools.partial(
                own_kernel, (head, pool, heads, rows, steps, block_len, spans, factor, group)
            ),
            out_shape=[jax.ShapeDtypeStruct(shape, f32) for shape in shapes],
            in_specs=[VMEM_SPEC, VMEM_SPEC, HBM_SPEC] + [VMEM_SPEC] * len(masks),
            out_specs=[VMEM_SPEC] * len(shapes),
            scratch_shapes=[
                pltpu.VMEM((chunks, height, width), f32),
                pltpu.VMEM((height, width), bf16),
                pltpu.VMEM((2, chunks, group, block_len, head_dim), bf16),
                pltpu.SemaphoreType.DMA((2, chunks)),
            ],
            compiler_params=pltpu.CompilerParams(vmem_limit_bytes=32 * MIB),
            cost_estimate=pl.CostEstimate(
                flops=4 * height * tokens * head_dim,
                bytes_accessed=pool_codes.size * 2 // heads,
                transcendentals=height * tokens,
            ),
            name="own_blocks",
        )(query_rows, fresh, pool_rows, *masks)

    *own_parts, log_rows, scale_rows = own(0, tables, length, flat_scales)
    if not general:
        seconds, own_parts, log_rows = lax.optimization_barrier((seconds, own_parts, log_rows))
    for head in range(1, heads):
        own_parts = own_parts + list(own(head, log_rows, scale_rows))

    if not general:
        held = {k: second for k, second in seconds.items() if k}
        for k in held:
            seconds[k ^ 1] = swap(held[k], 1)
        arrived = [held[k] for k in held] + firsts[::-1] + [seconds[0]]
        where = {k: i for i, k in enumerate(held)}
        where[0] = len(arrived) - 1
        places = [(len(held) + instances - 1 - k, 0) for k in range(instances)]
        for k in range(instances):
            if k == 1:
                places.append((places[1][0], 1))
            elif k in where:
                places.append((where[k], 0))
            else:
                places.append((len(arrived), 0))
                arrived.append(seconds[k])

    arrival_bytes = 6 * heads * height * slots * block_len + 2 * 12 * height * head_dim * heads
    arrival_bytes += 2 * slots * sent_bytes + 4 * requests * slots * block_len
    out, moved_to, more = pl.pallas_call(
        functools.partial(
            arrival_kernel, (pool, heads, rows, block_len, spans, listed, factor), places
        ),
        out_shape=[
            jax.ShapeDtypeStruct((requests, heads, rows, head_dim), bf16),
            jax.ShapeDtypeStruct((1, listed), jnp.int32),
            jax.ShapeDtypeStruct((1,), jnp.int32),
        ],
        in_specs=[VMEM_SPEC] * (3 + 3 * heads + len(arrived)),
        out_specs=[VMEM_SPEC, VMEM_SPEC, SMEM_SPEC],
        scratch_shapes=[
            pltpu.VMEM((requests, slots * block_len), f32),
            pltpu.VMEM((heads, height, slots * block_len), f32),
            pltpu.VMEM((heads, height, slots * block_len), bf16),
        ],
        compiler_params=pltpu.CompilerParams(vmem_limit_bytes=arrival_bytes + 8 * MIB),
        cost_estimate=pl.CostEstimate(
            flops=4 * heads * height * slots * block_len * head_dim,
            bytes_accessed=slots * sent_bytes,
            transcendentals=heads * height * slots * block_len,
        ),
        name="arrived_blocks",
    )(query_rows, tables, length, *own_parts, *arrived)
    out = out.reshape(requests, q_heads, steps, head_dim).transpose(0, 2, 1, 3)
    return out.reshape(requests, steps, q_heads * head_dim), moved_to, more


def shards(*args):
    out, moved_to, more = attend(False, *args)
    _, out = lax.while_loop(
        lambda state: state[0] > 1,
        lambda state: (jnp.int32(0), attend(True, *args)[0]),
        (more[0], out),
    )
    return out, moved_to


def solution(mesh):
    in_specs = (
        P(("groups", "inst"), None, "tp", None),
        P(("groups", "inst"), None, None, "tp", None),
        P(("groups", "inst"), None, "tp", None, None),
        P(("groups", "inst"), None, "tp"),
        P(("groups", "inst"), None),
        P(("groups", "inst")),
        P(("groups", "inst"), None),
        P(("groups", "inst"), None),
    )
    out_specs = (P(("groups", "inst"), None, "tp"), P(("groups", "inst"), None))
    return jax.shard_map(shards, mesh=mesh, in_specs=in_specs, out_specs=out_specs, check_vma=False)
```

```python
import functools
import math

import jax
import jax.numpy as jnp
from jax import lax
from jax.experimental import pallas as pl
from jax.experimental.pallas import tpu as pltpu
from jax.sharding import PartitionSpec as P

CAP = 2
EXTRA = 16
NEVER = -1e30
LOG2E = math.log2(math.e)
MIB = 1 << 20
SMEM_SPEC = pl.BlockSpec(memory_space=pltpu.SMEM)
VMEM_SPEC = pl.BlockSpec(memory_space=pltpu.VMEM)
HBM_SPEC = pl.BlockSpec(memory_space=pltpu.HBM)
NT = (((1,), (1,)), ((), ()))


def loop(count, body, init):
    if count <= 8:
        for i in range(count):
            init = body(i, init)
        return init
    return lax.fori_loop(0, count, body, init)


def pack_kernel(dims, dest_ref, block_ref, scale_ref, pool_ref, *refs):
    instances, listed, heads, pool, copies = dims
    send_refs, (index_ref, extra_ref, held_ref, in_sems, out_sems) = refs[:-5], refs[-5:]
    code_rows = held_ref.shape[1] - EXTRA
    me = lax.axis_index("inst")
    for entry in range(CAP * instances + 1):
        index_ref[entry] = 0

    def place(m, carry):
        dest = dest_ref[0, m]
        rank = loop(
            listed,
            lambda m2, n: n + jnp.where((dest_ref[0, m2] == dest) & (m2 < m), 1, 0),
            jnp.int32(0),
        )
        entry = jnp.bitwise_xor(dest, me) + jnp.where(rank > 0, instances, 0)
        index_ref[entry] = block_ref[0, m]
        index_ref[jnp.where(rank > 0, CAP * instances, entry)] = block_ref[0, m]
        return carry

    loop(listed, place, 0)
    loads, stores = [], []
    for i, (entry, _) in enumerate(copies):
        loads.append(
            pltpu.make_async_copy(
                pool_ref.at[index_ref[entry]], held_ref.at[i, pl.ds(0, code_rows)], in_sems.at[i]
            )
        )
        loads[i].start()
    lane = lax.broadcasted_iota(jnp.int32, (1, 128), 1)

    def spell(m, row):
        return jnp.where(lane == m, dest_ref[0, m].astype(jnp.float32), row)

    extra_ref[...] = jnp.zeros_like(extra_ref)
    extra_ref[2 * heads : 2 * heads + 1, :] = loop(
        listed, spell, jnp.zeros((1, 128), jnp.float32)
    )
    scales = [
        [scale_ref[part, h : h + 1, :].astype(jnp.float32) for h in range(heads)]
        for part in range(2)
    ]
    column = lax.broadcasted_iota(jnp.int32, (1, pool), 1)
    for i, (entry, _) in enumerate(copies):
        for part in range(2):
            for h in range(heads):
                one = jnp.where(column == index_ref[entry], scales[part][h], 0.0)
                row = part * heads + h
                extra_ref[row : row + 1, :] = jnp.broadcast_to(
                    jnp.sum(one, axis=1, keepdims=True), (1, 128)
                )
        held_ref[i, pl.ds(code_rows, EXTRA)] = extra_ref[...].astype(jnp.bfloat16)
    for i, (_, targets) in enumerate(copies):
        loads[i].wait()
        for output, row in targets:
            stores.append(
                pltpu.make_async_copy(
                    held_ref.at[i], send_refs[output].at[row], out_sems.at[len(stores)]
                )
            )
            stores[-1].start()
    for store in stores:
        store.wait()


def split(value, size):
    assert size & (size - 1) == 0
    return lax.shift_right_logical(value, size.bit_length() - 1), value & (size - 1)


def count_log(tables, length, ids, block_len, spans, store):
    requests, width = tables.shape[0], ids.shape[1]
    whole, rest = split(length, block_len)
    whole = jnp.broadcast_to(whole, (requests, width))
    full = jnp.zeros((requests, width), jnp.float32)
    part = jnp.zeros((requests, width), jnp.float32)
    for e in range(spans):
        hit = jnp.broadcast_to(tables[:, e : e + 1], (requests, width)) == ids
        full = full + jnp.where(hit & (whole > e), 1.0, 0.0)
        part = part + jnp.where(hit & (whole == e), 1.0, 0.0)

    def log2(count):
        return jnp.where(count > 0, jnp.log(jnp.maximum(count, 1.0)) * LOG2E, NEVER)

    beyond, within = log2(full), log2(full + part)
    shape = (requests, block_len)
    inside = lax.broadcasted_iota(jnp.int32, shape, 1) < jnp.broadcast_to(rest, shape)
    if width % 16:
        for b in range(width):
            store(
                b,
                jnp.where(
                    inside,
                    jnp.broadcast_to(within[:, b : b + 1], shape),
                    jnp.broadcast_to(beyond[:, b : b + 1], shape),
                ),
            )
        return
    both = jnp.concatenate([within, beyond], axis=0)
    high = both.astype(jnp.bfloat16)
    low = (both - high.astype(jnp.float32)).astype(jnp.bfloat16)
    terms = jnp.concatenate([high, low], axis=0)
    row = lax.broadcasted_iota(jnp.int32, (width, block_len), 0)
    for b in range(0, width, 2):
        spots = jnp.concatenate(
            [jnp.where(row == b + i, 1.0, 0.0).astype(jnp.bfloat16) for i in range(2)], axis=1
        )
        spread_out = jnp.dot(terms, spots, preferred_element_type=jnp.float32)
        value = spread_out[: 2 * requests] + spread_out[2 * requests :]
        for i in range(2):
            at = slice(i * block_len, (i + 1) * block_len)
            store(b + i, jnp.where(inside, value[:requests, at], value[requests:, at]))


def score_tiles(query, keys, log_ref, scale_row, rows, store):
    height, wide = min(256, query.shape[0]), min(256, keys.shape[0])
    for top in range(0, query.shape[0], height):
        for left in range(0, keys.shape[0], wide):
            part = lax.dot_general(
                query[top : top + height],
                keys[left : left + wide],
                NT,
                preferred_element_type=jnp.float32,
            )
            scale = scale_row[:, left : left + wide]
            for r in range(height // rows):
                request = top // rows + r
                store(
                    request * rows,
                    left,
                    part[r * rows : (r + 1) * rows] * scale
                    + log_ref[request : request + 1, left : left + wide],
                )


def lane_fold(value, op):
    parts = [value[:, i : i + 128] for i in range(0, value.shape[1], 128)]
    while len(parts) > 1:
        parts = [
            op(parts[i], parts[i + 1]) if i + 1 < len(parts) else parts[i]
            for i in range(0, len(parts), 2)
        ]
    return parts[0]


def spread(column, width):
    return jnp.concatenate([column] * (width // 128), axis=1)


def own_kernel(
    dims, q_ref, fresh_ref, pool_ref, *refs
):
    if dims[0] == 0:
        tables_ref, length_ref, scale_ref, acc_ref, top_ref, total_ref, log_ref, row_ref = refs[:8]
    else:
        log_ref, row_ref, acc_ref, top_ref, total_ref = refs[:5]
    t_ref, p_ref = refs[-2:]
    head, pool, heads, rows, steps, block_len, spans, factor, group = dims
    chunks = pool // group
    height, head_dim = q_ref.shape[1:]
    width = group * block_len

    def codes(part, chunk):
        blocks = pl.ds(chunk * group, group)
        at = pl.ds((part * heads + head) * block_len, block_len)
        return pool_ref[blocks, at].reshape(width, head_dim)

    if head == 0:
        ids = lax.broadcasted_iota(jnp.int32, (1, pool), 1)

        def store_log(b, value):
            lane = (b % group) * block_len
            log_ref[b // group, :, lane : lane + block_len] = value

        count_log(tables_ref[...], length_ref[...], ids, block_len, spans, store_log)
        for b in range(pool):
            lane = (b % group) * block_len
            row_ref[b // group, :, lane : lane + block_len] = jnp.broadcast_to(
                scale_ref[:, b : b + 1], (2 * heads, block_len)
            )
    shape = (height, fresh_ref.shape[2])
    row = lax.broadcasted_iota(jnp.int32, shape, 0)
    col = lax.broadcasted_iota(jnp.int32, shape, 1)
    (request, row_step), (owner, step) = split(row, rows), split(col, steps)
    seen = (request == owner) & (split(row_step, steps)[1] >= step)
    new_score = lax.dot_general(
        q_ref[head], fresh_ref[0, head], NT, preferred_element_type=jnp.float32
    )
    new_score = jnp.where(seen, new_score * (factor * LOG2E), -jnp.inf)
    acc_ref[...] = new_score
    top_ref[...] = lane_fold(new_score, jnp.maximum)

    def score(chunk, carry):

        def store(row, lane, value):
            t_ref[chunk, row : row + rows, lane : lane + value.shape[1]] = value

        score_tiles(
            q_ref[head],
            codes(0, chunk),
            log_ref.at[chunk],
            row_ref[chunk, head : head + 1, :] * (factor * LOG2E),
            rows,
            store,
        )
        for row in range(0, height, rows):
            at = pl.ds(row, rows)
            top_ref[at] = jnp.maximum(top_ref[at], lane_fold(t_ref[chunk, at], jnp.maximum))
        return carry

    lax.fori_loop(0, chunks, score, 0)

    top = jnp.broadcast_to(jnp.max(top_ref[...], axis=1, keepdims=True), (height, 128))
    top_ref[...] = top
    weight = jnp.exp2(acc_ref[...] - spread(top, acc_ref.shape[1]))
    total_ref[...] = lane_fold(weight, jnp.add)
    acc_ref[...] = jnp.dot(
        weight.astype(jnp.bfloat16), fresh_ref[1, head], preferred_element_type=jnp.float32
    )

    def apply(chunk, carry):
        scale = row_ref[chunk, heads + head : heads + head + 1, :]
        for row in range(0, height, rows):
            at = pl.ds(row, rows)
            weight = jnp.exp2(t_ref[chunk, at] - spread(top_ref[at], width))
            total_ref[at] += lane_fold(weight, jnp.add)
            p_ref[at] = (weight * scale).astype(jnp.bfloat16)
        acc_ref[...] += jnp.dot(
            p_ref[...],
            codes(1, chunk),
            preferred_element_type=jnp.float32,
        )
        return carry

    lax.fori_loop(0, chunks, apply, 0)


def arrival_ids(me, pool, lists, listed):
    instances = len(lists)
    lane = lax.broadcasted_iota(jnp.int32, (1, 128), 1)
    counts = [
        jnp.sum(
            jnp.where((row == me.astype(jnp.float32)) & (lane < listed), 1.0, 0.0),
            axis=1,
            keepdims=True,
        )
        for row in lists
    ]
    slot = lax.broadcasted_iota(jnp.int32, (1, instances * CAP), 1)
    ids = jnp.full(slot.shape, -1.0)
    for k in range(instances):
        first = jnp.full((1, 1), float(pool))
        for j in range(instances):
            lower = jnp.bitwise_xor(me, j) < jnp.bitwise_xor(me, k)
            first = first + jnp.where(lower, counts[j], 0.0)
        for r in range(CAP):
            name = jnp.where(counts[k] > r, first + r, -1.0)
            ids = jnp.where(slot == r * instances + k, jnp.broadcast_to(name, slot.shape), ids)
    moved = jnp.full((1, 128), float(pool))
    for j in range(instances):
        for m in range(listed):
            same = jnp.broadcast_to(lists[j][:, m : m + 1], (1, 128)) == lists[0]
            ahead = jnp.bitwise_xor(me, j) < me if j else lane > m
            moved = moved + jnp.where(same & ahead, 1.0, 0.0)
    more = jnp.zeros((1, 128))
    for row in lists:
        again = jnp.zeros((1, 128))
        for m in range(listed):
            same = jnp.broadcast_to(row[:, m : m + 1], (1, 128)) == row
            again = again + jnp.where(same & (lane > m) & (lane < listed), 1.0, 0.0)
        more = jnp.maximum(more, jnp.sum(again, axis=1, keepdims=True))
    return ids.astype(jnp.int32), moved[:, :listed].astype(jnp.int32), more


def arrival_kernel(dims, places, q_ref, tables_ref, length_ref, *refs):
    pool, heads, rows, block_len, spans, listed, factor = dims
    own_refs, code_refs = refs[: 3 * heads], refs[3 * heads : -6]
    out_ref, moved_ref, more_ref, log_ref, t_ref, p_ref = refs[-6:]
    height = q_ref.shape[1]
    width = 2 * block_len
    extra = 2 * heads * block_len
    slots = [(code_refs[array], row) for array, row in places]
    pairs = len(slots) // 2

    def pair(i, part, h):
        at = pl.ds((part * heads + h) * block_len, block_len)
        return jnp.concatenate([ref[r, at] for ref, r in slots[2 * i : 2 * i + 2]], axis=0)

    lists, scale_rows = [], []
    for ref, r in slots:
        values = ref[r, pl.ds(extra, EXTRA)].astype(jnp.float32)
        scale_rows.append(values)
        if len(lists) < len(slots) // CAP:
            lists.append(values[2 * heads : 2 * heads + 1])

    def scale_row(row):
        return jnp.concatenate([values[row : row + 1] for values in scale_rows], axis=1)

    ids, moved_ref[...], more = arrival_ids(lax.axis_index("inst"), pool, lists, listed)
    more_ref[0] = jnp.max(more).astype(jnp.int32)

    def store_log(b, value):
        log_ref[:, b * block_len : (b + 1) * block_len] = value

    count_log(tables_ref[...], length_ref[...], ids, block_len, spans, store_log)
    for h in range(heads):
        key_scale = scale_row(h) * (factor * LOG2E)
        for i in range(pairs):
            left = i * width

            def store(row, lane, value, h=h, left=left):
                t_ref[h, row : row + rows, left + lane : left + lane + value.shape[1]] = value

            score_tiles(
                q_ref[h],
                pair(i, 0, h),
                log_ref.at[:, left : left + width],
                key_scale[:, left : left + width],
                rows,
                store,
            )
    for h in range(heads):
        acc_ref, top_ref, total_ref = own_refs[3 * h : 3 * h + 3]
        scale = scale_row(heads + h)
        for row in range(0, height, rows):
            at = pl.ds(row, rows)
            score = t_ref[h, at]
            own_top = top_ref[at]
            top = jnp.maximum(
                own_top, jnp.max(lane_fold(score, jnp.maximum), axis=1, keepdims=True)
            )
            weight = jnp.exp2(score - spread(top, score.shape[1]))
            keep = jnp.exp2(own_top - top)
            total = jnp.sum(
                total_ref[at] * keep + lane_fold(weight, jnp.add), axis=1, keepdims=True
            )
            p_ref[h, at] = (weight * scale).astype(jnp.bfloat16)
            t_ref[h, at, 0:128] = keep
            t_ref[h, at, 128:256] = jnp.broadcast_to(1.0 / total, keep.shape)
        mixed = acc_ref[...] * t_ref[h, :, 0:128]
        for i in range(pairs):
            mixed = mixed + jnp.dot(
                p_ref[h, :, i * width : (i + 1) * width],
                pair(i, 1, h),
                preferred_element_type=jnp.float32,
            )
        result = (mixed * t_ref[h, :, 128:256]).astype(jnp.bfloat16)
        out_ref[:, h] = result.reshape(height // rows, rows, result.shape[-1])


def attend(
    general, queries, new_kv, pool_codes, pool_scales, tables, ctx_len, mig_block, mig_dest
):
    instances = lax.axis_size("inst")
    pool = pool_codes.shape[0]
    requests, steps, q_heads, head_dim = queries.shape
    heads = new_kv.shape[3]
    per_head = q_heads // heads
    spans = tables.shape[1]
    block_len = pool_codes.shape[3]
    listed = mig_dest.shape[1]
    factor = head_dim ** (-0.5)
    rows = per_head * steps
    height = requests * rows
    slots = instances * CAP
    group = 16
    f32, bf16 = jnp.float32, jnp.bfloat16
    code_rows = 2 * heads * block_len
    pool_rows = pool_codes.reshape(pool, code_rows, head_dim)
    sent_shape = (code_rows + EXTRA, head_dim)
    sent_bytes = 2 * math.prod(sent_shape)
    part_scales = jnp.transpose(pool_scales, (1, 2, 0))
    assert instances & (instances - 1) == 0 and 2 * heads < EXTRA and head_dim == 128

    def pack(sizes, copies):
        stores = sum(len(targets) for _, targets in copies)
        return pl.pallas_call(
            functools.partial(pack_kernel, (instances, listed, heads, pool, copies)),
            out_shape=[jax.ShapeDtypeStruct((size,) + sent_shape, bf16) for size in sizes],
            in_specs=[SMEM_SPEC, SMEM_SPEC, VMEM_SPEC, HBM_SPEC],
            out_specs=[HBM_SPEC] * len(sizes),
            scratch_shapes=[
                pltpu.SMEM((CAP * instances + 1,), jnp.int32),
                pltpu.VMEM((EXTRA, head_dim), f32),
                pltpu.VMEM((len(copies),) + sent_shape, bf16),
                pltpu.SemaphoreType.DMA((len(copies),)),
                pltpu.SemaphoreType.DMA((stores,)),
            ],
            compiler_params=pltpu.CompilerParams(vmem_limit_bytes=56 * MIB),
            cost_estimate=pl.CostEstimate(
                flops=0, bytes_accessed=2 * stores * sent_bytes, transcendentals=0
            ),
            name="pack_blocks",
        )(mig_dest, mig_block, part_scales, pool_rows)

    def swap(value, distance):
        return lax.ppermute(value, "inst", [(j, j ^ distance) for j in range(instances)])

    if general:
        send = pack(
            [CAP] * instances,
            [(r * instances + k, [(k, r)]) for k in range(instances) for r in range(CAP)],
        )
        arrived = [swap(send[k], k) for k in range(instances - 1, 0, -1)] + [send[0]]
        places = [(instances - 1 - k, r) for r in range(CAP) for k in range(instances)]
    else:
        any_second = CAP * instances
        (second,) = pack([1], [(any_second, [(0, 0)])])
        seconds = {0: second}
        bit = instances // 2
        while bit > 1:
            for k in list(seconds):
                seconds[k ^ bit] = swap(seconds[k], bit)
            bit //= 2
        mig_dest, second = lax.optimization_barrier((mig_dest, second))
        send = pack(
            [1, 2] + [1] * (instances - 2),
            [(k, [(k, 0)]) for k in list(range(instances))[::-1]] + [(any_second, [(1, 1)])],
        )
        firsts = [send[0]] + [swap(send[k], k) for k in range(1, instances)]
    part_scales, *send = lax.optimization_barrier((part_scales, *send))
    flat_scales = part_scales.reshape(2 * heads, pool).astype(f32)

    query_rows = (
        queries.reshape(requests, steps, heads, per_head, head_dim)
        .transpose(2, 0, 3, 1, 4)
        .reshape(heads, height, head_dim)
    )
    fresh_len = requests * steps
    fresh = new_kv.transpose(2, 3, 0, 1, 4).reshape(2, heads, fresh_len, head_dim)
    fresh = jnp.pad(fresh, ((0, 0), (0, 0), (0, -fresh_len % 128), (0, 0)))
    assert fresh.shape[2] == head_dim
    length = ctx_len[:, None]
    width = group * block_len
    chunks = pool // group
    tokens = pool * block_len

    mask_shapes = [(chunks, requests, width), (chunks, 2 * heads, width)]

    def own(head, *masks):
        shapes = [(height, head_dim)] * 3 + ([] if head else mask_shapes)
        return pl.pallas_call(
            functools.partial(
                own_kernel, (head, pool, heads, rows, steps, block_len, spans, factor, group)
            ),
            out_shape=[jax.ShapeDtypeStruct(shape, f32) for shape in shapes],
            in_specs=[VMEM_SPEC] * (3 + len(masks)),
            out_specs=[VMEM_SPEC] * len(shapes),
            scratch_shapes=[
                pltpu.VMEM((chunks, height, width), f32),
                pltpu.VMEM((height, width), bf16),
            ],
            compiler_params=pltpu.CompilerParams(vmem_limit_bytes=32 * MIB),
            cost_estimate=pl.CostEstimate(
                flops=4 * height * tokens * head_dim,
                bytes_accessed=pool_codes.size * 2 // heads,
                transcendentals=height * tokens,
            ),
            name="own_blocks",
        )(query_rows, fresh, pool_rows, *masks)

    *own_parts, log_rows, scale_rows = own(0, tables, length, flat_scales)
    if not general:
        seconds, own_parts, log_rows = lax.optimization_barrier((seconds, own_parts, log_rows))
    for head in range(1, heads):
        own_parts = own_parts + list(own(head, log_rows, scale_rows))

    if not general:
        held = {k: second for k, second in seconds.items() if k}
        for k in held:
            seconds[k ^ 1] = swap(held[k], 1)
        arrived = [held[k] for k in held] + firsts[::-1] + [seconds[0]]
        where = {k: i for i, k in enumerate(held)}
        where[0] = len(arrived) - 1
        places = [(len(held) + instances - 1 - k, 0) for k in range(instances)]
        for k in range(instances):
            if k == 1:
                places.append((places[1][0], 1))
            elif k in where:
                places.append((where[k], 0))
            else:
                places.append((len(arrived), 0))
                arrived.append(seconds[k])

    arrival_bytes = 6 * heads * height * slots * block_len + 2 * 12 * height * head_dim * heads
    arrival_bytes += 2 * slots * sent_bytes + 4 * requests * slots * block_len
    out, moved_to, more = pl.pallas_call(
        functools.partial(
            arrival_kernel, (pool, heads, rows, block_len, spans, listed, factor), places
        ),
        out_shape=[
            jax.ShapeDtypeStruct((requests, heads, rows, head_dim), bf16),
            jax.ShapeDtypeStruct((1, listed), jnp.int32),
            jax.ShapeDtypeStruct((1,), jnp.int32),
        ],
        in_specs=[VMEM_SPEC] * (3 + 3 * heads + len(arrived)),
        out_specs=[VMEM_SPEC, VMEM_SPEC, SMEM_SPEC],
        scratch_shapes=[
            pltpu.VMEM((requests, slots * block_len), f32),
            pltpu.VMEM((heads, height, slots * block_len), f32),
            pltpu.VMEM((heads, height, slots * block_len), bf16),
        ],
        compiler_params=pltpu.CompilerParams(vmem_limit_bytes=arrival_bytes + 8 * MIB),
        cost_estimate=pl.CostEstimate(
            flops=4 * heads * height * slots * block_len * head_dim,
            bytes_accessed=slots * sent_bytes,
            transcendentals=heads * height * slots * block_len,
        ),
        name="arrived_blocks",
    )(query_rows, tables, length, *own_parts, *arrived)
    out = out.reshape(requests, q_heads, steps, head_dim).transpose(0, 2, 1, 3)
    return out.reshape(requests, steps, q_heads * head_dim), moved_to, more


def shards(*args):
    out, moved_to, more = attend(False, *args)
    _, out = lax.while_loop(
        lambda state: state[0] > 1,
        lambda state: (jnp.int32(0), attend(True, *args)[0]),
        (more[0], out),
    )
    return out, moved_to


def solution(mesh):
    in_specs = (
        P(("groups", "inst"), None, "tp", None),
        P(("groups", "inst"), None, None, "tp", None),
        P(("groups", "inst"), None, "tp", None, None),
        P(("groups", "inst"), None, "tp"),
        P(("groups", "inst"), None),
        P(("groups", "inst")),
        P(("groups", "inst"), None),
        P(("groups", "inst"), None),
    )
    out_specs = (P(("groups", "inst"), None, "tp"), P(("groups", "inst"), None))
    return jax.shard_map(shards, mesh=mesh, in_specs=in_specs, out_specs=out_specs, check_vma=False)
```

```python
import functools
import math

import jax
import jax.numpy as jnp
from jax import lax
from jax.experimental import pallas as pl
from jax.experimental.pallas import tpu as pltpu
from jax.sharding import PartitionSpec as P

CAP = 2
EXTRA = 16
NEVER = -1e30
LOG2E = math.log2(math.e)
MIB = 1 << 20
SMEM_SPEC = pl.BlockSpec(memory_space=pltpu.SMEM)
VMEM_SPEC = pl.BlockSpec(memory_space=pltpu.VMEM)
HBM_SPEC = pl.BlockSpec(memory_space=pltpu.HBM)
NT = (((1,), (1,)), ((), ()))


def loop(count, body, init):
    if count <= 8:
        for i in range(count):
            init = body(i, init)
        return init
    return lax.fori_loop(0, count, body, init)


def pack_kernel(dims, dest_ref, block_ref, scale_ref, pool_ref, *refs):
    instances, listed, heads, pool, copies = dims
    send_refs, (index_ref, extra_ref, held_ref, in_sems, out_sems) = refs[:-5], refs[-5:]
    code_rows = held_ref.shape[1] - EXTRA
    me = lax.axis_index("inst")
    for entry in range(CAP * instances + 1):
        index_ref[entry] = 0

    def place(m, carry):
        dest = dest_ref[0, m]
        rank = loop(
            listed,
            lambda m2, n: n + jnp.where((dest_ref[0, m2] == dest) & (m2 < m), 1, 0),
            jnp.int32(0),
        )
        entry = jnp.bitwise_xor(dest, me) + jnp.where(rank > 0, instances, 0)
        index_ref[entry] = block_ref[0, m]
        index_ref[jnp.where(rank > 0, CAP * instances, entry)] = block_ref[0, m]
        return carry

    loop(listed, place, 0)
    loads, stores = [], []
    for i, (entry, _) in enumerate(copies):
        loads.append(
            pltpu.make_async_copy(
                pool_ref.at[index_ref[entry]], held_ref.at[i, pl.ds(0, code_rows)], in_sems.at[i]
            )
        )
        loads[i].start()
    lane = lax.broadcasted_iota(jnp.int32, (1, 128), 1)

    def spell(m, row):
        return jnp.where(lane == m, dest_ref[0, m].astype(jnp.float32), row)

    extra_ref[...] = jnp.zeros_like(extra_ref)
    extra_ref[2 * heads : 2 * heads + 1, :] = loop(
        listed, spell, jnp.zeros((1, 128), jnp.float32)
    )
    scales = [
        [scale_ref[part, h : h + 1, :].astype(jnp.float32) for h in range(heads)]
        for part in range(2)
    ]
    column = lax.broadcasted_iota(jnp.int32, (1, pool), 1)
    for i, (entry, _) in enumerate(copies):
        for part in range(2):
            for h in range(heads):
                one = jnp.where(column == index_ref[entry], scales[part][h], 0.0)
                row = part * heads + h
                extra_ref[row : row + 1, :] = jnp.broadcast_to(
                    jnp.sum(one, axis=1, keepdims=True), (1, 128)
                )
        held_ref[i, pl.ds(code_rows, EXTRA)] = extra_ref[...].astype(jnp.bfloat16)
    for i, (_, targets) in enumerate(copies):
        loads[i].wait()
        for output, row in targets:
            stores.append(
                pltpu.make_async_copy(
                    held_ref.at[i], send_refs[output].at[row], out_sems.at[len(stores)]
                )
            )
            stores[-1].start()
    for store in stores:
        store.wait()


def split(value, size):
    assert size & (size - 1) == 0
    return lax.shift_right_logical(value, size.bit_length() - 1), value & (size - 1)


def count_log(tables, length, ids, block_len, spans, store):
    requests, width = tables.shape[0], ids.shape[1]
    whole, rest = split(length, block_len)
    whole = jnp.broadcast_to(whole, (requests, width))
    full = jnp.zeros((requests, width), jnp.float32)
    part = jnp.zeros((requests, width), jnp.float32)
    for e in range(spans):
        hit = jnp.broadcast_to(tables[:, e : e + 1], (requests, width)) == ids
        full = full + jnp.where(hit & (whole > e), 1.0, 0.0)
        part = part + jnp.where(hit & (whole == e), 1.0, 0.0)

    def log2(count):
        return jnp.where(count > 0, jnp.log(jnp.maximum(count, 1.0)) * LOG2E, NEVER)

    beyond, within = log2(full), log2(full + part)
    shape = (requests, block_len)
    inside = lax.broadcasted_iota(jnp.int32, shape, 1) < jnp.broadcast_to(rest, shape)
    if width % 16:
        for b in range(width):
            store(
                b,
                jnp.where(
                    inside,
                    jnp.broadcast_to(within[:, b : b + 1], shape),
                    jnp.broadcast_to(beyond[:, b : b + 1], shape),
                ),
            )
        return
    both = jnp.concatenate([within, beyond], axis=0)
    high = both.astype(jnp.bfloat16)
    low = (both - high.astype(jnp.float32)).astype(jnp.bfloat16)
    terms = jnp.concatenate([high, low], axis=0)
    row = lax.broadcasted_iota(jnp.int32, (width, block_len), 0)
    for b in range(0, width, 2):
        spots = jnp.concatenate(
            [jnp.where(row == b + i, 1.0, 0.0).astype(jnp.bfloat16) for i in range(2)], axis=1
        )
        spread_out = jnp.dot(terms, spots, preferred_element_type=jnp.float32)
        value = spread_out[: 2 * requests] + spread_out[2 * requests :]
        for i in range(2):
            at = slice(i * block_len, (i + 1) * block_len)
            store(b + i, jnp.where(inside, value[:requests, at], value[requests:, at]))


def score_tiles(query, keys, log_ref, scale_row, rows, store):
    height, wide = min(256, query.shape[0]), min(256, keys.shape[0])
    for top in range(0, query.shape[0], height):
        for left in range(0, keys.shape[0], wide):
            part = lax.dot_general(
                query[top : top + height],
                keys[left : left + wide],
                NT,
                preferred_element_type=jnp.float32,
            )
            scale = scale_row[:, left : left + wide]
            for r in range(height // rows):
                request = top // rows + r
                store(
                    request * rows,
                    left,
                    part[r * rows : (r + 1) * rows] * scale
                    + log_ref[request : request + 1, left : left + wide],
                )


def lane_fold(value, op):
    parts = [value[:, i : i + 128] for i in range(0, value.shape[1], 128)]
    while len(parts) > 1:
        parts = [
            op(parts[i], parts[i + 1]) if i + 1 < len(parts) else parts[i]
            for i in range(0, len(parts), 2)
        ]
    return parts[0]


def spread(column, width):
    return jnp.concatenate([column] * (width // 128), axis=1)


def own_kernel(
    dims, q_ref, fresh_ref, pool_ref, *refs
):
    if dims[0] == 0:
        tables_ref, length_ref, scale_ref, acc_ref, top_ref, total_ref, log_ref, row_ref = refs[:8]
    else:
        log_ref, row_ref, acc_ref, top_ref, total_ref = refs[:5]
    t_ref, p_ref, codes_ref, sems = refs[-4:]
    head, pool, heads, rows, steps, block_len, spans, factor, group = dims
    chunks = pool // group
    height, head_dim = q_ref.shape[1:]
    width = group * block_len

    def load(part, chunk):
        return pltpu.make_async_copy(
            pool_ref.at[
                pl.ds(chunk * group, group), pl.ds((part * heads + head) * block_len, block_len)
            ],
            codes_ref.at[part, chunk],
            sems.at[part, chunk],
        )

    for part in range(2):
        for chunk in range(chunks):
            load(part, chunk).start()

    if head == 0:
        ids = lax.broadcasted_iota(jnp.int32, (1, pool), 1)

        def store_log(b, value):
            lane = (b % group) * block_len
            log_ref[b // group, :, lane : lane + block_len] = value

        count_log(tables_ref[...], length_ref[...], ids, block_len, spans, store_log)
        for b in range(pool):
            lane = (b % group) * block_len
            row_ref[b // group, :, lane : lane + block_len] = jnp.broadcast_to(
                scale_ref[:, b : b + 1], (2 * heads, block_len)
            )
    shape = (height, fresh_ref.shape[2])
    row = lax.broadcasted_iota(jnp.int32, shape, 0)
    col = lax.broadcasted_iota(jnp.int32, shape, 1)
    (request, row_step), (owner, step) = split(row, rows), split(col, steps)
    seen = (request == owner) & (split(row_step, steps)[1] >= step)
    new_score = lax.dot_general(
        q_ref[head], fresh_ref[0, head], NT, preferred_element_type=jnp.float32
    )
    new_score = jnp.where(seen, new_score * (factor * LOG2E), -jnp.inf)
    acc_ref[...] = new_score
    top_ref[...] = lane_fold(new_score, jnp.maximum)

    def score(chunk, carry):
        load(0, chunk).wait()

        def store(row, lane, value):
            at = pl.ds(row, rows)
            t_ref[chunk, at, lane : lane + value.shape[1]] = value
            top_ref[at] = jnp.maximum(top_ref[at], lane_fold(value, jnp.maximum))

        score_tiles(
            q_ref[head],
            codes_ref[0, chunk].reshape(width, head_dim),
            log_ref.at[chunk],
            row_ref[chunk, head : head + 1, :] * (factor * LOG2E),
            rows,
            store,
        )
        return carry

    lax.fori_loop(0, chunks, score, 0)

    top = jnp.broadcast_to(jnp.max(top_ref[...], axis=1, keepdims=True), (height, 128))
    top_ref[...] = top
    weight = jnp.exp2(acc_ref[...] - spread(top, acc_ref.shape[1]))
    total_ref[...] = lane_fold(weight, jnp.add)
    acc_ref[...] = jnp.dot(
        weight.astype(jnp.bfloat16), fresh_ref[1, head], preferred_element_type=jnp.float32
    )

    def apply(chunk, carry):
        load(1, chunk).wait()
        scale = row_ref[chunk, heads + head : heads + head + 1, :]
        tile = min(256, height)
        for start in range(0, height, tile):
            for row in range(start, start + tile, rows):
                at = pl.ds(row, rows)
                weight = jnp.exp2(t_ref[chunk, at] - spread(top_ref[at], width))
                total_ref[at] += lane_fold(weight, jnp.add)
                p_ref[at] = (weight * scale).astype(jnp.bfloat16)
            at = pl.ds(start, tile)
            acc_ref[at] += jnp.dot(
                p_ref[at], codes_ref[1, chunk].reshape(width, head_dim),
                preferred_element_type=jnp.float32,
            )
        return carry

    lax.fori_loop(0, chunks, apply, 0)


def arrival_ids(me, pool, lists, listed):
    instances = len(lists)
    lane = lax.broadcasted_iota(jnp.int32, (1, 128), 1)
    counts = [
        jnp.sum(
            jnp.where((row == me.astype(jnp.float32)) & (lane < listed), 1.0, 0.0),
            axis=1,
            keepdims=True,
        )
        for row in lists
    ]
    slot = lax.broadcasted_iota(jnp.int32, (1, instances * CAP), 1)
    ids = jnp.full(slot.shape, -1.0)
    for k in range(instances):
        first = jnp.full((1, 1), float(pool))
        for j in range(instances):
            lower = jnp.bitwise_xor(me, j) < jnp.bitwise_xor(me, k)
            first = first + jnp.where(lower, counts[j], 0.0)
        for r in range(CAP):
            name = jnp.where(counts[k] > r, first + r, -1.0)
            ids = jnp.where(slot == r * instances + k, jnp.broadcast_to(name, slot.shape), ids)
    moved = jnp.full((1, 128), float(pool))
    for j in range(instances):
        for m in range(listed):
            same = jnp.broadcast_to(lists[j][:, m : m + 1], (1, 128)) == lists[0]
            ahead = jnp.bitwise_xor(me, j) < me if j else lane > m
            moved = moved + jnp.where(same & ahead, 1.0, 0.0)
    more = jnp.zeros((1, 128))
    for row in lists:
        again = jnp.zeros((1, 128))
        for m in range(listed):
            same = jnp.broadcast_to(row[:, m : m + 1], (1, 128)) == row
            again = again + jnp.where(same & (lane > m) & (lane < listed), 1.0, 0.0)
        more = jnp.maximum(more, jnp.sum(again, axis=1, keepdims=True))
    return ids.astype(jnp.int32), moved[:, :listed].astype(jnp.int32), more


def arrival_kernel(dims, places, q_ref, tables_ref, length_ref, *refs):
    pool, heads, rows, block_len, spans, listed, factor = dims
    own_refs, code_refs = refs[: 3 * heads], refs[3 * heads : -6]
    out_ref, moved_ref, more_ref, log_ref, t_ref, p_ref = refs[-6:]
    height = q_ref.shape[1]
    width = 2 * block_len
    extra = 2 * heads * block_len
    slots = [(code_refs[array], row) for array, row in places]
    pairs = len(slots) // 2

    def pair(i, part, h):
        at = pl.ds((part * heads + h) * block_len, block_len)
        return jnp.concatenate([ref[r, at] for ref, r in slots[2 * i : 2 * i + 2]], axis=0)

    lists, scale_rows = [], []
    for ref, r in slots:
        values = ref[r, pl.ds(extra, EXTRA)].astype(jnp.float32)
        scale_rows.append(values)
        if len(lists) < len(slots) // CAP:
            lists.append(values[2 * heads : 2 * heads + 1])

    def scale_row(row):
        return jnp.concatenate([values[row : row + 1] for values in scale_rows], axis=1)

    ids, moved_ref[...], more = arrival_ids(lax.axis_index("inst"), pool, lists, listed)
    more_ref[0] = jnp.max(more).astype(jnp.int32)

    def store_log(b, value):
        log_ref[:, b * block_len : (b + 1) * block_len] = value

    count_log(tables_ref[...], length_ref[...], ids, block_len, spans, store_log)
    for h in range(heads):
        key_scale = scale_row(h) * (factor * LOG2E)
        for i in range(pairs):
            left = i * width

            def store(row, lane, value, h=h, left=left):
                t_ref[h, row : row + rows, left + lane : left + lane + value.shape[1]] = value

            score_tiles(
                q_ref[h],
                pair(i, 0, h),
                log_ref.at[:, left : left + width],
                key_scale[:, left : left + width],
                rows,
                store,
            )
    for h in range(heads):
        acc_ref, top_ref, total_ref = own_refs[3 * h : 3 * h + 3]
        scale = scale_row(heads + h)
        for row in range(0, height, rows):
            at = pl.ds(row, rows)
            score = t_ref[h, at]
            own_top = top_ref[at]
            top = jnp.maximum(
                own_top, jnp.max(lane_fold(score, jnp.maximum), axis=1, keepdims=True)
            )
            weight = jnp.exp2(score - spread(top, score.shape[1]))
            keep = jnp.exp2(own_top - top)
            total = jnp.sum(
                total_ref[at] * keep + lane_fold(weight, jnp.add), axis=1, keepdims=True
            )
            p_ref[h, at] = (weight * scale).astype(jnp.bfloat16)
            t_ref[h, at, 0:128] = keep
            t_ref[h, at, 128:256] = jnp.broadcast_to(1.0 / total, keep.shape)
        mixed = acc_ref[...] * t_ref[h, :, 0:128]
        for i in range(pairs):
            mixed = mixed + jnp.dot(
                p_ref[h, :, i * width : (i + 1) * width],
                pair(i, 1, h),
                preferred_element_type=jnp.float32,
            )
        result = (mixed * t_ref[h, :, 128:256]).astype(jnp.bfloat16)
        out_ref[:, h] = result.reshape(height // rows, rows, result.shape[-1])


def attend(
    general, queries, new_kv, pool_codes, pool_scales, tables, ctx_len, mig_block, mig_dest
):
    instances = lax.axis_size("inst")
    pool = pool_codes.shape[0]
    requests, steps, q_heads, head_dim = queries.shape
    heads = new_kv.shape[3]
    per_head = q_heads // heads
    spans = tables.shape[1]
    block_len = pool_codes.shape[3]
    listed = mig_dest.shape[1]
    factor = head_dim ** (-0.5)
    rows = per_head * steps
    height = requests * rows
    slots = instances * CAP
    group = 16
    f32, bf16 = jnp.float32, jnp.bfloat16
    code_rows = 2 * heads * block_len
    pool_rows = pool_codes.reshape(pool, code_rows, head_dim)
    sent_shape = (code_rows + EXTRA, head_dim)
    sent_bytes = 2 * math.prod(sent_shape)
    part_scales = jnp.transpose(pool_scales, (1, 2, 0))
    assert instances & (instances - 1) == 0 and 2 * heads < EXTRA and head_dim == 128

    def pack(sizes, copies):
        stores = sum(len(targets) for _, targets in copies)
        return pl.pallas_call(
            functools.partial(pack_kernel, (instances, listed, heads, pool, copies)),
            out_shape=[jax.ShapeDtypeStruct((size,) + sent_shape, bf16) for size in sizes],
            in_specs=[SMEM_SPEC, SMEM_SPEC, VMEM_SPEC, HBM_SPEC],
            out_specs=[HBM_SPEC] * len(sizes),
            scratch_shapes=[
                pltpu.SMEM((CAP * instances + 1,), jnp.int32),
                pltpu.VMEM((EXTRA, head_dim), f32),
                pltpu.VMEM((len(copies),) + sent_shape, bf16),
                pltpu.SemaphoreType.DMA((len(copies),)),
                pltpu.SemaphoreType.DMA((stores,)),
            ],
            compiler_params=pltpu.CompilerParams(vmem_limit_bytes=56 * MIB),
            cost_estimate=pl.CostEstimate(
                flops=0, bytes_accessed=2 * stores * sent_bytes, transcendentals=0
            ),
            name="pack_blocks",
        )(mig_dest, mig_block, part_scales, pool_rows)

    def swap(value, distance):
        return lax.ppermute(value, "inst", [(j, j ^ distance) for j in range(instances)])

    if general:
        send = pack(
            [CAP] * instances,
            [(r * instances + k, [(k, r)]) for k in range(instances) for r in range(CAP)],
        )
        arrived = [swap(send[k], k) for k in range(instances - 1, 0, -1)] + [send[0]]
        places = [(instances - 1 - k, r) for r in range(CAP) for k in range(instances)]
    else:
        any_second = CAP * instances
        (second,) = pack([1], [(any_second, [(0, 0)])])
        seconds = {0: second}
        bit = instances // 2
        while bit > 1:
            for k in list(seconds):
                seconds[k ^ bit] = swap(seconds[k], bit)
            bit //= 2
        mig_dest, second = lax.optimization_barrier((mig_dest, second))
        send = pack(
            [1, 2] + [1] * (instances - 2),
            [(k, [(k, 0)]) for k in list(range(instances))[::-1]] + [(any_second, [(1, 1)])],
        )
        firsts = [send[0]] + [swap(send[k], k) for k in range(1, instances)]
    part_scales, *send = lax.optimization_barrier((part_scales, *send))
    flat_scales = part_scales.reshape(2 * heads, pool).astype(f32)

    query_rows = (
        queries.reshape(requests, steps, heads, per_head, head_dim)
        .transpose(2, 0, 3, 1, 4)
        .reshape(heads, height, head_dim)
    )
    fresh_len = requests * steps
    fresh = new_kv.transpose(2, 3, 0, 1, 4).reshape(2, heads, fresh_len, head_dim)
    fresh = jnp.pad(fresh, ((0, 0), (0, 0), (0, -fresh_len % 128), (0, 0)))
    assert fresh.shape[2] == head_dim
    length = ctx_len[:, None]
    width = group * block_len
    chunks = pool // group
    tokens = pool * block_len

    mask_shapes = [(chunks, requests, width), (chunks, 2 * heads, width)]

    def own(head, *masks):
        shapes = [(height, head_dim)] * 3 + ([] if head else mask_shapes)
        return pl.pallas_call(
            functools.partial(
                own_kernel, (head, pool, heads, rows, steps, block_len, spans, factor, group)
            ),
            out_shape=[jax.ShapeDtypeStruct(shape, f32) for shape in shapes],
            in_specs=[VMEM_SPEC, VMEM_SPEC, HBM_SPEC] + [VMEM_SPEC] * len(masks),
            out_specs=[VMEM_SPEC] * len(shapes),
            scratch_shapes=[
                pltpu.VMEM((chunks, height, width), f32),
                pltpu.VMEM((height, width), bf16),
                pltpu.VMEM((2, chunks, group, block_len, head_dim), bf16),
                pltpu.SemaphoreType.DMA((2, chunks)),
            ],
            compiler_params=pltpu.CompilerParams(vmem_limit_bytes=32 * MIB),
            cost_estimate=pl.CostEstimate(
                flops=4 * height * tokens * head_dim,
                bytes_accessed=pool_codes.size * 2 // heads,
                transcendentals=height * tokens,
            ),
            name="own_blocks",
        )(query_rows, fresh, pool_rows, *masks)

    *own_parts, log_rows, scale_rows = own(0, tables, length, flat_scales)
    if not general:
        seconds, own_parts, log_rows = lax.optimization_barrier((seconds, own_parts, log_rows))
    for head in range(1, heads):
        own_parts = own_parts + list(own(head, log_rows, scale_rows))

    if not general:
        held = {k: second for k, second in seconds.items() if k}
        for k in held:
            seconds[k ^ 1] = swap(held[k], 1)
        arrived = [held[k] for k in held] + firsts[::-1] + [seconds[0]]
        where = {k: i for i, k in enumerate(held)}
        where[0] = len(arrived) - 1
        places = [(len(held) + instances - 1 - k, 0) for k in range(instances)]
        for k in range(instances):
            if k == 1:
                places.append((places[1][0], 1))
            elif k in where:
                places.append((where[k], 0))
            else:
                places.append((len(arrived), 0))
                arrived.append(seconds[k])

    arrival_bytes = 6 * heads * height * slots * block_len + 2 * 12 * height * head_dim * heads
    arrival_bytes += 2 * slots * sent_bytes + 4 * requests * slots * block_len
    out, moved_to, more = pl.pallas_call(
        functools.partial(
            arrival_kernel, (pool, heads, rows, block_len, spans, listed, factor), places
        ),
        out_shape=[
            jax.ShapeDtypeStruct((requests, heads, rows, head_dim), bf16),
            jax.ShapeDtypeStruct((1, listed), jnp.int32),
            jax.ShapeDtypeStruct((1,), jnp.int32),
        ],
        in_specs=[VMEM_SPEC] * (3 + 3 * heads + len(arrived)),
        out_specs=[VMEM_SPEC, VMEM_SPEC, SMEM_SPEC],
        scratch_shapes=[
            pltpu.VMEM((requests, slots * block_len), f32),
            pltpu.VMEM((heads, height, slots * block_len), f32),
            pltpu.VMEM((heads, height, slots * block_len), bf16),
        ],
        compiler_params=pltpu.CompilerParams(vmem_limit_bytes=arrival_bytes + 8 * MIB),
        cost_estimate=pl.CostEstimate(
            flops=4 * heads * height * slots * block_len * head_dim,
            bytes_accessed=slots * sent_bytes,
            transcendentals=heads * height * slots * block_len,
        ),
        name="arrived_blocks",
    )(query_rows, tables, length, *own_parts, *arrived)
    out = out.reshape(requests, q_heads, steps, head_dim).transpose(0, 2, 1, 3)
    return out.reshape(requests, steps, q_heads * head_dim), moved_to, more


def shards(*args):
    out, moved_to, more = attend(False, *args)
    _, out = lax.while_loop(
        lambda state: state[0] > 1,
        lambda state: (jnp.int32(0), attend(True, *args)[0]),
        (more[0], out),
    )
    return out, moved_to


def solution(mesh):
    in_specs = (
        P(("groups", "inst"), None, "tp", None),
        P(("groups", "inst"), None, None, "tp", None),
        P(("groups", "inst"), None, "tp", None, None),
        P(("groups", "inst"), None, "tp"),
        P(("groups", "inst"), None),
        P(("groups", "inst")),
        P(("groups", "inst"), None),
        P(("groups", "inst"), None),
    )
    out_specs = (P(("groups", "inst"), None, "tp"), P(("groups", "inst"), None))
    return jax.shard_map(shards, mesh=mesh, in_specs=in_specs, out_specs=out_specs, check_vma=False)
```

```python
import functools
import math

import jax
import jax.numpy as jnp
from jax import lax
from jax.experimental import pallas as pl
from jax.experimental.pallas import tpu as pltpu
from jax.sharding import PartitionSpec as P

CAP = 2
EXTRA = 16
NEVER = -1e30
LOG2E = math.log2(math.e)
MIB = 1 << 20
SMEM_SPEC = pl.BlockSpec(memory_space=pltpu.SMEM)
VMEM_SPEC = pl.BlockSpec(memory_space=pltpu.VMEM)
HBM_SPEC = pl.BlockSpec(memory_space=pltpu.HBM)
NT = (((1,), (1,)), ((), ()))


def loop(count, body, init):
    if count <= 8:
        for i in range(count):
            init = body(i, init)
        return init
    return lax.fori_loop(0, count, body, init)


def pack_kernel(dims, dest_ref, block_ref, scale_ref, pool_ref, *refs):
    instances, listed, heads, pool, copies = dims
    send_refs, (index_ref, extra_ref, held_ref, in_sems, out_sems) = refs[:-5], refs[-5:]
    code_rows = held_ref.shape[1] - EXTRA
    me = lax.axis_index("inst")
    for entry in range(CAP * instances + 1):
        index_ref[entry] = 0

    def place(m, carry):
        dest = dest_ref[0, m]
        rank = loop(
            listed,
            lambda m2, n: n + jnp.where((dest_ref[0, m2] == dest) & (m2 < m), 1, 0),
            jnp.int32(0),
        )
        entry = jnp.bitwise_xor(dest, me) + jnp.where(rank > 0, instances, 0)
        index_ref[entry] = block_ref[0, m]
        index_ref[jnp.where(rank > 0, CAP * instances, entry)] = block_ref[0, m]
        return carry

    loop(listed, place, 0)
    loads, stores = [], []
    for i, (entry, _) in enumerate(copies):
        loads.append(
            pltpu.make_async_copy(
                pool_ref.at[index_ref[entry]], held_ref.at[i, pl.ds(0, code_rows)], in_sems.at[i]
            )
        )
        loads[i].start()
    lane = lax.broadcasted_iota(jnp.int32, (1, 128), 1)

    def spell(m, row):
        return jnp.where(lane == m, dest_ref[0, m].astype(jnp.float32), row)

    extra_ref[...] = jnp.zeros_like(extra_ref)
    extra_ref[2 * heads : 2 * heads + 1, :] = loop(
        listed, spell, jnp.zeros((1, 128), jnp.float32)
    )
    scales = [
        [scale_ref[part, h : h + 1, :].astype(jnp.float32) for h in range(heads)]
        for part in range(2)
    ]
    column = lax.broadcasted_iota(jnp.int32, (1, pool), 1)
    for i, (entry, _) in enumerate(copies):
        for part in range(2):
            for h in range(heads):
                one = jnp.where(column == index_ref[entry], scales[part][h], 0.0)
                row = part * heads + h
                extra_ref[row : row + 1, :] = jnp.broadcast_to(
                    jnp.sum(one, axis=1, keepdims=True), (1, 128)
                )
        held_ref[i, pl.ds(code_rows, EXTRA)] = extra_ref[...].astype(jnp.bfloat16)
    for i, (_, targets) in enumerate(copies):
        loads[i].wait()
        for output, row in targets:
            stores.append(
                pltpu.make_async_copy(
                    held_ref.at[i], send_refs[output].at[row], out_sems.at[len(stores)]
                )
            )
            stores[-1].start()
    for store in stores:
        store.wait()


def split(value, size):
    assert size & (size - 1) == 0
    return lax.shift_right_logical(value, size.bit_length() - 1), value & (size - 1)


def count_log(tables, length, ids, block_len, spans, store):
    requests, width = tables.shape[0], ids.shape[1]
    whole, rest = split(length, block_len)
    whole = jnp.broadcast_to(whole, (requests, width))
    full = jnp.zeros((requests, width), jnp.float32)
    part = jnp.zeros((requests, width), jnp.float32)
    for e in range(spans):
        hit = jnp.broadcast_to(tables[:, e : e + 1], (requests, width)) == ids
        full = full + jnp.where(hit & (whole > e), 1.0, 0.0)
        part = part + jnp.where(hit & (whole == e), 1.0, 0.0)

    def log2(count):
        return jnp.where(count > 0, jnp.log(jnp.maximum(count, 1.0)) * LOG2E, NEVER)

    beyond, within = log2(full), log2(full + part)
    shape = (requests, block_len)
    inside = lax.broadcasted_iota(jnp.int32, shape, 1) < jnp.broadcast_to(rest, shape)
    if width % 16:
        for b in range(width):
            store(
                b,
                jnp.where(
                    inside,
                    jnp.broadcast_to(within[:, b : b + 1], shape),
                    jnp.broadcast_to(beyond[:, b : b + 1], shape),
                ),
            )
        return
    both = jnp.concatenate([within, beyond], axis=0)
    high = both.astype(jnp.bfloat16)
    low = (both - high.astype(jnp.float32)).astype(jnp.bfloat16)
    terms = jnp.concatenate([high, low], axis=0)
    row = lax.broadcasted_iota(jnp.int32, (width, block_len), 0)
    for b in range(0, width, 2):
        spots = jnp.concatenate(
            [jnp.where(row == b + i, 1.0, 0.0).astype(jnp.bfloat16) for i in range(2)], axis=1
        )
        spread_out = jnp.dot(terms, spots, preferred_element_type=jnp.float32)
        value = spread_out[: 2 * requests] + spread_out[2 * requests :]
        for i in range(2):
            at = slice(i * block_len, (i + 1) * block_len)
            store(b + i, jnp.where(inside, value[:requests, at], value[requests:, at]))


def score_tiles(query, keys, log_ref, scale_row, rows, store):
    height, wide = min(256, query.shape[0]), min(256, keys.shape[0])
    for top in range(0, query.shape[0], height):
        for left in range(0, keys.shape[0], wide):
            part = lax.dot_general(
                query[top : top + height],
                keys[left : left + wide],
                NT,
                preferred_element_type=jnp.float32,
            )
            scale = scale_row[:, left : left + wide]
            for r in range(height // rows):
                request = top // rows + r
                store(
                    request * rows,
                    left,
                    part[r * rows : (r + 1) * rows] * scale
                    + log_ref[request : request + 1, left : left + wide],
                )


def lane_fold(value, op):
    parts = [value[:, i : i + 128] for i in range(0, value.shape[1], 128)]
    while len(parts) > 1:
        parts = [
            op(parts[i], parts[i + 1]) if i + 1 < len(parts) else parts[i]
            for i in range(0, len(parts), 2)
        ]
    return parts[0]


def spread(column, width):
    return jnp.concatenate([column] * (width // 128), axis=1)


def own_kernel(
    dims, q_ref, fresh_ref, pool_ref, *refs
):
    if dims[0] == 0:
        tables_ref, length_ref, scale_ref, acc_ref, top_ref, total_ref, log_ref, row_ref = refs[:8]
    else:
        log_ref, row_ref, acc_ref, top_ref, total_ref = refs[:5]
    t_ref, p_ref, codes_ref, sems = refs[-4:]
    head, pool, heads, rows, steps, block_len, spans, factor, group = dims
    chunks = pool // group
    height, head_dim = q_ref.shape[1:]
    width = group * block_len

    def arrival(part, chunk):
        return pltpu.make_async_copy(
            pool_ref.at[
                pl.ds(chunk * group, group), pl.ds((part * heads + head) * block_len, block_len)
            ],
            codes_ref.at[part, chunk],
            sems.at[part, chunk],
        )

    def start_copies(part):
        for b in range(pool):
            pltpu.make_async_copy(
                pool_ref.at[b, pl.ds((part * heads + head) * block_len, block_len)],
                codes_ref.at[part, b // group, b % group],
                sems.at[part, b // group],
            ).start()

    start_copies(0)
    start_copies(1)

    if head == 0:
        ids = lax.broadcasted_iota(jnp.int32, (1, pool), 1)

        def store_log(b, value):
            lane = (b % group) * block_len
            log_ref[b // group, :, lane : lane + block_len] = value

        count_log(tables_ref[...], length_ref[...], ids, block_len, spans, store_log)
        for b in range(pool):
            lane = (b % group) * block_len
            row_ref[b // group, :, lane : lane + block_len] = jnp.broadcast_to(
                scale_ref[:, b : b + 1], (2 * heads, block_len)
            )
    shape = (height, fresh_ref.shape[2])
    row = lax.broadcasted_iota(jnp.int32, shape, 0)
    col = lax.broadcasted_iota(jnp.int32, shape, 1)
    (request, row_step), (owner, step) = split(row, rows), split(col, steps)
    seen = (request == owner) & (split(row_step, steps)[1] >= step)
    new_score = lax.dot_general(
        q_ref[head], fresh_ref[0, head], NT, preferred_element_type=jnp.float32
    )
    new_score = jnp.where(seen, new_score * (factor * LOG2E), -jnp.inf)
    acc_ref[...] = new_score
    top_ref[...] = lane_fold(new_score, jnp.maximum)

    def score(chunk, carry):
        arrival(0, chunk).wait()

        def store(row, lane, value):
            t_ref[chunk, row : row + rows, lane : lane + value.shape[1]] = value

        score_tiles(
            q_ref[head],
            codes_ref[0, chunk].reshape(width, head_dim),
            log_ref.at[chunk],
            row_ref[chunk, head : head + 1, :] * (factor * LOG2E),
            rows,
            store,
        )
        for row in range(0, height, rows):
            at = pl.ds(row, rows)
            top_ref[at] = jnp.maximum(top_ref[at], lane_fold(t_ref[chunk, at], jnp.maximum))
        return carry

    lax.fori_loop(0, chunks, score, 0)

    top = jnp.broadcast_to(jnp.max(top_ref[...], axis=1, keepdims=True), (height, 128))
    top_ref[...] = top
    weight = jnp.exp2(acc_ref[...] - spread(top, acc_ref.shape[1]))
    total_ref[...] = lane_fold(weight, jnp.add)
    acc_ref[...] = jnp.dot(
        weight.astype(jnp.bfloat16), fresh_ref[1, head], preferred_element_type=jnp.float32
    )

    def apply(chunk, carry):
        arrival(1, chunk).wait()
        scale = row_ref[chunk, heads + head : heads + head + 1, :]
        for row in range(0, height, rows):
            at = pl.ds(row, rows)
            weight = jnp.exp2(t_ref[chunk, at] - spread(top_ref[at], width))
            total_ref[at] += lane_fold(weight, jnp.add)
            p_ref[at] = (weight * scale).astype(jnp.bfloat16)
        acc_ref[...] += jnp.dot(
            p_ref[...],
            codes_ref[1, chunk].reshape(width, head_dim),
            preferred_element_type=jnp.float32,
        )
        return carry

    lax.fori_loop(0, chunks, apply, 0)


def arrival_ids(me, pool, lists, listed):
    instances = len(lists)
    lane = lax.broadcasted_iota(jnp.int32, (1, 128), 1)
    counts = [
        jnp.sum(
            jnp.where((row == me.astype(jnp.float32)) & (lane < listed), 1.0, 0.0),
            axis=1,
            keepdims=True,
        )
        for row in lists
    ]
    slot = lax.broadcasted_iota(jnp.int32, (1, instances * CAP), 1)
    ids = jnp.full(slot.shape, -1.0)
    for k in range(instances):
        first = jnp.full((1, 1), float(pool))
        for j in range(instances):
            lower = jnp.bitwise_xor(me, j) < jnp.bitwise_xor(me, k)
            first = first + jnp.where(lower, counts[j], 0.0)
        for r in range(CAP):
            name = jnp.where(counts[k] > r, first + r, -1.0)
            ids = jnp.where(slot == r * instances + k, jnp.broadcast_to(name, slot.shape), ids)
    moved = jnp.full((1, 128), float(pool))
    for j in range(instances):
        for m in range(listed):
            same = jnp.broadcast_to(lists[j][:, m : m + 1], (1, 128)) == lists[0]
            ahead = jnp.bitwise_xor(me, j) < me if j else lane > m
            moved = moved + jnp.where(same & ahead, 1.0, 0.0)
    more = jnp.zeros((1, 128))
    for row in lists:
        again = jnp.zeros((1, 128))
        for m in range(listed):
            same = jnp.broadcast_to(row[:, m : m + 1], (1, 128)) == row
            again = again + jnp.where(same & (lane > m) & (lane < listed), 1.0, 0.0)
        more = jnp.maximum(more, jnp.sum(again, axis=1, keepdims=True))
    return ids.astype(jnp.int32), moved[:, :listed].astype(jnp.int32), more


def arrival_kernel(dims, places, q_ref, tables_ref, length_ref, *refs):
    pool, heads, rows, block_len, spans, listed, factor = dims
    own_refs, code_refs = refs[: 3 * heads], refs[3 * heads : -6]
    out_ref, moved_ref, more_ref, log_ref, t_ref, p_ref = refs[-6:]
    height = q_ref.shape[1]
    width = 2 * block_len
    extra = 2 * heads * block_len
    slots = [(code_refs[array], row) for array, row in places]
    pairs = len(slots) // 2

    def pair(i, part, h):
        at = pl.ds((part * heads + h) * block_len, block_len)
        return jnp.concatenate([ref[r, at] for ref, r in slots[2 * i : 2 * i + 2]], axis=0)

    lists, scale_rows = [], []
    for ref, r in slots:
        values = ref[r, pl.ds(extra, EXTRA)].astype(jnp.float32)
        scale_rows.append(values)
        if len(lists) < len(slots) // CAP:
            lists.append(values[2 * heads : 2 * heads + 1])

    def scale_row(row):
        return jnp.concatenate([values[row : row + 1] for values in scale_rows], axis=1)

    ids, moved_ref[...], more = arrival_ids(lax.axis_index("inst"), pool, lists, listed)
    more_ref[0] = jnp.max(more).astype(jnp.int32)

    def store_log(b, value):
        log_ref[:, b * block_len : (b + 1) * block_len] = value

    count_log(tables_ref[...], length_ref[...], ids, block_len, spans, store_log)
    for h in range(heads):
        key_scale = scale_row(h) * (factor * LOG2E)
        for i in range(pairs):
            left = i * width

            def store(row, lane, value, h=h, left=left):
                t_ref[h, row : row + rows, left + lane : left + lane + value.shape[1]] = value

            score_tiles(
                q_ref[h],
                pair(i, 0, h),
                log_ref.at[:, left : left + width],
                key_scale[:, left : left + width],
                rows,
                store,
            )
    for h in range(heads):
        acc_ref, top_ref, total_ref = own_refs[3 * h : 3 * h + 3]
        scale = scale_row(heads + h)
        for row in range(0, height, rows):
            at = pl.ds(row, rows)
            score = t_ref[h, at]
            own_top = top_ref[at]
            top = jnp.maximum(
                own_top, jnp.max(lane_fold(score, jnp.maximum), axis=1, keepdims=True)
            )
            weight = jnp.exp2(score - spread(top, score.shape[1]))
            keep = jnp.exp2(own_top - top)
            total = jnp.sum(
                total_ref[at] * keep + lane_fold(weight, jnp.add), axis=1, keepdims=True
            )
            p_ref[h, at] = (weight * scale).astype(jnp.bfloat16)
            t_ref[h, at, 0:128] = keep
            t_ref[h, at, 128:256] = jnp.broadcast_to(1.0 / total, keep.shape)
        mixed = acc_ref[...] * t_ref[h, :, 0:128]
        for i in range(pairs):
            mixed = mixed + jnp.dot(
                p_ref[h, :, i * width : (i + 1) * width],
                pair(i, 1, h),
                preferred_element_type=jnp.float32,
            )
        result = (mixed * t_ref[h, :, 128:256]).astype(jnp.bfloat16)
        out_ref[:, h] = result.reshape(height // rows, rows, result.shape[-1])


def attend(
    general, queries, new_kv, pool_codes, pool_scales, tables, ctx_len, mig_block, mig_dest
):
    instances = lax.axis_size("inst")
    pool = pool_codes.shape[0]
    requests, steps, q_heads, head_dim = queries.shape
    heads = new_kv.shape[3]
    per_head = q_heads // heads
    spans = tables.shape[1]
    block_len = pool_codes.shape[3]
    listed = mig_dest.shape[1]
    factor = head_dim ** (-0.5)
    rows = per_head * steps
    height = requests * rows
    slots = instances * CAP
    group = 16
    f32, bf16 = jnp.float32, jnp.bfloat16
    code_rows = 2 * heads * block_len
    pool_rows = pool_codes.reshape(pool, code_rows, head_dim)
    sent_shape = (code_rows + EXTRA, head_dim)
    sent_bytes = 2 * math.prod(sent_shape)
    part_scales = jnp.transpose(pool_scales, (1, 2, 0))
    assert instances & (instances - 1) == 0 and 2 * heads < EXTRA and head_dim == 128

    def pack(sizes, copies):
        stores = sum(len(targets) for _, targets in copies)
        return pl.pallas_call(
            functools.partial(pack_kernel, (instances, listed, heads, pool, copies)),
            out_shape=[jax.ShapeDtypeStruct((size,) + sent_shape, bf16) for size in sizes],
            in_specs=[SMEM_SPEC, SMEM_SPEC, VMEM_SPEC, HBM_SPEC],
            out_specs=[HBM_SPEC] * len(sizes),
            scratch_shapes=[
                pltpu.SMEM((CAP * instances + 1,), jnp.int32),
                pltpu.VMEM((EXTRA, head_dim), f32),
                pltpu.VMEM((len(copies),) + sent_shape, bf16),
                pltpu.SemaphoreType.DMA((len(copies),)),
                pltpu.SemaphoreType.DMA((stores,)),
            ],
            compiler_params=pltpu.CompilerParams(vmem_limit_bytes=56 * MIB),
            cost_estimate=pl.CostEstimate(
                flops=0, bytes_accessed=2 * stores * sent_bytes, transcendentals=0
            ),
            name="pack_blocks",
        )(mig_dest, mig_block, part_scales, pool_rows)

    def swap(value, distance):
        return lax.ppermute(value, "inst", [(j, j ^ distance) for j in range(instances)])

    if general:
        send = pack(
            [CAP] * instances,
            [(r * instances + k, [(k, r)]) for k in range(instances) for r in range(CAP)],
        )
        arrived = [swap(send[k], k) for k in range(instances - 1, 0, -1)] + [send[0]]
        places = [(instances - 1 - k, r) for r in range(CAP) for k in range(instances)]
    else:
        any_second = CAP * instances
        (second,) = pack([1], [(any_second, [(0, 0)])])
        seconds = {0: second}
        bit = instances // 2
        while bit > 1:
            for k in list(seconds):
                seconds[k ^ bit] = swap(seconds[k], bit)
            bit //= 2
        mig_dest, second = lax.optimization_barrier((mig_dest, second))
        send = pack(
            [1, 2] + [1] * (instances - 2),
            [(k, [(k, 0)]) for k in list(range(instances))[::-1]] + [(any_second, [(1, 1)])],
        )
        firsts = [send[0]] + [swap(send[k], k) for k in range(1, instances)]
    part_scales, *send = lax.optimization_barrier((part_scales, *send))
    flat_scales = part_scales.reshape(2 * heads, pool).astype(f32)

    query_rows = (
        queries.reshape(requests, steps, heads, per_head, head_dim)
        .transpose(2, 0, 3, 1, 4)
        .reshape(heads, height, head_dim)
    )
    fresh_len = requests * steps
    fresh = new_kv.transpose(2, 3, 0, 1, 4).reshape(2, heads, fresh_len, head_dim)
    fresh = jnp.pad(fresh, ((0, 0), (0, 0), (0, -fresh_len % 128), (0, 0)))
    assert fresh.shape[2] == head_dim
    length = ctx_len[:, None]
    width = group * block_len
    chunks = pool // group
    tokens = pool * block_len

    mask_shapes = [(chunks, requests, width), (chunks, 2 * heads, width)]

    def own(head, *masks):
        shapes = [(height, head_dim)] * 3 + ([] if head else mask_shapes)
        return pl.pallas_call(
            functools.partial(
                own_kernel, (head, pool, heads, rows, steps, block_len, spans, factor, group)
            ),
            out_shape=[jax.ShapeDtypeStruct(shape, f32) for shape in shapes],
            in_specs=[VMEM_SPEC, VMEM_SPEC, HBM_SPEC] + [VMEM_SPEC] * len(masks),
            out_specs=[VMEM_SPEC] * len(shapes),
            scratch_shapes=[
                pltpu.VMEM((chunks, height, width), f32),
                pltpu.VMEM((height, width), bf16),
                pltpu.VMEM((2, chunks, group, block_len, head_dim), bf16),
                pltpu.SemaphoreType.DMA((2, chunks)),
            ],
            compiler_params=pltpu.CompilerParams(vmem_limit_bytes=32 * MIB),
            cost_estimate=pl.CostEstimate(
                flops=4 * height * tokens * head_dim,
                bytes_accessed=pool_codes.size * 2 // heads,
                transcendentals=height * tokens,
            ),
            name="own_blocks",
        )(query_rows, fresh, pool_rows, *masks)

    *own_parts, log_rows, scale_rows = own(0, tables, length, flat_scales)
    if not general:
        seconds, own_parts, log_rows = lax.optimization_barrier((seconds, own_parts, log_rows))
    for head in range(1, heads):
        own_parts = own_parts + list(own(head, log_rows, scale_rows))

    if not general:
        held = {k: second for k, second in seconds.items() if k}
        for k in held:
            seconds[k ^ 1] = swap(held[k], 1)
        arrived = [held[k] for k in held] + firsts[::-1] + [seconds[0]]
        where = {k: i for i, k in enumerate(held)}
        where[0] = len(arrived) - 1
        places = [(len(held) + instances - 1 - k, 0) for k in range(instances)]
        for k in range(instances):
            if k == 1:
                places.append((places[1][0], 1))
            elif k in where:
                places.append((where[k], 0))
            else:
                places.append((len(arrived), 0))
                arrived.append(seconds[k])

    arrival_bytes = 6 * heads * height * slots * block_len + 2 * 12 * height * head_dim * heads
    arrival_bytes += 2 * slots * sent_bytes + 4 * requests * slots * block_len
    out, moved_to, more = pl.pallas_call(
        functools.partial(
            arrival_kernel, (pool, heads, rows, block_len, spans, listed, factor), places
        ),
        out_shape=[
            jax.ShapeDtypeStruct((requests, heads, rows, head_dim), bf16),
            jax.ShapeDtypeStruct((1, listed), jnp.int32),
            jax.ShapeDtypeStruct((1,), jnp.int32),
        ],
        in_specs=[VMEM_SPEC] * (3 + 3 * heads + len(arrived)),
        out_specs=[VMEM_SPEC, VMEM_SPEC, SMEM_SPEC],
        scratch_shapes=[
            pltpu.VMEM((requests, slots * block_len), f32),
            pltpu.VMEM((heads, height, slots * block_len), f32),
            pltpu.VMEM((heads, height, slots * block_len), bf16),
        ],
        compiler_params=pltpu.CompilerParams(vmem_limit_bytes=arrival_bytes + 8 * MIB),
        cost_estimate=pl.CostEstimate(
            flops=4 * heads * height * slots * block_len * head_dim,
            bytes_accessed=slots * sent_bytes,
            transcendentals=heads * height * slots * block_len,
        ),
        name="arrived_blocks",
    )(query_rows, tables, length, *own_parts, *arrived)
    out = out.reshape(requests, q_heads, steps, head_dim).transpose(0, 2, 1, 3)
    return out.reshape(requests, steps, q_heads * head_dim), moved_to, more


def shards(*args):
    out, moved_to, more = attend(False, *args)
    _, out = lax.while_loop(
        lambda state: state[0] > 1,
        lambda state: (jnp.int32(0), attend(True, *args)[0]),
        (more[0], out),
    )
    return out, moved_to


def solution(mesh):
    in_specs = (
        P(("groups", "inst"), None, "tp", None),
        P(("groups", "inst"), None, None, "tp", None),
        P(("groups", "inst"), None, "tp", None, None),
        P(("groups", "inst"), None, "tp"),
        P(("groups", "inst"), None),
        P(("groups", "inst")),
        P(("groups", "inst"), None),
        P(("groups", "inst"), None),
    )
    out_specs = (P(("groups", "inst"), None, "tp"), P(("groups", "inst"), None))
    return jax.shard_map(shards, mesh=mesh, in_specs=in_specs, out_specs=out_specs, check_vma=False)
```

```python
import functools
import math

import jax
import jax.numpy as jnp
from jax import lax
from jax.experimental import pallas as pl
from jax.experimental.pallas import tpu as pltpu
from jax.sharding import PartitionSpec as P

CAP = 2
EXTRA = 16
NEVER = -1e30
LOG2E = math.log2(math.e)
MIB = 1 << 20
SMEM_SPEC = pl.BlockSpec(memory_space=pltpu.SMEM)
VMEM_SPEC = pl.BlockSpec(memory_space=pltpu.VMEM)
HBM_SPEC = pl.BlockSpec(memory_space=pltpu.HBM)
NT = (((1,), (1,)), ((), ()))


def loop(count, body, init):
    if count <= 8:
        for i in range(count):
            init = body(i, init)
        return init
    return lax.fori_loop(0, count, body, init)


def pack_kernel(dims, dest_ref, block_ref, scale_ref, pool_ref, *refs):
    instances, listed, heads, pool, copies = dims
    send_refs, (index_ref, extra_ref, held_ref, in_sems, out_sems) = refs[:-5], refs[-5:]
    code_rows = held_ref.shape[1] - EXTRA
    me = lax.axis_index("inst")
    for entry in range(CAP * instances + 1):
        index_ref[entry] = 0

    def place(m, carry):
        dest = dest_ref[0, m]
        rank = loop(
            listed,
            lambda m2, n: n + jnp.where((dest_ref[0, m2] == dest) & (m2 < m), 1, 0),
            jnp.int32(0),
        )
        entry = jnp.bitwise_xor(dest, me) + jnp.where(rank > 0, instances, 0)
        index_ref[entry] = block_ref[0, m]
        index_ref[jnp.where(rank > 0, CAP * instances, entry)] = block_ref[0, m]
        return carry

    loop(listed, place, 0)
    loads, stores = [], []
    for i, (entry, _) in enumerate(copies):
        loads.append(
            pltpu.make_async_copy(
                pool_ref.at[index_ref[entry]], held_ref.at[i, pl.ds(0, code_rows)], in_sems.at[i]
            )
        )
        loads[i].start()
    lane = lax.broadcasted_iota(jnp.int32, (1, 128), 1)

    def spell(m, row):
        return jnp.where(lane == m, dest_ref[0, m].astype(jnp.float32), row)

    extra_ref[...] = jnp.zeros_like(extra_ref)
    extra_ref[2 * heads : 2 * heads + 1, :] = loop(
        listed, spell, jnp.zeros((1, 128), jnp.float32)
    )
    scales = [
        [scale_ref[part, h : h + 1, :].astype(jnp.float32) for h in range(heads)]
        for part in range(2)
    ]
    column = lax.broadcasted_iota(jnp.int32, (1, pool), 1)
    for i, (entry, _) in enumerate(copies):
        for part in range(2):
            for h in range(heads):
                one = jnp.where(column == index_ref[entry], scales[part][h], 0.0)
                row = part * heads + h
                extra_ref[row : row + 1, :] = jnp.broadcast_to(
                    jnp.sum(one, axis=1, keepdims=True), (1, 128)
                )
        held_ref[i, pl.ds(code_rows, EXTRA)] = extra_ref[...].astype(jnp.bfloat16)
    for i, (_, targets) in enumerate(copies):
        loads[i].wait()
        for output, row in targets:
            stores.append(
                pltpu.make_async_copy(
                    held_ref.at[i], send_refs[output].at[row], out_sems.at[len(stores)]
                )
            )
            stores[-1].start()
    for store in stores:
        store.wait()


def split(value, size):
    assert size & (size - 1) == 0
    return lax.shift_right_logical(value, size.bit_length() - 1), value & (size - 1)


def count_log(tables, length, ids, block_len, spans, store):
    requests, width = tables.shape[0], ids.shape[1]
    whole, rest = split(length, block_len)
    whole = jnp.broadcast_to(whole, (requests, width))
    full = jnp.zeros((requests, width), jnp.float32)
    part = jnp.zeros((requests, width), jnp.float32)
    for e in range(spans):
        hit = jnp.broadcast_to(tables[:, e : e + 1], (requests, width)) == ids
        full = full + jnp.where(hit & (whole > e), 1.0, 0.0)
        part = part + jnp.where(hit & (whole == e), 1.0, 0.0)

    def log2(count):
        return jnp.where(count > 0, jnp.log(jnp.maximum(count, 1.0)) * LOG2E, NEVER)

    beyond, within = log2(full), log2(full + part)
    shape = (requests, block_len)
    inside = lax.broadcasted_iota(jnp.int32, shape, 1) < jnp.broadcast_to(rest, shape)
    if width % 16:
        for b in range(width):
            store(
                b,
                jnp.where(
                    inside,
                    jnp.broadcast_to(within[:, b : b + 1], shape),
                    jnp.broadcast_to(beyond[:, b : b + 1], shape),
                ),
            )
        return
    both = jnp.concatenate([within, beyond], axis=0)
    high = both.astype(jnp.bfloat16)
    low = (both - high.astype(jnp.float32)).astype(jnp.bfloat16)
    terms = jnp.concatenate([high, low], axis=0)
    row = lax.broadcasted_iota(jnp.int32, (width, block_len), 0)
    for b in range(0, width, 2):
        spots = jnp.concatenate(
            [jnp.where(row == b + i, 1.0, 0.0).astype(jnp.bfloat16) for i in range(2)], axis=1
        )
        spread_out = jnp.dot(terms, spots, preferred_element_type=jnp.float32)
        value = spread_out[: 2 * requests] + spread_out[2 * requests :]
        for i in range(2):
            at = slice(i * block_len, (i + 1) * block_len)
            store(b + i, jnp.where(inside, value[:requests, at], value[requests:, at]))


def score_tiles(query, keys, log_ref, scale_row, rows, store):
    height, wide = min(512, query.shape[0]), min(256, keys.shape[0])
    for top in range(0, query.shape[0], height):
        for left in range(0, keys.shape[0], wide):
            part = lax.dot_general(
                query[top : top + height],
                keys[left : left + wide],
                NT,
                preferred_element_type=jnp.float32,
            )
            scale = scale_row[:, left : left + wide]
            for r in range(height // rows):
                request = top // rows + r
                store(
                    request * rows,
                    left,
                    part[r * rows : (r + 1) * rows] * scale
                    + log_ref[request : request + 1, left : left + wide],
                )


def lane_fold(value, op):
    parts = [value[:, i : i + 128] for i in range(0, value.shape[1], 128)]
    while len(parts) > 1:
        parts = [
            op(parts[i], parts[i + 1]) if i + 1 < len(parts) else parts[i]
            for i in range(0, len(parts), 2)
        ]
    return parts[0]


def spread(column, width):
    return jnp.concatenate([column] * (width // 128), axis=1)


def own_kernel(
    dims, q_ref, fresh_ref, pool_ref, *refs
):
    if dims[0] == 0:
        tables_ref, length_ref, scale_ref, acc_ref, top_ref, total_ref, log_ref, row_ref = refs[:8]
    else:
        log_ref, row_ref, acc_ref, top_ref, total_ref = refs[:5]
    t_ref, p_ref, codes_ref, sems = refs[-4:]
    head, pool, heads, rows, steps, block_len, spans, factor, group = dims
    chunks = pool // group
    height, head_dim = q_ref.shape[1:]
    width = group * block_len

    def load(part, chunk):
        return pltpu.make_async_copy(
            pool_ref.at[
                pl.ds(chunk * group, group), pl.ds((part * heads + head) * block_len, block_len)
            ],
            codes_ref.at[part, chunk],
            sems.at[part, chunk],
        )

    for part in range(2):
        for chunk in range(chunks):
            load(part, chunk).start()

    if head == 0:
        ids = lax.broadcasted_iota(jnp.int32, (1, pool), 1)

        def store_log(b, value):
            lane = (b % group) * block_len
            log_ref[b // group, :, lane : lane + block_len] = value

        count_log(tables_ref[...], length_ref[...], ids, block_len, spans, store_log)
        for b in range(pool):
            lane = (b % group) * block_len
            row_ref[b // group, :, lane : lane + block_len] = jnp.broadcast_to(
                scale_ref[:, b : b + 1], (2 * heads, block_len)
            )
    shape = (height, fresh_ref.shape[2])
    row = lax.broadcasted_iota(jnp.int32, shape, 0)
    col = lax.broadcasted_iota(jnp.int32, shape, 1)
    (request, row_step), (owner, step) = split(row, rows), split(col, steps)
    seen = (request == owner) & (split(row_step, steps)[1] >= step)
    new_score = lax.dot_general(
        q_ref[head], fresh_ref[0, head], NT, preferred_element_type=jnp.float32
    )
    new_score = jnp.where(seen, new_score * (factor * LOG2E), -jnp.inf)
    acc_ref[...] = new_score
    top_ref[...] = lane_fold(new_score, jnp.maximum)

    def score(chunk, carry):
        load(0, chunk).wait()

        def store(row, lane, value):
            t_ref[chunk, row : row + rows, lane : lane + value.shape[1]] = value

        score_tiles(
            q_ref[head],
            codes_ref[0, chunk].reshape(width, head_dim),
            log_ref.at[chunk],
            row_ref[chunk, head : head + 1, :] * (factor * LOG2E),
            rows,
            store,
        )
        for row in range(0, height, rows):
            at = pl.ds(row, rows)
            top_ref[at] = jnp.maximum(top_ref[at], lane_fold(t_ref[chunk, at], jnp.maximum))
        return carry

    lax.fori_loop(0, chunks, score, 0)

    top = jnp.broadcast_to(jnp.max(top_ref[...], axis=1, keepdims=True), (height, 128))
    top_ref[...] = top
    weight = jnp.exp2(acc_ref[...] - spread(top, acc_ref.shape[1]))
    total_ref[...] = lane_fold(weight, jnp.add)
    acc_ref[...] = jnp.dot(
        weight.astype(jnp.bfloat16), fresh_ref[1, head], preferred_element_type=jnp.float32
    )

    def apply(chunk, carry):
        load(1, chunk).wait()
        scale = row_ref[chunk, heads + head : heads + head + 1, :]
        for row in range(0, height, rows):
            at = pl.ds(row, rows)
            weight = jnp.exp2(t_ref[chunk, at] - spread(top_ref[at], width))
            total_ref[at] += lane_fold(weight, jnp.add)
            p_ref[at] = (weight * scale).astype(jnp.bfloat16)
        acc_ref[...] += jnp.dot(
            p_ref[...],
            codes_ref[1, chunk].reshape(width, head_dim),
            preferred_element_type=jnp.float32,
        )
        return carry

    lax.fori_loop(0, chunks, apply, 0)


def arrival_ids(me, pool, lists, listed):
    instances = len(lists)
    lane = lax.broadcasted_iota(jnp.int32, (1, 128), 1)
    counts = [
        jnp.sum(
            jnp.where((row == me.astype(jnp.float32)) & (lane < listed), 1.0, 0.0),
            axis=1,
            keepdims=True,
        )
        for row in lists
    ]
    slot = lax.broadcasted_iota(jnp.int32, (1, instances * CAP), 1)
    ids = jnp.full(slot.shape, -1.0)
    for k in range(instances):
        first = jnp.full((1, 1), float(pool))
        for j in range(instances):
            lower = jnp.bitwise_xor(me, j) < jnp.bitwise_xor(me, k)
            first = first + jnp.where(lower, counts[j], 0.0)
        for r in range(CAP):
            name = jnp.where(counts[k] > r, first + r, -1.0)
            ids = jnp.where(slot == r * instances + k, jnp.broadcast_to(name, slot.shape), ids)
    moved = jnp.full((1, 128), float(pool))
    for j in range(instances):
        for m in range(listed):
            same = jnp.broadcast_to(lists[j][:, m : m + 1], (1, 128)) == lists[0]
            ahead = jnp.bitwise_xor(me, j) < me if j else lane > m
            moved = moved + jnp.where(same & ahead, 1.0, 0.0)
    more = jnp.zeros((1, 128))
    for row in lists:
        again = jnp.zeros((1, 128))
        for m in range(listed):
            same = jnp.broadcast_to(row[:, m : m + 1], (1, 128)) == row
            again = again + jnp.where(same & (lane > m) & (lane < listed), 1.0, 0.0)
        more = jnp.maximum(more, jnp.sum(again, axis=1, keepdims=True))
    return ids.astype(jnp.int32), moved[:, :listed].astype(jnp.int32), more


def arrival_kernel(dims, places, q_ref, tables_ref, length_ref, *refs):
    pool, heads, rows, block_len, spans, listed, factor = dims
    own_refs, code_refs = refs[: 3 * heads], refs[3 * heads : -6]
    out_ref, moved_ref, more_ref, log_ref, t_ref, p_ref = refs[-6:]
    height = q_ref.shape[1]
    width = 2 * block_len
    extra = 2 * heads * block_len
    slots = [(code_refs[array], row) for array, row in places]
    pairs = len(slots) // 2

    def pair(i, part, h):
        at = pl.ds((part * heads + h) * block_len, block_len)
        return jnp.concatenate([ref[r, at] for ref, r in slots[2 * i : 2 * i + 2]], axis=0)

    lists, scale_rows = [], []
    for ref, r in slots:
        values = ref[r, pl.ds(extra, EXTRA)].astype(jnp.float32)
        scale_rows.append(values)
        if len(lists) < len(slots) // CAP:
            lists.append(values[2 * heads : 2 * heads + 1])

    def scale_row(row):
        return jnp.concatenate([values[row : row + 1] for values in scale_rows], axis=1)

    ids, moved_ref[...], more = arrival_ids(lax.axis_index("inst"), pool, lists, listed)
    more_ref[0] = jnp.max(more).astype(jnp.int32)

    def store_log(b, value):
        log_ref[:, b * block_len : (b + 1) * block_len] = value

    count_log(tables_ref[...], length_ref[...], ids, block_len, spans, store_log)
    for h in range(heads):
        key_scale = scale_row(h) * (factor * LOG2E)
        for i in range(pairs):
            left = i * width

            def store(row, lane, value, h=h, left=left):
                t_ref[h, row : row + rows, left + lane : left + lane + value.shape[1]] = value

            score_tiles(
                q_ref[h],
                pair(i, 0, h),
                log_ref.at[:, left : left + width],
                key_scale[:, left : left + width],
                rows,
                store,
            )
    for h in range(heads):
        acc_ref, top_ref, total_ref = own_refs[3 * h : 3 * h + 3]
        scale = scale_row(heads + h)
        for row in range(0, height, rows):
            at = pl.ds(row, rows)
            score = t_ref[h, at]
            own_top = top_ref[at]
            top = jnp.maximum(
                own_top, jnp.max(lane_fold(score, jnp.maximum), axis=1, keepdims=True)
            )
            weight = jnp.exp2(score - spread(top, score.shape[1]))
            keep = jnp.exp2(own_top - top)
            total = jnp.sum(
                total_ref[at] * keep + lane_fold(weight, jnp.add), axis=1, keepdims=True
            )
            p_ref[h, at] = (weight * scale).astype(jnp.bfloat16)
            t_ref[h, at, 0:128] = keep
            t_ref[h, at, 128:256] = jnp.broadcast_to(1.0 / total, keep.shape)
        mixed = acc_ref[...] * t_ref[h, :, 0:128]
        for i in range(pairs):
            mixed = mixed + jnp.dot(
                p_ref[h, :, i * width : (i + 1) * width],
                pair(i, 1, h),
                preferred_element_type=jnp.float32,
            )
        result = (mixed * t_ref[h, :, 128:256]).astype(jnp.bfloat16)
        out_ref[:, h] = result.reshape(height // rows, rows, result.shape[-1])


def attend(
    general, queries, new_kv, pool_codes, pool_scales, tables, ctx_len, mig_block, mig_dest
):
    instances = lax.axis_size("inst")
    pool = pool_codes.shape[0]
    requests, steps, q_heads, head_dim = queries.shape
    heads = new_kv.shape[3]
    per_head = q_heads // heads
    spans = tables.shape[1]
    block_len = pool_codes.shape[3]
    listed = mig_dest.shape[1]
    factor = head_dim ** (-0.5)
    rows = per_head * steps
    height = requests * rows
    slots = instances * CAP
    group = 16
    f32, bf16 = jnp.float32, jnp.bfloat16
    code_rows = 2 * heads * block_len
    pool_rows = pool_codes.reshape(pool, code_rows, head_dim)
    sent_shape = (code_rows + EXTRA, head_dim)
    sent_bytes = 2 * math.prod(sent_shape)
    part_scales = jnp.transpose(pool_scales, (1, 2, 0))
    assert instances & (instances - 1) == 0 and 2 * heads < EXTRA and head_dim == 128

    def pack(sizes, copies):
        stores = sum(len(targets) for _, targets in copies)
        return pl.pallas_call(
            functools.partial(pack_kernel, (instances, listed, heads, pool, copies)),
            out_shape=[jax.ShapeDtypeStruct((size,) + sent_shape, bf16) for size in sizes],
            in_specs=[SMEM_SPEC, SMEM_SPEC, VMEM_SPEC, HBM_SPEC],
            out_specs=[HBM_SPEC] * len(sizes),
            scratch_shapes=[
                pltpu.SMEM((CAP * instances + 1,), jnp.int32),
                pltpu.VMEM((EXTRA, head_dim), f32),
                pltpu.VMEM((len(copies),) + sent_shape, bf16),
                pltpu.SemaphoreType.DMA((len(copies),)),
                pltpu.SemaphoreType.DMA((stores,)),
            ],
            compiler_params=pltpu.CompilerParams(vmem_limit_bytes=56 * MIB),
            cost_estimate=pl.CostEstimate(
                flops=0, bytes_accessed=2 * stores * sent_bytes, transcendentals=0
            ),
            name="pack_blocks",
        )(mig_dest, mig_block, part_scales, pool_rows)

    def swap(value, distance):
        return lax.ppermute(value, "inst", [(j, j ^ distance) for j in range(instances)])

    if general:
        send = pack(
            [CAP] * instances,
            [(r * instances + k, [(k, r)]) for k in range(instances) for r in range(CAP)],
        )
        arrived = [swap(send[k], k) for k in range(instances - 1, 0, -1)] + [send[0]]
        places = [(instances - 1 - k, r) for r in range(CAP) for k in range(instances)]
    else:
        any_second = CAP * instances
        (second,) = pack([1], [(any_second, [(0, 0)])])
        seconds = {0: second}
        bit = instances // 2
        while bit > 1:
            for k in list(seconds):
                seconds[k ^ bit] = swap(seconds[k], bit)
            bit //= 2
        mig_dest, second = lax.optimization_barrier((mig_dest, second))
        send = pack(
            [1, 2] + [1] * (instances - 2),
            [(k, [(k, 0)]) for k in list(range(instances))[::-1]] + [(any_second, [(1, 1)])],
        )
        firsts = [send[0]] + [swap(send[k], k) for k in range(1, instances)]
    part_scales, *send = lax.optimization_barrier((part_scales, *send))
    flat_scales = part_scales.reshape(2 * heads, pool).astype(f32)

    query_rows = (
        queries.reshape(requests, steps, heads, per_head, head_dim)
        .transpose(2, 0, 3, 1, 4)
        .reshape(heads, height, head_dim)
    )
    fresh_len = requests * steps
    fresh = new_kv.transpose(2, 3, 0, 1, 4).reshape(2, heads, fresh_len, head_dim)
    fresh = jnp.pad(fresh, ((0, 0), (0, 0), (0, -fresh_len % 128), (0, 0)))
    assert fresh.shape[2] == head_dim
    length = ctx_len[:, None]
    width = group * block_len
    chunks = pool // group
    tokens = pool * block_len

    mask_shapes = [(chunks, requests, width), (chunks, 2 * heads, width)]

    def own(head, *masks):
        shapes = [(height, head_dim)] * 3 + ([] if head else mask_shapes)
        return pl.pallas_call(
            functools.partial(
                own_kernel, (head, pool, heads, rows, steps, block_len, spans, factor, group)
            ),
            out_shape=[jax.ShapeDtypeStruct(shape, f32) for shape in shapes],
            in_specs=[VMEM_SPEC, VMEM_SPEC, HBM_SPEC] + [VMEM_SPEC] * len(masks),
            out_specs=[VMEM_SPEC] * len(shapes),
            scratch_shapes=[
                pltpu.VMEM((chunks, height, width), f32),
                pltpu.VMEM((height, width), bf16),
                pltpu.VMEM((2, chunks, group, block_len, head_dim), bf16),
                pltpu.SemaphoreType.DMA((2, chunks)),
            ],
            compiler_params=pltpu.CompilerParams(vmem_limit_bytes=32 * MIB),
            cost_estimate=pl.CostEstimate(
                flops=4 * height * tokens * head_dim,
                bytes_accessed=pool_codes.size * 2 // heads,
                transcendentals=height * tokens,
            ),
            name="own_blocks",
        )(query_rows, fresh, pool_rows, *masks)

    *own_parts, log_rows, scale_rows = own(0, tables, length, flat_scales)
    if not general:
        seconds, own_parts, log_rows = lax.optimization_barrier((seconds, own_parts, log_rows))
    for head in range(1, heads):
        own_parts = own_parts + list(own(head, log_rows, scale_rows))

    if not general:
        held = {k: second for k, second in seconds.items() if k}
        for k in held:
            seconds[k ^ 1] = swap(held[k], 1)
        arrived = [held[k] for k in held] + firsts[::-1] + [seconds[0]]
        where = {k: i for i, k in enumerate(held)}
        where[0] = len(arrived) - 1
        places = [(len(held) + instances - 1 - k, 0) for k in range(instances)]
        for k in range(instances):
            if k == 1:
                places.append((places[1][0], 1))
            elif k in where:
                places.append((where[k], 0))
            else:
                places.append((len(arrived), 0))
                arrived.append(seconds[k])

    arrival_bytes = 6 * heads * height * slots * block_len + 2 * 12 * height * head_dim * heads
    arrival_bytes += 2 * slots * sent_bytes + 4 * requests * slots * block_len
    out, moved_to, more = pl.pallas_call(
        functools.partial(
            arrival_kernel, (pool, heads, rows, block_len, spans, listed, factor), places
        ),
        out_shape=[
            jax.ShapeDtypeStruct((requests, heads, rows, head_dim), bf16),
            jax.ShapeDtypeStruct((1, listed), jnp.int32),
            jax.ShapeDtypeStruct((1,), jnp.int32),
        ],
        in_specs=[VMEM_SPEC] * (3 + 3 * heads + len(arrived)),
        out_specs=[VMEM_SPEC, VMEM_SPEC, SMEM_SPEC],
        scratch_shapes=[
            pltpu.VMEM((requests, slots * block_len), f32),
            pltpu.VMEM((heads, height, slots * block_len), f32),
            pltpu.VMEM((heads, height, slots * block_len), bf16),
        ],
        compiler_params=pltpu.CompilerParams(vmem_limit_bytes=arrival_bytes + 8 * MIB),
        cost_estimate=pl.CostEstimate(
            flops=4 * heads * height * slots * block_len * head_dim,
            bytes_accessed=slots * sent_bytes,
            transcendentals=heads * height * slots * block_len,
        ),
        name="arrived_blocks",
    )(query_rows, tables, length, *own_parts, *arrived)
    out = out.reshape(requests, q_heads, steps, head_dim).transpose(0, 2, 1, 3)
    return out.reshape(requests, steps, q_heads * head_dim), moved_to, more


def shards(*args):
    out, moved_to, more = attend(False, *args)
    _, out = lax.while_loop(
        lambda state: state[0] > 1,
        lambda state: (jnp.int32(0), attend(True, *args)[0]),
        (more[0], out),
    )
    return out, moved_to


def solution(mesh):
    in_specs = (
        P(("groups", "inst"), None, "tp", None),
        P(("groups", "inst"), None, None, "tp", None),
        P(("groups", "inst"), None, "tp", None, None),
        P(("groups", "inst"), None, "tp"),
        P(("groups", "inst"), None),
        P(("groups", "inst")),
        P(("groups", "inst"), None),
        P(("groups", "inst"), None),
    )
    out_specs = (P(("groups", "inst"), None, "tp"), P(("groups", "inst"), None))
    return jax.shard_map(shards, mesh=mesh, in_specs=in_specs, out_specs=out_specs, check_vma=False)
```

```python
import functools
import math

import jax
import jax.numpy as jnp
from jax import lax
from jax.experimental import pallas as pl
from jax.experimental.pallas import tpu as pltpu
from jax.sharding import PartitionSpec as P

CAP = 2
EXTRA = 16
NEVER = -1e30
LOG2E = math.log2(math.e)
MIB = 1 << 20
SMEM_SPEC = pl.BlockSpec(memory_space=pltpu.SMEM)
VMEM_SPEC = pl.BlockSpec(memory_space=pltpu.VMEM)
HBM_SPEC = pl.BlockSpec(memory_space=pltpu.HBM)
NT = (((1,), (1,)), ((), ()))


def loop(count, body, init):
    if count <= 8:
        for i in range(count):
            init = body(i, init)
        return init
    return lax.fori_loop(0, count, body, init)


def pack_kernel(dims, dest_ref, block_ref, scale_ref, pool_ref, *refs):
    instances, listed, heads, pool, copies = dims
    send_refs, (index_ref, extra_ref, held_ref, in_sems, out_sems) = refs[:-5], refs[-5:]
    code_rows = held_ref.shape[1] - EXTRA
    me = lax.axis_index("inst")
    for entry in range(CAP * instances + 1):
        index_ref[entry] = 0

    def place(m, carry):
        dest = dest_ref[0, m]
        rank = loop(
            listed,
            lambda m2, n: n + jnp.where((dest_ref[0, m2] == dest) & (m2 < m), 1, 0),
            jnp.int32(0),
        )
        entry = jnp.bitwise_xor(dest, me) + jnp.where(rank > 0, instances, 0)
        index_ref[entry] = block_ref[0, m]
        index_ref[jnp.where(rank > 0, CAP * instances, entry)] = block_ref[0, m]
        return carry

    loop(listed, place, 0)
    loads, stores = [], []
    for i, (entry, _) in enumerate(copies):
        loads.append(
            pltpu.make_async_copy(
                pool_ref.at[index_ref[entry]], held_ref.at[i, pl.ds(0, code_rows)], in_sems.at[i]
            )
        )
        loads[i].start()
    lane = lax.broadcasted_iota(jnp.int32, (1, 128), 1)

    def spell(m, row):
        return jnp.where(lane == m, dest_ref[0, m].astype(jnp.float32), row)

    extra_ref[...] = jnp.zeros_like(extra_ref)
    extra_ref[2 * heads : 2 * heads + 1, :] = loop(
        listed, spell, jnp.zeros((1, 128), jnp.float32)
    )
    scales = [
        [scale_ref[part, h : h + 1, :].astype(jnp.float32) for h in range(heads)]
        for part in range(2)
    ]
    column = lax.broadcasted_iota(jnp.int32, (1, pool), 1)
    for i, (entry, _) in enumerate(copies):
        for part in range(2):
            for h in range(heads):
                one = jnp.where(column == index_ref[entry], scales[part][h], 0.0)
                row = part * heads + h
                extra_ref[row : row + 1, :] = jnp.broadcast_to(
                    jnp.sum(one, axis=1, keepdims=True), (1, 128)
                )
        held_ref[i, pl.ds(code_rows, EXTRA)] = extra_ref[...].astype(jnp.bfloat16)
    for i, (_, targets) in enumerate(copies):
        loads[i].wait()
        for output, row in targets:
            stores.append(
                pltpu.make_async_copy(
                    held_ref.at[i], send_refs[output].at[row], out_sems.at[len(stores)]
                )
            )
            stores[-1].start()
    for store in stores:
        store.wait()


def split(value, size):
    assert size & (size - 1) == 0
    return lax.shift_right_logical(value, size.bit_length() - 1), value & (size - 1)


def count_log(tables, length, ids, block_len, spans, store):
    requests, width = tables.shape[0], ids.shape[1]
    whole, rest = split(length, block_len)
    whole = jnp.broadcast_to(whole, (requests, width))
    full = jnp.zeros((requests, width), jnp.float32)
    part = jnp.zeros((requests, width), jnp.float32)
    for e in range(spans):
        hit = jnp.broadcast_to(tables[:, e : e + 1], (requests, width)) == ids
        full = full + jnp.where(hit & (whole > e), 1.0, 0.0)
        part = part + jnp.where(hit & (whole == e), 1.0, 0.0)

    def log2(count):
        return jnp.where(count > 0, jnp.log(jnp.maximum(count, 1.0)) * LOG2E, NEVER)

    beyond, within = log2(full), log2(full + part)
    shape = (requests, block_len)
    inside = lax.broadcasted_iota(jnp.int32, shape, 1) < jnp.broadcast_to(rest, shape)
    if width % 16:
        for b in range(width):
            store(
                b,
                jnp.where(
                    inside,
                    jnp.broadcast_to(within[:, b : b + 1], shape),
                    jnp.broadcast_to(beyond[:, b : b + 1], shape),
                ),
            )
        return
    both = jnp.concatenate([within, beyond], axis=0)
    high = both.astype(jnp.bfloat16)
    low = (both - high.astype(jnp.float32)).astype(jnp.bfloat16)
    terms = jnp.concatenate([high, low], axis=0)
    row = lax.broadcasted_iota(jnp.int32, (width, block_len), 0)
    for b in range(0, width, 2):
        spots = jnp.concatenate(
            [jnp.where(row == b + i, 1.0, 0.0).astype(jnp.bfloat16) for i in range(2)], axis=1
        )
        spread_out = jnp.dot(terms, spots, preferred_element_type=jnp.float32)
        value = spread_out[: 2 * requests] + spread_out[2 * requests :]
        for i in range(2):
            at = slice(i * block_len, (i + 1) * block_len)
            store(b + i, jnp.where(inside, value[:requests, at], value[requests:, at]))


def score_tiles(query, keys, log_ref, scale_row, rows, store):
    height, wide = min(512, query.shape[0]), min(256, keys.shape[0])
    for top in range(0, query.shape[0], height):
        for left in range(0, keys.shape[0], wide):
            part = lax.dot_general(
                query[top : top + height],
                keys[left : left + wide],
                NT,
                preferred_element_type=jnp.float32,
            )
            scale = scale_row[:, left : left + wide]
            for r in range(height // rows):
                request = top // rows + r
                store(
                    request * rows,
                    left,
                    part[r * rows : (r + 1) * rows] * scale
                    + log_ref[request : request + 1, left : left + wide],
                )


def lane_fold(value, op):
    parts = [value[:, i : i + 128] for i in range(0, value.shape[1], 128)]
    while len(parts) > 1:
        parts = [
            op(parts[i], parts[i + 1]) if i + 1 < len(parts) else parts[i]
            for i in range(0, len(parts), 2)
        ]
    return parts[0]


def spread(column, width):
    return jnp.concatenate([column] * (width // 128), axis=1)


def own_kernel(
    dims, q_ref, fresh_ref, pool_ref, *refs
):
    if dims[0] == 0:
        tables_ref, length_ref, scale_ref, acc_ref, top_ref, total_ref, log_ref, row_ref = refs[:8]
    else:
        log_ref, row_ref, acc_ref, top_ref, total_ref = refs[:5]
    t_ref, p_ref, codes_ref, sems = refs[-4:]
    head, pool, heads, rows, steps, block_len, spans, factor, group = dims
    chunks = pool // group
    height, head_dim = q_ref.shape[1:]
    width = group * block_len

    def load(part, chunk):
        return pltpu.make_async_copy(
            pool_ref.at[
                pl.ds(chunk * group, group), pl.ds((part * heads + head) * block_len, block_len)
            ],
            codes_ref.at[part, chunk],
            sems.at[part, chunk],
        )

    for part in range(2):
        for chunk in range(chunks):
            load(part, chunk).start()

    if head == 0:
        ids = lax.broadcasted_iota(jnp.int32, (1, pool), 1)

        def store_log(b, value):
            lane = (b % group) * block_len
            log_ref[b // group, :, lane : lane + block_len] = value

        count_log(tables_ref[...], length_ref[...], ids, block_len, spans, store_log)
        for b in range(pool):
            lane = (b % group) * block_len
            row_ref[b // group, :, lane : lane + block_len] = jnp.broadcast_to(
                scale_ref[:, b : b + 1], (2 * heads, block_len)
            )
    shape = (height, fresh_ref.shape[2])
    row = lax.broadcasted_iota(jnp.int32, shape, 0)
    col = lax.broadcasted_iota(jnp.int32, shape, 1)
    (request, row_step), (owner, step) = split(row, rows), split(col, steps)
    seen = (request == owner) & (split(row_step, steps)[1] >= step)
    new_score = lax.dot_general(
        q_ref[head], fresh_ref[0, head], NT, preferred_element_type=jnp.float32
    )
    new_score = jnp.where(seen, new_score * (factor * LOG2E), -jnp.inf)
    acc_ref[...] = new_score
    top_ref[...] = lane_fold(new_score, jnp.maximum)

    def score(chunk, carry):
        load(0, chunk).wait()

        def store(row, lane, value):
            t_ref[chunk, row : row + rows, lane : lane + value.shape[1]] = value

        score_tiles(
            q_ref[head],
            codes_ref[0, chunk].reshape(width, head_dim),
            log_ref.at[chunk],
            row_ref[chunk, head : head + 1, :] * (factor * LOG2E),
            rows,
            store,
        )
        for row in range(0, height, rows):
            at = pl.ds(row, rows)
            top_ref[at] = jnp.maximum(top_ref[at], lane_fold(t_ref[chunk, at], jnp.maximum))
        return carry

    lax.fori_loop(0, chunks, score, 0)

    top = jnp.broadcast_to(jnp.max(top_ref[...], axis=1, keepdims=True), (height, 128))
    top_ref[...] = top
    weight = jnp.exp2(acc_ref[...] - spread(top, acc_ref.shape[1]))
    total_ref[...] = lane_fold(weight, jnp.add)
    acc_ref[...] = jnp.dot(
        weight.astype(jnp.bfloat16), fresh_ref[1, head], preferred_element_type=jnp.float32
    )

    def apply(chunk, carry):
        load(1, chunk).wait()
        scale = row_ref[chunk, heads + head : heads + head + 1, :]
        for row in range(0, height, rows):
            at = pl.ds(row, rows)
            weight = jnp.exp2(t_ref[chunk, at] - spread(top_ref[at], width))
            total_ref[at] += lane_fold(weight, jnp.add)
            p_ref[at] = (weight * scale).astype(jnp.bfloat16)
        acc_ref[...] += jnp.dot(
            p_ref[...],
            codes_ref[1, chunk].reshape(width, head_dim),
            preferred_element_type=jnp.float32,
        )
        return carry

    lax.fori_loop(0, chunks, apply, 0)


def arrival_ids(me, pool, lists, listed):
    instances = len(lists)
    lane = lax.broadcasted_iota(jnp.int32, (1, 128), 1)
    counts = [
        jnp.sum(
            jnp.where((row == me.astype(jnp.float32)) & (lane < listed), 1.0, 0.0),
            axis=1,
            keepdims=True,
        )
        for row in lists
    ]
    slot = lax.broadcasted_iota(jnp.int32, (1, instances * CAP), 1)
    ids = jnp.full(slot.shape, -1.0)
    for k in range(instances):
        first = jnp.full((1, 1), float(pool))
        for j in range(instances):
            lower = jnp.bitwise_xor(me, j) < jnp.bitwise_xor(me, k)
            first = first + jnp.where(lower, counts[j], 0.0)
        for r in range(CAP):
            name = jnp.where(counts[k] > r, first + r, -1.0)
            ids = jnp.where(slot == r * instances + k, jnp.broadcast_to(name, slot.shape), ids)
    moved = jnp.full((1, 128), float(pool))
    for j in range(instances):
        for m in range(listed):
            same = jnp.broadcast_to(lists[j][:, m : m + 1], (1, 128)) == lists[0]
            ahead = jnp.bitwise_xor(me, j) < me if j else lane > m
            moved = moved + jnp.where(same & ahead, 1.0, 0.0)
    more = jnp.zeros((1, 128))
    for row in lists:
        again = jnp.zeros((1, 128))
        for m in range(listed):
            same = jnp.broadcast_to(row[:, m : m + 1], (1, 128)) == row
            again = again + jnp.where(same & (lane > m) & (lane < listed), 1.0, 0.0)
        more = jnp.maximum(more, jnp.sum(again, axis=1, keepdims=True))
    return ids.astype(jnp.int32), moved[:, :listed].astype(jnp.int32), more


def arrival_kernel(dims, places, q_ref, tables_ref, length_ref, *refs):
    pool, heads, rows, block_len, spans, listed, factor = dims
    own_refs, code_refs = refs[: 3 * heads], refs[3 * heads : -6]
    out_ref, moved_ref, more_ref, log_ref, t_ref, p_ref = refs[-6:]
    height = q_ref.shape[1]
    width = 2 * block_len
    extra = 2 * heads * block_len
    slots = [(code_refs[array], row) for array, row in places]
    pairs = len(slots) // 2

    def pair(i, part, h):
        at = pl.ds((part * heads + h) * block_len, block_len)
        return jnp.concatenate([ref[r, at] for ref, r in slots[2 * i : 2 * i + 2]], axis=0)

    lists, scale_rows = [], []
    for ref, r in slots:
        values = ref[r, pl.ds(extra, EXTRA)].astype(jnp.float32)
        scale_rows.append(values)
        if len(lists) < len(slots) // CAP:
            lists.append(values[2 * heads : 2 * heads + 1])

    def scale_row(row):
        return jnp.concatenate([values[row : row + 1] for values in scale_rows], axis=1)

    ids, moved_ref[...], more = arrival_ids(lax.axis_index("inst"), pool, lists, listed)
    more_ref[0] = jnp.max(more).astype(jnp.int32)

    def store_log(b, value):
        log_ref[:, b * block_len : (b + 1) * block_len] = value

    count_log(tables_ref[...], length_ref[...], ids, block_len, spans, store_log)
    for h in range(heads):
        key_scale = scale_row(h) * (factor * LOG2E)
        for i in range(pairs):
            left = i * width

            def store(row, lane, value, h=h, left=left):
                t_ref[h, row : row + rows, left + lane : left + lane + value.shape[1]] = value

            score_tiles(
                q_ref[h],
                pair(i, 0, h),
                log_ref.at[:, left : left + width],
                key_scale[:, left : left + width],
                rows,
                store,
            )
    for h in range(heads):
        acc_ref, top_ref, total_ref = own_refs[3 * h : 3 * h + 3]
        scale = scale_row(heads + h)
        for row in range(0, height, rows):
            at = pl.ds(row, rows)
            score = t_ref[h, at]
            own_top = top_ref[at]
            top = jnp.maximum(
                own_top, jnp.max(lane_fold(score, jnp.maximum), axis=1, keepdims=True)
            )
            weight = jnp.exp2(score - spread(top, score.shape[1]))
            keep = jnp.exp2(own_top - top)
            total = jnp.sum(
                total_ref[at] * keep + lane_fold(weight, jnp.add), axis=1, keepdims=True
            )
            p_ref[h, at] = (weight * scale).astype(jnp.bfloat16)
            t_ref[h, at, 0:128] = keep
            t_ref[h, at, 128:256] = jnp.broadcast_to(1.0 / total, keep.shape)
        mixed = acc_ref[...] * t_ref[h, :, 0:128]
        for i in range(pairs):
            mixed = mixed + jnp.dot(
                p_ref[h, :, i * width : (i + 1) * width],
                pair(i, 1, h),
                preferred_element_type=jnp.float32,
            )
        result = (mixed * t_ref[h, :, 128:256]).astype(jnp.bfloat16)
        out_ref[:, h] = result.reshape(height // rows, rows, result.shape[-1])


def attend(
    general, queries, new_kv, pool_codes, pool_scales, tables, ctx_len, mig_block, mig_dest
):
    instances = lax.axis_size("inst")
    pool = pool_codes.shape[0]
    requests, steps, q_heads, head_dim = queries.shape
    heads = new_kv.shape[3]
    per_head = q_heads // heads
    spans = tables.shape[1]
    block_len = pool_codes.shape[3]
    listed = mig_dest.shape[1]
    factor = head_dim ** (-0.5)
    rows = per_head * steps
    height = requests * rows
    slots = instances * CAP
    group = 24
    f32, bf16 = jnp.float32, jnp.bfloat16
    code_rows = 2 * heads * block_len
    pool_rows = pool_codes.reshape(pool, code_rows, head_dim)
    sent_shape = (code_rows + EXTRA, head_dim)
    sent_bytes = 2 * math.prod(sent_shape)
    part_scales = jnp.transpose(pool_scales, (1, 2, 0))
    assert instances & (instances - 1) == 0 and 2 * heads < EXTRA and head_dim == 128

    def pack(sizes, copies):
        stores = sum(len(targets) for _, targets in copies)
        return pl.pallas_call(
            functools.partial(pack_kernel, (instances, listed, heads, pool, copies)),
            out_shape=[jax.ShapeDtypeStruct((size,) + sent_shape, bf16) for size in sizes],
            in_specs=[SMEM_SPEC, SMEM_SPEC, VMEM_SPEC, HBM_SPEC],
            out_specs=[HBM_SPEC] * len(sizes),
            scratch_shapes=[
                pltpu.SMEM((CAP * instances + 1,), jnp.int32),
                pltpu.VMEM((EXTRA, head_dim), f32),
                pltpu.VMEM((len(copies),) + sent_shape, bf16),
                pltpu.SemaphoreType.DMA((len(copies),)),
                pltpu.SemaphoreType.DMA((stores,)),
            ],
            compiler_params=pltpu.CompilerParams(vmem_limit_bytes=56 * MIB),
            cost_estimate=pl.CostEstimate(
                flops=0, bytes_accessed=2 * stores * sent_bytes, transcendentals=0
            ),
            name="pack_blocks",
        )(mig_dest, mig_block, part_scales, pool_rows)

    def swap(value, distance):
        return lax.ppermute(value, "inst", [(j, j ^ distance) for j in range(instances)])

    if general:
        send = pack(
            [CAP] * instances,
            [(r * instances + k, [(k, r)]) for k in range(instances) for r in range(CAP)],
        )
        arrived = [swap(send[k], k) for k in range(instances - 1, 0, -1)] + [send[0]]
        places = [(instances - 1 - k, r) for r in range(CAP) for k in range(instances)]
    else:
        any_second = CAP * instances
        (second,) = pack([1], [(any_second, [(0, 0)])])
        seconds = {0: second}
        bit = instances // 2
        while bit > 1:
            for k in list(seconds):
                seconds[k ^ bit] = swap(seconds[k], bit)
            bit //= 2
        mig_dest, second = lax.optimization_barrier((mig_dest, second))
        send = pack(
            [1, 2] + [1] * (instances - 2),
            [(k, [(k, 0)]) for k in list(range(instances))[::-1]] + [(any_second, [(1, 1)])],
        )
        firsts = [send[0]] + [swap(send[k], k) for k in range(1, instances)]
    part_scales, *send = lax.optimization_barrier((part_scales, *send))
    flat_scales = part_scales.reshape(2 * heads, pool).astype(f32)

    query_rows = (
        queries.reshape(requests, steps, heads, per_head, head_dim)
        .transpose(2, 0, 3, 1, 4)
        .reshape(heads, height, head_dim)
    )
    fresh_len = requests * steps
    fresh = new_kv.transpose(2, 3, 0, 1, 4).reshape(2, heads, fresh_len, head_dim)
    fresh = jnp.pad(fresh, ((0, 0), (0, 0), (0, -fresh_len % 128), (0, 0)))
    assert fresh.shape[2] == head_dim
    length = ctx_len[:, None]
    width = group * block_len
    chunks = pool // group
    tokens = pool * block_len

    mask_shapes = [(chunks, requests, width), (chunks, 2 * heads, width)]

    def own(head, *masks):
        shapes = [(height, head_dim)] * 3 + ([] if head else mask_shapes)
        return pl.pallas_call(
            functools.partial(
                own_kernel, (head, pool, heads, rows, steps, block_len, spans, factor, group)
            ),
            out_shape=[jax.ShapeDtypeStruct(shape, f32) for shape in shapes],
            in_specs=[VMEM_SPEC, VMEM_SPEC, HBM_SPEC] + [VMEM_SPEC] * len(masks),
            out_specs=[VMEM_SPEC] * len(shapes),
            scratch_shapes=[
                pltpu.VMEM((chunks, height, width), f32),
                pltpu.VMEM((height, width), bf16),
                pltpu.VMEM((2, chunks, group, block_len, head_dim), bf16),
                pltpu.SemaphoreType.DMA((2, chunks)),
            ],
            compiler_params=pltpu.CompilerParams(vmem_limit_bytes=32 * MIB),
            cost_estimate=pl.CostEstimate(
                flops=4 * height * tokens * head_dim,
                bytes_accessed=pool_codes.size * 2 // heads,
                transcendentals=height * tokens,
            ),
            name="own_blocks",
        )(query_rows, fresh, pool_rows, *masks)

    *own_parts, log_rows, scale_rows = own(0, tables, length, flat_scales)
    if not general:
        seconds, own_parts, log_rows = lax.optimization_barrier((seconds, own_parts, log_rows))
    for head in range(1, heads):
        own_parts = own_parts + list(own(head, log_rows, scale_rows))

    if not general:
        held = {k: second for k, second in seconds.items() if k}
        for k in held:
            seconds[k ^ 1] = swap(held[k], 1)
        arrived = [held[k] for k in held] + firsts[::-1] + [seconds[0]]
        where = {k: i for i, k in enumerate(held)}
        where[0] = len(arrived) - 1
        places = [(len(held) + instances - 1 - k, 0) for k in range(instances)]
        for k in range(instances):
            if k == 1:
                places.append((places[1][0], 1))
            elif k in where:
                places.append((where[k], 0))
            else:
                places.append((len(arrived), 0))
                arrived.append(seconds[k])

    arrival_bytes = 6 * heads * height * slots * block_len + 2 * 12 * height * head_dim * heads
    arrival_bytes += 2 * slots * sent_bytes + 4 * requests * slots * block_len
    out, moved_to, more = pl.pallas_call(
        functools.partial(
            arrival_kernel, (pool, heads, rows, block_len, spans, listed, factor), places
        ),
        out_shape=[
            jax.ShapeDtypeStruct((requests, heads, rows, head_dim), bf16),
            jax.ShapeDtypeStruct((1, listed), jnp.int32),
            jax.ShapeDtypeStruct((1,), jnp.int32),
        ],
        in_specs=[VMEM_SPEC] * (3 + 3 * heads + len(arrived)),
        out_specs=[VMEM_SPEC, VMEM_SPEC, SMEM_SPEC],
        scratch_shapes=[
            pltpu.VMEM((requests, slots * block_len), f32),
            pltpu.VMEM((heads, height, slots * block_len), f32),
            pltpu.VMEM((heads, height, slots * block_len), bf16),
        ],
        compiler_params=pltpu.CompilerParams(vmem_limit_bytes=arrival_bytes + 8 * MIB),
        cost_estimate=pl.CostEstimate(
            flops=4 * heads * height * slots * block_len * head_dim,
            bytes_accessed=slots * sent_bytes,
            transcendentals=heads * height * slots * block_len,
        ),
        name="arrived_blocks",
    )(query_rows, tables, length, *own_parts, *arrived)
    out = out.reshape(requests, q_heads, steps, head_dim).transpose(0, 2, 1, 3)
    return out.reshape(requests, steps, q_heads * head_dim), moved_to, more


def shards(*args):
    out, moved_to, more = attend(False, *args)
    _, out = lax.while_loop(
        lambda state: state[0] > 1,
        lambda state: (jnp.int32(0), attend(True, *args)[0]),
        (more[0], out),
    )
    return out, moved_to


def solution(mesh):
    in_specs = (
        P(("groups", "inst"), None, "tp", None),
        P(("groups", "inst"), None, None, "tp", None),
        P(("groups", "inst"), None, "tp", None, None),
        P(("groups", "inst"), None, "tp"),
        P(("groups", "inst"), None),
        P(("groups", "inst")),
        P(("groups", "inst"), None),
        P(("groups", "inst"), None),
    )
    out_specs = (P(("groups", "inst"), None, "tp"), P(("groups", "inst"), None))
    return jax.shard_map(shards, mesh=mesh, in_specs=in_specs, out_specs=out_specs, check_vma=False)
```

```python
import functools
import math

import jax
import jax.numpy as jnp
from jax import lax
from jax.experimental import pallas as pl
from jax.experimental.pallas import tpu as pltpu
from jax.sharding import PartitionSpec as P

CAP = 2
EXTRA = 16
NEVER = -1e30
LOG2E = math.log2(math.e)
MIB = 1 << 20
SMEM_SPEC = pl.BlockSpec(memory_space=pltpu.SMEM)
VMEM_SPEC = pl.BlockSpec(memory_space=pltpu.VMEM)
HBM_SPEC = pl.BlockSpec(memory_space=pltpu.HBM)
NT = (((1,), (1,)), ((), ()))


def loop(count, body, init):
    if count <= 8:
        for i in range(count):
            init = body(i, init)
        return init
    return lax.fori_loop(0, count, body, init)


def pack_kernel(dims, dest_ref, block_ref, scale_ref, pool_ref, *refs):
    instances, listed, heads, pool, copies = dims
    send_refs, (index_ref, extra_ref, held_ref, in_sems, out_sems) = refs[:-5], refs[-5:]
    code_rows = held_ref.shape[1] - EXTRA
    me = lax.axis_index("inst")
    for entry in range(CAP * instances + 1):
        index_ref[entry] = 0

    def place(m, carry):
        dest = dest_ref[0, m]
        rank = loop(
            listed,
            lambda m2, n: n + jnp.where((dest_ref[0, m2] == dest) & (m2 < m), 1, 0),
            jnp.int32(0),
        )
        entry = jnp.bitwise_xor(dest, me) + jnp.where(rank > 0, instances, 0)
        index_ref[entry] = block_ref[0, m]
        index_ref[jnp.where(rank > 0, CAP * instances, entry)] = block_ref[0, m]
        return carry

    loop(listed, place, 0)
    loads, stores = [], []
    for i, (entry, _) in enumerate(copies):
        loads.append(
            pltpu.make_async_copy(
                pool_ref.at[index_ref[entry]], held_ref.at[i, pl.ds(0, code_rows)], in_sems.at[i]
            )
        )
        loads[i].start()
    lane = lax.broadcasted_iota(jnp.int32, (1, 128), 1)

    def spell(m, row):
        return jnp.where(lane == m, dest_ref[0, m].astype(jnp.float32), row)

    extra_ref[...] = jnp.zeros_like(extra_ref)
    extra_ref[2 * heads : 2 * heads + 1, :] = loop(
        listed, spell, jnp.zeros((1, 128), jnp.float32)
    )
    scales = [
        [scale_ref[part, h : h + 1, :].astype(jnp.float32) for h in range(heads)]
        for part in range(2)
    ]
    column = lax.broadcasted_iota(jnp.int32, (1, pool), 1)
    for i, (entry, _) in enumerate(copies):
        for part in range(2):
            for h in range(heads):
                one = jnp.where(column == index_ref[entry], scales[part][h], 0.0)
                row = part * heads + h
                extra_ref[row : row + 1, :] = jnp.broadcast_to(
                    jnp.sum(one, axis=1, keepdims=True), (1, 128)
                )
        held_ref[i, pl.ds(code_rows, EXTRA)] = extra_ref[...].astype(jnp.bfloat16)
    for i, (_, targets) in enumerate(copies):
        loads[i].wait()
        for output, row in targets:
            stores.append(
                pltpu.make_async_copy(
                    held_ref.at[i], send_refs[output].at[row], out_sems.at[len(stores)]
                )
            )
            stores[-1].start()
    for store in stores:
        store.wait()


def split(value, size):
    assert size & (size - 1) == 0
    return lax.shift_right_logical(value, size.bit_length() - 1), value & (size - 1)


def count_log(tables, length, ids, block_len, spans, store):
    requests, width = tables.shape[0], ids.shape[1]
    whole, rest = split(length, block_len)
    whole = jnp.broadcast_to(whole, (requests, width))
    full = jnp.zeros((requests, width), jnp.float32)
    part = jnp.zeros((requests, width), jnp.float32)
    for e in range(spans):
        hit = jnp.broadcast_to(tables[:, e : e + 1], (requests, width)) == ids
        full = full + jnp.where(hit & (whole > e), 1.0, 0.0)
        part = part + jnp.where(hit & (whole == e), 1.0, 0.0)

    def log2(count):
        return jnp.where(count > 0, jnp.log(jnp.maximum(count, 1.0)) * LOG2E, NEVER)

    beyond, within = log2(full), log2(full + part)
    shape = (requests, block_len)
    inside = lax.broadcasted_iota(jnp.int32, shape, 1) < jnp.broadcast_to(rest, shape)
    if width % 16:
        for b in range(width):
            store(
                b,
                jnp.where(
                    inside,
                    jnp.broadcast_to(within[:, b : b + 1], shape),
                    jnp.broadcast_to(beyond[:, b : b + 1], shape),
                ),
            )
        return
    both = jnp.concatenate([within, beyond], axis=0)
    high = both.astype(jnp.bfloat16)
    low = (both - high.astype(jnp.float32)).astype(jnp.bfloat16)
    terms = jnp.concatenate([high, low], axis=0)
    row = lax.broadcasted_iota(jnp.int32, (width, block_len), 0)
    for b in range(0, width, 2):
        spots = jnp.concatenate(
            [jnp.where(row == b + i, 1.0, 0.0).astype(jnp.bfloat16) for i in range(2)], axis=1
        )
        spread_out = jnp.dot(terms, spots, preferred_element_type=jnp.float32)
        value = spread_out[: 2 * requests] + spread_out[2 * requests :]
        for i in range(2):
            at = slice(i * block_len, (i + 1) * block_len)
            store(b + i, jnp.where(inside, value[:requests, at], value[requests:, at]))


def score_tiles(query, keys, log_ref, scale_row, rows, store):
    height, wide = min(512, query.shape[0]), min(256, keys.shape[0])
    for top in range(0, query.shape[0], height):
        for left in range(0, keys.shape[0], wide):
            part = lax.dot_general(
                query[top : top + height],
                keys[left : left + wide],
                NT,
                preferred_element_type=jnp.float32,
            )
            scale = scale_row[:, left : left + wide]
            for r in range(height // rows):
                request = top // rows + r
                store(
                    request * rows,
                    left,
                    part[r * rows : (r + 1) * rows] * scale
                    + log_ref[request : request + 1, left : left + wide],
                )


def lane_fold(value, op):
    parts = [value[:, i : i + 128] for i in range(0, value.shape[1], 128)]
    while len(parts) > 1:
        parts = [
            op(parts[i], parts[i + 1]) if i + 1 < len(parts) else parts[i]
            for i in range(0, len(parts), 2)
        ]
    return parts[0]


def spread(column, width):
    return jnp.concatenate([column] * (width // 128), axis=1)


def own_kernel(
    dims, q_ref, fresh_ref, pool_ref, *refs
):
    if dims[0] == 0:
        tables_ref, length_ref, scale_ref, acc_ref, top_ref, total_ref, log_ref, row_ref = refs[:8]
    else:
        log_ref, row_ref, acc_ref, top_ref, total_ref = refs[:5]
    t_ref, p_ref, codes_ref, sems = refs[-4:]
    head, pool, heads, rows, steps, block_len, spans, factor, group = dims
    chunks = pool // group
    height, head_dim = q_ref.shape[1:]
    width = group * block_len

    def load(part, chunk):
        return pltpu.make_async_copy(
            pool_ref.at[
                pl.ds(chunk * group, group), pl.ds((part * heads + head) * block_len, block_len)
            ],
            codes_ref.at[part, chunk],
            sems.at[part, chunk],
        )

    for part in range(2):
        for chunk in range(chunks):
            load(part, chunk).start()

    if head == 0:
        ids = lax.broadcasted_iota(jnp.int32, (1, pool), 1)

        def store_log(b, value):
            lane = (b % group) * block_len
            log_ref[b // group, :, lane : lane + block_len] = value

        count_log(tables_ref[...], length_ref[...], ids, block_len, spans, store_log)
        for b in range(pool):
            lane = (b % group) * block_len
            row_ref[b // group, :, lane : lane + block_len] = jnp.broadcast_to(
                scale_ref[:, b : b + 1], (2 * heads, block_len)
            )
    shape = (height, fresh_ref.shape[2])
    row = lax.broadcasted_iota(jnp.int32, shape, 0)
    col = lax.broadcasted_iota(jnp.int32, shape, 1)
    (request, row_step), (owner, step) = split(row, rows), split(col, steps)
    seen = (request == owner) & (split(row_step, steps)[1] >= step)
    new_score = lax.dot_general(
        q_ref[head], fresh_ref[0, head], NT, preferred_element_type=jnp.float32
    )
    new_score = jnp.where(seen, new_score * (factor * LOG2E), -jnp.inf)
    acc_ref[...] = new_score
    top_ref[...] = lane_fold(new_score, jnp.maximum)

    def score(chunk, carry):
        load(0, chunk).wait()

        def store(row, lane, value):
            t_ref[chunk, row : row + rows, lane : lane + value.shape[1]] = value

        score_tiles(
            q_ref[head],
            codes_ref[0, chunk].reshape(width, head_dim),
            log_ref.at[chunk],
            row_ref[chunk, head : head + 1, :] * (factor * LOG2E),
            rows,
            store,
        )
        for row in range(0, height, rows):
            at = pl.ds(row, rows)
            top_ref[at] = jnp.maximum(top_ref[at], lane_fold(t_ref[chunk, at], jnp.maximum))
        return carry

    lax.fori_loop(0, chunks, score, 0)

    top = jnp.broadcast_to(jnp.max(top_ref[...], axis=1, keepdims=True), (height, 128))
    top_ref[...] = top
    weight = jnp.exp2(acc_ref[...] - spread(top, acc_ref.shape[1]))
    total_ref[...] = lane_fold(weight, jnp.add)
    acc_ref[...] = jnp.dot(
        weight.astype(jnp.bfloat16), fresh_ref[1, head], preferred_element_type=jnp.float32
    )

    def apply(chunk, carry):
        load(1, chunk).wait()
        scale = row_ref[chunk, heads + head : heads + head + 1, :]
        for row in range(0, height, rows):
            at = pl.ds(row, rows)
            for lane in range(0, width, 1024):
                part = slice(lane, lane + 1024)
                weight = jnp.exp2(t_ref[chunk, at, part] - spread(top_ref[at], 1024))
                total_ref[at] += lane_fold(weight, jnp.add)
                p_ref[at, part] = (weight * scale[:, part]).astype(jnp.bfloat16)
        acc_ref[...] += jnp.dot(
            p_ref[...],
            codes_ref[1, chunk].reshape(width, head_dim),
            preferred_element_type=jnp.float32,
        )
        return carry

    lax.fori_loop(0, chunks, apply, 0)


def arrival_ids(me, pool, lists, listed):
    instances = len(lists)
    lane = lax.broadcasted_iota(jnp.int32, (1, 128), 1)
    counts = [
        jnp.sum(
            jnp.where((row == me.astype(jnp.float32)) & (lane < listed), 1.0, 0.0),
            axis=1,
            keepdims=True,
        )
        for row in lists
    ]
    slot = lax.broadcasted_iota(jnp.int32, (1, instances * CAP), 1)
    ids = jnp.full(slot.shape, -1.0)
    for k in range(instances):
        first = jnp.full((1, 1), float(pool))
        for j in range(instances):
            lower = jnp.bitwise_xor(me, j) < jnp.bitwise_xor(me, k)
            first = first + jnp.where(lower, counts[j], 0.0)
        for r in range(CAP):
            name = jnp.where(counts[k] > r, first + r, -1.0)
            ids = jnp.where(slot == r * instances + k, jnp.broadcast_to(name, slot.shape), ids)
    moved = jnp.full((1, 128), float(pool))
    for j in range(instances):
        for m in range(listed):
            same = jnp.broadcast_to(lists[j][:, m : m + 1], (1, 128)) == lists[0]
            ahead = jnp.bitwise_xor(me, j) < me if j else lane > m
            moved = moved + jnp.where(same & ahead, 1.0, 0.0)
    more = jnp.zeros((1, 128))
    for row in lists:
        again = jnp.zeros((1, 128))
        for m in range(listed):
            same = jnp.broadcast_to(row[:, m : m + 1], (1, 128)) == row
            again = again + jnp.where(same & (lane > m) & (lane < listed), 1.0, 0.0)
        more = jnp.maximum(more, jnp.sum(again, axis=1, keepdims=True))
    return ids.astype(jnp.int32), moved[:, :listed].astype(jnp.int32), more


def arrival_kernel(dims, places, q_ref, tables_ref, length_ref, *refs):
    pool, heads, rows, block_len, spans, listed, factor = dims
    own_refs, code_refs = refs[: 3 * heads], refs[3 * heads : -6]
    out_ref, moved_ref, more_ref, log_ref, t_ref, p_ref = refs[-6:]
    height = q_ref.shape[1]
    width = 2 * block_len
    extra = 2 * heads * block_len
    slots = [(code_refs[array], row) for array, row in places]
    pairs = len(slots) // 2

    def pair(i, part, h):
        at = pl.ds((part * heads + h) * block_len, block_len)
        return jnp.concatenate([ref[r, at] for ref, r in slots[2 * i : 2 * i + 2]], axis=0)

    lists, scale_rows = [], []
    for ref, r in slots:
        values = ref[r, pl.ds(extra, EXTRA)].astype(jnp.float32)
        scale_rows.append(values)
        if len(lists) < len(slots) // CAP:
            lists.append(values[2 * heads : 2 * heads + 1])

    def scale_row(row):
        return jnp.concatenate([values[row : row + 1] for values in scale_rows], axis=1)

    ids, moved_ref[...], more = arrival_ids(lax.axis_index("inst"), pool, lists, listed)
    more_ref[0] = jnp.max(more).astype(jnp.int32)

    def store_log(b, value):
        log_ref[:, b * block_len : (b + 1) * block_len] = value

    count_log(tables_ref[...], length_ref[...], ids, block_len, spans, store_log)
    for h in range(heads):
        key_scale = scale_row(h) * (factor * LOG2E)
        for i in range(pairs):
            left = i * width

            def store(row, lane, value, h=h, left=left):
                t_ref[h, row : row + rows, left + lane : left + lane + value.shape[1]] = value

            score_tiles(
                q_ref[h],
                pair(i, 0, h),
                log_ref.at[:, left : left + width],
                key_scale[:, left : left + width],
                rows,
                store,
            )
    for h in range(heads):
        acc_ref, top_ref, total_ref = own_refs[3 * h : 3 * h + 3]
        scale = scale_row(heads + h)
        for row in range(0, height, rows):
            at = pl.ds(row, rows)
            score = t_ref[h, at]
            own_top = top_ref[at]
            top = jnp.maximum(
                own_top, jnp.max(lane_fold(score, jnp.maximum), axis=1, keepdims=True)
            )
            weight = jnp.exp2(score - spread(top, score.shape[1]))
            keep = jnp.exp2(own_top - top)
            total = jnp.sum(
                total_ref[at] * keep + lane_fold(weight, jnp.add), axis=1, keepdims=True
            )
            p_ref[h, at] = (weight * scale).astype(jnp.bfloat16)
            t_ref[h, at, 0:128] = keep
            t_ref[h, at, 128:256] = jnp.broadcast_to(1.0 / total, keep.shape)
        mixed = acc_ref[...] * t_ref[h, :, 0:128]
        for i in range(pairs):
            mixed = mixed + jnp.dot(
                p_ref[h, :, i * width : (i + 1) * width],
                pair(i, 1, h),
                preferred_element_type=jnp.float32,
            )
        result = (mixed * t_ref[h, :, 128:256]).astype(jnp.bfloat16)
        out_ref[:, h] = result.reshape(height // rows, rows, result.shape[-1])


def attend(
    general, queries, new_kv, pool_codes, pool_scales, tables, ctx_len, mig_block, mig_dest
):
    instances = lax.axis_size("inst")
    pool = pool_codes.shape[0]
    requests, steps, q_heads, head_dim = queries.shape
    heads = new_kv.shape[3]
    per_head = q_heads // heads
    spans = tables.shape[1]
    block_len = pool_codes.shape[3]
    listed = mig_dest.shape[1]
    factor = head_dim ** (-0.5)
    rows = per_head * steps
    height = requests * rows
    slots = instances * CAP
    group = 24
    f32, bf16 = jnp.float32, jnp.bfloat16
    code_rows = 2 * heads * block_len
    pool_rows = pool_codes.reshape(pool, code_rows, head_dim)
    sent_shape = (code_rows + EXTRA, head_dim)
    sent_bytes = 2 * math.prod(sent_shape)
    part_scales = jnp.transpose(pool_scales, (1, 2, 0))
    assert instances & (instances - 1) == 0 and 2 * heads < EXTRA and head_dim == 128

    def pack(sizes, copies):
        stores = sum(len(targets) for _, targets in copies)
        return pl.pallas_call(
            functools.partial(pack_kernel, (instances, listed, heads, pool, copies)),
            out_shape=[jax.ShapeDtypeStruct((size,) + sent_shape, bf16) for size in sizes],
            in_specs=[SMEM_SPEC, SMEM_SPEC, VMEM_SPEC, HBM_SPEC],
            out_specs=[HBM_SPEC] * len(sizes),
            scratch_shapes=[
                pltpu.SMEM((CAP * instances + 1,), jnp.int32),
                pltpu.VMEM((EXTRA, head_dim), f32),
                pltpu.VMEM((len(copies),) + sent_shape, bf16),
                pltpu.SemaphoreType.DMA((len(copies),)),
                pltpu.SemaphoreType.DMA((stores,)),
            ],
            compiler_params=pltpu.CompilerParams(vmem_limit_bytes=56 * MIB),
            cost_estimate=pl.CostEstimate(
                flops=0, bytes_accessed=2 * stores * sent_bytes, transcendentals=0
            ),
            name="pack_blocks",
        )(mig_dest, mig_block, part_scales, pool_rows)

    def swap(value, distance):
        return lax.ppermute(value, "inst", [(j, j ^ distance) for j in range(instances)])

    if general:
        send = pack(
            [CAP] * instances,
            [(r * instances + k, [(k, r)]) for k in range(instances) for r in range(CAP)],
        )
        arrived = [swap(send[k], k) for k in range(instances - 1, 0, -1)] + [send[0]]
        places = [(instances - 1 - k, r) for r in range(CAP) for k in range(instances)]
    else:
        any_second = CAP * instances
        (second,) = pack([1], [(any_second, [(0, 0)])])
        seconds = {0: second}
        bit = instances // 2
        while bit > 1:
            for k in list(seconds):
                seconds[k ^ bit] = swap(seconds[k], bit)
            bit //= 2
        mig_dest, second = lax.optimization_barrier((mig_dest, second))
        send = pack(
            [1, 2] + [1] * (instances - 2),
            [(k, [(k, 0)]) for k in list(range(instances))[::-1]] + [(any_second, [(1, 1)])],
        )
        firsts = [send[0]] + [swap(send[k], k) for k in range(1, instances)]
    part_scales, *send = lax.optimization_barrier((part_scales, *send))
    flat_scales = part_scales.reshape(2 * heads, pool).astype(f32)

    query_rows = (
        queries.reshape(requests, steps, heads, per_head, head_dim)
        .transpose(2, 0, 3, 1, 4)
        .reshape(heads, height, head_dim)
    )
    fresh_len = requests * steps
    fresh = new_kv.transpose(2, 3, 0, 1, 4).reshape(2, heads, fresh_len, head_dim)
    fresh = jnp.pad(fresh, ((0, 0), (0, 0), (0, -fresh_len % 128), (0, 0)))
    assert fresh.shape[2] == head_dim
    length = ctx_len[:, None]
    width = group * block_len
    chunks = pool // group
    tokens = pool * block_len

    mask_shapes = [(chunks, requests, width), (chunks, 2 * heads, width)]

    def own(head, *masks):
        shapes = [(height, head_dim)] * 3 + ([] if head else mask_shapes)
        return pl.pallas_call(
            functools.partial(
                own_kernel, (head, pool, heads, rows, steps, block_len, spans, factor, group)
            ),
            out_shape=[jax.ShapeDtypeStruct(shape, f32) for shape in shapes],
            in_specs=[VMEM_SPEC, VMEM_SPEC, HBM_SPEC] + [VMEM_SPEC] * len(masks),
            out_specs=[VMEM_SPEC] * len(shapes),
            scratch_shapes=[
                pltpu.VMEM((chunks, height, width), f32),
                pltpu.VMEM((height, width), bf16),
                pltpu.VMEM((2, chunks, group, block_len, head_dim), bf16),
                pltpu.SemaphoreType.DMA((2, chunks)),
            ],
            compiler_params=pltpu.CompilerParams(vmem_limit_bytes=32 * MIB),
            cost_estimate=pl.CostEstimate(
                flops=4 * height * tokens * head_dim,
                bytes_accessed=pool_codes.size * 2 // heads,
                transcendentals=height * tokens,
            ),
            name="own_blocks",
        )(query_rows, fresh, pool_rows, *masks)

    *own_parts, log_rows, scale_rows = own(0, tables, length, flat_scales)
    if not general:
        seconds, own_parts, log_rows = lax.optimization_barrier((seconds, own_parts, log_rows))
    for head in range(1, heads):
        own_parts = own_parts + list(own(head, log_rows, scale_rows))

    if not general:
        held = {k: second for k, second in seconds.items() if k}
        for k in held:
            seconds[k ^ 1] = swap(held[k], 1)
        arrived = [held[k] for k in held] + firsts[::-1] + [seconds[0]]
        where = {k: i for i, k in enumerate(held)}
        where[0] = len(arrived) - 1
        places = [(len(held) + instances - 1 - k, 0) for k in range(instances)]
        for k in range(instances):
            if k == 1:
                places.append((places[1][0], 1))
            elif k in where:
                places.append((where[k], 0))
            else:
                places.append((len(arrived), 0))
                arrived.append(seconds[k])

    arrival_bytes = 6 * heads * height * slots * block_len + 2 * 12 * height * head_dim * heads
    arrival_bytes += 2 * slots * sent_bytes + 4 * requests * slots * block_len
    out, moved_to, more = pl.pallas_call(
        functools.partial(
            arrival_kernel, (pool, heads, rows, block_len, spans, listed, factor), places
        ),
        out_shape=[
            jax.ShapeDtypeStruct((requests, heads, rows, head_dim), bf16),
            jax.ShapeDtypeStruct((1, listed), jnp.int32),
            jax.ShapeDtypeStruct((1,), jnp.int32),
        ],
        in_specs=[VMEM_SPEC] * (3 + 3 * heads + len(arrived)),
        out_specs=[VMEM_SPEC, VMEM_SPEC, SMEM_SPEC],
        scratch_shapes=[
            pltpu.VMEM((requests, slots * block_len), f32),
            pltpu.VMEM((heads, height, slots * block_len), f32),
            pltpu.VMEM((heads, height, slots * block_len), bf16),
        ],
        compiler_params=pltpu.CompilerParams(vmem_limit_bytes=arrival_bytes + 8 * MIB),
        cost_estimate=pl.CostEstimate(
            flops=4 * heads * height * slots * block_len * head_dim,
            bytes_accessed=slots * sent_bytes,
            transcendentals=heads * height * slots * block_len,
        ),
        name="arrived_blocks",
    )(query_rows, tables, length, *own_parts, *arrived)
    out = out.reshape(requests, q_heads, steps, head_dim).transpose(0, 2, 1, 3)
    return out.reshape(requests, steps, q_heads * head_dim), moved_to, more


def shards(*args):
    out, moved_to, more = attend(False, *args)
    _, out = lax.while_loop(
        lambda state: state[0] > 1,
        lambda state: (jnp.int32(0), attend(True, *args)[0]),
        (more[0], out),
    )
    return out, moved_to


def solution(mesh):
    in_specs = (
        P(("groups", "inst"), None, "tp", None),
        P(("groups", "inst"), None, None, "tp", None),
        P(("groups", "inst"), None, "tp", None, None),
        P(("groups", "inst"), None, "tp"),
        P(("groups", "inst"), None),
        P(("groups", "inst")),
        P(("groups", "inst"), None),
        P(("groups", "inst"), None),
    )
    out_specs = (P(("groups", "inst"), None, "tp"), P(("groups", "inst"), None))
    return jax.shard_map(shards, mesh=mesh, in_specs=in_specs, out_specs=out_specs, check_vma=False)
```
